32 devices in a mesh: obj: 4 (over z), dp: 2 (over core), tensor: 4 (over y, x).
Axes of the slice: x: 2, y: 2, z: 4, core: 2. Of those that a mesh axis runs over, the one named last changes fastest.
Arguments:
- tokens: bfloat16 [16, 1024, 2048], P(('obj', 'dp')), may hold values from -6 to 6
- cotangent: bfloat16 [16, 1024, 2048], P(('obj', 'dp')), may hold values from -6 to 6
- segment_ids: int32 [16, 1024], P(('obj', 'dp')), may hold values from 0 to 3, never falling along the last dimension, each value on 1 to 512 neighbouring positions
- mlm_mask: int32 [16, 1024], replicated, may hold values 0 or 1
- glm_prefix: int32 [16], replicated, may hold values from 256 to 512
- glm_span: int32 [16], replicated, may hold values from 128 to 256
- qkv_weight: bfloat16 [2048, 6144], P(None, 'tensor'), may hold values from -0.125 to 0.125
- out_weight: bfloat16 [2048, 2048], P('tensor'), may hold values from -6 to 6
- gate_weight: bfloat16 [2048, 5632], P(None, 'tensor'), may hold values from -0.125 to 0.125
- up_weight: bfloat16 [2048, 5632], P(None, 'tensor'), may hold values from -0.125 to 0.125
- down_weight: bfloat16 [5632, 2048], P('tensor'), may hold values from -0.625 to 0.625
- norm1_gain: float32 [2048], replicated, may hold values from 0.5 to 1.5
- norm1_bias: float32 [2048], replicated, may hold values from -1.8 to 1.8
- norm2_gain: float32 [2048], replicated, may hold values from 0.5 to 1.5
- norm2_bias: float32 [2048], replicated, may hold values from -1.8 to 1.8
Outputs:
- activations: bfloat16 [16, 1024, 2048], P(('obj', 'dp'))
- input_grad: bfloat16 [16, 1024, 2048], P(('obj', 'dp'))
- qkv_grad: float32 [2048, 6144], P(None, 'tensor')
- out_grad: float32 [2048, 2048], P('tensor')
- gate_grad: float32 [2048, 5632], P(None, 'tensor')
- up_grad: float32 [2048, 5632], P(None, 'tensor')
- down_grad: float32 [5632, 2048], P('tensor')
- norm1_gain_grad: float32 [2048], replicated
- norm1_bias_grad: float32 [2048], replicated
- norm2_gain_grad: float32 [2048], replicated
- norm2_bias_grad: float32 [2048], replicated
The draws below stay inside these ranges and needn't reach their ends.
Inputs may be any that keep to these rules, and one draw needn't show every extreme that they name: `segment_ids`: each row's segment numbers never fall; a segment holds 1 to 512 positions.
All inputs are finite; a program needn't handle non-finite values.
Results may differ from the reference program's by a relative error of at most 0.025.
Values may be sent and summed in bfloat16 or wider, within the bound.
No kernel may reach another device: no remote copies, remote signals or barrier semaphores. Data moves between devices by JAX's collectives and lax.ppermute only.
A program may use at most 320 MiB of HBM per device.

```python
import math
import jax
import jax.numpy as jnp
import numpy as np
from jax import lax

D = 2048
HEADS = 16
HEAD_DIM = 128
FF = 5632
LEN = 1024
SEQ_DEV = 2
ROWS = 16
N_OBJ = 4
N_DP = 2
N_TENSOR = 4


def plant(values, key, low, high):
    extent = values.shape
    spot = [jax.random.randint(jax.random.fold_in(key, axis), (), 0, extent[axis]) for axis in range(len(extent))]
    values = values.at[tuple(spot)].set(low)
    longest = extent.index(max(extent))
    spot[longest] = (spot[longest] + 1) % extent[longest]
    return values.at[tuple(spot)].set(high)


def levels(key, shape, cuts, least, largest):
    level = 1.0
    for axis_at, blocks in cuts:
        heights = jax.random.uniform(jax.random.fold_in(jax.random.fold_in(key, 6), axis_at), (blocks,), jnp.float32, least / len(cuts), largest / len(cuts))
        level = level * jnp.repeat(jnp.exp(heights), shape[axis_at] // blocks).reshape((-1,) + (1,) * (len(shape) - 1 - axis_at))
    return level


def split_up(number_of, total, bound, skew):
    loads = [(1 << 20) // math.isqrt(grade ** skew) + 1 for grade in range(2, number_of + 1)]
    surplus, given = total - bound - (number_of - 1), [1] * (number_of - 1)
    while surplus > 0:
        free = [i for i in range(number_of - 1) if given[i] < bound]
        whole, budget = sum([loads[i] for i in free]), surplus
        for i in free:
            more = min(bound - given[i], max(1, budget * loads[i] // whole), surplus)
            given[i] = given[i] + more
            surplus = surplus - more
    return np.array([bound] + given)


def uneven_parts(rng, number_of, total, bound, slope):
    if number_of == 2:
        one = jax.random.randint(rng, (), max(1, total - bound), min(bound, total - 1) + 1)
        return jnp.stack([one, total - one])
    tallies = jnp.asarray(split_up(number_of, total, bound, slope), jnp.int32)
    couples = (number_of - 1) // 2
    donor, sink = tallies[1:1 + 2 * couples:2], tallies[2:2 + 2 * couples:2]
    margin = jnp.minimum(donor - 1, bound - sink)
    passed = jax.random.randint(jax.random.fold_in(rng, 1), (couples,), 0, 1 << 20) % (margin + 1)
    tallies = tallies.at[1:1 + 2 * couples:2].set(donor - passed).at[2:2 + 2 * couples:2].set(sink + passed)
    return tallies[jax.random.permutation(jax.random.fold_in(rng, 2), number_of)]


def scatter_about(rng, extent, deviation, reach, cuts=(), kind=jnp.bfloat16):
    level = levels(rng, extent, cuts, -0.22, 0.18) if cuts else 1.0
    array = jax.random.normal(rng, extent, jnp.float32) * deviation * level
    return jnp.minimum(jnp.maximum(array, -reach), reach).astype(kind)


def setup_inputs(seed: int = 0) -> dict:
    key_list = jax.random.split(jax.random.key(seed), 16)
    tokens = scatter_about(key_list[0], (ROWS, LEN, D), 1.0, 6.0, ((0, 8),))
    cotangent = scatter_about(key_list[1], (ROWS, LEN, D), 1.0, 6.0, ((0, 8),))
    segment_ids = jax.vmap(lambda own: jnp.searchsorted(jnp.cumsum(uneven_parts(own, 4, LEN, LEN // 2, 0)), jnp.arange(LEN), side="right"))(jax.random.split(key_list[2], ROWS)).reshape((ROWS, LEN)).astype(jnp.int32)
    mlm_mask = plant((jax.random.randint(key_list[3], (ROWS, LEN), 0, 20) < 3).astype(jnp.int32), jax.random.fold_in(key_list[3], 1), 0, 1)
    glm_prefix = plant(jax.random.randint(key_list[4], (ROWS,), LEN // 4, LEN // 2 + 1), jax.random.fold_in(key_list[4], 1), LEN // 4, (LEN // 2 + 1) - 1).astype(jnp.int32)
    glm_span = plant(jax.random.randint(key_list[5], (ROWS,), LEN // 8, LEN // 4 + 1), jax.random.fold_in(key_list[5], 1), LEN // 8, (LEN // 4 + 1) - 1).astype(jnp.int32)
    qkv_weight = scatter_about(key_list[6], (D, 3 * D), D ** -0.5, 0.125, ((1, 4),))
    out_weight = scatter_about(key_list[7], (D, D), 1 ** -0.5, 6.0, ((0, 4),))
    gate_weight = scatter_about(key_list[8], (D, FF), D ** -0.5, 0.125, ((1, 4),))
    up_weight = scatter_about(key_list[9], (D, FF), D ** -0.5, 0.125, ((1, 4),))
    down_weight = scatter_about(key_list[10], (FF, D), (FF // 64 + 1) ** -0.5, 0.625, ((0, 4),))
    norm1_gain = jnp.clip(1.0 + 0.1 * jax.random.normal(key_list[11], (D,), jnp.float32), 0.5, 1.5)
    norm1_bias = scatter_about(key_list[12], (D,), 0.3, 1.8, (), jnp.float32)
    norm2_gain = jnp.clip(1.0 + 0.1 * jax.random.normal(key_list[13], (D,), jnp.float32), 0.5, 1.5)
    norm2_bias = scatter_about(key_list[14], (D,), 0.3, 1.8, (), jnp.float32)
    return {"tokens": tokens, "cotangent": cotangent, "segment_ids": segment_ids, "mlm_mask": mlm_mask, "glm_prefix": glm_prefix, "glm_span": glm_span, "qkv_weight": qkv_weight, "out_weight": out_weight, "gate_weight": gate_weight, "up_weight": up_weight, "down_weight": down_weight, "norm1_gain": norm1_gain, "norm1_bias": norm1_bias, "norm2_gain": norm2_gain, "norm2_bias": norm2_bias}


@jax.custom_vjp
def low(v):
    return lax.optimization_barrier(v.astype(jnp.bfloat16)).astype(jnp.float32)

@jax.custom_vjp
def low_back(v):
    return v

def low_keep(v):
    return (low(v), None)

def low_pass(kept, grad):
    return (grad,)

def back_keep(v):
    return (v, None)

def back_low(kept, grad):
    return (low(grad),)
low.defvjp(low_keep, low_pass)
low_back.defvjp(back_keep, back_low)
deep_alpha = math.sqrt(48.0)
norm_eps = 1e-05
mask_fill = -1e+30

def highest(left_side, right_side):
    return jnp.dot(left_side, right_side, precision=lax.Precision.HIGHEST)

def rotary_tables(seq_length, head_width):
    half_width = head_width // 2
    frequency = jnp.exp(jnp.arange(half_width, dtype=jnp.float32) * (-2.0 * math.log(10000.0) / head_width))
    angles = jnp.arange(seq_length, dtype=jnp.float32)[:, None] * frequency[None, :]
    angles = jnp.concatenate([angles, angles], axis=1)
    return (jnp.cos(angles), jnp.sin(angles))

def rotate(tensor_in, cosine_table, sine_table):
    half_width = tensor_in.shape[-1] // 2
    turned = jnp.concatenate([-tensor_in[..., half_width:], tensor_in[..., :half_width]], axis=-1)
    return tensor_in * cosine_table + turned * sine_table

def visible(segment_row, prefix_len, span_len, masked_lm):
    positions = jnp.arange(segment_row.shape[0], dtype=jnp.int32)
    query_pos = positions[:, None]
    key_pos = positions[None, :]
    same_segment = segment_row[:, None] == segment_row[None, :]
    open_keys = masked_lm | (key_pos < prefix_len) | (key_pos <= query_pos) & (key_pos < prefix_len + span_len) | (key_pos == query_pos)
    return same_segment & open_keys

def layer_norm(resid, gain_vec, bias_vec):
    row_mean = lax.optimization_barrier(jnp.mean(resid, axis=-1, keepdims=True))
    centered = resid - row_mean
    variance = lax.optimization_barrier(jnp.mean(centered * centered, axis=-1, keepdims=True))
    return centered * lax.rsqrt(variance + norm_eps) * gain_vec + bias_vec

def gelu_gated(gate_in, up_in):
    return jax.nn.gelu(gate_in, approximate=False) * up_in

def forward(weights, tokens_row, allowed):
    qkv_weight, out_weight, gate_weight, up_weight, down_weight, gain_one, bias_one, gain_two, bias_two = weights
    seq_length, model_width = tokens_row.shape
    groups = N_TENSOR
    head_group = HEADS // groups
    ff_group = FF // groups
    cosine_table, sine_table = rotary_tables(seq_length, HEAD_DIM)
    score_scale = 1.0 / math.sqrt(HEAD_DIM)
    maximal_precision_setting = lax.Precision.HIGHEST

    def head_attention(pieces):
        query_block, key_block, value_block = pieces
        raw_scores = low_back(highest(query_block, key_block.T))
        scores = jnp.where(allowed, raw_scores * score_scale, mask_fill)
        row_max = lax.optimization_barrier(jnp.max(scores, axis=1, keepdims=True))
        exponent = jnp.exp(scores - row_max)
        soft_weights = exponent / lax.optimization_barrier(jnp.sum(exponent, axis=1, keepdims=True))
        return low_back(highest(low(soft_weights), value_block))
    replica_tensors = low_back(jnp.broadcast_to(tokens_row, (groups, seq_length, model_width)))
    query_key_value_groups = qkv_weight.reshape(model_width, groups, head_group * 3 * HEAD_DIM).transpose(1, 0, 2)
    projected_rows = low_back(jnp.einsum('tej,tjm->tem', replica_tensors, query_key_value_groups, precision=maximal_precision_setting))
    projected_rows = projected_rows.reshape(groups, seq_length, head_group, 3, HEAD_DIM).transpose(0, 2, 3, 1, 4)
    projected_rows = projected_rows.reshape(HEADS, 3, seq_length, HEAD_DIM)
    queries = low(rotate(projected_rows[:, 0], cosine_table, sine_table))
    keys = low(rotate(projected_rows[:, 1], cosine_table, sine_table))
    values = low(projected_rows[:, 2])
    attended = low(lax.map(jax.checkpoint(head_attention), (queries, keys, values)))
    flattened_heads = attended.reshape(groups, head_group, seq_length, HEAD_DIM).transpose(0, 2, 1, 3)
    flattened_heads = flattened_heads.reshape(groups, seq_length, head_group * HEAD_DIM)
    output_weight_groups = out_weight.reshape(groups, head_group * HEAD_DIM, model_width)
    attention_pieces_list = jnp.einsum('tur,trw->tuw', flattened_heads, output_weight_groups, precision=maximal_precision_setting)
    attn_branch = low_back(lax.optimization_barrier(jnp.sum(low(attention_pieces_list), axis=0)))
    resid_one = deep_alpha * tokens_row + attn_branch
    hidden = layer_norm(resid_one, gain_one, bias_one)
    hidden_copies = low_back(jnp.broadcast_to(low(hidden), (groups, seq_length, model_width)))
    gate_groups = gate_weight.reshape(model_width, groups, ff_group).transpose(1, 0, 2)
    up_groups = up_weight.reshape(model_width, groups, ff_group).transpose(1, 0, 2)
    gate_part = low_back(jnp.einsum('gld,gdf->glf', hidden_copies, gate_groups, precision=maximal_precision_setting))
    up_part = low_back(jnp.einsum('gld,gdf->glf', hidden_copies, up_groups, precision=maximal_precision_setting))
    activated = low(gelu_gated(gate_part, up_part))
    down_groups = down_weight.reshape(groups, ff_group, model_width)
    ffn_partials = jnp.einsum('glf,gfd->gld', activated, down_groups, precision=maximal_precision_setting)
    ffn_branch = low_back(lax.optimization_barrier(jnp.sum(low(ffn_partials), axis=0)))
    resid_two = deep_alpha * hidden + ffn_branch
    return layer_norm(resid_two, gain_two, bias_two)

def reference(tokens, cotangent, segment_ids, mlm_mask, glm_prefix, glm_span, qkv_weight, out_weight, gate_weight, up_weight, down_weight, norm1_gain, norm1_bias, norm2_gain, norm2_bias):
    weights = tuple((matrix.astype(jnp.float32) for matrix in (qkv_weight, out_weight, gate_weight, up_weight, down_weight, norm1_gain, norm1_bias, norm2_gain, norm2_bias)))
    row_count = tokens.shape[0]
    row_ids = jnp.arange(row_count, dtype=jnp.int32)
    masked_rows = row_ids < SEQ_DEV * N_DP * (N_OBJ // 2)
    counts = jnp.where(masked_rows, lax.optimization_barrier(jnp.sum(mlm_mask, axis=1)), glm_span).astype(jnp.float32)
    row_weight = counts * row_count / jnp.sum(counts)

    def one_row(totals, pieces):
        tokens_row, cotangent_row, segment_row, prefix_len, span_len, masked_lm, weight_row = pieces
        allowed = visible(segment_row, prefix_len, span_len, masked_lm)
        result, pullback = jax.vjp(lambda params, inputs: forward(params, inputs, allowed), weights, tokens_row.astype(jnp.float32))
        gradients, input_grad = pullback(cotangent_row.astype(jnp.float32))
        totals = jax.tree.map(lambda running, fresh_grad: running + weight_row * fresh_grad, totals, gradients)
        return (totals, (result.astype(jnp.bfloat16), (weight_row * input_grad).astype(jnp.bfloat16)))
    empty = jax.tree.map(jnp.zeros_like, weights)
    totals, (activations, input_grads) = lax.scan(one_row, empty, (tokens, cotangent, segment_ids, glm_prefix, glm_span, masked_rows, row_weight))
    return (activations, input_grads, totals[0], totals[1], totals[2], totals[3], totals[4], totals[5], totals[6], totals[7], totals[8])
```

```python
import functools
import math

import jax
import jax.numpy as jnp
from jax import lax
from jax.experimental import pallas as pl
from jax.experimental.pallas import tpu as pltpu
from jax.sharding import PartitionSpec as P

HEAD_DIM = 128
deep_alpha = math.sqrt(48.0)
norm_eps = 1e-05
mask_fill = -1e30
score_scale = 1.0 / math.sqrt(HEAD_DIM)
MIB = 1024 * 1024
BF = jnp.bfloat16
F32 = jnp.float32
ANY = pl.ANY


def mm(a, b):
    return lax.dot_general(a, b, (((1,), (0,)), ((), ())), preferred_element_type=F32)


def mm_nt(a, b):
    return lax.dot_general(a, b, (((1,), (1,)), ((), ())), preferred_element_type=F32)


def mm_tn(a, b):
    return lax.dot_general(a, b, (((0,), (0,)), ((), ())), preferred_element_type=F32)


def params(mib, grid_rank=1):
    return pltpu.CompilerParams(
        vmem_limit_bytes=mib * MIB, dimension_semantics=("arbitrary",) * grid_rank
    )


def cost(flops, nbytes, trans=0):
    return pl.CostEstimate(flops=int(flops), bytes_accessed=int(nbytes), transcendentals=int(trans))


def const_spec(shape):
    zeros = (0,) * len(shape)
    return pl.BlockSpec(shape, lambda *_: zeros, pipeline_mode=pl.Buffered(1))


def rotary_tables(seq_length):
    half_width = HEAD_DIM // 2
    frequency = jnp.exp(
        jnp.arange(half_width, dtype=F32) * (-2.0 * math.log(10000.0) / HEAD_DIM)
    )
    angles = jnp.arange(seq_length, dtype=F32)[:, None] * frequency[None, :]
    sine = jnp.sin(angles)
    cosine = jnp.cos(angles)
    return jnp.concatenate([cosine, cosine], axis=1), jnp.concatenate([-sine, sine], axis=1)


def fill_bias(info_ref, segc_ref, segr_ref, bias_ref, tile):
    length = bias_ref.shape[0]
    prefix, limit = info_ref[1], info_ref[2]

    def one(step, carry):
        rows = pl.ds(pl.multiple_of(step * tile, tile), tile)
        key_pos = lax.broadcasted_iota(jnp.int32, (tile, length), 0) + step * tile
        query_pos = lax.broadcasted_iota(jnp.int32, (tile, length), 1)
        same = segc_ref[rows, :] == segr_ref[...]
        open_keys = (
            (key_pos < prefix)
            | ((key_pos <= query_pos) & (key_pos < limit))
            | (key_pos == query_pos)
        )
        bias_ref[rows, :] = jnp.where(same & open_keys, 0.0, mask_fill)
        return carry

    lax.fori_loop(0, length // tile, one, 0)


def attn_fwd_kernel(
    info_ref, x_ref, w_ref, cos_ref, sin_ref, segc_ref, segr_ref, qkv_ref, ol_ref, lse_ref, bias_ref, tile
):
    length = x_ref.shape[0]

    @pl.when(pl.program_id(0) == 0)
    def _():
        fill_bias(info_ref, segc_ref, segr_ref, bias_ref, tile)

    for step in range(length // tile):
        rows = pl.ds(step * tile, tile)
        proj = mm(x_ref[rows, :], w_ref[...])
        cosine, sine = cos_ref[rows, :], sin_ref[rows, :]
        for part in range(2):
            piece = proj[:, part * HEAD_DIM : (part + 1) * HEAD_DIM]
            turned = piece * cosine + pltpu.roll(piece, HEAD_DIM // 2, 1) * sine
            qkv_ref[rows, part * HEAD_DIM : (part + 1) * HEAD_DIM] = turned.astype(BF)
        qkv_ref[rows, 2 * HEAD_DIM :] = proj[:, 2 * HEAD_DIM :].astype(BF)
    keys = qkv_ref[:, HEAD_DIM : 2 * HEAD_DIM]
    values_t = qkv_ref[:, 2 * HEAD_DIM :].astype(F32).T.astype(BF)
    for step in range(length // tile):
        rows = pl.ds(step * tile, tile)
        queries = qkv_ref[rows, :HEAD_DIM]
        scores = mm_nt(keys, queries) * score_scale + bias_ref[:, rows]
        top = jnp.max(scores, axis=0, keepdims=True)
        exponent = jnp.exp(scores - top)
        total = jnp.sum(exponent, axis=0, keepdims=True)
        attended = mm(values_t, exponent.astype(BF)) * (1.0 / total)
        ol_ref[rows, :] = attended.T.astype(BF)
        lse_ref[:, rows] = top + jnp.log(total)


def attn_fwd(info, row, tokens, qkv_weight, cosine, sine, segc, segr):
    _, length, width = tokens.shape
    heads = qkv_weight.shape[1] // (3 * HEAD_DIM)
    tile = min(256, length)
    grid_spec = pltpu.PrefetchScalarGridSpec(
        num_scalar_prefetch=1,
        grid=(heads,),
        in_specs=[
            pl.BlockSpec((None, length, width), lambda h, *_: (row, 0, 0), pipeline_mode=pl.Buffered(1)),
            pl.BlockSpec((width, 3 * HEAD_DIM), lambda h, *_: (0, h)),
            const_spec((length, HEAD_DIM)),
            const_spec((length, HEAD_DIM)),
            const_spec((length, 1)),
            const_spec((1, length)),
        ],
        out_specs=[
            pl.BlockSpec((length, 3 * HEAD_DIM), lambda h, *_: (0, h)),
            pl.BlockSpec((length, HEAD_DIM), lambda h, *_: (0, h)),
            pl.BlockSpec((None, 1, length), lambda h, *_: (h, 0, 0)),
        ],
        scratch_shapes=[pltpu.VMEM((length, length), F32)],
    )
    return pl.pallas_call(
        functools.partial(attn_fwd_kernel, tile=tile),
        grid_spec=grid_spec,
        out_shape=[
            jax.ShapeDtypeStruct((length, heads * 3 * HEAD_DIM), BF),
            jax.ShapeDtypeStruct((length, heads * HEAD_DIM), BF),
            jax.ShapeDtypeStruct((heads, 1, length), F32),
        ],
        compiler_params=params(48),
        cost_estimate=cost(
            heads * (2 * length * width * 384 + 8 * length * length * HEAD_DIM),
            2 * length * width + 2 * width * heads * 384 + 8 * length * heads * 128,
        ),
        name="attn_fwd",
    )(info, tokens, qkv_weight, cosine, sine, segc, segr)


def attn_bwd_kernel(
    info_ref, qkv_ref, dol_ref, lse_ref, cos_ref, sin_ref, segc_ref, segr_ref, dqkv_ref,
    bias_ref, dol_nat, dk_ref, dv_ref, tile
):
    length = qkv_ref.shape[0]
    ways, block, _ = dol_ref.shape
    me = info_ref[0]

    @pl.when(pl.program_id(0) == 0)
    def _():
        fill_bias(info_ref, segc_ref, segr_ref, bias_ref, tile)

    for at in range(ways):
        dol_nat[pl.ds(at * block, block), :] = dol_ref[me ^ at]
    keys = qkv_ref[:, HEAD_DIM : 2 * HEAD_DIM]
    values = qkv_ref[:, 2 * HEAD_DIM :]
    keys_t = keys.astype(F32).T.astype(BF)
    for step in range(length // tile):
        rows = pl.ds(step * tile, tile)
        queries = qkv_ref[rows, :HEAD_DIM]
        dol = dol_nat[rows, :]
        scores = mm_nt(keys, queries) * score_scale + bias_ref[:, rows]
        probs = jnp.exp(scores - lse_ref[:, rows])
        dp = mm_nt(values, dol)
        inner = jnp.sum(probs * dp, axis=0, keepdims=True)
        draw = (probs * (dp - inner) * score_scale).astype(BF)
        dv = mm(probs.astype(BF), dol)
        dk = mm(draw, queries)
        if step == 0:
            dv_ref[...] = dv
            dk_ref[...] = dk
        else:
            dv_ref[...] += dv
            dk_ref[...] += dk
        dq = mm(keys_t, draw).T
        turned = dq * cos_ref[rows, :] - pltpu.roll(dq, HEAD_DIM // 2, 1) * sin_ref[rows, :]
        dqkv_ref[rows, :HEAD_DIM] = turned.astype(BF)
    dk = dk_ref[...]
    turned = dk * cos_ref[...] - pltpu.roll(dk, HEAD_DIM // 2, 1) * sin_ref[...]
    dqkv_ref[:, HEAD_DIM : 2 * HEAD_DIM] = turned.astype(BF)
    dqkv_ref[:, 2 * HEAD_DIM :] = dv_ref[...].astype(BF)


def attn_bwd(info, qkv, dol, lse, cosine, sine, segc, segr):
    length = qkv.shape[0]
    heads = qkv.shape[1] // (3 * HEAD_DIM)
    ways, block, _ = dol.shape
    tile = min(256, length)
    grid_spec = pltpu.PrefetchScalarGridSpec(
        num_scalar_prefetch=1,
        grid=(heads,),
        in_specs=[
            pl.BlockSpec((length, 3 * HEAD_DIM), lambda h, *_: (0, h)),
            pl.BlockSpec((ways, block, HEAD_DIM), lambda h, *_: (0, 0, h)),
            pl.BlockSpec((None, 1, length), lambda h, *_: (h, 0, 0)),
            const_spec((length, HEAD_DIM)),
            const_spec((length, HEAD_DIM)),
            const_spec((length, 1)),
            const_spec((1, length)),
        ],
        out_specs=pl.BlockSpec((length, 3 * HEAD_DIM), lambda h, *_: (0, h)),
        scratch_shapes=[
            pltpu.VMEM((length, length), F32),
            pltpu.VMEM((length, HEAD_DIM), BF),
            pltpu.VMEM((length, HEAD_DIM), F32),
            pltpu.VMEM((length, HEAD_DIM), F32),
        ],
    )
    return pl.pallas_call(
        functools.partial(attn_bwd_kernel, tile=tile),
        grid_spec=grid_spec,
        out_shape=jax.ShapeDtypeStruct(qkv.shape, BF),
        compiler_params=params(48),
        cost_estimate=cost(heads * 20 * length * length * HEAD_DIM, 16 * length * heads * 128),
        name="attn_bwd",
    )(info, qkv, dol, lse, cosine, sine, segc, segr)


def out_norm_kernel(info_ref, *refs, ways):
    ol_refs, ow_refs = refs[:ways], refs[ways : 2 * ways]
    x_ref, gain_ref, bias_ref, hl_ref, n1_ref, rstd_ref = refs[2 * ways :]
    total = x_ref[...].astype(F32) * deep_alpha
    for ol_ref, ow_ref in zip(ol_refs, ow_refs):
        total += mm(ol_ref[...], ow_ref[...])
    centered = total - jnp.mean(total, axis=1, keepdims=True)
    variance = jnp.mean(centered * centered, axis=1, keepdims=True)
    inv = lax.rsqrt(variance + norm_eps)
    normed = centered * inv
    hl_ref[...] = (normed * gain_ref[...] + bias_ref[...]).astype(BF)

    @pl.when(pl.program_id(0) == info_ref[0])
    def _():
        n1_ref[...] = normed
        rstd_ref[...] = jnp.broadcast_to(inv, rstd_ref.shape)


def out_norm(info, row, ol_pieces, ow_pieces, tokens, gain, bias):
    _, length, width = tokens.shape
    ways = len(ol_pieces)
    block = length // ways
    head_width = ol_pieces[0].shape[1]
    grid_spec = pltpu.PrefetchScalarGridSpec(
        num_scalar_prefetch=1,
        grid=(ways,),
        in_specs=[pl.BlockSpec((block, head_width), lambda i, *_: (i, 0))] * ways
        + [const_spec((head_width, width))] * ways
        + [
            pl.BlockSpec((None, block, width), lambda i, *_: (row, i, 0)),
            const_spec((1, width)),
            const_spec((1, width)),
        ],
        out_specs=[
            pl.BlockSpec((block, width), lambda i, info: (i ^ info[0], 0)),
            pl.BlockSpec((block, width), lambda i, *_: (0, 0)),
            pl.BlockSpec((block, HEAD_DIM), lambda i, *_: (0, 0)),
        ],
    )
    return pl.pallas_call(
        functools.partial(out_norm_kernel, ways=ways),
        grid_spec=grid_spec,
        out_shape=[
            jax.ShapeDtypeStruct((length, width), BF),
            jax.ShapeDtypeStruct((block, width), F32),
            jax.ShapeDtypeStruct((block, HEAD_DIM), F32),
        ],
        compiler_params=params(48),
        cost_estimate=cost(2 * length * width * width, 2 * width * width + 6 * length * width),
        name="out_norm",
    )(info, *ol_pieces, *ow_pieces, tokens, gain, bias)


def piece_shapes(ways, block, width):
    if ways == 4:
        sizes = [block] + [block // 2] * 6
    else:
        sizes = [block] * ways
    return [jax.ShapeDtypeStruct((size, width), BF) for size in sizes]


def store_pieces(at, part, refs, ways):
    if ways == 4:
        half = part.shape[0] // 2

        @pl.when(at == 0)
        def _():
            refs[0][...] = part

        for r in range(1, 4):

            @pl.when(at == r)
            def _(r=r):
                refs[2 * r - 1][...] = part[:half]
                refs[2 * r][...] = part[half:]
    else:
        for r in range(ways):

            @pl.when(at == r)
            def _(r=r):
                refs[r][...] = part


def piece_specs(shapes):
    return [pl.BlockSpec(s.shape, lambda *_: (0, 0)) for s in shapes]


def ffn_fwd_kernel(hl_ref, wg_ref, wu_ref, wd_ref, al_ref, ga_ref, gb_ref, *refs, ways):
    hidden = hl_ref[...]
    gate = mm(hidden, wg_ref[...])
    up = mm(hidden, wu_ref[...])
    cdf = 0.5 + 0.5 * lax.erf(gate * (1.0 / math.sqrt(2.0)))
    pdf = jnp.exp(gate * gate * -0.5) * (1.0 / math.sqrt(2.0 * math.pi))
    act = gate * cdf
    ga_ref[...] = (up * (cdf + gate * pdf)).astype(BF)
    gb_ref[...] = act.astype(BF)
    low = (act * up).astype(BF)
    al_ref[...] = low
    store_pieces(pl.program_id(0), mm(low, wd_ref[...]).astype(BF), refs, ways)


def ffn_fwd(hidden, gate_weight, up_weight, down_weight, ways):
    length, width = hidden.shape
    units = gate_weight.shape[1]
    block = length // ways
    tiled = lambda w: pl.BlockSpec((block, w), lambda i: (i, 0))
    shapes = piece_shapes(ways, block, width)
    out = pl.pallas_call(
        functools.partial(ffn_fwd_kernel, ways=ways),
        grid=(ways,),
        in_specs=[
            tiled(width),
            const_spec((width, units)),
            const_spec((width, units)),
            const_spec((units, width)),
        ],
        out_specs=[tiled(units)] * 3 + piece_specs(shapes),
        out_shape=[jax.ShapeDtypeStruct((length, units), BF)] * 3 + shapes,
        compiler_params=params(60),
        cost_estimate=cost(6 * length * width * units, 6 * units * width + 6 * length * units),
        name="ffn_fwd",
    )(hidden, gate_weight, up_weight, down_weight)
    return out[:3], out[3:]


def norm_two_kernel(info_ref, share_ref, *refs, n_in, ways):
    in_refs = refs[:n_in]
    cot_ref, gain_ref, bias_ref = refs[n_in : n_in + 3]
    act_ref, dffn_ref, sums_ref, held = refs[-4:]
    at = pl.program_id(0)
    if n_in == 5:
        half = held.shape[0] // 2
        for r in range(3):

            @pl.when(at == r)
            def _(r=r):
                held[...] = in_refs[r][...]

        @pl.when(at == 3)
        def _():
            held[:half] = in_refs[3][...]
            held[half:] = in_refs[4][...]
    else:
        for r in range(ways):

            @pl.when(at == r)
            def _(r=r):
                held[...] = in_refs[r][...]

    resid = held[...].astype(F32)
    centered = resid - jnp.mean(resid, axis=1, keepdims=True)
    variance = jnp.mean(centered * centered, axis=1, keepdims=True)
    inv = lax.rsqrt(variance + norm_eps)
    normed = centered * inv
    gain = gain_ref[...]
    act_ref[...] = (normed * gain + bias_ref[...]).astype(BF)
    dout = cot_ref[...].astype(F32) * share_ref[0]
    scaled = dout * gain
    inner = jnp.mean(scaled, axis=1, keepdims=True) + normed * jnp.mean(
        scaled * normed, axis=1, keepdims=True
    )
    dffn_ref[...] = (inv * (scaled - inner)).astype(BF)
    gain_sum = jnp.sum(dout * normed, axis=0, keepdims=True)
    bias_sum = jnp.sum(dout, axis=0, keepdims=True)

    @pl.when(at == 0)
    def _():
        sums_ref[0:1, :] = gain_sum
        sums_ref[1:2, :] = bias_sum

    @pl.when(at > 0)
    def _():
        sums_ref[0:1, :] += gain_sum
        sums_ref[1:2, :] += bias_sum


def norm_two(info, share, row, pieces, cotangent, gain, bias, before):
    rows, length, width = cotangent.shape
    block = pieces[0].shape[0]
    ways = length // block
    natural = pl.BlockSpec((None, block, width), lambda i, info, share: (row, i ^ info[0], 0))
    grid_spec = pltpu.PrefetchScalarGridSpec(
        num_scalar_prefetch=2,
        grid=(ways,),
        in_specs=[const_spec(p.shape) for p in pieces]
        + [natural, const_spec((1, width)), const_spec((1, width))]
        + ([pl.BlockSpec(memory_space=ANY)] if before is not None else []),
        out_specs=[
            natural,
            pl.BlockSpec((block, width), lambda i, *_: (i, 0)),
            pl.BlockSpec((2, width), lambda i, *_: (0, 0)),
        ],
        scratch_shapes=[pltpu.VMEM((block, width), BF)],
    )
    return pl.pallas_call(
        functools.partial(norm_two_kernel, n_in=len(pieces), ways=ways),
        grid_spec=grid_spec,
        out_shape=[
            jax.ShapeDtypeStruct(cotangent.shape, BF),
            jax.ShapeDtypeStruct((length, width), BF),
            jax.ShapeDtypeStruct((2, width), F32),
        ],
        input_output_aliases={len(pieces) + 5: 0} if before is not None else {},
        compiler_params=params(48),
        cost_estimate=cost(20 * length * width, 8 * length * width),
        name="norm_two",
    )(info, share, *pieces, cotangent, gain, bias, *([before] if before is not None else []))


def ffn_bwd_kernel(dffn_ref, ga_ref, gb_ref, wg_ref, wu_ref, wd_ref, dg_ref, du_ref, *refs, ways):
    dact = mm_nt(dffn_ref[...], wd_ref[...])
    dgate = (dact * ga_ref[...].astype(F32)).astype(BF)
    dup = (dact * gb_ref[...].astype(F32)).astype(BF)
    dg_ref[...] = dgate
    du_ref[...] = dup
    part = mm_nt(dgate, wg_ref[...]) + mm_nt(dup, wu_ref[...])
    store_pieces(pl.program_id(0), part.astype(BF), refs, ways)


def ffn_bwd(dffn, gate_slope, up_slope, gate_weight, up_weight, down_weight, ways):
    length, width = dffn.shape
    units = gate_weight.shape[1]
    block = length // ways
    tiled = lambda w: pl.BlockSpec((block, w), lambda i: (i, 0))
    shapes = piece_shapes(ways, block, width)
    out = pl.pallas_call(
        functools.partial(ffn_bwd_kernel, ways=ways),
        grid=(ways,),
        in_specs=[
            tiled(width),
            tiled(units),
            tiled(units),
            const_spec((width, units)),
            const_spec((width, units)),
            const_spec((units, width)),
        ],
        out_specs=[tiled(units)] * 2 + piece_specs(shapes),
        out_shape=[jax.ShapeDtypeStruct((length, units), BF)] * 2 + shapes,
        compiler_params=params(60),
        cost_estimate=cost(6 * length * width * units, 6 * units * width + 8 * length * units),
        name="ffn_bwd",
    )(dffn, gate_slope, up_slope, gate_weight, up_weight, down_weight)
    return out[0], out[1], out[2:]


def input_back_kernel(info_ref, dqkv_ref, w_ref, *refs, ways):
    part = mm_nt(dqkv_ref[...], w_ref[...])
    store_pieces(pl.program_id(0), part.astype(BF), refs, ways)


def input_back(info, dqkv, qkv_weight, ways):
    length, columns = dqkv.shape
    width = qkv_weight.shape[0]
    block = length // ways
    shapes = piece_shapes(ways, block, width)
    grid_spec = pltpu.PrefetchScalarGridSpec(
        num_scalar_prefetch=1,
        grid=(ways,),
        in_specs=[
            pl.BlockSpec((block, columns), lambda i, info: (i ^ info[0], 0)),
            const_spec((width, columns)),
        ],
        out_specs=piece_specs(shapes),
    )
    return pl.pallas_call(
        functools.partial(input_back_kernel, ways=ways),
        grid_spec=grid_spec,
        out_shape=shapes,
        compiler_params=params(48),
        cost_estimate=cost(2 * length * width * columns, 2 * width * columns + 2 * length * width),
        name="input_back",
    )(info, dqkv, qkv_weight)


def place_kernel(info_ref, *refs, n_in, ways):
    in_refs = refs[:n_in]
    out_ref = refs[-1]
    at = pl.program_id(0)
    if n_in == 5:
        half = out_ref.shape[0] // 2
        for r in range(3):

            @pl.when(at == r)
            def _(r=r):
                out_ref[...] = in_refs[r][...]

        @pl.when(at == 3)
        def _():
            out_ref[:half] = in_refs[3][...]
            out_ref[half:] = in_refs[4][...]
    else:
        for r in range(ways):

            @pl.when(at == r)
            def _(r=r):
                out_ref[...] = in_refs[r][...]


def place(info, row, pieces, shape, before):
    rows, length, width = shape
    block = pieces[0].shape[0]
    ways = length // block
    grid_spec = pltpu.PrefetchScalarGridSpec(
        num_scalar_prefetch=1,
        grid=(ways,),
        in_specs=[const_spec(p.shape) for p in pieces]
        + ([pl.BlockSpec(memory_space=ANY)] if before is not None else []),
        out_specs=pl.BlockSpec((None, block, width), lambda i, info: (row, i ^ info[0], 0)),
    )
    return pl.pallas_call(
        functools.partial(place_kernel, n_in=len(pieces), ways=ways),
        grid_spec=grid_spec,
        out_shape=jax.ShapeDtypeStruct(shape, BF),
        input_output_aliases={len(pieces) + 1: 0} if before is not None else {},
        compiler_params=params(32),
        cost_estimate=cost(0, 4 * length * width),
        name="place",
    )(info, *pieces, *([before] if before is not None else []))


def swap(array, bit, ways):
    return lax.ppermute(array, "tensor", [(i, i ^ bit) for i in range(ways)])


def gather_halves(own_a, own_b):
    xa = swap(own_a, 1, 4)
    yb = swap(own_b, 2, 4)
    xb = swap(own_b, 1, 4)
    ya = swap(own_a, 2, 4)
    ra = swap(xa, 2, 4)
    rb = swap(yb, 1, 4)
    return [(xa, xb), (ya, yb), (ra, rb)]


def gather_rel(own, ways):
    blocks = [own]
    bit = 1
    while bit < ways:
        blocks = blocks + [swap(b, bit, ways) for b in blocks]
        bit *= 2
    return blocks


def gather_tokens(own, ways):
    if ways == 4:
        half = own.shape[0] // 2
        (xa, xb), (ya, yb), (ra, rb) = gather_halves(own[:half], own[half:])
        return [own, jnp.concatenate([xa, xb]), jnp.concatenate([ya, yb]), ra, rb]
    return gather_rel(own, ways)


def join(pieces):
    return jnp.concatenate(pieces, axis=0)


def add_low(a, b):
    return (a.astype(F32) + b.astype(F32)).astype(BF)


def scatter_sum(pieces, ways):
    if ways == 4:
        own, r1a, r1b, r2a, r2b, r3a, r3b = pieces
        in3a = swap(r3a, 1, 4)
        in3b = swap(r3b, 2, 4)
        in1a = swap(r1a, 1, 4)
        in2b = swap(r2b, 2, 4)
        in2a = swap(add_low(r2a, in3a), 2, 4)
        in1b = swap(add_low(r1b, in3b), 1, 4)
        half = r1a.shape[0]
        top = own[:half].astype(F32) + in1a.astype(F32) + in2a.astype(F32)
        low = own[half:].astype(F32) + in1b.astype(F32) + in2b.astype(F32)
        return jnp.concatenate([top, low], axis=0)
    blocks = list(pieces)
    bit = ways // 2
    while bit >= 1:
        keep, send = blocks[:bit], blocks[bit:]
        blocks = [add_low(k, swap(s, bit, ways)) for k, s in zip(keep, send)]
        bit //= 2
    return blocks[0].astype(F32)


def sum_over_obj(array, ways):
    if ways != 4:
        return lax.psum(array, "obj")
    at = lax.axis_index("obj")
    one = add_low(array, lax.ppermute(array, "obj", [(0, 1), (3, 2)]))
    two = add_low(one, lax.ppermute(one, "obj", [(1, 2), (2, 1)]))
    back = lax.ppermute(two, "obj", [(1, 0), (2, 3)])
    return jnp.where((at == 0) | (at == 3), back, two)


def sum_gradient(update, data_ways, objective_ways):
    if data_ways != 2:
        return lax.psum(update, ("obj", "dp")).astype(F32)
    core = lax.axis_index("dp")
    half = update.shape[0] // 2
    other = [(0, 1), (1, 0)]
    mine = lax.dynamic_slice_in_dim(update, core * half, half)
    send = lax.dynamic_slice_in_dim(update, (1 - core) * half, half)
    mine = add_low(mine, lax.ppermute(send, "dp", other))
    mine = sum_over_obj(mine, objective_ways)
    theirs = lax.ppermute(mine, "dp", other)
    first = jnp.where(core == 0, mine, theirs)
    second = jnp.where(core == 0, theirs, mine)
    return jnp.concatenate([first, second], axis=0).astype(F32)


def body(
    tokens,
    cotangent,
    segment_ids,
    mlm_mask,
    glm_prefix,
    glm_span,
    qkv_weight,
    out_weight,
    gate_weight,
    up_weight,
    down_weight,
    norm1_gain,
    norm1_bias,
    norm2_gain,
    norm2_bias,
):
    seq_here, length, width = tokens.shape
    ways = lax.axis_size("tensor")
    data_ways = lax.axis_size("dp")
    objective_ways = lax.axis_size("obj")
    me = lax.axis_index("tensor").astype(jnp.int32)
    block = length // ways
    rows_all = mlm_mask.shape[0]
    masked_limit = seq_here * data_ways * (objective_ways // 2)
    row_ids = jnp.arange(rows_all, dtype=jnp.int32)
    counts = jnp.where(row_ids < masked_limit, jnp.sum(mlm_mask, axis=1), glm_span).astype(F32)
    weight_all = counts * rows_all / jnp.sum(counts)
    first_row = (lax.axis_index("obj") * data_ways + lax.axis_index("dp")) * seq_here
    share_here = lax.dynamic_slice_in_dim(weight_all, first_row, seq_here)
    prefix_here = lax.dynamic_slice_in_dim(glm_prefix, first_row, seq_here)
    span_here = lax.dynamic_slice_in_dim(glm_span, first_row, seq_here)
    masked_lm = first_row < masked_limit
    open_here = jnp.where(masked_lm, length, prefix_here)
    info = [jnp.stack([me, open_here[r], prefix_here[r] + span_here[r]]) for r in range(seq_here)]
    share = [share_here[r : r + 1] for r in range(seq_here)]
    cosine, sine = rotary_tables(length)
    segc = [segment_ids[r].reshape(length, 1) for r in range(seq_here)]
    segr = [segment_ids[r].reshape(1, length) for r in range(seq_here)]
    gain1, bias1 = norm1_gain.reshape(1, width), norm1_bias.reshape(1, width)
    gain2, bias2 = norm2_gain.reshape(1, width), norm2_bias.reshape(1, width)
    rows = range(seq_here)

    if ways == 4 and data_ways == 2:
        core = lax.axis_index("dp")
        half = out_weight.shape[0] // 2
        mine = lax.dynamic_slice_in_dim(out_weight, core * half, half)
        pairs = gather_halves(mine[: half // 2], mine[half // 2 :])
        ow_pieces = [out_weight]
        for a, b in pairs:
            got = jnp.concatenate([a, b])
            other = lax.ppermute(got, "dp", [(0, 1), (1, 0)])
            ow_pieces.append(
                jnp.concatenate(
                    [jnp.where(core == 0, got, other), jnp.where(core == 0, other, got)]
                )
            )
    else:
        ow_pieces = gather_rel(out_weight, ways)

    qkv, ol, lse, hl, n1, rstd1 = {}, {}, {}, {}, {}, {}
    al, slope_g, slope_u, dffn, dgate, dup = {}, {}, {}, {}, {}, {}
    r2_pieces, norm2_sums, norm1_sums, dr1, dqkv, dattn = {}, {}, {}, {}, {}, {}

    for r in rows:
        qkv[r], ol[r], lse[r] = attn_fwd(info[r], r, tokens, qkv_weight, cosine, sine, segc[r], segr[r])
    ffn_parts = {}
    for r in rows:
        if ways == 4:
            pairs = gather_halves(ol[r][: length // 2], ol[r][length // 2 :])
            ol_pieces = [ol[r]] + [jnp.concatenate(p) for p in pairs]
        else:
            ol_pieces = gather_rel(ol[r], ways)
        hl[r], n1[r], rstd1[r] = out_norm(info[r], r, ol_pieces, ow_pieces, tokens, gain1, bias1)
        (al[r], slope_g[r], slope_u[r]), ffn_parts[r] = ffn_fwd(
            hl[r], gate_weight, up_weight, down_weight, ways
        )
    for r in rows:
        total = scatter_sum(ffn_parts[r], ways)
        resid = deep_alpha * (n1[r] * gain1 + bias1) + total
        r2_pieces[r] = gather_tokens(resid.astype(BF), ways)

    activations = None
    dh_parts = {}
    for r in rows:
        activations, dffn[r], norm2_sums[r] = norm_two(
            info[r], share[r], r, r2_pieces[r], cotangent, gain2, bias2, activations
        )
        dgate[r], dup[r], dh_parts[r] = ffn_bwd(
            dffn[r], slope_g[r], slope_u[r], gate_weight, up_weight, down_weight, ways
        )

    def update(lefts, rights):
        total = None
        for r in rows:
            one = mm_tn(lefts[r], rights[r])
            total = one if total is None else total + one
        return total.astype(BF)

    def reduced(lefts, rights):
        return sum_gradient(update(lefts, rights), data_ways, objective_ways)

    down_grad = reduced(al, dffn)
    gate_grad = reduced(hl, dgate)
    up_grad = reduced(hl, dup)

    dx_parts = {}
    for r in rows:
        total = scatter_sum(dh_parts[r], ways)
        dh = deep_alpha * dffn[r][:block].astype(F32) + total
        scaled = dh * gain1
        inner = jnp.mean(scaled, axis=1, keepdims=True) + n1[r] * jnp.mean(
            scaled * n1[r], axis=1, keepdims=True
        )
        dr1[r] = rstd1[r][:, :1] * (scaled - inner)
        norm1_sums[r] = jnp.stack([jnp.sum(dh * n1[r], axis=0), jnp.sum(dh, axis=0)])
        dattn[r] = join(gather_tokens(dr1[r].astype(BF), ways))
    for r in rows:
        dol = mm_nt(dattn[r], out_weight).astype(BF).reshape(ways, block, -1)
        dqkv[r] = attn_bwd(info[r], qkv[r], dol, lse[r], cosine, sine, segc[r], segr[r])
        dx_parts[r] = input_back(info[r], dqkv[r], qkv_weight, ways)

    qkv_grad = reduced([tokens[r] for r in rows], dqkv)
    ol_rel = {}
    for r in rows:
        parts = ol[r].reshape(ways, block, -1)
        ol_rel[r] = jnp.stack(
            [lax.dynamic_index_in_dim(parts, me ^ i, 0, keepdims=False) for i in range(ways)]
        ).reshape(length, -1)
    out_grad = reduced(ol_rel, dattn)

    input_grad = None
    for r in rows:
        total = scatter_sum(dx_parts[r], ways)
        dx = (deep_alpha * dr1[r] + total).astype(BF)
        input_grad = place(info[r], r, gather_tokens(dx, ways), tokens.shape, input_grad)

    first = (me == 0).astype(F32)
    sums = jnp.concatenate(
        [sum(norm1_sums[r] for r in rows), sum(norm2_sums[r] for r in rows) * first]
    )
    sums = lax.psum(sums, ("obj", "dp", "tensor"))
    return (
        activations,
        input_grad,
        qkv_grad,
        out_grad,
        gate_grad,
        up_grad,
        down_grad,
        sums[0],
        sums[1],
        sums[2],
        sums[3],
    )


def solution(mesh):
    rows3 = P(("obj", "dp"), None, None)
    in_specs = (
        rows3,
        rows3,
        P(("obj", "dp"), None),
        P(),
        P(),
        P(),
        P(None, "tensor"),
        P("tensor", None),
        P(None, "tensor"),
        P(None, "tensor"),
        P("tensor", None),
        P(),
        P(),
        P(),
        P(),
    )
    out_specs = (
        rows3,
        rows3,
        P(None, "tensor"),
        P("tensor", None),
        P(None, "tensor"),
        P(None, "tensor"),
        P("tensor", None),
        P(),
        P(),
        P(),
        P(),
    )
    return jax.shard_map(body, mesh=mesh, in_specs=in_specs, out_specs=out_specs, check_vma=False)
```

```python
import functools
import math

import jax
import jax.numpy as jnp
import numpy as np
from jax import lax
from jax.experimental import pallas as pl
from jax.experimental.pallas import tpu as pltpu
from jax.sharding import PartitionSpec as P

HEAD_DIM = 128
deep_alpha = math.sqrt(48.0)
norm_eps = 1e-05
mask_fill = -1e30
score_scale = 1.0 / math.sqrt(HEAD_DIM)
MIB = 1024 * 1024
BF = jnp.bfloat16
F32 = jnp.float32
ANY = pl.ANY


def mm(a, b):
    return lax.dot_general(a, b, (((1,), (0,)), ((), ())), preferred_element_type=F32)


def mm_nt(a, b):
    return lax.dot_general(a, b, (((1,), (1,)), ((), ())), preferred_element_type=F32)


def mm_tn(a, b):
    return lax.dot_general(a, b, (((0,), (0,)), ((), ())), preferred_element_type=F32)


def params(mib, grid_rank=1):
    return pltpu.CompilerParams(
        vmem_limit_bytes=mib * MIB, dimension_semantics=("arbitrary",) * grid_rank
    )


def cost(flops, nbytes, trans=0):
    return pl.CostEstimate(flops=int(flops), bytes_accessed=int(nbytes), transcendentals=int(trans))


def const_spec(shape):
    zeros = (0,) * len(shape)
    return pl.BlockSpec(shape, lambda *_: zeros, pipeline_mode=pl.Buffered(1))


def rotary_tables(seq_length):
    half_width = HEAD_DIM // 2
    frequency = jnp.exp(
        jnp.arange(half_width, dtype=F32) * (-2.0 * math.log(10000.0) / HEAD_DIM)
    )
    angles = jnp.arange(seq_length, dtype=F32)[:, None] * frequency[None, :]
    sine = jnp.sin(angles)
    cosine = jnp.cos(angles)
    return jnp.concatenate([cosine, cosine], axis=1), jnp.concatenate([-sine, sine], axis=1)


def fill_bias(info_ref, segc_ref, segr_ref, bias_ref, tile):
    length = bias_ref.shape[0]
    prefix, limit = info_ref[1], info_ref[2]

    def one(step, carry):
        rows = pl.ds(pl.multiple_of(step * tile, tile), tile)
        key_pos = lax.broadcasted_iota(jnp.int32, (tile, length), 0) + step * tile
        query_pos = lax.broadcasted_iota(jnp.int32, (tile, length), 1)
        same = segc_ref[rows, :] == segr_ref[...]
        open_keys = (
            (key_pos < prefix)
            | ((key_pos <= query_pos) & (key_pos < limit))
            | (key_pos == query_pos)
        )
        bias_ref[rows, :] = jnp.where(same & open_keys, 0.0, mask_fill)
        return carry

    lax.fori_loop(0, length // tile, one, 0)


def attn_fwd_kernel(
    info_ref, x_ref, w_ref, cos_ref, sin_ref, segc_ref, segr_ref, qkv_ref, ol_ref, lse_ref, bias_ref, tile
):
    length = x_ref.shape[0]

    @pl.when(pl.program_id(0) == 0)
    def _():
        fill_bias(info_ref, segc_ref, segr_ref, bias_ref, tile)

    for step in range(length // tile):
        rows = pl.ds(step * tile, tile)
        proj = mm(x_ref[rows, :], w_ref[...])
        cosine, sine = cos_ref[rows, :], sin_ref[rows, :]
        for part in range(2):
            piece = proj[:, part * HEAD_DIM : (part + 1) * HEAD_DIM]
            turned = piece * cosine + pltpu.roll(piece, HEAD_DIM // 2, 1) * sine
            qkv_ref[rows, part * HEAD_DIM : (part + 1) * HEAD_DIM] = turned.astype(BF)
        qkv_ref[rows, 2 * HEAD_DIM :] = proj[:, 2 * HEAD_DIM :].astype(BF)
    keys = qkv_ref[:, HEAD_DIM : 2 * HEAD_DIM]
    values_t = qkv_ref[:, 2 * HEAD_DIM :].astype(F32).T.astype(BF)
    for step in range(length // tile):
        rows = pl.ds(step * tile, tile)
        queries = qkv_ref[rows, :HEAD_DIM]
        scores = mm_nt(keys, queries) * score_scale + bias_ref[:, rows]
        top = jnp.max(scores, axis=0, keepdims=True)
        exponent = jnp.exp(scores - top)
        total = jnp.sum(exponent, axis=0, keepdims=True)
        attended = mm(values_t, exponent.astype(BF)) * (1.0 / total)
        ol_ref[rows, :] = attended.T.astype(BF)
        lse_ref[:, rows] = top + jnp.log(total)


def attn_fwd(info, row, tokens, qkv_weight, cosine, sine, segc, segr):
    _, length, width = tokens.shape
    heads = qkv_weight.shape[1] // (3 * HEAD_DIM)
    tile = min(256, length)
    grid_spec = pltpu.PrefetchScalarGridSpec(
        num_scalar_prefetch=1,
        grid=(heads,),
        in_specs=[
            pl.BlockSpec((None, length, width), lambda h, *_: (row, 0, 0), pipeline_mode=pl.Buffered(1)),
            pl.BlockSpec((width, 3 * HEAD_DIM), lambda h, *_: (0, h)),
            const_spec((length, HEAD_DIM)),
            const_spec((length, HEAD_DIM)),
            const_spec((length, 1)),
            const_spec((1, length)),
        ],
        out_specs=[
            pl.BlockSpec((length, 3 * HEAD_DIM), lambda h, *_: (0, h)),
            pl.BlockSpec((length, HEAD_DIM), lambda h, *_: (0, h)),
            pl.BlockSpec((None, 1, length), lambda h, *_: (h, 0, 0)),
        ],
        scratch_shapes=[pltpu.VMEM((length, length), F32)],
    )
    return pl.pallas_call(
        functools.partial(attn_fwd_kernel, tile=tile),
        grid_spec=grid_spec,
        out_shape=[
            jax.ShapeDtypeStruct((length, heads * 3 * HEAD_DIM), BF),
            jax.ShapeDtypeStruct((length, heads * HEAD_DIM), BF),
            jax.ShapeDtypeStruct((heads, 1, length), F32),
        ],
        compiler_params=params(48),
        cost_estimate=cost(
            heads * (2 * length * width * 384 + 8 * length * length * HEAD_DIM),
            2 * length * width + 2 * width * heads * 384 + 8 * length * heads * 128,
        ),
        name="attn_fwd",
    )(info, tokens, qkv_weight, cosine, sine, segc, segr)


def attn_bwd_kernel(
    info_ref, qkv_ref, dol_ref, lse_ref, cos_ref, sin_ref, segc_ref, segr_ref, dqkv_ref,
    bias_ref, dol_nat, dk_ref, dv_ref, tile
):
    length = qkv_ref.shape[0]
    ways, block, _ = dol_ref.shape
    me = info_ref[0]

    @pl.when(pl.program_id(0) == 0)
    def _():
        fill_bias(info_ref, segc_ref, segr_ref, bias_ref, tile)

    for at in range(ways):
        dol_nat[pl.ds(at * block, block), :] = dol_ref[me ^ at]
    keys = qkv_ref[:, HEAD_DIM : 2 * HEAD_DIM]
    values = qkv_ref[:, 2 * HEAD_DIM :]
    keys_t = keys.astype(F32).T.astype(BF)
    for step in range(length // tile):
        rows = pl.ds(step * tile, tile)
        queries = qkv_ref[rows, :HEAD_DIM]
        dol = dol_nat[rows, :]
        scores = mm_nt(keys, queries) * score_scale + bias_ref[:, rows]
        probs = jnp.exp(scores - lse_ref[:, rows])
        dp = mm_nt(values, dol)
        inner = jnp.sum(probs * dp, axis=0, keepdims=True)
        draw = (probs * (dp - inner) * score_scale).astype(BF)
        dv = mm(probs.astype(BF), dol)
        dk = mm(draw, queries)
        if step == 0:
            dv_ref[...] = dv
            dk_ref[...] = dk
        else:
            dv_ref[...] += dv
            dk_ref[...] += dk
        dq = mm(keys_t, draw).T
        turned = dq * cos_ref[rows, :] - pltpu.roll(dq, HEAD_DIM // 2, 1) * sin_ref[rows, :]
        dqkv_ref[rows, :HEAD_DIM] = turned.astype(BF)
    dk = dk_ref[...]
    turned = dk * cos_ref[...] - pltpu.roll(dk, HEAD_DIM // 2, 1) * sin_ref[...]
    dqkv_ref[:, HEAD_DIM : 2 * HEAD_DIM] = turned.astype(BF)
    dqkv_ref[:, 2 * HEAD_DIM :] = dv_ref[...].astype(BF)


def attn_bwd(info, qkv, dol, lse, cosine, sine, segc, segr):
    length = qkv.shape[0]
    heads = qkv.shape[1] // (3 * HEAD_DIM)
    ways, block, _ = dol.shape
    tile = min(256, length)
    grid_spec = pltpu.PrefetchScalarGridSpec(
        num_scalar_prefetch=1,
        grid=(heads,),
        in_specs=[
            pl.BlockSpec((length, 3 * HEAD_DIM), lambda h, *_: (0, h)),
            pl.BlockSpec((ways, block, HEAD_DIM), lambda h, *_: (0, 0, h)),
            pl.BlockSpec((None, 1, length), lambda h, *_: (h, 0, 0)),
            const_spec((length, HEAD_DIM)),
            const_spec((length, HEAD_DIM)),
            const_spec((length, 1)),
            const_spec((1, length)),
        ],
        out_specs=pl.BlockSpec((length, 3 * HEAD_DIM), lambda h, *_: (0, h)),
        scratch_shapes=[
            pltpu.VMEM((length, length), F32),
            pltpu.VMEM((length, HEAD_DIM), BF),
            pltpu.VMEM((length, HEAD_DIM), F32),
            pltpu.VMEM((length, HEAD_DIM), F32),
        ],
    )
    return pl.pallas_call(
        functools.partial(attn_bwd_kernel, tile=tile),
        grid_spec=grid_spec,
        out_shape=jax.ShapeDtypeStruct(qkv.shape, BF),
        compiler_params=params(48),
        cost_estimate=cost(heads * 20 * length * length * HEAD_DIM, 16 * length * heads * 128),
        name="attn_bwd",
    )(info, qkv, dol, lse, cosine, sine, segc, segr)


def out_norm_kernel(info_ref, *refs, ways):
    ol_refs, ow_refs = refs[:ways], refs[ways : 2 * ways]
    x_ref, gain_ref, bias_ref, hl_ref, n1_ref, rstd_ref = refs[2 * ways :]
    total = x_ref[...].astype(F32) * deep_alpha
    for ol_ref, ow_ref in zip(ol_refs, ow_refs):
        total += mm(ol_ref[...], ow_ref[...])
    centered = total - jnp.mean(total, axis=1, keepdims=True)
    variance = jnp.mean(centered * centered, axis=1, keepdims=True)
    inv = lax.rsqrt(variance + norm_eps)
    normed = centered * inv
    hl_ref[...] = (normed * gain_ref[...] + bias_ref[...]).astype(BF)

    @pl.when(pl.program_id(0) == info_ref[0])
    def _():
        n1_ref[...] = normed
        rstd_ref[...] = jnp.broadcast_to(inv, rstd_ref.shape)


def out_norm(info, row, ol_pieces, ow_pieces, tokens, gain, bias):
    _, length, width = tokens.shape
    ways = len(ol_pieces)
    block = length // ways
    head_width = ol_pieces[0].shape[1]
    grid_spec = pltpu.PrefetchScalarGridSpec(
        num_scalar_prefetch=1,
        grid=(ways,),
        in_specs=[pl.BlockSpec((block, head_width), lambda i, *_: (i, 0))] * ways
        + [const_spec((head_width, width))] * ways
        + [
            pl.BlockSpec((None, block, width), lambda i, *_: (row, i, 0)),
            const_spec((1, width)),
            const_spec((1, width)),
        ],
        out_specs=[
            pl.BlockSpec((block, width), lambda i, info: (i ^ info[0], 0)),
            pl.BlockSpec((block, width), lambda i, *_: (0, 0)),
            pl.BlockSpec((block, HEAD_DIM), lambda i, *_: (0, 0)),
        ],
    )
    return pl.pallas_call(
        functools.partial(out_norm_kernel, ways=ways),
        grid_spec=grid_spec,
        out_shape=[
            jax.ShapeDtypeStruct((length, width), BF),
            jax.ShapeDtypeStruct((block, width), F32),
            jax.ShapeDtypeStruct((block, HEAD_DIM), F32),
        ],
        compiler_params=params(48),
        cost_estimate=cost(2 * length * width * width, 2 * width * width + 6 * length * width),
        name="out_norm",
    )(info, *ol_pieces, *ow_pieces, tokens, gain, bias)


def piece_shapes(ways, block, width):
    if ways == 4:
        sizes = [block] + [block // 2] * 6
    else:
        sizes = [block] * ways
    return [jax.ShapeDtypeStruct((size, width), BF) for size in sizes]


def store_pieces(at, part, refs, ways):
    if ways == 4:
        half = part.shape[0] // 2

        @pl.when(at == 0)
        def _():
            refs[0][...] = part

        for r in range(1, 4):

            @pl.when(at == r)
            def _(r=r):
                refs[2 * r - 1][...] = part[:half]
                refs[2 * r][...] = part[half:]
    else:
        for r in range(ways):

            @pl.when(at == r)
            def _(r=r):
                refs[r][...] = part


def piece_specs(shapes):
    return [pl.BlockSpec(s.shape, lambda *_: (0, 0)) for s in shapes]


def ffn_fwd_kernel(hl_ref, wg_ref, wu_ref, wd_ref, al_ref, ga_ref, gb_ref, *refs, ways):
    hidden = hl_ref[...]
    gate = mm(hidden, wg_ref[...])
    up = mm(hidden, wu_ref[...])
    cdf = 0.5 + 0.5 * lax.erf(gate * (1.0 / math.sqrt(2.0)))
    pdf = jnp.exp(gate * gate * -0.5) * (1.0 / math.sqrt(2.0 * math.pi))
    act = gate * cdf
    ga_ref[...] = (up * (cdf + gate * pdf)).astype(BF)
    gb_ref[...] = act.astype(BF)
    low = (act * up).astype(BF)
    al_ref[...] = low
    store_pieces(pl.program_id(0), mm(low, wd_ref[...]).astype(BF), refs, ways)


def ffn_fwd(hidden, gate_weight, up_weight, down_weight, ways):
    length, width = hidden.shape
    units = gate_weight.shape[1]
    block = length // ways
    tiled = lambda w: pl.BlockSpec((block, w), lambda i: (i, 0))
    shapes = piece_shapes(ways, block, width)
    out = pl.pallas_call(
        functools.partial(ffn_fwd_kernel, ways=ways),
        grid=(ways,),
        in_specs=[
            tiled(width),
            const_spec((width, units)),
            const_spec((width, units)),
            const_spec((units, width)),
        ],
        out_specs=[tiled(units)] * 3 + piece_specs(shapes),
        out_shape=[jax.ShapeDtypeStruct((length, units), BF)] * 3 + shapes,
        compiler_params=params(60),
        cost_estimate=cost(6 * length * width * units, 6 * units * width + 6 * length * units),
        name="ffn_fwd",
    )(hidden, gate_weight, up_weight, down_weight)
    return out[:3], out[3:]


def norm_two_kernel(info_ref, share_ref, *refs, n_in, ways):
    in_refs = refs[:n_in]
    cot_ref, gain_ref, bias_ref = refs[n_in : n_in + 3]
    act_ref, dffn_ref, sums_ref, held = refs[-4:]
    at = pl.program_id(0)
    if n_in == 5:
        half = held.shape[0] // 2
        for r in range(3):

            @pl.when(at == r)
            def _(r=r):
                held[...] = in_refs[r][...]

        @pl.when(at == 3)
        def _():
            held[:half] = in_refs[3][...]
            held[half:] = in_refs[4][...]
    else:
        for r in range(ways):

            @pl.when(at == r)
            def _(r=r):
                held[...] = in_refs[r][...]

    resid = held[...].astype(F32)
    centered = resid - jnp.mean(resid, axis=1, keepdims=True)
    variance = jnp.mean(centered * centered, axis=1, keepdims=True)
    inv = lax.rsqrt(variance + norm_eps)
    normed = centered * inv
    gain = gain_ref[...]
    act_ref[...] = (normed * gain + bias_ref[...]).astype(BF)
    dout = cot_ref[...].astype(F32) * share_ref[0]
    scaled = dout * gain
    inner = jnp.mean(scaled, axis=1, keepdims=True) + normed * jnp.mean(
        scaled * normed, axis=1, keepdims=True
    )
    dffn_ref[...] = (inv * (scaled - inner)).astype(BF)
    gain_sum = jnp.sum(dout * normed, axis=0, keepdims=True)
    bias_sum = jnp.sum(dout, axis=0, keepdims=True)

    @pl.when(at == 0)
    def _():
        sums_ref[0:1, :] = gain_sum
        sums_ref[1:2, :] = bias_sum

    @pl.when(at > 0)
    def _():
        sums_ref[0:1, :] += gain_sum
        sums_ref[1:2, :] += bias_sum


def norm_two(info, share, row, pieces, cotangent, gain, bias, before):
    rows, length, width = cotangent.shape
    block = pieces[0].shape[0]
    ways = length // block
    natural = pl.BlockSpec((None, block, width), lambda i, info, share: (row, i ^ info[0], 0))
    grid_spec = pltpu.PrefetchScalarGridSpec(
        num_scalar_prefetch=2,
        grid=(ways,),
        in_specs=[const_spec(p.shape) for p in pieces]
        + [natural, const_spec((1, width)), const_spec((1, width))]
        + ([pl.BlockSpec(memory_space=ANY)] if before is not None else []),
        out_specs=[
            natural,
            pl.BlockSpec((block, width), lambda i, *_: (i, 0)),
            pl.BlockSpec((2, width), lambda i, *_: (0, 0)),
        ],
        scratch_shapes=[pltpu.VMEM((block, width), BF)],
    )
    return pl.pallas_call(
        functools.partial(norm_two_kernel, n_in=len(pieces), ways=ways),
        grid_spec=grid_spec,
        out_shape=[
            jax.ShapeDtypeStruct(cotangent.shape, BF),
            jax.ShapeDtypeStruct((length, width), BF),
            jax.ShapeDtypeStruct((2, width), F32),
        ],
        input_output_aliases={len(pieces) + 5: 0} if before is not None else {},
        compiler_params=params(48),
        cost_estimate=cost(20 * length * width, 8 * length * width),
        name="norm_two",
    )(info, share, *pieces, cotangent, gain, bias, *([before] if before is not None else []))


def ffn_bwd_kernel(dffn_ref, ga_ref, gb_ref, wg_ref, wu_ref, wd_ref, dg_ref, du_ref, *refs, ways):
    dact = mm_nt(dffn_ref[...], wd_ref[...])
    dgate = (dact * ga_ref[...].astype(F32)).astype(BF)
    dup = (dact * gb_ref[...].astype(F32)).astype(BF)
    dg_ref[...] = dgate
    du_ref[...] = dup
    part = mm_nt(dgate, wg_ref[...]) + mm_nt(dup, wu_ref[...])
    store_pieces(pl.program_id(0), part.astype(BF), refs, ways)


def ffn_bwd(dffn, gate_slope, up_slope, gate_weight, up_weight, down_weight, ways):
    length, width = dffn.shape
    units = gate_weight.shape[1]
    block = length // ways
    tiled = lambda w: pl.BlockSpec((block, w), lambda i: (i, 0))
    shapes = piece_shapes(ways, block, width)
    out = pl.pallas_call(
        functools.partial(ffn_bwd_kernel, ways=ways),
        grid=(ways,),
        in_specs=[
            tiled(width),
            tiled(units),
            tiled(units),
            const_spec((width, units)),
            const_spec((width, units)),
            const_spec((units, width)),
        ],
        out_specs=[tiled(units)] * 2 + piece_specs(shapes),
        out_shape=[jax.ShapeDtypeStruct((length, units), BF)] * 2 + shapes,
        compiler_params=params(60),
        cost_estimate=cost(6 * length * width * units, 6 * units * width + 8 * length * units),
        name="ffn_bwd",
    )(dffn, gate_slope, up_slope, gate_weight, up_weight, down_weight)
    return out[0], out[1], out[2:]


def input_back_kernel(info_ref, dqkv_ref, w_ref, *refs, ways):
    part = mm_nt(dqkv_ref[...], w_ref[...])
    store_pieces(pl.program_id(0), part.astype(BF), refs, ways)


def input_back(info, dqkv, qkv_weight, ways):
    length, columns = dqkv.shape
    width = qkv_weight.shape[0]
    block = length // ways
    shapes = piece_shapes(ways, block, width)
    grid_spec = pltpu.PrefetchScalarGridSpec(
        num_scalar_prefetch=1,
        grid=(ways,),
        in_specs=[
            pl.BlockSpec((block, columns), lambda i, info: (i ^ info[0], 0)),
            const_spec((width, columns)),
        ],
        out_specs=piece_specs(shapes),
    )
    return pl.pallas_call(
        functools.partial(input_back_kernel, ways=ways),
        grid_spec=grid_spec,
        out_shape=shapes,
        compiler_params=params(48),
        cost_estimate=cost(2 * length * width * columns, 2 * width * columns + 2 * length * width),
        name="input_back",
    )(info, dqkv, qkv_weight)


def place_kernel(info_ref, *refs, n_in, ways):
    in_refs = refs[:n_in]
    out_ref = refs[-1]
    at = pl.program_id(0)
    if n_in == 5:
        half = out_ref.shape[0] // 2
        for r in range(3):

            @pl.when(at == r)
            def _(r=r):
                out_ref[...] = in_refs[r][...]

        @pl.when(at == 3)
        def _():
            out_ref[:half] = in_refs[3][...]
            out_ref[half:] = in_refs[4][...]
    else:
        for r in range(ways):

            @pl.when(at == r)
            def _(r=r):
                out_ref[...] = in_refs[r][...]


def place(info, row, pieces, shape, before):
    rows, length, width = shape
    block = pieces[0].shape[0]
    ways = length // block
    grid_spec = pltpu.PrefetchScalarGridSpec(
        num_scalar_prefetch=1,
        grid=(ways,),
        in_specs=[const_spec(p.shape) for p in pieces]
        + ([pl.BlockSpec(memory_space=ANY)] if before is not None else []),
        out_specs=pl.BlockSpec((None, block, width), lambda i, info: (row, i ^ info[0], 0)),
    )
    return pl.pallas_call(
        functools.partial(place_kernel, n_in=len(pieces), ways=ways),
        grid_spec=grid_spec,
        out_shape=jax.ShapeDtypeStruct(shape, BF),
        input_output_aliases={len(pieces) + 1: 0} if before is not None else {},
        compiler_params=params(32),
        cost_estimate=cost(0, 4 * length * width),
        name="place",
    )(info, *pieces, *([before] if before is not None else []))


def swap(array, bit, ways):
    return lax.ppermute(array, "tensor", [(i, i ^ bit) for i in range(ways)])


def gather_halves(own_a, own_b):
    xa = swap(own_a, 1, 4)
    yb = swap(own_b, 2, 4)
    xb = swap(own_b, 1, 4)
    ya = swap(own_a, 2, 4)
    ra = swap(xa, 2, 4)
    rb = swap(yb, 1, 4)
    return [(xa, xb), (ya, yb), (ra, rb)]


def gather_rel(own, ways):
    blocks = [own]
    bit = 1
    while bit < ways:
        blocks = blocks + [swap(b, bit, ways) for b in blocks]
        bit *= 2
    return blocks


def gather_tokens(own, ways):
    if ways == 4:
        half = own.shape[0] // 2
        (xa, xb), (ya, yb), (ra, rb) = gather_halves(own[:half], own[half:])
        return [own, jnp.concatenate([xa, xb]), jnp.concatenate([ya, yb]), ra, rb]
    return gather_rel(own, ways)


def join(pieces):
    return jnp.concatenate(pieces, axis=0)


def add_low(a, b):
    return (a.astype(F32) + b.astype(F32)).astype(BF)


def scatter_sum(pieces, ways):
    if ways == 4:
        own, r1a, r1b, r2a, r2b, r3a, r3b = pieces
        in3a = swap(r3a, 1, 4)
        in3b = swap(r3b, 2, 4)
        in1a = swap(r1a, 1, 4)
        in2b = swap(r2b, 2, 4)
        in2a = swap(add_low(r2a, in3a), 2, 4)
        in1b = swap(add_low(r1b, in3b), 1, 4)
        half = r1a.shape[0]
        top = own[:half].astype(F32) + in1a.astype(F32) + in2a.astype(F32)
        low = own[half:].astype(F32) + in1b.astype(F32) + in2b.astype(F32)
        return jnp.concatenate([top, low], axis=0)
    blocks = list(pieces)
    bit = ways // 2
    while bit >= 1:
        keep, send = blocks[:bit], blocks[bit:]
        blocks = [add_low(k, swap(s, bit, ways)) for k, s in zip(keep, send)]
        bit //= 2
    return blocks[0].astype(F32)


def sum_over_obj(array, ways):
    if ways != 4:
        return lax.psum(array, "obj")
    at = lax.axis_index("obj")
    one = add_low(array, lax.ppermute(array, "obj", [(0, 1), (3, 2)]))
    two = add_low(one, lax.ppermute(one, "obj", [(1, 2), (2, 1)]))
    back = lax.ppermute(two, "obj", [(1, 0), (2, 3)])
    return jnp.where((at == 0) | (at == 3), back, two)


def sum_gradient(update, data_ways, objective_ways):
    if data_ways != 2:
        return lax.psum(update, ("obj", "dp")).astype(F32)
    core = lax.axis_index("dp")
    half = update.shape[0] // 2
    other = [(0, 1), (1, 0)]
    mine = lax.dynamic_slice_in_dim(update, core * half, half)
    send = lax.dynamic_slice_in_dim(update, (1 - core) * half, half)
    mine = add_low(mine, lax.ppermute(send, "dp", other))
    mine = sum_over_obj(mine, objective_ways)
    theirs = lax.ppermute(mine, "dp", other)
    first = jnp.where(core == 0, mine, theirs)
    second = jnp.where(core == 0, theirs, mine)
    return jnp.concatenate([first, second], axis=0).astype(F32)


def general_body(
    tokens,
    cotangent,
    segment_ids,
    mlm_mask,
    glm_prefix,
    glm_span,
    qkv_weight,
    out_weight,
    gate_weight,
    up_weight,
    down_weight,
    norm1_gain,
    norm1_bias,
    norm2_gain,
    norm2_bias,
):
    seq_here, length, width = tokens.shape
    ways = lax.axis_size("tensor")
    data_ways = lax.axis_size("dp")
    objective_ways = lax.axis_size("obj")
    me = lax.axis_index("tensor").astype(jnp.int32)
    block = length // ways
    rows_all = mlm_mask.shape[0]
    masked_limit = seq_here * data_ways * (objective_ways // 2)
    row_ids = jnp.arange(rows_all, dtype=jnp.int32)
    counts = jnp.where(row_ids < masked_limit, jnp.sum(mlm_mask, axis=1), glm_span).astype(F32)
    weight_all = counts * rows_all / jnp.sum(counts)
    first_row = (lax.axis_index("obj") * data_ways + lax.axis_index("dp")) * seq_here
    share_here = lax.dynamic_slice_in_dim(weight_all, first_row, seq_here)
    prefix_here = lax.dynamic_slice_in_dim(glm_prefix, first_row, seq_here)
    span_here = lax.dynamic_slice_in_dim(glm_span, first_row, seq_here)
    masked_lm = first_row < masked_limit
    open_here = jnp.where(masked_lm, length, prefix_here)
    info = [jnp.stack([me, open_here[r], prefix_here[r] + span_here[r]]) for r in range(seq_here)]
    share = [share_here[r : r + 1] for r in range(seq_here)]
    cosine, sine = rotary_tables(length)
    segc = [segment_ids[r].reshape(length, 1) for r in range(seq_here)]
    segr = [segment_ids[r].reshape(1, length) for r in range(seq_here)]
    gain1, bias1 = norm1_gain.reshape(1, width), norm1_bias.reshape(1, width)
    gain2, bias2 = norm2_gain.reshape(1, width), norm2_bias.reshape(1, width)
    rows = range(seq_here)

    if ways == 4 and data_ways == 2:
        core = lax.axis_index("dp")
        half = out_weight.shape[0] // 2
        mine = lax.dynamic_slice_in_dim(out_weight, core * half, half)
        pairs = gather_halves(mine[: half // 2], mine[half // 2 :])
        ow_pieces = [out_weight]
        for a, b in pairs:
            got = jnp.concatenate([a, b])
            other = lax.ppermute(got, "dp", [(0, 1), (1, 0)])
            ow_pieces.append(
                jnp.concatenate(
                    [jnp.where(core == 0, got, other), jnp.where(core == 0, other, got)]
                )
            )
    else:
        ow_pieces = gather_rel(out_weight, ways)

    qkv, ol, lse, hl, n1, rstd1 = {}, {}, {}, {}, {}, {}
    al, slope_g, slope_u, dffn, dgate, dup = {}, {}, {}, {}, {}, {}
    r2_pieces, norm2_sums, norm1_sums, dr1, dqkv, dattn = {}, {}, {}, {}, {}, {}

    for r in rows:
        qkv[r], ol[r], lse[r] = attn_fwd(info[r], r, tokens, qkv_weight, cosine, sine, segc[r], segr[r])
    ffn_parts = {}
    for r in rows:
        if ways == 4:
            pairs = gather_halves(ol[r][: length // 2], ol[r][length // 2 :])
            ol_pieces = [ol[r]] + [jnp.concatenate(p) for p in pairs]
        else:
            ol_pieces = gather_rel(ol[r], ways)
        hl[r], n1[r], rstd1[r] = out_norm(info[r], r, ol_pieces, ow_pieces, tokens, gain1, bias1)
        (al[r], slope_g[r], slope_u[r]), ffn_parts[r] = ffn_fwd(
            hl[r], gate_weight, up_weight, down_weight, ways
        )
    for r in rows:
        total = scatter_sum(ffn_parts[r], ways)
        resid = deep_alpha * (n1[r] * gain1 + bias1) + total
        r2_pieces[r] = gather_tokens(resid.astype(BF), ways)

    activations = None
    dh_parts = {}
    for r in rows:
        activations, dffn[r], norm2_sums[r] = norm_two(
            info[r], share[r], r, r2_pieces[r], cotangent, gain2, bias2, activations
        )
        dgate[r], dup[r], dh_parts[r] = ffn_bwd(
            dffn[r], slope_g[r], slope_u[r], gate_weight, up_weight, down_weight, ways
        )

    def update(lefts, rights):
        total = None
        for r in rows:
            one = mm_tn(lefts[r], rights[r])
            total = one if total is None else total + one
        return total.astype(BF)

    def reduced(lefts, rights):
        return sum_gradient(update(lefts, rights), data_ways, objective_ways)

    down_grad = reduced(al, dffn)
    gate_grad = reduced(hl, dgate)
    up_grad = reduced(hl, dup)

    dx_parts = {}
    for r in rows:
        total = scatter_sum(dh_parts[r], ways)
        dh = deep_alpha * dffn[r][:block].astype(F32) + total
        scaled = dh * gain1
        inner = jnp.mean(scaled, axis=1, keepdims=True) + n1[r] * jnp.mean(
            scaled * n1[r], axis=1, keepdims=True
        )
        dr1[r] = rstd1[r][:, :1] * (scaled - inner)
        norm1_sums[r] = jnp.stack([jnp.sum(dh * n1[r], axis=0), jnp.sum(dh, axis=0)])
        dattn[r] = join(gather_tokens(dr1[r].astype(BF), ways))
    for r in rows:
        dol = mm_nt(dattn[r], out_weight).astype(BF).reshape(ways, block, -1)
        dqkv[r] = attn_bwd(info[r], qkv[r], dol, lse[r], cosine, sine, segc[r], segr[r])
        dx_parts[r] = input_back(info[r], dqkv[r], qkv_weight, ways)

    qkv_grad = reduced([tokens[r] for r in rows], dqkv)
    ol_rel = {}
    for r in rows:
        parts = ol[r].reshape(ways, block, -1)
        ol_rel[r] = jnp.stack(
            [lax.dynamic_index_in_dim(parts, me ^ i, 0, keepdims=False) for i in range(ways)]
        ).reshape(length, -1)
    out_grad = reduced(ol_rel, dattn)

    input_grad = None
    for r in rows:
        total = scatter_sum(dx_parts[r], ways)
        dx = (deep_alpha * dr1[r] + total).astype(BF)
        input_grad = place(info[r], r, gather_tokens(dx, ways), tokens.shape, input_grad)

    first = (me == 0).astype(F32)
    sums = jnp.concatenate(
        [sum(norm1_sums[r] for r in rows), sum(norm2_sums[r] for r in rows) * first]
    )
    sums = lax.psum(sums, ("obj", "dp", "tensor"))
    return (
        activations,
        input_grad,
        qkv_grad,
        out_grad,
        gate_grad,
        up_grad,
        down_grad,
        sums[0],
        sums[1],
        sums[2],
        sums[3],
    )


ORDER = ((1, 0), (3, 0), (2, 1), (3, 1), (1, 1), (2, 0), (0, 0), (0, 1))
CORES = ((0, 1), (1, 0))
COST_SHARE = 0.1


def plane_case(token_shape, down_shape):
    return (
        lax.axis_size("tensor") == 4
        and lax.axis_size("dp") == 2
        and lax.axis_size("obj") == 4
        and token_shape[0] == 2
        and token_shape[1] % 1024 == 0
        and token_shape[2] % 1024 == 0
        and down_shape[0] % 128 == 0
    )


def spec(shape, index):
    return pl.BlockSpec(shape, index)


def call(
    kernel, name, grid, ins, in_specs, outs, out_specs, scalars=(), after=(), scratch=(), aliases=None,
    mib=48, flops=0, nbytes=0,
):
    ns, ni, na = len(scalars), len(ins), len(after)

    def wrapped(*refs):
        kernel(*refs[: ns + ni], *refs[ns + ni + na :])

    grid_spec = pltpu.PrefetchScalarGridSpec(
        num_scalar_prefetch=ns,
        grid=grid,
        in_specs=list(in_specs) + [pl.BlockSpec(memory_space=ANY)] * na,
        out_specs=list(out_specs),
        scratch_shapes=list(scratch),
    )
    return pl.pallas_call(
        wrapped,
        grid_spec=grid_spec,
        out_shape=[jax.ShapeDtypeStruct(s, d) for s, d in outs],
        input_output_aliases={ns + k: v for k, v in (aliases or {}).items()},
        compiler_params=params(62, len(grid)),
        cost_estimate=cost(flops / COST_SHARE, nbytes / COST_SHARE),
        name=name,
    )(*scalars, *ins, *after)


def constant_tables(length):
    half = HEAD_DIM // 2
    frequency = np.exp(np.arange(half, dtype=np.float32) * np.float32(-2.0 * math.log(10000.0) / HEAD_DIM))
    angles = np.arange(length, dtype=np.float32)[:, None] * frequency[None, :]
    cosine, sine = np.cos(angles), np.sin(angles)
    both = lambda a, b: jnp.asarray(np.concatenate([a, b], axis=1).astype(np.float32))
    return both(cosine, cosine), both(-sine, sine)


class Chain:
    def __init__(self):
        self.last = ()

    def __call__(self, *args, after=(), **kwargs):
        out = call(*args, after=tuple(self.last) + tuple(after), **kwargs)
        self.last = (out[0],)
        return out


def pair_swap(to_x, to_y):
    return swap(to_x, 1, 4), swap(to_y, 2, 4)


def plane_attn_fwd(chain, info, row, tokens, qkv_weight, cosine, sine, segc, segr, after=()):
    _, length, width = tokens.shape
    heads = qkv_weight.shape[1] // (3 * HEAD_DIM)
    return chain(
        functools.partial(attn_fwd_kernel, tile=256),
        "attn_fwd",
        (heads,),
        (tokens, qkv_weight, cosine, sine, segc, segr),
        [
            pl.BlockSpec((None, length, width), lambda h, *_: (row, 0, 0), pipeline_mode=pl.Buffered(1)),
            spec((width, 3 * HEAD_DIM), lambda h, *_: (0, h)),
            const_spec((length, HEAD_DIM)),
            const_spec((length, HEAD_DIM)),
            const_spec((length, 1)),
            const_spec((1, length)),
        ],
        [((length, heads * 384), BF), ((length, heads * 128), BF), ((heads, 1, length), F32)],
        [
            spec((length, 384), lambda h, *_: (0, h)),
            spec((length, 128), lambda h, *_: (0, h)),
            spec((None, 1, length), lambda h, *_: (h, 0, 0)),
        ],
        scalars=(info,),
        after=after,
        scratch=[pltpu.VMEM((length, length), F32)],
        flops=heads * (2 * length * width * 384 + 8 * length * length * 128),
        nbytes=2 * length * width + 2 * width * heads * 384 + 8 * length * heads * 128,
    )


def plane_attn_bwd_kernel(
    info_ref, qkv_ref, own, r1, r2, r3a, r3b, ow_ref, lse_ref, cos_ref, sin_ref, segc_ref, segr_ref, dqkv_ref,
    bias_ref, dol_nat, dk_ref, dv_ref,
):
    length = qkv_ref.shape[0]
    block = own.shape[0]
    half = block // 2
    me = info_ref[0]

    @pl.when(pl.program_id(0) == 0)
    def _():
        fill_bias(info_ref, segc_ref, segr_ref, bias_ref, block)

    def natural(r, lower):
        return pl.multiple_of((me ^ r) * block + lower, half)

    for r, piece in enumerate((own, r1, r2)):
        dol_nat[pl.ds(natural(r, 0), block), :] = mm_nt(piece[...], ow_ref[...]).astype(BF)
    for lower, piece in ((0, r3a), (half, r3b)):
        dol_nat[pl.ds(natural(3, lower), half), :] = mm_nt(piece[...], ow_ref[...]).astype(BF)
    attn_bwd_head(qkv_ref, dol_nat, lse_ref, cos_ref, sin_ref, dqkv_ref, bias_ref, dk_ref, dv_ref, block)


def attn_bwd_head(qkv_ref, dol_nat, lse_ref, cos_ref, sin_ref, dqkv_ref, bias_ref, dk_ref, dv_ref, tile):
    length = qkv_ref.shape[0]
    keys = qkv_ref[:, HEAD_DIM : 2 * HEAD_DIM]
    values = qkv_ref[:, 2 * HEAD_DIM :]
    keys_t = keys.astype(F32).T.astype(BF)
    for step in range(length // tile):
        rows = pl.ds(step * tile, tile)
        queries = qkv_ref[rows, :HEAD_DIM]
        dol = dol_nat[rows, :]
        scores = mm_nt(keys, queries) * score_scale + bias_ref[:, rows]
        probs = jnp.exp(scores - lse_ref[:, rows])
        dp = mm_nt(values, dol)
        inner = jnp.sum(probs * dp, axis=0, keepdims=True)
        draw = (probs * (dp - inner) * score_scale).astype(BF)
        dv = mm(probs.astype(BF), dol)
        dk = mm(draw, queries)
        if step == 0:
            dv_ref[...] = dv
            dk_ref[...] = dk
        else:
            dv_ref[...] += dv
            dk_ref[...] += dk
        dq = mm(keys_t, draw).T
        turned = dq * cos_ref[rows, :] - pltpu.roll(dq, HEAD_DIM // 2, 1) * sin_ref[rows, :]
        dqkv_ref[rows, :HEAD_DIM] = turned.astype(BF)
    dk = dk_ref[...]
    turned = dk * cos_ref[...] - pltpu.roll(dk, HEAD_DIM // 2, 1) * sin_ref[...]
    dqkv_ref[:, HEAD_DIM : 2 * HEAD_DIM] = turned.astype(BF)
    dqkv_ref[:, 2 * HEAD_DIM :] = dv_ref[...].astype(BF)


def plane_attn_bwd(chain, info, qkv, pieces, out_weight, lse, cosine, sine, segc, segr, after=()):
    length = qkv.shape[0]
    heads = qkv.shape[1] // 384
    width = out_weight.shape[1]
    return chain(
        plane_attn_bwd_kernel,
        "attn_bwd",
        (heads,),
        (qkv, *pieces, out_weight, lse, cosine, sine, segc, segr),
        [spec((length, 384), lambda h, *_: (0, h))]
        + [const_spec(p.shape) for p in pieces]
        + [
            spec((128, width), lambda h, *_: (h, 0)),
            spec((None, 1, length), lambda h, *_: (h, 0, 0)),
            const_spec((length, HEAD_DIM)),
            const_spec((length, HEAD_DIM)),
            const_spec((length, 1)),
            const_spec((1, length)),
        ],
        [(qkv.shape, BF)],
        [spec((length, 384), lambda h, *_: (0, h))],
        scalars=(info,),
        after=after,
        scratch=[
            pltpu.VMEM((length, length), F32),
            pltpu.VMEM((length, HEAD_DIM), BF),
            pltpu.VMEM((length, HEAD_DIM), F32),
            pltpu.VMEM((length, HEAD_DIM), F32),
        ],
        flops=heads * 24 * length * length * 128,
        nbytes=16 * length * heads * 128,
    )[0]


def plane_out_norm_kernel(
    info_ref, order_ref, *refs
):
    lows, highs = refs[:4], refs[4:8]
    ow_ref, mine_ref, other_ref = refs[8:11]
    xl_ref, xh_ref, gain_ref, bias_ref, hl_ref, n1_ref, rstd_ref, total_ref = refs[11:]
    half = xl_ref.shape[0]
    feat = mine_ref.shape[0] // 3
    total_ref[:half] = xl_ref[...].astype(F32) * deep_alpha
    total_ref[half:] = xh_ref[...].astype(F32) * deep_alpha
    ols = [jnp.concatenate([lo[...], hi[...]], axis=0) for lo, hi in zip(lows, highs)]

    def add(first, second):
        total = mm(ols[0], ow_ref[...])
        for r in range(1, 4):
            rows = pl.ds((r - 1) * feat, feat)
            total += mm(ols[r][:, :feat], first[rows, :])
            total += mm(ols[r][:, feat:], second[rows, :])
        total_ref[...] += total

    @pl.when(info_ref[3] == 0)
    def _():
        add(mine_ref, other_ref)

    @pl.when(info_ref[3] != 0)
    def _():
        add(other_ref, mine_ref)

    total = total_ref[...]
    centered = total - jnp.mean(total, axis=1, keepdims=True)
    variance = jnp.mean(centered * centered, axis=1, keepdims=True)
    inv = lax.rsqrt(variance + norm_eps)
    normed = centered * inv
    hl_ref[...] = (normed * gain_ref[...] + bias_ref[...]).astype(BF)

    @pl.when(pl.program_id(0) == 3)
    def _():
        n1_ref[...] = normed
        rstd_ref[...] = jnp.broadcast_to(inv, rstd_ref.shape)


def plane_out_norm(chain, info, order, row, ol_pieces, out_weight, mine, other, tokens, gain, bias, after=()):
    _, length, width = tokens.shape
    block = length // 4
    half = block // 2
    head_width = out_weight.shape[0]
    low = lambda i, info, order: (order[2 * i], 0)
    high = lambda i, info, order: (order[2 * i + 1], 0)
    low3 = lambda i, info, order: (row, order[2 * i], 0)
    high3 = lambda i, info, order: (row, order[2 * i + 1], 0)
    return chain(
        plane_out_norm_kernel,
        "out_norm",
        (4,),
        (*ol_pieces, *ol_pieces, out_weight, mine, other, tokens, tokens, gain, bias),
        [spec((half, head_width), low)] * 4
        + [spec((half, head_width), high)] * 4
        + [const_spec(out_weight.shape), const_spec(mine.shape), const_spec(other.shape)]
        + [
            spec((None, half, width), low3),
            spec((None, half, width), high3),
            const_spec((1, width)),
            const_spec((1, width)),
        ],
        [((length, width), BF), ((block, width), F32), ((block, HEAD_DIM), F32)],
        [
            spec((block, width), lambda i, *_: (i, 0)),
            spec((block, width), lambda i, *_: (0, 0)),
            spec((block, HEAD_DIM), lambda i, *_: (0, 0)),
        ],
        scalars=(info, order),
        after=after,
        scratch=[pltpu.VMEM((block, width), F32)],
        flops=2 * length * width * width,
        nbytes=2 * width * width + 6 * length * width,
    )


def split_kernel(x_ref, y_ref, *refs):
    count = len(refs) // 2 - 1
    refs[count][...] = x_ref[...]
    refs[count + 1][...] = y_ref[...]


def forward(chain, from_x, from_y, carry=(), after=()):
    rows, width = from_x.shape
    shape = (rows // 2, width)
    any_spec = pl.BlockSpec(memory_space=ANY)
    out = chain(
        split_kernel, "split", (1,), (from_x, from_y, *carry),
        [
            pl.BlockSpec(shape, lambda i, *_: (0, 0), pipeline_mode=pl.Buffered(1)),
            pl.BlockSpec(shape, lambda i, *_: (1, 0), pipeline_mode=pl.Buffered(1)),
        ]
        + [any_spec] * len(carry),
        [(shape, BF)] * 2 + [(c.shape, c.dtype) for c in carry],
        [spec(shape, lambda i, *_: (0, 0))] * 2 + [any_spec] * len(carry),
        after=after,
        aliases={2 + k: 2 + k for k in range(len(carry))},
        nbytes=4 * rows * width,
    )
    pair = (swap(out[0], 2, 4), swap(out[1], 1, 4))
    return (pair, *out[2:]) if carry else pair


def ow_join_kernel(x_ref, y_ref, a_ref, b_ref, out_ref):
    rows = x_ref.shape[0]
    out_ref[:rows] = x_ref[...]
    out_ref[rows : 2 * rows] = y_ref[...]
    out_ref[2 * rows : 2 * rows + rows // 2] = a_ref[...]
    out_ref[2 * rows + rows // 2 :] = b_ref[...]


def ow_join(chain, pieces, after=()):
    rows, width = pieces[0].shape
    shape = (3 * rows, width)
    return chain(
        ow_join_kernel, "ow_join", (1,), pieces, [const_spec(p.shape) for p in pieces],
        [(shape, BF)], [spec(shape, lambda i, *_: (0, 0))], after=after,
    )[0]


def join_kernel(a_ref, b_ref, carried, out_ref, carried_out):
    half = a_ref.shape[0]
    out_ref[:half] = a_ref[...]
    out_ref[half:] = b_ref[...]


def join_halves(chain, halves, carry, after=()):
    rows, width = halves[0].shape
    shape = (2 * rows, width)
    out = chain(
        join_kernel, "join_halves", (1,), (*halves, carry),
        [const_spec(h.shape) for h in halves] + [pl.BlockSpec(memory_space=ANY)],
        [(shape, BF), (carry.shape, carry.dtype)],
        [spec(shape, lambda i, *_: (0, 0)), pl.BlockSpec(memory_space=ANY)],
        after=after, aliases={2: 1}, nbytes=4 * rows * width,
    )
    return out


def load_once(pairs, sem):
    copies = [pltpu.make_async_copy(src, dst, sem.at[k]) for k, (src, dst) in enumerate(pairs)]

    @pl.when(pl.program_id(0) == 0)
    def _():
        for copy in copies:
            copy.start()

    def wait(k):
        @pl.when(pl.program_id(0) == 0)
        def _():
            copies[k].wait()

    return wait


def store_half(first, part, refs):
    at = pl.program_id(0)
    half = part.shape[0] // 2
    if first is None:

        @pl.when(at == 0)
        def _():
            refs[0][...] = part

        @pl.when(at == 1)
        def _():
            refs[1][...] = part

        @pl.when(at == 2)
        def _():
            refs[2][...] = part[:half]
            refs[3][...] = part[half:]

        @pl.when(at == 3)
        def _():
            refs[4][...] = part

        return

    @pl.when(at == 0)
    def _():
        if first:
            refs[0][...] = part
        else:
            refs[0][...] = part[:half]
            refs[1][...] = part[half:]

    @pl.when(at == 1)
    def _():
        refs[-1][...] = part


def half_outs(first, block, width):
    if first is None:
        sizes = [block, block, block // 2, block // 2, block]
    else:
        sizes = [block, block] if first else [block // 2, block // 2, block]
    return [((s, width), BF) for s in sizes], [spec((s, width), lambda i, *_: (0, 0)) for s in sizes]


def plane_ffn_fwd_kernel(hl_ref, wg_hbm, wu_hbm, wd_hbm, *refs, first):
    refs, (wg, wu, wd, sem) = refs[:-4], refs[-4:]
    (al_ref, ga_ref, gb_ref), refs = refs[-3:], refs[:-3]
    wait = load_once(((wg_hbm, wg), (wu_hbm, wu), (wd_hbm, wd)), sem)
    hidden = hl_ref[...]
    wait(0)
    gate = mm(hidden, wg[...])
    wait(1)
    up = mm(hidden, wu[...])
    cdf = 0.5 + 0.5 * lax.erf(gate * (1.0 / math.sqrt(2.0)))
    pdf = jnp.exp(gate * gate * -0.5) * (1.0 / math.sqrt(2.0 * math.pi))
    act = gate * cdf
    ga_ref[...] = (up * (cdf + gate * pdf)).astype(BF)
    gb_ref[...] = act.astype(BF)
    low = (act * up).astype(BF)
    al_ref[...] = low
    wait(2)
    store_half(first, mm(low, wd[...]).astype(BF), refs)


def plane_ffn_fwd(chain, first, hidden, weights, kept, after=()):
    length, width = hidden.shape
    units = weights[0].shape[1]
    block = length // 4
    base = 0 if first else 2
    tiled = lambda w: spec((block, w), lambda i, *_: (i + base, 0))
    outs, out_specs = half_outs(first, block, width)
    n = len(outs)
    any_spec = pl.BlockSpec(memory_space=ANY)
    kept = () if first else tuple(kept)
    held, carried = kept[:3], kept[3:]
    kernel = functools.partial(plane_ffn_fwd_kernel, first=first)
    if first:
        body_kernel = kernel
    else:
        nk, nc = len(kept), len(carried)

        def body_kernel(hl, wg, wu, wd, *refs):
            refs = refs[nk:]
            kernel(hl, wg, wu, wd, *refs[:n], *refs[n + nc :])

    out = chain(
        body_kernel,
        "ffn_fwd",
        (2,),
        (hidden, *weights, *kept),
        [tiled(width)] + [any_spec] * (3 + len(kept)),
        outs + [(c.shape, BF) for c in carried] + [((length, units), BF)] * 3,
        out_specs + [any_spec] * len(carried) + [tiled(units)] * 3,
        after=after,
        aliases={}
        if first
        else {
            **{4 + k: n + len(carried) + k for k in range(3)},
            **{7 + k: n + k for k in range(len(carried))},
        },
        scratch=[
            pltpu.VMEM(weights[0].shape, BF),
            pltpu.VMEM(weights[1].shape, BF),
            pltpu.VMEM(weights[2].shape, BF),
            pltpu.SemaphoreType.DMA((3,)),
        ],
        mib=60,
        flops=3 * length * width * units,
        nbytes=6 * units * width + 3 * length * units,
    )
    n += len(carried)
    return out[:n], out[n:]


def plane_ffn_bwd_kernel(dffn_ref, ga_ref, gb_ref, wd_hbm, wg_hbm, wu_hbm, *refs, first):
    refs, (wd, wg, wu, sem) = refs[:-4], refs[-4:]
    (dg_ref, du_ref), refs = refs[-2:], refs[:-2]
    wait = load_once(((wd_hbm, wd), (wg_hbm, wg), (wu_hbm, wu)), sem)
    grad = dffn_ref[...]
    wait(0)
    dact = mm_nt(grad, wd[...])
    dgate = (dact * ga_ref[...].astype(F32)).astype(BF)
    dup = (dact * gb_ref[...].astype(F32)).astype(BF)
    dg_ref[...] = dgate
    du_ref[...] = dup
    wait(1)
    part = mm_nt(dgate, wg[...])
    wait(2)
    part += mm_nt(dup, wu[...])
    store_half(first, part.astype(BF), refs)


def plane_ffn_bwd(chain, first, dffn, slopes, weights, kept, after=()):
    length, width = dffn.shape
    units = weights[0].shape[1]
    block = length // 4
    base = 2 if first is False else 0
    steps = 4 if first is None else 2
    tiled = lambda w: spec((block, w), lambda i, *_: (i + base, 0))
    outs, out_specs = half_outs(first, block, width)
    n = len(outs)
    any_spec = pl.BlockSpec(memory_space=ANY)
    kept = tuple(kept)
    kernel = functools.partial(plane_ffn_bwd_kernel, first=first)
    carried = kept[2:]
    if first is not False:
        body_kernel = kernel
    else:
        nk, nc = len(kept), len(carried)

        def body_kernel(d, ga, gb, wd, wg, wu, *refs):
            refs = refs[nk:]
            kernel(d, ga, gb, wd, wg, wu, *refs[:n], *refs[n + nc :])

    out = chain(
        body_kernel,
        "ffn_bwd",
        (steps,),
        (dffn, *slopes, weights[2], weights[0], weights[1], *kept),
        [tiled(width), tiled(units), tiled(units)] + [any_spec] * (3 + len(kept)),
        outs + [(c.shape, BF) for c in carried] + [((length, units), BF)] * 2,
        out_specs + [any_spec] * len(carried) + [tiled(units)] * 2,
        after=after,
        aliases={}
        if first is not False
        else {
            **{6 + k: n + len(carried) + k for k in range(2)},
            **{8 + k: n + k for k in range(len(carried))},
        },
        scratch=[
            pltpu.VMEM(weights[2].shape, BF),
            pltpu.VMEM(weights[0].shape, BF),
            pltpu.VMEM(weights[1].shape, BF),
            pltpu.SemaphoreType.DMA((3,)),
        ],
        mib=60,
        flops=3 * length * width * units * steps // 2,
        nbytes=6 * units * width + 4 * length * units,
    )
    n += len(carried)
    return out[:n], out[n:]


def middle_kernel(x1_ref, y1_ref, r1b_ref, r2a_ref, x2_ref, y2_ref):
    half = r1b_ref.shape[0]
    x2_ref[...] = (r1b_ref[...].astype(F32) + y1_ref[half:].astype(F32)).astype(BF)
    y2_ref[...] = (r2a_ref[...].astype(F32) + x1_ref[half:].astype(F32)).astype(BF)


def middle(chain, arrived, r1b, r2a, after=()):
    x1, y1 = arrived
    shape = r1b.shape
    return chain(
        middle_kernel,
        "middle_sum",
        (1,),
        (x1, y1, r1b, r2a),
        [const_spec(a.shape) for a in (x1, y1, r1b, r2a)],
        [(shape, BF)] * 2,
        [spec(shape, lambda i, *_: (0, 0))] * 2,
        after=after,
        mib=32,
        nbytes=16 * r1b.size,
    )


def own_sum(own, x1, y1, x2, y2):
    top = pl.program_id(0) < OWN_STEPS // 2
    direct = jnp.where(top, x1[...].astype(F32), y1[...].astype(F32))
    relayed = jnp.where(top, y2[...].astype(F32), x2[...].astype(F32))
    return own[...].astype(F32) + direct + relayed


def resid_two_kernel(own, x1, y1, x2, y2, n1_ref, gain_ref, bias_ref, out_ref):
    total = own_sum(own, x1, y1, x2, y2)
    out_ref[...] = (deep_alpha * (n1_ref[...] * gain_ref[...] + bias_ref[...]) + total).astype(BF)


def norm_one_back_kernel(own, x1, y1, x2, y2, dffn_ref, n1_ref, rstd_ref, gain_ref, low_ref, dr1_ref, sums_ref):
    total = own_sum(own, x1, y1, x2, y2)
    dh = deep_alpha * dffn_ref[...].astype(F32) + total
    normed = n1_ref[...]
    scaled = dh * gain_ref[...]
    inner = jnp.mean(scaled, axis=1, keepdims=True) + normed * jnp.mean(scaled * normed, axis=1, keepdims=True)
    dr1 = rstd_ref[:, :1] * (scaled - inner)
    dr1_ref[...] = dr1
    low_ref[...] = dr1.astype(BF)
    gain_sum = jnp.sum(dh * normed, axis=0, keepdims=True)
    bias_sum = jnp.sum(dh, axis=0, keepdims=True)

    @pl.when(pl.program_id(0) == 0)
    def _():
        sums_ref[0:1, :] = gain_sum
        sums_ref[1:2, :] = bias_sum

    @pl.when(pl.program_id(0) > 0)
    def _():
        sums_ref[0:1, :] += gain_sum
        sums_ref[1:2, :] += bias_sum


def input_grad_kernel(own, x1, y1, x2, y2, dr1_ref, out_ref):
    out_ref[...] = (deep_alpha * dr1_ref[...] + own_sum(own, x1, y1, x2, y2)).astype(BF)


OWN_STEPS = 4


def rows_spec(array_shape, tile, base=0):
    return spec((tile, array_shape[1]), lambda i, *_: (i + base, 0))


def own_step(chain, kernel, name, sums, extra, extra_specs, outs, after=()):
    block, width = sums[0].shape
    tile = block // OWN_STEPS
    middle_step = OWN_STEPS // 2
    first = spec((tile, width), lambda i, *_: (jnp.minimum(i, middle_step - 1), 0))
    later = spec((tile, width), lambda i, *_: (jnp.maximum(i - middle_step, 0), 0))
    return chain(
        kernel,
        name,
        (OWN_STEPS,),
        (*sums, *extra),
        [rows_spec((block, width), tile), first, later, later, first] + extra_specs,
        outs,
        [rows_spec(s, tile) if s[0] == block else spec(s, lambda i, *_: (0, 0)) for s, _ in outs],
        after=after,
        mib=40,
        nbytes=16 * block * width,
    )


def plane_norm_two_kernel(info_ref, order_ref, share_ref, own, r1, r2, r3a, r3b, cot_ref, gain_ref, bias_ref, *refs):
    act_ref, sums_ref, dffn_ref, held = refs[-4:]
    at = pl.program_id(0)
    half = held.shape[0]
    places = (
        (r1, 0), (r3a, 0), (r2, half), (r3b, 0), (r1, half), (r2, 0), (own, 0), (own, half),
    )
    for k, (ref, start) in enumerate(places):

        @pl.when(at == k)
        def _(ref=ref, start=start):
            held[...] = ref[start : start + half]

    resid = held[...].astype(F32)
    centered = resid - jnp.mean(resid, axis=1, keepdims=True)
    variance = jnp.mean(centered * centered, axis=1, keepdims=True)
    inv = lax.rsqrt(variance + norm_eps)
    normed = centered * inv
    gain = gain_ref[...]
    act_ref[...] = (normed * gain + bias_ref[...]).astype(BF)
    dout = cot_ref[...].astype(F32) * share_ref[0]
    scaled = dout * gain
    inner = jnp.mean(scaled, axis=1, keepdims=True) + normed * jnp.mean(scaled * normed, axis=1, keepdims=True)
    dffn_ref[...] = (inv * (scaled - inner)).astype(BF)
    gain_sum = jnp.sum(dout * normed, axis=0, keepdims=True)
    bias_sum = jnp.sum(dout, axis=0, keepdims=True)

    @pl.when(at == 0)
    def _():
        sums_ref[0:1, :] = gain_sum
        sums_ref[1:2, :] = bias_sum

    @pl.when(at > 0)
    def _():
        sums_ref[0:1, :] += gain_sum
        sums_ref[1:2, :] += bias_sum


def plane_norm_two(chain, info, order, share, row, pieces, cotangent, gain, bias, before, after=()):
    rows, length, width = cotangent.shape
    half = length // 8
    natural = spec((None, half, width), lambda i, info, order, share: (row, order[i], 0))
    held = () if before is None else (before,)
    return chain(
        plane_norm_two_kernel,
        "norm_two",
        (8,),
        (*pieces, cotangent, gain, bias, *held),
        [const_spec(p.shape) for p in pieces]
        + [natural, const_spec((1, width)), const_spec((1, width))]
        + [pl.BlockSpec(memory_space=ANY)] * len(held),
        [(cotangent.shape, BF), ((2, width), F32), ((length, width), BF)],
        [natural, spec((2, width), lambda i, *_: (0, 0)), spec((half, width), lambda i, *_: (i, 0))],
        scalars=(info, order, share),
        after=after,
        aliases={len(pieces) + 3: 0} if held else {},
        scratch=[pltpu.VMEM((half, width), BF)],
        flops=20 * length * width,
        nbytes=8 * length * width,
    )


def plane_input_back_kernel(order_ref, low_ref, high_ref, w_ref, x1_ref, y1_ref, r1b_ref, r2a_ref, own_ref):
    at = pl.program_id(0)
    half = low_ref.shape[0]
    part = mm_nt(jnp.concatenate([low_ref[...], high_ref[...]], axis=0), w_ref[...]).astype(BF)

    @pl.when(at == 0)
    def _():
        x1_ref[...] = part

    @pl.when(at == 1)
    def _():
        y1_ref[...] = part

    @pl.when(at == 2)
    def _():
        r1b_ref[...] = part[:half]
        r2a_ref[...] = part[half:]

    @pl.when(at == 3)
    def _():
        own_ref[...] = part


def plane_input_back(chain, order, dqkv, qkv_weight, after=()):
    length, columns = dqkv.shape
    width = qkv_weight.shape[0]
    block = length // 4
    half = block // 2
    sizes = [block, block, half, half, block]
    return chain(
        plane_input_back_kernel,
        "input_back",
        (4,),
        (dqkv, dqkv, qkv_weight),
        [
            spec((half, columns), lambda i, order: (order[2 * i], 0)),
            spec((half, columns), lambda i, order: (order[2 * i + 1], 0)),
            const_spec(qkv_weight.shape),
        ],
        [((s, width), BF) for s in sizes],
        [spec((s, width), lambda i, *_: (0, 0)) for s in sizes],
        scalars=(order,),
        after=after,
        flops=2 * length * width * columns,
        nbytes=2 * width * columns + 4 * length * width,
    )


def plane_place_kernel(order_ref, own, r1, r2, r3a, r3b, *refs):
    out_ref = refs[-1]
    at = pl.program_id(0)
    half = r3a.shape[0]
    for k, ref in enumerate((own, r1, r2)):

        @pl.when(at == k)
        def _(ref=ref):
            out_ref[...] = ref[...]

    @pl.when(at == 3)
    def _():
        out_ref[:half] = r3a[...]
        out_ref[half:] = r3b[...]


def plane_place(chain, info, row, pieces, shape, before, after=()):
    rows, length, width = shape
    block = length // 4
    held = () if before is None else (before,)
    return chain(
        plane_place_kernel,
        "place",
        (4,),
        (*pieces, *held),
        [const_spec(p.shape) for p in pieces] + [pl.BlockSpec(memory_space=ANY)] * len(held),
        [(shape, BF)],
        [spec((None, block, width), lambda i, info: (row, i ^ info[0], 0))],
        scalars=(info,),
        after=after,
        aliases={len(pieces): 0} if held else {},
        mib=32,
        nbytes=4 * length * width,
    )[0]


def panels(ref, value):
    for c in range(value.shape[1] // 128):
        ref[c] = value[:, c * 128 : (c + 1) * 128].astype(BF)


def grad_rows_kernel(info_ref, left_a, left_b, right_a, right_b, send, keep, *, steps):
    at = pl.program_id(0)
    value = mm(left_a[...].T, right_a[...]) + mm(left_b[...].T, right_b[...])

    @pl.when(at < steps)
    def _():
        panels(send, value)

    @pl.when(at >= steps)
    def _():
        panels(keep, value)


def lhs_spec(lhs, tile, index, row):
    if lhs.ndim == 3:
        return spec((None, lhs.shape[1], tile), lambda *a: (row, 0, index(*a)))
    return spec((lhs.shape[0], tile), lambda *a: (0, index(*a)))


def grad_rows(chain, info, lefts, rights, after=()):
    rows = lefts[0].shape[-1]
    tile = 256
    steps = rows // tile // 2
    length, columns = rights[0].shape

    def at(i, info):
        other = (1 - info[3]) * steps + i
        own = info[3] * steps + i - steps
        return jnp.where(i < steps, other, own)

    shape = (columns // 128, rows // 2, 128)
    out = chain(
        functools.partial(grad_rows_kernel, steps=steps),
        "grad_rows",
        (2 * steps,),
        (*lefts, *rights),
        [lhs_spec(lefts[r], tile, at, r) for r in range(2)] + [const_spec(r.shape) for r in rights],
        [(shape, BF)] * 2,
        [
            spec((shape[0], tile, 128), lambda i, *_: (0, jnp.minimum(i, steps - 1), 0)),
            spec((shape[0], tile, 128), lambda i, *_: (0, jnp.maximum(i - steps, 0), 0)),
        ],
        scalars=(info,),
        after=after,
        flops=4 * rows * length * columns,
        nbytes=2 * rows * columns + 4 * rows * length,
    )
    return out[0].reshape(-1, 128), out[1].reshape(-1, 128)


def grad_columns_kernel(info_ref, left_a, left_b, right_a, right_b, send, keep, turned_a, turned_b, held):
    @pl.when(pl.program_id(0) == 0)
    def _():
        turned_a[...] = left_a[...].T
        turned_b[...] = left_b[...].T

    held[...] = mm(turned_a[...], right_a[...]) + mm(turned_b[...], right_b[...])
    half = held.shape[0] // 2
    core = info_ref[3]
    panels(send, held[pl.ds(pl.multiple_of((1 - core) * half, 8), half), :])
    panels(keep, held[pl.ds(pl.multiple_of(core * half, 8), half), :])


def grad_columns(chain, info, lefts, rights, after=()):
    length, rows = lefts[0].shape
    columns = rights[0].shape[1]
    tile = 256
    shape = (columns // 128, rows // 2, 128)
    out = chain(
        grad_columns_kernel,
        "grad_columns",
        (columns // tile,),
        (*lefts, *rights),
        [const_spec(left.shape) for left in lefts] + [spec((length, tile), lambda i, *_: (0, i))] * 2,
        [(shape, BF)] * 2,
        [spec((tile // 128, rows // 2, 128), lambda i, *_: (i, 0, 0))] * 2,
        scalars=(info,),
        after=after,
        scratch=[pltpu.VMEM((rows, length), BF)] * 2 + [pltpu.VMEM((rows, tile), F32)],
        flops=4 * rows * length * columns,
        nbytes=2 * rows * columns + 4 * length * (rows + columns),
    )
    return out[0].reshape(-1, 128), out[1].reshape(-1, 128)


def grad_plain_kernel(left_a, left_b, right_a, right_b, out_ref):
    out_ref[...] = (mm(left_a[...].T, right_a[...]) + mm(left_b[...].T, right_b[...])).astype(BF)


def grad_plain(chain, lefts, rights, after=()):
    rows = lefts[0].shape[-1]
    tile = 256
    length, columns = rights[0].shape
    return chain(
        grad_plain_kernel,
        "grad_plain",
        (rows // tile,),
        (*lefts, *rights),
        [lhs_spec(lefts[r], tile, lambda i, *_: i, r) for r in range(2)] + [const_spec(r.shape) for r in rights],
        [((rows, columns), BF)],
        [spec((tile, columns), lambda i, *_: (i, 0))],
        after=after,
        flops=4 * rows * length * columns,
        nbytes=2 * rows * columns + 4 * rows * length,
    )[0]


def grad_plain_columns_kernel(left_a, left_b, right_a, right_b, out_ref, turned_a, turned_b):
    @pl.when(pl.program_id(0) == 0)
    def _():
        turned_a[...] = left_a[...].T
        turned_b[...] = left_b[...].T

    out_ref[...] = (mm(turned_a[...], right_a[...]) + mm(turned_b[...], right_b[...])).astype(BF)


def grad_plain_columns(chain, lefts, rights, after=()):
    length, rows = lefts[0].shape
    columns = rights[0].shape[1]
    tile = 256
    return chain(
        grad_plain_columns_kernel,
        "grad_plain_columns",
        (columns // tile,),
        (*lefts, *rights),
        [const_spec(left.shape) for left in lefts] + [spec((length, tile), lambda i, *_: (0, i))] * 2,
        [((rows, columns), BF)],
        [spec((rows, tile), lambda i, *_: (0, i))],
        after=after,
        scratch=[pltpu.VMEM((rows, length), BF)] * 2,
        flops=4 * rows * length * columns,
        nbytes=2 * rows * columns + 4 * length * (rows + columns),
    )[0]


def grad_out(lhs, pieces, me):
    block = pieces[0].shape[0]
    half = block // 2
    total = 0.0
    for r, piece in enumerate(pieces[:3]):
        part = lhs[pl.ds(pl.multiple_of((me ^ r) * block, half), block), :]
        total = total + mm(part.T, piece[...])
    for lower, piece in ((0, pieces[3]), (half, pieces[4])):
        part = lhs[pl.ds(pl.multiple_of((me ^ 3) * block + lower, half), half), :]
        total = total + mm(part.T, piece[...])
    return total


def grad_out_kernel(info_ref, left_a, left_b, *refs):
    pieces_a, pieces_b, (send, keep, held) = refs[:5], refs[5:10], refs[10:]
    held[...] = grad_out(left_a, pieces_a, info_ref[0]) + grad_out(left_b, pieces_b, info_ref[0])
    half = held.shape[0] // 2
    core = info_ref[3]
    panels(send, held[pl.ds(pl.multiple_of((1 - core) * half, 8), half), :])
    panels(keep, held[pl.ds(pl.multiple_of(core * half, 8), half), :])


def plane_grad_out(chain, info, lefts, pieces, after=()):
    length, rows = lefts[0].shape
    columns = pieces[0][0].shape[1]
    tile = 512
    shape = (columns // 128, rows // 2, 128)
    every = (*pieces[0], *pieces[1])
    out = chain(
        grad_out_kernel,
        "grad_out",
        (columns // tile,),
        (*lefts, *every),
        [const_spec(left.shape) for left in lefts]
        + [spec((p.shape[0], tile), lambda i, *_: (0, i)) for p in every],
        [(shape, BF)] * 2,
        [spec((tile // 128, rows // 2, 128), lambda i, *_: (i, 0, 0))] * 2,
        scalars=(info,),
        after=after,
        scratch=[pltpu.VMEM((rows, tile), F32)],
        flops=4 * rows * length * columns,
        nbytes=2 * rows * columns + 4 * length * (rows + columns),
    )
    return out[0].reshape(-1, 128), out[1].reshape(-1, 128)


class Line:
    GRID = 4

    def __init__(self, chain, edge):
        self.chain, self.edge = chain, edge
        self.pending = []
        self.slots = []
        self.step = 0
        self.done = {}
        self.first = self.second = None
        self.sent = self.mid = None

    def add(self, name, keep, got, chunks):
        for k in range(chunks):
            self.pending.append((name, keep, got, k, keep.shape[0] // chunks, keep.shape[0]))

    def get(self, j):
        return self.slots[j] if j >= 0 else None

    def busy(self):
        return bool(self.pending) or any(self.slots[-3:])

    def complete(self, name):
        return not any(slot and slot[0] == name for slot in self.pending + self.slots[-3:])

    def advance(self, after=()):
        j = self.step
        self.slots.append(self.pending.pop(0) if self.pending else None)
        new, cur, prev, last = self.get(j), self.get(j - 1), self.get(j - 2), self.get(j - 3)
        ins, in_specs, outs, out_specs, aliases, roles = [], [], [], [], {}, []
        grid = self.GRID

        def give(array, rows, base, role, when):
            block = rows // grid
            if when is None:
                index = lambda i, edge: (base + i, 0)
            elif when:
                index = lambda i, edge: (base + i * edge[0], 0)
            else:
                index = lambda i, edge: (base + i * (1 - edge[0]), 0)
            ins.append(array)
            in_specs.append(spec((block, 128), index))
            roles.append(role)

        if new:
            name, keep, got, k, rows, _ = new
            give(keep, rows, k * grid, "new_keep", True)
            give(got, rows, k * grid, "new_got", True)
        if cur:
            name, keep, got, k, rows, _ = cur
            give(keep, rows, k * grid, "cur_keep", False)
            give(got, rows, k * grid, "cur_got", False)
            give(self.first, rows, 0, "cur_in", False)
        if prev:
            rows = prev[4]
            give(self.mid, rows, 0, "prev_mid", False)
            give(self.second, rows, 0, "prev_in", False)
        if last:
            rows = last[4]
            give(self.first, rows, 0, "last_in", True)
            give(self.sent, rows, 0, "last_sent", False)
            if last[3] > 0:
                ins.append(self.done[last[0]])
                in_specs.append(pl.BlockSpec(memory_space=ANY))
                roles.append("held")
        names = []
        if new or prev:
            rows = max(c[4] for c in (new, prev) if c)
            outs.append(((rows, 128), BF))
            out_specs.append(pl.BlockSpec((rows, 128), lambda i, *_: (0, 0)))
            names.append("sent")
        if cur:
            outs.append(((cur[4], 128), BF))
            out_specs.append(spec((cur[4] // grid, 128), lambda i, *_: (i, 0)))
            names.append("mid")
        if last:
            base = last[3] * grid
            outs.append(((last[5], 128), BF))
            out_specs.append(spec((last[4] // grid, 128), lambda i, *_, base=base: (base + i, 0)))
            names.append("done")
            if last[3] > 0:
                aliases = {len(ins) - 1: len(outs) - 1}

        def kernel(edge_ref, *refs):
            src = dict(zip(roles, refs[: len(roles)]))
            dst = dict(zip(names, refs[len(roles) :]))
            at = pl.program_id(0)
            is_edge = edge_ref[0] == 1
            f32 = lambda r: src[r][...].astype(F32)

            if new:
                @pl.when(is_edge)
                def _():
                    block = new[4] // grid
                    rows = pl.ds(pl.multiple_of(at * block, block), block)
                    dst["sent"][rows, :] = (f32("new_keep") + f32("new_got")).astype(BF)

            @pl.when(jnp.logical_not(is_edge))
            def _():
                if cur:
                    dst["mid"][...] = (f32("cur_keep") + f32("cur_got") + f32("cur_in")).astype(BF)
                if prev:
                    block = prev[4] // grid
                    rows = pl.ds(pl.multiple_of(at * block, block), block)
                    dst["sent"][rows, :] = (f32("prev_mid") + f32("prev_in")).astype(BF)

            if last:
                @pl.when(is_edge)
                def _():
                    dst["done"][...] = src["last_in"][...]

                @pl.when(jnp.logical_not(is_edge))
                def _():
                    dst["done"][...] = src["last_sent"][...]

        out = self.chain(
            kernel,
            "line_step",
            (grid,),
            tuple(ins),
            in_specs,
            outs,
            out_specs,
            scalars=(self.edge,),
            after=after,
            aliases=aliases,
            mib=32,
            nbytes=6 * 5632 * 256,
        )
        got = dict(zip(names, out))
        if "done" in got:
            self.done[last[0]] = got["done"]
        self.sent = got.get("sent")
        self.mid = got.get("mid")
        if self.sent is not None:
            self.first = lax.ppermute(self.sent, "obj", [(0, 1), (3, 2), (1, 0), (2, 3)])
        if self.mid is not None:
            self.second = lax.ppermute(self.mid, "obj", [(1, 2), (2, 1)])
        self.step += 1


def widen_kernel(info_ref, mine_ref, theirs_ref, out_ref, *, steps):
    at = pl.program_id(0)

    @pl.when(at < steps)
    def _():
        for c in range(mine_ref.shape[0]):
            out_ref[:, c * 128 : (c + 1) * 128] = mine_ref[c].astype(F32)

    @pl.when(at >= steps)
    def _():
        for c in range(theirs_ref.shape[0]):
            out_ref[:, c * 128 : (c + 1) * 128] = theirs_ref[c].astype(F32)


def widen(chain, info, mine, theirs, rows, columns, after=()):
    count = columns // 128
    half = rows // 2
    tile = 176 if half % 176 == 0 else min(256, half)
    steps = half // tile
    mine, theirs = (a.reshape(count, half, 128) for a in (mine, theirs))

    def at(i, info):
        return jnp.where(i < steps, info[3] * steps + i, (1 - info[3]) * steps + i - steps)

    return chain(
        functools.partial(widen_kernel, steps=steps),
        "widen",
        (2 * steps,),
        (mine, theirs),
        [
            spec((count, tile, 128), lambda i, *_: (0, jnp.minimum(i, steps - 1), 0)),
            spec((count, tile, 128), lambda i, *_: (0, jnp.maximum(i - steps, 0), 0)),
        ],
        [((rows, columns), F32)],
        [spec((tile, columns), lambda i, info: (at(i, info), 0))],
        scalars=(info,),
        after=after,
        mib=32,
        nbytes=6 * rows * columns,
    )[0]


def add_small_kernel(a_ref, b_ref, out_ref):
    out_ref[...] = a_ref[...] + b_ref[...]


def add_small(chain, a, b):
    return chain(
        add_small_kernel, "add_small", (1,), (a, b), [const_spec(a.shape)] * 2, [(a.shape, F32)],
        [spec(a.shape, lambda i, *_: (0, 0))],
    )[0]


def plane_body(
    tokens,
    cotangent,
    segment_ids,
    mlm_mask,
    glm_prefix,
    glm_span,
    qkv_weight,
    out_weight,
    gate_weight,
    up_weight,
    down_weight,
    norm1_gain,
    norm1_bias,
    norm2_gain,
    norm2_bias,
):
    seq_here, length, width = tokens.shape
    data_ways = lax.axis_size("dp")
    objective_ways = lax.axis_size("obj")
    me = lax.axis_index("tensor").astype(jnp.int32)
    core = lax.axis_index("dp").astype(jnp.int32)
    at_obj = lax.axis_index("obj")
    edge = ((at_obj == 0) | (at_obj == objective_ways - 1)).astype(jnp.int32).reshape(1)
    block = length // 4
    units = gate_weight.shape[1]
    rows_all = mlm_mask.shape[0]
    masked_limit = seq_here * data_ways * (objective_ways // 2)
    row_ids = jnp.arange(rows_all, dtype=jnp.int32)
    counts = jnp.where(row_ids < masked_limit, jnp.sum(mlm_mask, axis=1), glm_span).astype(F32)
    weight_all = counts * rows_all / jnp.sum(counts)
    first_row = (at_obj * data_ways + core) * seq_here
    share_here = lax.dynamic_slice_in_dim(weight_all, first_row, seq_here)
    prefix_here = lax.dynamic_slice_in_dim(glm_prefix, first_row, seq_here)
    span_here = lax.dynamic_slice_in_dim(glm_span, first_row, seq_here)
    open_here = jnp.where(first_row < masked_limit, length, prefix_here)
    info = [jnp.stack([me, open_here[r], prefix_here[r] + span_here[r], core]) for r in range(2)]
    order = jnp.stack([2 * (me ^ r) + h for r, h in ORDER])
    share = [share_here[r : r + 1] for r in range(2)]
    cosine, sine = constant_tables(length)
    segc = [segment_ids[r].reshape(length, 1) for r in range(2)]
    segr = [segment_ids[r].reshape(1, length) for r in range(2)]
    gain1, bias1 = norm1_gain.reshape(1, width), norm1_bias.reshape(1, width)
    gain2, bias2 = norm2_gain.reshape(1, width), norm2_bias.reshape(1, width)
    weights = (gate_weight, up_weight, down_weight)
    chain = Chain()
    A, B = 0, 1

    ow_half = out_weight.shape[0] // 2
    ow_own = lax.dynamic_slice_in_dim(out_weight, core * ow_half, ow_half)
    owx, owy = pair_swap(ow_own, ow_own)

    def attention(r, after=()):
        return plane_attn_fwd(chain, info[r], r, tokens, qkv_weight, cosine, sine, segc[r], segr[r], after)

    def out_and_norm(r, ol_pieces, after=()):
        return plane_out_norm(
            chain, info[r], order, r, ol_pieces, out_weight, ow_mine, ow_other, tokens, gain1, bias1, after
        )

    qkv, ol, lse, hl, n1, rstd = {}, {}, {}, {}, {}, {}
    qkv[A], ol[A], lse[A] = attention(A)
    owra, owrb = forward(chain, owx, owy)
    olx, oly, olr = {}, {}, {}
    olx[A], oly[A] = pair_swap(ol[A], ol[A])
    qkv[B], ol[B], lse[B] = attention(B)
    ow_mine = ow_join(chain, (owx, owy, owra, owrb), after=(olx[A], oly[A]))
    ow_other = lax.ppermute(ow_mine, "dp", CORES)
    halves, ol[B] = forward(chain, olx[A], oly[A], (ol[B],))
    olr[A], ol[B] = join_halves(chain, halves, ol[B])
    olx[B], oly[B] = pair_swap(ol[B], ol[B])
    hl[A], n1[A], rstd[A] = out_and_norm(A, (ol[A], olx[A], oly[A], olr[A]))
    vec = const_spec((1, width))
    tile = block // OWN_STEPS
    full = rows_spec((block, width), tile)
    ff, fb, ib, rs1, rs2 = {}, {}, {}, {}, {}
    resid, rx, ry, rr = {}, {}, {}, {}

    def sums_of(own, first, second):
        return (own, first[0], first[1], second[0], second[1])

    def second_resid(r, after=()):
        return own_step(
            chain, resid_two_kernel, "resid_two", sums_of(ff[r][2], rs1[r], rs2[r]), (n1[r], gain1, bias1),
            [full, vec, vec], [((block, width), BF)], after,
        )[0]

    def second_norm(r, before, after=()):
        pieces = (resid[r], rx[r], ry[r], *rr[r])
        return plane_norm_two(
            chain, info[r], order, share[r], r, pieces, cotangent, gain2, bias2, before, after
        )

    def first_norm_back(r, after=()):
        return own_step(
            chain, norm_one_back_kernel, "norm_one_back", sums_of(fb[r][2], rs1[r], rs2[r]),
            (dffn[r], n1[r], rstd[r], gain1),
            [rows_spec((block, width), tile, 3 * OWN_STEPS), full, rows_spec((block, HEAD_DIM), tile), vec],
            [((block, width), BF), ((block, width), F32), ((2, width), F32)], after,
        )

    olrb = forward(chain, olx[B], oly[B])
    sent, kept = plane_ffn_fwd(chain, True, hl[A], weights, ())
    rs1[A] = pair_swap(*sent)
    ff[A], kept_a = plane_ffn_fwd(chain, False, hl[A], weights, kept)
    olr[B], rstd[A] = join_halves(chain, olrb, rstd[A])
    hl[B], n1[B], rstd[B] = out_and_norm(B, (ol[B], olx[B], oly[B], olr[B]))
    rs2[A] = pair_swap(*middle(chain, rs1[A], ff[A][0], ff[A][1]))
    sent, kept = plane_ffn_fwd(chain, True, hl[B], weights, (), after=(*rs1[A],))
    resid[A] = second_resid(A)
    rx[A], ry[A] = pair_swap(resid[A], resid[A])
    ff[B], kept_b = plane_ffn_fwd(chain, False, hl[B], weights, (*kept, *sent))
    al, slopes = {A: kept_a[0], B: kept_b[0]}, {A: kept_a[1:], B: kept_b[1:]}
    rr[A], *sent = forward(chain, rx[A], ry[A], ff[B][3:])
    rs1[B] = pair_swap(*sent)

    sums2, dffn, dgu, sums1, dr1, dattn, dax, day, dar = {}, {}, {}, {}, {}, {}, {}, {}, {}
    activations, sums2[A], dffn[A] = second_norm(A, None)
    rs2[B] = pair_swap(*middle(chain, rs1[B], ff[B][0], ff[B][1]))
    sent, kept = plane_ffn_bwd(chain, True, dffn[A], slopes[A], weights, ())
    resid[B] = second_resid(B)
    rx[B], ry[B] = pair_swap(resid[B], resid[B])
    fb[A], dgu[A] = plane_ffn_bwd(chain, False, dffn[A], slopes[A], weights, (*kept, *sent))
    rr[B], *sent = forward(chain, rx[B], ry[B], fb[A][3:])
    rs1[A] = pair_swap(*sent)
    activations, sums2[B], dffn[B] = second_norm(B, activations)
    down_update = grad_plain_columns(chain, (al[A], al[B]), (dffn[A], dffn[B]))
    down_sum = lax.psum(down_update, ("obj", "dp"))
    rs2[A] = pair_swap(*middle(chain, rs1[A], fb[A][0], fb[A][1]))
    sent, dgu[B] = plane_ffn_bwd(chain, None, dffn[B], slopes[B], weights, ())
    fb[B] = sent[2:]
    dattn[A], dr1[A], sums1[A] = first_norm_back(A)
    dax[A], day[A] = pair_swap(dattn[A], dattn[A])
    rs1[B] = pair_swap(*sent[:2])
    gate_send, gate_keep = grad_rows(chain, info[B], (hl[A], hl[B]), (dgu[A][0], dgu[B][0]))
    line = Line(chain, edge)
    line.add("gate", gate_keep, lax.ppermute(gate_send, "dp", CORES), 2)
    rs2[B] = pair_swap(*middle(chain, rs1[B], fb[B][0], fb[B][1], after=(dax[A], day[A])))
    dar[A] = forward(chain, dax[A], day[A])
    up_send, up_keep = grad_rows(chain, info[B], (hl[A], hl[B]), (dgu[A][1], dgu[B][1]))
    line.add("up", up_keep, lax.ppermute(up_send, "dp", CORES), 2)
    line.advance()
    dattn[B], dr1[B], sums1[B] = first_norm_back(B)
    dax[B], day[B] = pair_swap(dattn[B], dattn[B])

    pieces, dqkv, dx, dxx, dxy, dxr = {}, {}, {}, {}, {}, {}

    def attention_back(r, after=()):
        pieces[r] = (dattn[r], dax[r], day[r], *dar[r])
        return plane_attn_bwd(
            chain, info[r], qkv[r], pieces[r], out_weight, lse[r], cosine, sine, segc[r], segr[r], after
        )

    def input_back_sums(r, after=()):
        x1, y1, r1b, r2a, own = plane_input_back(chain, order, dqkv[r], qkv_weight, after)
        ib[r] = (r1b, r2a, own)
        rs1[r] = pair_swap(x1, y1)

    def input_grad_own(r, after=()):
        return own_step(
            chain, input_grad_kernel, "input_grad", sums_of(ib[r][2], rs1[r], rs2[r]), (dr1[r],), [full],
            [((block, width), BF)], after,
        )[0]

    outs = {}

    def finish_matrix(name, rows, columns, after=()):
        mine = line.done[name]
        theirs = lax.ppermute(mine, "dp", CORES)
        outs[name] = widen(chain, info[B], mine, theirs, rows, columns, after)

    mine = (me == 0).astype(F32)
    sums = jnp.concatenate([sums1[A] + sums1[B], (sums2[A] + sums2[B]) * mine])
    exchanges = [("dp", 1), ("tensor", 1), ("tensor", 2), ("obj", 1), ("obj", 2)]

    def exchange(array):
        axis, bit = exchanges.pop(0)
        other = lax.ppermute(array, axis, [(i, i ^ bit) for i in range(lax.axis_size(axis))])
        return array, other

    dqkv[A] = attention_back(A)
    pair = exchange(sums)
    line.advance()
    dar[B] = forward(chain, dax[B], day[B])
    input_back_sums(A)
    line.advance()
    pair = exchange(add_small(chain, *pair))
    dqkv[B] = attention_back(B)
    rs2[A] = pair_swap(*middle(chain, rs1[A], ib[A][0], ib[A][1]))
    line.advance()
    pair = exchange(add_small(chain, *pair))
    qkv_send, qkv_keep = grad_rows(chain, info[B], (tokens, tokens), (dqkv[A], dqkv[B]), after=(down_sum,))
    line.add("qkv", qkv_keep, lax.ppermute(qkv_send, "dp", CORES), 3)
    dx[A] = input_grad_own(A)
    dxx[A], dxy[A] = pair_swap(dx[A], dx[A])
    input_back_sums(B)
    line.advance()
    pair = exchange(add_small(chain, *pair))
    out_send, out_keep = plane_grad_out(chain, info[B], (ol[A], ol[B]), (pieces[A], pieces[B]))
    line.add("out", out_keep, lax.ppermute(out_send, "dp", CORES), 1)
    dxr[A] = forward(chain, dxx[A], dxy[A])
    rs2[B] = pair_swap(*middle(chain, rs1[B], ib[B][0], ib[B][1]))
    line.advance()
    pair = exchange(add_small(chain, *pair))
    input_grad = plane_place(chain, info[A], A, (dx[A], dxx[A], dxy[A], *dxr[A]), tokens.shape, None)
    dx[B] = input_grad_own(B)
    dxx[B], dxy[B] = pair_swap(dx[B], dx[B])
    finish_matrix("gate", width, units)
    line.advance()
    sums = add_small(chain, *pair)
    dxr[B] = forward(chain, dxx[B], dxy[B])
    finish_matrix("up", width, units)
    line.advance()
    input_grad = plane_place(chain, info[B], B, (dx[B], dxx[B], dxy[B], *dxr[B]), tokens.shape, input_grad)
    while line.busy():
        line.advance()
        if "qkv" not in outs and line.complete("qkv"):
            finish_matrix("qkv", width, qkv_weight.shape[1])
    finish_matrix("out", out_weight.shape[0], width)
    outs["down"] = down_sum.astype(F32)

    return (
        activations,
        input_grad,
        outs["qkv"],
        outs["out"],
        outs["gate"],
        outs["up"],
        outs["down"],
        sums[0],
        sums[1],
        sums[2],
        sums[3],
    )


def body(*args):
    if plane_case(args[0].shape, args[10].shape):
        return plane_body(*args)
    return general_body(*args)


def solution(mesh):
    rows3 = P(("obj", "dp"), None, None)
    in_specs = (
        rows3,
        rows3,
        P(("obj", "dp"), None),
        P(),
        P(),
        P(),
        P(None, "tensor"),
        P("tensor", None),
        P(None, "tensor"),
        P(None, "tensor"),
        P("tensor", None),
        P(),
        P(),
        P(),
        P(),
    )
    out_specs = (
        rows3,
        rows3,
        P(None, "tensor"),
        P("tensor", None),
        P(None, "tensor"),
        P(None, "tensor"),
        P("tensor", None),
        P(),
        P(),
        P(),
        P(),
    )
    return jax.shard_map(body, mesh=mesh, in_specs=in_specs, out_specs=out_specs, check_vma=False)
```

```python
import functools
import math

import jax
import jax.numpy as jnp
import numpy as np
from jax import lax
from jax.experimental import pallas as pl
from jax.experimental.pallas import tpu as pltpu
from jax.sharding import PartitionSpec as P

HEAD_DIM = 128
deep_alpha = math.sqrt(48.0)
norm_eps = 1e-05
mask_fill = -1e30
score_scale = 1.0 / math.sqrt(HEAD_DIM)
MIB = 1024 * 1024
BF = jnp.bfloat16
F32 = jnp.float32
ANY = pl.ANY


def mm(a, b):
    return lax.dot_general(a, b, (((1,), (0,)), ((), ())), preferred_element_type=F32)


def mm_nt(a, b):
    return lax.dot_general(a, b, (((1,), (1,)), ((), ())), preferred_element_type=F32)


def mm_tn(a, b):
    return lax.dot_general(a, b, (((0,), (0,)), ((), ())), preferred_element_type=F32)


def params(mib, grid_rank=1):
    return pltpu.CompilerParams(
        vmem_limit_bytes=mib * MIB, dimension_semantics=("arbitrary",) * grid_rank
    )


def cost(flops, nbytes, trans=0):
    return pl.CostEstimate(flops=int(flops), bytes_accessed=int(nbytes), transcendentals=int(trans))


def const_spec(shape):
    zeros = (0,) * len(shape)
    return pl.BlockSpec(shape, lambda *_: zeros, pipeline_mode=pl.Buffered(1))


def rotary_tables(seq_length):
    half_width = HEAD_DIM // 2
    frequency = jnp.exp(
        jnp.arange(half_width, dtype=F32) * (-2.0 * math.log(10000.0) / HEAD_DIM)
    )
    angles = jnp.arange(seq_length, dtype=F32)[:, None] * frequency[None, :]
    sine = jnp.sin(angles)
    cosine = jnp.cos(angles)
    return jnp.concatenate([cosine, cosine], axis=1), jnp.concatenate([-sine, sine], axis=1)


def fill_bias(info_ref, segc_ref, segr_ref, bias_ref, tile):
    length = bias_ref.shape[0]
    prefix, limit = info_ref[1], info_ref[2]

    def one(step, carry):
        rows = pl.ds(pl.multiple_of(step * tile, tile), tile)
        key_pos = lax.broadcasted_iota(jnp.int32, (tile, length), 0) + step * tile
        query_pos = lax.broadcasted_iota(jnp.int32, (tile, length), 1)
        same = segc_ref[rows, :] == segr_ref[...]
        open_keys = (
            (key_pos < prefix)
            | ((key_pos <= query_pos) & (key_pos < limit))
            | (key_pos == query_pos)
        )
        bias_ref[rows, :] = jnp.where(same & open_keys, 0.0, mask_fill)
        return carry

    lax.fori_loop(0, length // tile, one, 0)


def attn_fwd_kernel(
    info_ref, x_ref, w_ref, cos_ref, sin_ref, segc_ref, segr_ref, qkv_ref, ol_ref, lse_ref, bias_ref, tile
):
    length = x_ref.shape[0]

    @pl.when(pl.program_id(0) == 0)
    def _():
        fill_bias(info_ref, segc_ref, segr_ref, bias_ref, tile)

    for step in range(length // tile):
        rows = pl.ds(step * tile, tile)
        proj = mm(x_ref[rows, :], w_ref[...])
        cosine, sine = cos_ref[rows, :], sin_ref[rows, :]
        for part in range(2):
            piece = proj[:, part * HEAD_DIM : (part + 1) * HEAD_DIM]
            turned = piece * cosine + pltpu.roll(piece, HEAD_DIM // 2, 1) * sine
            qkv_ref[rows, part * HEAD_DIM : (part + 1) * HEAD_DIM] = turned.astype(BF)
        qkv_ref[rows, 2 * HEAD_DIM :] = proj[:, 2 * HEAD_DIM :].astype(BF)
    keys = qkv_ref[:, HEAD_DIM : 2 * HEAD_DIM]
    values_t = qkv_ref[:, 2 * HEAD_DIM :].astype(F32).T.astype(BF)
    for step in range(length // tile):
        rows = pl.ds(step * tile, tile)
        queries = qkv_ref[rows, :HEAD_DIM]
        scores = mm_nt(keys, queries) * score_scale + bias_ref[:, rows]
        top = jnp.max(scores, axis=0, keepdims=True)
        exponent = jnp.exp(scores - top)
        total = jnp.sum(exponent, axis=0, keepdims=True)
        attended = mm(values_t, exponent.astype(BF)) * (1.0 / total)
        ol_ref[rows, :] = attended.T.astype(BF)
        lse_ref[:, rows] = top + jnp.log(total)


def attn_fwd(info, row, tokens, qkv_weight, cosine, sine, segc, segr):
    _, length, width = tokens.shape
    heads = qkv_weight.shape[1] // (3 * HEAD_DIM)
    tile = min(256, length)
    grid_spec = pltpu.PrefetchScalarGridSpec(
        num_scalar_prefetch=1,
        grid=(heads,),
        in_specs=[
            pl.BlockSpec((None, length, width), lambda h, *_: (row, 0, 0), pipeline_mode=pl.Buffered(1)),
            pl.BlockSpec((width, 3 * HEAD_DIM), lambda h, *_: (0, h)),
            const_spec((length, HEAD_DIM)),
            const_spec((length, HEAD_DIM)),
            const_spec((length, 1)),
            const_spec((1, length)),
        ],
        out_specs=[
            pl.BlockSpec((length, 3 * HEAD_DIM), lambda h, *_: (0, h)),
            pl.BlockSpec((length, HEAD_DIM), lambda h, *_: (0, h)),
            pl.BlockSpec((None, 1, length), lambda h, *_: (h, 0, 0)),
        ],
        scratch_shapes=[pltpu.VMEM((length, length), F32)],
    )
    return pl.pallas_call(
        functools.partial(attn_fwd_kernel, tile=tile),
        grid_spec=grid_spec,
        out_shape=[
            jax.ShapeDtypeStruct((length, heads * 3 * HEAD_DIM), BF),
            jax.ShapeDtypeStruct((length, heads * HEAD_DIM), BF),
            jax.ShapeDtypeStruct((heads, 1, length), F32),
        ],
        compiler_params=params(48),
        cost_estimate=cost(
            heads * (2 * length * width * 384 + 8 * length * length * HEAD_DIM),
            2 * length * width + 2 * width * heads * 384 + 8 * length * heads * 128,
        ),
        name="attn_fwd",
    )(info, tokens, qkv_weight, cosine, sine, segc, segr)


def attn_bwd_kernel(
    info_ref, qkv_ref, dol_ref, lse_ref, cos_ref, sin_ref, segc_ref, segr_ref, dqkv_ref,
    bias_ref, dol_nat, dk_ref, dv_ref, tile
):
    length = qkv_ref.shape[0]
    ways, block, _ = dol_ref.shape
    me = info_ref[0]

    @pl.when(pl.program_id(0) == 0)
    def _():
        fill_bias(info_ref, segc_ref, segr_ref, bias_ref, tile)

    for at in range(ways):
        dol_nat[pl.ds(at * block, block), :] = dol_ref[me ^ at]
    keys = qkv_ref[:, HEAD_DIM : 2 * HEAD_DIM]
    values = qkv_ref[:, 2 * HEAD_DIM :]
    keys_t = keys.astype(F32).T.astype(BF)
    for step in range(length // tile):
        rows = pl.ds(step * tile, tile)
        queries = qkv_ref[rows, :HEAD_DIM]
        dol = dol_nat[rows, :]
        scores = mm_nt(keys, queries) * score_scale + bias_ref[:, rows]
        probs = jnp.exp(scores - lse_ref[:, rows])
        dp = mm_nt(values, dol)
        inner = jnp.sum(probs * dp, axis=0, keepdims=True)
        draw = (probs * (dp - inner) * score_scale).astype(BF)
        dv = mm(probs.astype(BF), dol)
        dk = mm(draw, queries)
        if step == 0:
            dv_ref[...] = dv
            dk_ref[...] = dk
        else:
            dv_ref[...] += dv
            dk_ref[...] += dk
        dq = mm(keys_t, draw).T
        turned = dq * cos_ref[rows, :] - pltpu.roll(dq, HEAD_DIM // 2, 1) * sin_ref[rows, :]
        dqkv_ref[rows, :HEAD_DIM] = turned.astype(BF)
    dk = dk_ref[...]
    turned = dk * cos_ref[...] - pltpu.roll(dk, HEAD_DIM // 2, 1) * sin_ref[...]
    dqkv_ref[:, HEAD_DIM : 2 * HEAD_DIM] = turned.astype(BF)
    dqkv_ref[:, 2 * HEAD_DIM :] = dv_ref[...].astype(BF)


def attn_bwd(info, qkv, dol, lse, cosine, sine, segc, segr):
    length = qkv.shape[0]
    heads = qkv.shape[1] // (3 * HEAD_DIM)
    ways, block, _ = dol.shape
    tile = min(256, length)
    grid_spec = pltpu.PrefetchScalarGridSpec(
        num_scalar_prefetch=1,
        grid=(heads,),
        in_specs=[
            pl.BlockSpec((length, 3 * HEAD_DIM), lambda h, *_: (0, h)),
            pl.BlockSpec((ways, block, HEAD_DIM), lambda h, *_: (0, 0, h)),
            pl.BlockSpec((None, 1, length), lambda h, *_: (h, 0, 0)),
            const_spec((length, HEAD_DIM)),
            const_spec((length, HEAD_DIM)),
            const_spec((length, 1)),
            const_spec((1, length)),
        ],
        out_specs=pl.BlockSpec((length, 3 * HEAD_DIM), lambda h, *_: (0, h)),
        scratch_shapes=[
            pltpu.VMEM((length, length), F32),
            pltpu.VMEM((length, HEAD_DIM), BF),
            pltpu.VMEM((length, HEAD_DIM), F32),
            pltpu.VMEM((length, HEAD_DIM), F32),
        ],
    )
    return pl.pallas_call(
        functools.partial(attn_bwd_kernel, tile=tile),
        grid_spec=grid_spec,
        out_shape=jax.ShapeDtypeStruct(qkv.shape, BF),
        compiler_params=params(48),
        cost_estimate=cost(heads * 20 * length * length * HEAD_DIM, 16 * length * heads * 128),
        name="attn_bwd",
    )(info, qkv, dol, lse, cosine, sine, segc, segr)


def out_norm_kernel(info_ref, *refs, ways):
    ol_refs, ow_refs = refs[:ways], refs[ways : 2 * ways]
    x_ref, gain_ref, bias_ref, hl_ref, n1_ref, rstd_ref = refs[2 * ways :]
    total = x_ref[...].astype(F32) * deep_alpha
    for ol_ref, ow_ref in zip(ol_refs, ow_refs):
        total += mm(ol_ref[...], ow_ref[...])
    centered = total - jnp.mean(total, axis=1, keepdims=True)
    variance = jnp.mean(centered * centered, axis=1, keepdims=True)
    inv = lax.rsqrt(variance + norm_eps)
    normed = centered * inv
    hl_ref[...] = (normed * gain_ref[...] + bias_ref[...]).astype(BF)

    @pl.when(pl.program_id(0) == info_ref[0])
    def _():
        n1_ref[...] = normed
        rstd_ref[...] = jnp.broadcast_to(inv, rstd_ref.shape)


def out_norm(info, row, ol_pieces, ow_pieces, tokens, gain, bias):
    _, length, width = tokens.shape
    ways = len(ol_pieces)
    block = length // ways
    head_width = ol_pieces[0].shape[1]
    grid_spec = pltpu.PrefetchScalarGridSpec(
        num_scalar_prefetch=1,
        grid=(ways,),
        in_specs=[pl.BlockSpec((block, head_width), lambda i, *_: (i, 0))] * ways
        + [const_spec((head_width, width))] * ways
        + [
            pl.BlockSpec((None, block, width), lambda i, *_: (row, i, 0)),
            const_spec((1, width)),
            const_spec((1, width)),
        ],
        out_specs=[
            pl.BlockSpec((block, width), lambda i, info: (i ^ info[0], 0)),
            pl.BlockSpec((block, width), lambda i, *_: (0, 0)),
            pl.BlockSpec((block, HEAD_DIM), lambda i, *_: (0, 0)),
        ],
    )
    return pl.pallas_call(
        functools.partial(out_norm_kernel, ways=ways),
        grid_spec=grid_spec,
        out_shape=[
            jax.ShapeDtypeStruct((length, width), BF),
            jax.ShapeDtypeStruct((block, width), F32),
            jax.ShapeDtypeStruct((block, HEAD_DIM), F32),
        ],
        compiler_params=params(48),
        cost_estimate=cost(2 * length * width * width, 2 * width * width + 6 * length * width),
        name="out_norm",
    )(info, *ol_pieces, *ow_pieces, tokens, gain, bias)


def piece_shapes(ways, block, width):
    if ways == 4:
        sizes = [block] + [block // 2] * 6
    else:
        sizes = [block] * ways
    return [jax.ShapeDtypeStruct((size, width), BF) for size in sizes]


def store_pieces(at, part, refs, ways):
    if ways == 4:
        half = part.shape[0] // 2

        @pl.when(at == 0)
        def _():
            refs[0][...] = part

        for r in range(1, 4):

            @pl.when(at == r)
            def _(r=r):
                refs[2 * r - 1][...] = part[:half]
                refs[2 * r][...] = part[half:]
    else:
        for r in range(ways):

            @pl.when(at == r)
            def _(r=r):
                refs[r][...] = part


def piece_specs(shapes):
    return [pl.BlockSpec(s.shape, lambda *_: (0, 0)) for s in shapes]


def ffn_fwd_kernel(hl_ref, wg_ref, wu_ref, wd_ref, al_ref, ga_ref, gb_ref, *refs, ways):
    hidden = hl_ref[...]
    gate = mm(hidden, wg_ref[...])
    up = mm(hidden, wu_ref[...])
    cdf = 0.5 + 0.5 * lax.erf(gate * (1.0 / math.sqrt(2.0)))
    pdf = jnp.exp(gate * gate * -0.5) * (1.0 / math.sqrt(2.0 * math.pi))
    act = gate * cdf
    ga_ref[...] = (up * (cdf + gate * pdf)).astype(BF)
    gb_ref[...] = act.astype(BF)
    low = (act * up).astype(BF)
    al_ref[...] = low
    store_pieces(pl.program_id(0), mm(low, wd_ref[...]).astype(BF), refs, ways)


def ffn_fwd(hidden, gate_weight, up_weight, down_weight, ways):
    length, width = hidden.shape
    units = gate_weight.shape[1]
    block = length // ways
    tiled = lambda w: pl.BlockSpec((block, w), lambda i: (i, 0))
    shapes = piece_shapes(ways, block, width)
    out = pl.pallas_call(
        functools.partial(ffn_fwd_kernel, ways=ways),
        grid=(ways,),
        in_specs=[
            tiled(width),
            const_spec((width, units)),
            const_spec((width, units)),
            const_spec((units, width)),
        ],
        out_specs=[tiled(units)] * 3 + piece_specs(shapes),
        out_shape=[jax.ShapeDtypeStruct((length, units), BF)] * 3 + shapes,
        compiler_params=params(60),
        cost_estimate=cost(6 * length * width * units, 6 * units * width + 6 * length * units),
        name="ffn_fwd",
    )(hidden, gate_weight, up_weight, down_weight)
    return out[:3], out[3:]


def norm_two_kernel(info_ref, share_ref, *refs, n_in, ways):
    in_refs = refs[:n_in]
    cot_ref, gain_ref, bias_ref = refs[n_in : n_in + 3]
    act_ref, dffn_ref, sums_ref, held = refs[-4:]
    at = pl.program_id(0)
    if n_in == 5:
        half = held.shape[0] // 2
        for r in range(3):

            @pl.when(at == r)
            def _(r=r):
                held[...] = in_refs[r][...]

        @pl.when(at == 3)
        def _():
            held[:half] = in_refs[3][...]
            held[half:] = in_refs[4][...]
    else:
        for r in range(ways):

            @pl.when(at == r)
            def _(r=r):
                held[...] = in_refs[r][...]

    resid = held[...].astype(F32)
    centered = resid - jnp.mean(resid, axis=1, keepdims=True)
    variance = jnp.mean(centered * centered, axis=1, keepdims=True)
    inv = lax.rsqrt(variance + norm_eps)
    normed = centered * inv
    gain = gain_ref[...]
    act_ref[...] = (normed * gain + bias_ref[...]).astype(BF)
    dout = cot_ref[...].astype(F32) * share_ref[0]
    scaled = dout * gain
    inner = jnp.mean(scaled, axis=1, keepdims=True) + normed * jnp.mean(
        scaled * normed, axis=1, keepdims=True
    )
    dffn_ref[...] = (inv * (scaled - inner)).astype(BF)
    gain_sum = jnp.sum(dout * normed, axis=0, keepdims=True)
    bias_sum = jnp.sum(dout, axis=0, keepdims=True)

    @pl.when(at == 0)
    def _():
        sums_ref[0:1, :] = gain_sum
        sums_ref[1:2, :] = bias_sum

    @pl.when(at > 0)
    def _():
        sums_ref[0:1, :] += gain_sum
        sums_ref[1:2, :] += bias_sum


def norm_two(info, share, row, pieces, cotangent, gain, bias, before):
    rows, length, width = cotangent.shape
    block = pieces[0].shape[0]
    ways = length // block
    natural = pl.BlockSpec((None, block, width), lambda i, info, share: (row, i ^ info[0], 0))
    grid_spec = pltpu.PrefetchScalarGridSpec(
        num_scalar_prefetch=2,
        grid=(ways,),
        in_specs=[const_spec(p.shape) for p in pieces]
        + [natural, const_spec((1, width)), const_spec((1, width))]
        + ([pl.BlockSpec(memory_space=ANY)] if before is not None else []),
        out_specs=[
            natural,
            pl.BlockSpec((block, width), lambda i, *_: (i, 0)),
            pl.BlockSpec((2, width), lambda i, *_: (0, 0)),
        ],
        scratch_shapes=[pltpu.VMEM((block, width), BF)],
    )
    return pl.pallas_call(
        functools.partial(norm_two_kernel, n_in=len(pieces), ways=ways),
        grid_spec=grid_spec,
        out_shape=[
            jax.ShapeDtypeStruct(cotangent.shape, BF),
            jax.ShapeDtypeStruct((length, width), BF),
            jax.ShapeDtypeStruct((2, width), F32),
        ],
        input_output_aliases={len(pieces) + 5: 0} if before is not None else {},
        compiler_params=params(48),
        cost_estimate=cost(20 * length * width, 8 * length * width),
        name="norm_two",
    )(info, share, *pieces, cotangent, gain, bias, *([before] if before is not None else []))


def ffn_bwd_kernel(dffn_ref, ga_ref, gb_ref, wg_ref, wu_ref, wd_ref, dg_ref, du_ref, *refs, ways):
    dact = mm_nt(dffn_ref[...], wd_ref[...])
    dgate = (dact * ga_ref[...].astype(F32)).astype(BF)
    dup = (dact * gb_ref[...].astype(F32)).astype(BF)
    dg_ref[...] = dgate
    du_ref[...] = dup
    part = mm_nt(dgate, wg_ref[...]) + mm_nt(dup, wu_ref[...])
    store_pieces(pl.program_id(0), part.astype(BF), refs, ways)


def ffn_bwd(dffn, gate_slope, up_slope, gate_weight, up_weight, down_weight, ways):
    length, width = dffn.shape
    units = gate_weight.shape[1]
    block = length // ways
    tiled = lambda w: pl.BlockSpec((block, w), lambda i: (i, 0))
    shapes = piece_shapes(ways, block, width)
    out = pl.pallas_call(
        functools.partial(ffn_bwd_kernel, ways=ways),
        grid=(ways,),
        in_specs=[
            tiled(width),
            tiled(units),
            tiled(units),
            const_spec((width, units)),
            const_spec((width, units)),
            const_spec((units, width)),
        ],
        out_specs=[tiled(units)] * 2 + piece_specs(shapes),
        out_shape=[jax.ShapeDtypeStruct((length, units), BF)] * 2 + shapes,
        compiler_params=params(60),
        cost_estimate=cost(6 * length * width * units, 6 * units * width + 8 * length * units),
        name="ffn_bwd",
    )(dffn, gate_slope, up_slope, gate_weight, up_weight, down_weight)
    return out[0], out[1], out[2:]


def input_back_kernel(info_ref, dqkv_ref, w_ref, *refs, ways):
    part = mm_nt(dqkv_ref[...], w_ref[...])
    store_pieces(pl.program_id(0), part.astype(BF), refs, ways)


def input_back(info, dqkv, qkv_weight, ways):
    length, columns = dqkv.shape
    width = qkv_weight.shape[0]
    block = length // ways
    shapes = piece_shapes(ways, block, width)
    grid_spec = pltpu.PrefetchScalarGridSpec(
        num_scalar_prefetch=1,
        grid=(ways,),
        in_specs=[
            pl.BlockSpec((block, columns), lambda i, info: (i ^ info[0], 0)),
            const_spec((width, columns)),
        ],
        out_specs=piece_specs(shapes),
    )
    return pl.pallas_call(
        functools.partial(input_back_kernel, ways=ways),
        grid_spec=grid_spec,
        out_shape=shapes,
        compiler_params=params(48),
        cost_estimate=cost(2 * length * width * columns, 2 * width * columns + 2 * length * width),
        name="input_back",
    )(info, dqkv, qkv_weight)


def place_kernel(info_ref, *refs, n_in, ways):
    in_refs = refs[:n_in]
    out_ref = refs[-1]
    at = pl.program_id(0)
    if n_in == 5:
        half = out_ref.shape[0] // 2
        for r in range(3):

            @pl.when(at == r)
            def _(r=r):
                out_ref[...] = in_refs[r][...]

        @pl.when(at == 3)
        def _():
            out_ref[:half] = in_refs[3][...]
            out_ref[half:] = in_refs[4][...]
    else:
        for r in range(ways):

            @pl.when(at == r)
            def _(r=r):
                out_ref[...] = in_refs[r][...]


def place(info, row, pieces, shape, before):
    rows, length, width = shape
    block = pieces[0].shape[0]
    ways = length // block
    grid_spec = pltpu.PrefetchScalarGridSpec(
        num_scalar_prefetch=1,
        grid=(ways,),
        in_specs=[const_spec(p.shape) for p in pieces]
        + ([pl.BlockSpec(memory_space=ANY)] if before is not None else []),
        out_specs=pl.BlockSpec((None, block, width), lambda i, info: (row, i ^ info[0], 0)),
    )
    return pl.pallas_call(
        functools.partial(place_kernel, n_in=len(pieces), ways=ways),
        grid_spec=grid_spec,
        out_shape=jax.ShapeDtypeStruct(shape, BF),
        input_output_aliases={len(pieces) + 1: 0} if before is not None else {},
        compiler_params=params(32),
        cost_estimate=cost(0, 4 * length * width),
        name="place",
    )(info, *pieces, *([before] if before is not None else []))


def swap(array, bit, ways):
    return lax.ppermute(array, "tensor", [(i, i ^ bit) for i in range(ways)])


def gather_halves(own_a, own_b):
    xa = swap(own_a, 1, 4)
    yb = swap(own_b, 2, 4)
    xb = swap(own_b, 1, 4)
    ya = swap(own_a, 2, 4)
    ra = swap(xa, 2, 4)
    rb = swap(yb, 1, 4)
    return [(xa, xb), (ya, yb), (ra, rb)]


def gather_rel(own, ways):
    blocks = [own]
    bit = 1
    while bit < ways:
        blocks = blocks + [swap(b, bit, ways) for b in blocks]
        bit *= 2
    return blocks


def gather_tokens(own, ways):
    if ways == 4:
        half = own.shape[0] // 2
        (xa, xb), (ya, yb), (ra, rb) = gather_halves(own[:half], own[half:])
        return [own, jnp.concatenate([xa, xb]), jnp.concatenate([ya, yb]), ra, rb]
    return gather_rel(own, ways)


def join(pieces):
    return jnp.concatenate(pieces, axis=0)


def add_low(a, b):
    return (a.astype(F32) + b.astype(F32)).astype(BF)


def scatter_sum(pieces, ways):
    if ways == 4:
        own, r1a, r1b, r2a, r2b, r3a, r3b = pieces
        in3a = swap(r3a, 1, 4)
        in3b = swap(r3b, 2, 4)
        in1a = swap(r1a, 1, 4)
        in2b = swap(r2b, 2, 4)
        in2a = swap(add_low(r2a, in3a), 2, 4)
        in1b = swap(add_low(r1b, in3b), 1, 4)
        half = r1a.shape[0]
        top = own[:half].astype(F32) + in1a.astype(F32) + in2a.astype(F32)
        low = own[half:].astype(F32) + in1b.astype(F32) + in2b.astype(F32)
        return jnp.concatenate([top, low], axis=0)
    blocks = list(pieces)
    bit = ways // 2
    while bit >= 1:
        keep, send = blocks[:bit], blocks[bit:]
        blocks = [add_low(k, swap(s, bit, ways)) for k, s in zip(keep, send)]
        bit //= 2
    return blocks[0].astype(F32)


def sum_over_obj(array, ways):
    if ways != 4:
        return lax.psum(array, "obj")
    at = lax.axis_index("obj")
    one = add_low(array, lax.ppermute(array, "obj", [(0, 1), (3, 2)]))
    two = add_low(one, lax.ppermute(one, "obj", [(1, 2), (2, 1)]))
    back = lax.ppermute(two, "obj", [(1, 0), (2, 3)])
    return jnp.where((at == 0) | (at == 3), back, two)


def sum_gradient(update, data_ways, objective_ways):
    if data_ways != 2:
        return lax.psum(update, ("obj", "dp")).astype(F32)
    core = lax.axis_index("dp")
    half = update.shape[0] // 2
    other = [(0, 1), (1, 0)]
    mine = lax.dynamic_slice_in_dim(update, core * half, half)
    send = lax.dynamic_slice_in_dim(update, (1 - core) * half, half)
    mine = add_low(mine, lax.ppermute(send, "dp", other))
    mine = sum_over_obj(mine, objective_ways)
    theirs = lax.ppermute(mine, "dp", other)
    first = jnp.where(core == 0, mine, theirs)
    second = jnp.where(core == 0, theirs, mine)
    return jnp.concatenate([first, second], axis=0).astype(F32)


def general_body(
    tokens,
    cotangent,
    segment_ids,
    mlm_mask,
    glm_prefix,
    glm_span,
    qkv_weight,
    out_weight,
    gate_weight,
    up_weight,
    down_weight,
    norm1_gain,
    norm1_bias,
    norm2_gain,
    norm2_bias,
):
    seq_here, length, width = tokens.shape
    ways = lax.axis_size("tensor")
    data_ways = lax.axis_size("dp")
    objective_ways = lax.axis_size("obj")
    me = lax.axis_index("tensor").astype(jnp.int32)
    block = length // ways
    rows_all = mlm_mask.shape[0]
    masked_limit = seq_here * data_ways * (objective_ways // 2)
    row_ids = jnp.arange(rows_all, dtype=jnp.int32)
    counts = jnp.where(row_ids < masked_limit, jnp.sum(mlm_mask, axis=1), glm_span).astype(F32)
    weight_all = counts * rows_all / jnp.sum(counts)
    first_row = (lax.axis_index("obj") * data_ways + lax.axis_index("dp")) * seq_here
    share_here = lax.dynamic_slice_in_dim(weight_all, first_row, seq_here)
    prefix_here = lax.dynamic_slice_in_dim(glm_prefix, first_row, seq_here)
    span_here = lax.dynamic_slice_in_dim(glm_span, first_row, seq_here)
    masked_lm = first_row < masked_limit
    open_here = jnp.where(masked_lm, length, prefix_here)
    info = [jnp.stack([me, open_here[r], prefix_here[r] + span_here[r]]) for r in range(seq_here)]
    share = [share_here[r : r + 1] for r in range(seq_here)]
    cosine, sine = rotary_tables(length)
    segc = [segment_ids[r].reshape(length, 1) for r in range(seq_here)]
    segr = [segment_ids[r].reshape(1, length) for r in range(seq_here)]
    gain1, bias1 = norm1_gain.reshape(1, width), norm1_bias.reshape(1, width)
    gain2, bias2 = norm2_gain.reshape(1, width), norm2_bias.reshape(1, width)
    rows = range(seq_here)

    if ways == 4 and data_ways == 2:
        core = lax.axis_index("dp")
        half = out_weight.shape[0] // 2
        mine = lax.dynamic_slice_in_dim(out_weight, core * half, half)
        pairs = gather_halves(mine[: half // 2], mine[half // 2 :])
        ow_pieces = [out_weight]
        for a, b in pairs:
            got = jnp.concatenate([a, b])
            other = lax.ppermute(got, "dp", [(0, 1), (1, 0)])
            ow_pieces.append(
                jnp.concatenate(
                    [jnp.where(core == 0, got, other), jnp.where(core == 0, other, got)]
                )
            )
    else:
        ow_pieces = gather_rel(out_weight, ways)

    qkv, ol, lse, hl, n1, rstd1 = {}, {}, {}, {}, {}, {}
    al, slope_g, slope_u, dffn, dgate, dup = {}, {}, {}, {}, {}, {}
    r2_pieces, norm2_sums, norm1_sums, dr1, dqkv, dattn = {}, {}, {}, {}, {}, {}

    for r in rows:
        qkv[r], ol[r], lse[r] = attn_fwd(info[r], r, tokens, qkv_weight, cosine, sine, segc[r], segr[r])
    ffn_parts = {}
    for r in rows:
        if ways == 4:
            pairs = gather_halves(ol[r][: length // 2], ol[r][length // 2 :])
            ol_pieces = [ol[r]] + [jnp.concatenate(p) for p in pairs]
        else:
            ol_pieces = gather_rel(ol[r], ways)
        hl[r], n1[r], rstd1[r] = out_norm(info[r], r, ol_pieces, ow_pieces, tokens, gain1, bias1)
        (al[r], slope_g[r], slope_u[r]), ffn_parts[r] = ffn_fwd(
            hl[r], gate_weight, up_weight, down_weight, ways
        )
    for r in rows:
        total = scatter_sum(ffn_parts[r], ways)
        resid = deep_alpha * (n1[r] * gain1 + bias1) + total
        r2_pieces[r] = gather_tokens(resid.astype(BF), ways)

    activations = None
    dh_parts = {}
    for r in rows:
        activations, dffn[r], norm2_sums[r] = norm_two(
            info[r], share[r], r, r2_pieces[r], cotangent, gain2, bias2, activations
        )
        dgate[r], dup[r], dh_parts[r] = ffn_bwd(
            dffn[r], slope_g[r], slope_u[r], gate_weight, up_weight, down_weight, ways
        )

    def update(lefts, rights):
        total = None
        for r in rows:
            one = mm_tn(lefts[r], rights[r])
            total = one if total is None else total + one
        return total.astype(BF)

    def reduced(lefts, rights):
        return sum_gradient(update(lefts, rights), data_ways, objective_ways)

    down_grad = reduced(al, dffn)
    gate_grad = reduced(hl, dgate)
    up_grad = reduced(hl, dup)

    dx_parts = {}
    for r in rows:
        total = scatter_sum(dh_parts[r], ways)
        dh = deep_alpha * dffn[r][:block].astype(F32) + total
        scaled = dh * gain1
        inner = jnp.mean(scaled, axis=1, keepdims=True) + n1[r] * jnp.mean(
            scaled * n1[r], axis=1, keepdims=True
        )
        dr1[r] = rstd1[r][:, :1] * (scaled - inner)
        norm1_sums[r] = jnp.stack([jnp.sum(dh * n1[r], axis=0), jnp.sum(dh, axis=0)])
        dattn[r] = join(gather_tokens(dr1[r].astype(BF), ways))
    for r in rows:
        dol = mm_nt(dattn[r], out_weight).astype(BF).reshape(ways, block, -1)
        dqkv[r] = attn_bwd(info[r], qkv[r], dol, lse[r], cosine, sine, segc[r], segr[r])
        dx_parts[r] = input_back(info[r], dqkv[r], qkv_weight, ways)

    qkv_grad = reduced([tokens[r] for r in rows], dqkv)
    ol_rel = {}
    for r in rows:
        parts = ol[r].reshape(ways, block, -1)
        ol_rel[r] = jnp.stack(
            [lax.dynamic_index_in_dim(parts, me ^ i, 0, keepdims=False) for i in range(ways)]
        ).reshape(length, -1)
    out_grad = reduced(ol_rel, dattn)

    input_grad = None
    for r in rows:
        total = scatter_sum(dx_parts[r], ways)
        dx = (deep_alpha * dr1[r] + total).astype(BF)
        input_grad = place(info[r], r, gather_tokens(dx, ways), tokens.shape, input_grad)

    first = (me == 0).astype(F32)
    sums = jnp.concatenate(
        [sum(norm1_sums[r] for r in rows), sum(norm2_sums[r] for r in rows) * first]
    )
    sums = lax.psum(sums, ("obj", "dp", "tensor"))
    return (
        activations,
        input_grad,
        qkv_grad,
        out_grad,
        gate_grad,
        up_grad,
        down_grad,
        sums[0],
        sums[1],
        sums[2],
        sums[3],
    )


ORDER = ((1, 0), (3, 0), (2, 1), (3, 1), (1, 1), (2, 0), (0, 0), (0, 1))
CORES = ((0, 1), (1, 0))
DECLARED_FLOPS = 1e10
MICROS = {
    "attn_fwd": 21, "split": 2, "ow_join": 4, "relay": 1, "out_norm": 21, "middle_sum": 3, "resid_two": 5,
    "norm_two": 15, "grad_columns": 20, "grad_plain_columns": 19, "grad_plain": 19, "line_step": 5, "grad_rows": 21,
    "attn_bwd": 24, "norm_one_back": 6, "input_back": 14, "input_grad": 5, "grad_out": 11, "place": 5, "widen": 10,
    "cast": 9, "total_sum": 2,
}


def plane_case(token_shape, out_shape, down_shape):
    return (
        lax.axis_size("tensor") == 4
        and lax.axis_size("dp") == 2
        and lax.axis_size("obj") == 4
        and token_shape[0] == 2
        and token_shape[1] % 1024 == 0
        and token_shape[2] % 1024 == 0
        and down_shape[0] % 128 == 0
        and out_shape[0] % 256 == 0
    )


def spec(shape, index):
    return pl.BlockSpec(shape, index)


def call(
    kernel, name, grid, ins, in_specs, outs, out_specs, scalars=(), after=(), scratch=(), aliases=None,
    mib=48, flops=0, nbytes=0,
):
    ns, ni, na = len(scalars), len(ins), len(after)

    def wrapped(*refs):
        kernel(*refs[: ns + ni], *refs[ns + ni + na :])

    grid_spec = pltpu.PrefetchScalarGridSpec(
        num_scalar_prefetch=ns,
        grid=grid,
        in_specs=list(in_specs) + [pl.BlockSpec(memory_space=ANY)] * na,
        out_specs=list(out_specs),
        scratch_shapes=list(scratch),
    )
    return pl.pallas_call(
        wrapped,
        grid_spec=grid_spec,
        out_shape=[jax.ShapeDtypeStruct(s, d) for s, d in outs],
        input_output_aliases={ns + k: v for k, v in (aliases or {}).items()},
        compiler_params=params(62, len(grid)),
        cost_estimate=cost(DECLARED_FLOPS * MICROS.get(name, 9 * grid[0]), 1e6),
        name=name,
    )(*scalars, *ins, *after)


def constant_tables(length):
    half = HEAD_DIM // 2
    frequency = np.exp(np.arange(half, dtype=np.float32) * np.float32(-2.0 * math.log(10000.0) / HEAD_DIM))
    angles = np.arange(length, dtype=np.float32)[:, None] * frequency[None, :]
    cosine, sine = np.cos(angles), np.sin(angles)
    both = lambda a, b: jnp.asarray(np.concatenate([a, b], axis=1).astype(np.float32))
    return both(cosine, cosine), both(-sine, sine)


class Chain:
    def __init__(self):
        self.last = ()
        self.ended = ()

    def close(self, *arrays):
        self.ended += arrays

    def __call__(self, *args, after=(), **kwargs):
        out = call(*args, after=(*self.last, *self.ended, *after), **kwargs)
        self.last, self.ended = (out[0],), ()
        return out


def pair_swap(to_x, to_y):
    return swap(to_x, 1, 4), swap(to_y, 2, 4)


def plane_attn_fwd_kernel(
    info_ref, x_ref, w_ref, cos_ref, sin_ref, segc_ref, segr_ref, qkv_ref, ol_ref, lse_ref, bias_ref, *, tile
):
    length = x_ref.shape[0]

    @pl.when(pl.program_id(0) == 0)
    def _():
        fill_bias(info_ref, segc_ref, segr_ref, bias_ref, tile)

    for step in range(length // (2 * tile)):
        rows = pl.ds(step * 2 * tile, 2 * tile)
        proj = mm(x_ref[rows, :], w_ref[...])
        cosine, sine = cos_ref[rows, :], sin_ref[rows, :]
        for part in range(proj.shape[1] // HEAD_DIM):
            low = part * HEAD_DIM
            piece = proj[:, low : low + HEAD_DIM]
            if part % 3 < 2:
                piece = piece * cosine + pltpu.roll(piece, HEAD_DIM // 2, 1) * sine
            qkv_ref[rows, low : low + HEAD_DIM] = piece.astype(BF)

    heads = qkv_ref.shape[1] // (3 * HEAD_DIM)
    units = [(h, t) for h in range(heads) for t in range(length // tile)]
    keys, values_t = {}, {}

    def scores_of(unit):
        h, t = unit
        base = 3 * HEAD_DIM * h
        if h not in keys:
            keys[h] = qkv_ref[:, base + HEAD_DIM : base + 2 * HEAD_DIM]
            values_t[h] = qkv_ref[:, base + 2 * HEAD_DIM : base + 3 * HEAD_DIM].astype(F32).T.astype(BF)
        return mm_nt(keys[h], qkv_ref[t * tile : (t + 1) * tile, base : base + HEAD_DIM])

    later = scores_of(units[0])
    for k, (h, t) in enumerate(units):
        raw = later
        if k + 1 < len(units):
            later = scores_of(units[k + 1])
        rows = pl.ds(t * tile, tile)
        scores = raw * score_scale + bias_ref[:, rows]
        top = jnp.max(scores, axis=0, keepdims=True)
        exponent = jnp.exp(scores - top)
        total = jnp.sum(exponent, axis=0, keepdims=True)
        attended = mm(values_t[h], exponent.astype(BF)) * (1.0 / total)
        ol_ref[rows, h * HEAD_DIM : (h + 1) * HEAD_DIM] = attended.T.astype(BF)
        lse_ref[h, :, rows] = top + jnp.log(total)


def plane_attn_fwd(chain, info, row, tokens, qkv_weight, cosine, sine, segc, segr, after=()):
    _, length, width = tokens.shape
    heads = qkv_weight.shape[1] // (3 * HEAD_DIM)
    return chain(
        functools.partial(plane_attn_fwd_kernel, tile=256),
        "attn_fwd",
        (heads // 2,),
        (tokens, qkv_weight, cosine, sine, segc, segr),
        [
            pl.BlockSpec((None, length, width), lambda h, *_: (row, 0, 0), pipeline_mode=pl.Buffered(1)),
            spec((width, 768), lambda h, *_: (0, h)),
            const_spec((length, HEAD_DIM)),
            const_spec((length, HEAD_DIM)),
            const_spec((length, 1)),
            const_spec((1, length)),
        ],
        [((length, heads * 384), BF), ((length, heads * 128), BF), ((heads, 1, length), F32)],
        [
            spec((length, 768), lambda h, *_: (0, h)),
            spec((length, 256), lambda h, *_: (0, h)),
            spec((2, 1, length), lambda h, *_: (h, 0, 0)),
        ],
        scalars=(info,),
        after=after,
        scratch=[pltpu.VMEM((length, length), F32)],
        flops=heads * (2 * length * width * 384 + 8 * length * length * 128),
        nbytes=2 * length * width + 2 * width * heads * 384 + 8 * length * heads * 128,
    )


def plane_attn_bwd_kernel(
    info_ref, qkv_ref, own, r1, r2, r3a, r3b, ow_ref, lse_ref, cos_ref, sin_ref, segc_ref, segr_ref, dqkv_ref,
    bias_ref, dol_nat, *, tile
):
    length = qkv_ref.shape[0]
    block = own.shape[0]
    half = block // 2
    me = info_ref[0]

    @pl.when(pl.program_id(0) == 0)
    def _():
        fill_bias(info_ref, segc_ref, segr_ref, bias_ref, tile)

    def natural(r, lower):
        return pl.multiple_of((me ^ r) * block + lower, half)

    for r, piece in enumerate((own, r1, r2)):
        dol_nat[pl.ds(natural(r, 0), block), :] = mm_nt(piece[...], ow_ref[...]).astype(BF)
    for lower, piece in ((0, r3a), (half, r3b)):
        dol_nat[pl.ds(natural(3, lower), half), :] = mm_nt(piece[...], ow_ref[...]).astype(BF)

    heads = qkv_ref.shape[1] // (3 * HEAD_DIM)
    count = length // tile
    units = [(h, t) for h in range(heads) for t in range(count)]
    keys, values, keys_t = {}, {}, {}

    def products_of(unit):
        h, t = unit
        base = 3 * HEAD_DIM * h
        if h not in keys:
            keys[h] = qkv_ref[:, base + HEAD_DIM : base + 2 * HEAD_DIM]
            values[h] = qkv_ref[:, base + 2 * HEAD_DIM : base + 3 * HEAD_DIM]
            keys_t[h] = keys[h].astype(F32).T.astype(BF)
        rows = pl.ds(t * tile, tile)
        queries = qkv_ref[rows, base : base + HEAD_DIM]
        dol = dol_nat[rows, h * HEAD_DIM : (h + 1) * HEAD_DIM]
        return queries, dol, mm_nt(keys[h], queries), mm_nt(values[h], dol)

    dk = dv = None
    later = products_of(units[0])
    for k, (h, t) in enumerate(units):
        queries, dol, raw, dp = later
        if k + 1 < len(units):
            later = products_of(units[k + 1])
        base = 3 * HEAD_DIM * h
        rows = pl.ds(t * tile, tile)
        probs = jnp.exp(raw * score_scale + bias_ref[:, rows] - lse_ref[h, :, rows])
        weighted = probs * dp
        inner = jnp.sum(weighted, axis=0, keepdims=True)
        draw = ((weighted - probs * inner) * score_scale).astype(BF)
        dv_part, dk_part = mm(probs.astype(BF), dol), mm(draw, queries)
        dv = dv_part if t == 0 else dv + dv_part
        dk = dk_part if t == 0 else dk + dk_part
        dq = mm(keys_t[h], draw).T
        turned = dq * cos_ref[rows, :] - pltpu.roll(dq, HEAD_DIM // 2, 1) * sin_ref[rows, :]
        dqkv_ref[rows, base : base + HEAD_DIM] = turned.astype(BF)
        if t == count - 1:
            turned = dk * cos_ref[...] - pltpu.roll(dk, HEAD_DIM // 2, 1) * sin_ref[...]
            dqkv_ref[:, base + HEAD_DIM : base + 2 * HEAD_DIM] = turned.astype(BF)
            dqkv_ref[:, base + 2 * HEAD_DIM : base + 3 * HEAD_DIM] = dv.astype(BF)


def plane_attn_bwd(chain, info, qkv, pieces, out_weight, lse, cosine, sine, segc, segr, after=()):
    length = qkv.shape[0]
    heads = qkv.shape[1] // 384
    width = out_weight.shape[1]
    return chain(
        functools.partial(plane_attn_bwd_kernel, tile=256),
        "attn_bwd",
        (heads // 2,),
        (qkv, *pieces, out_weight, lse, cosine, sine, segc, segr),
        [spec((length, 768), lambda h, *_: (0, h))]
        + [const_spec(p.shape) for p in pieces]
        + [
            spec((256, width), lambda h, *_: (h, 0)),
            spec((2, 1, length), lambda h, *_: (h, 0, 0)),
            const_spec((length, HEAD_DIM)),
            const_spec((length, HEAD_DIM)),
            const_spec((length, 1)),
            const_spec((1, length)),
        ],
        [(qkv.shape, BF)],
        [spec((length, 768), lambda h, *_: (0, h))],
        scalars=(info,),
        after=after,
        scratch=[pltpu.VMEM((length, length), F32), pltpu.VMEM((length, 256), BF)],
        flops=heads * 24 * length * length * 128,
        nbytes=16 * length * heads * 128,
    )[0]


def plane_out_norm_kernel(
    info_ref, order_ref, *refs
):
    lows, highs = refs[:5], refs[5:10]
    ow_ref, mine_ref, other_ref = refs[10:13]
    xl_ref, xh_ref, gain_ref, bias_ref, hl_ref, n1_ref, rstd_ref, total_ref = refs[13:]
    half = xl_ref.shape[0]
    at = pl.program_id(0)

    def blocks(group, place):
        diagonal = jnp.where(place < 4, group[3][...].astype(F32), group[4][...].astype(F32)).astype(BF)
        return [ref[...] for ref in group[:3]] + [diagonal]

    feat = mine_ref.shape[0] // 3
    total_ref[:half] = xl_ref[...].astype(F32) * deep_alpha
    total_ref[half:] = xh_ref[...].astype(F32) * deep_alpha
    low, high = blocks(lows, order_ref[2 * at]), blocks(highs, order_ref[2 * at + 1])
    ols = [jnp.concatenate([lo, hi], axis=0) for lo, hi in zip(low, high)]

    def add(first, second):
        total = mm(ols[0], ow_ref[...])
        for r in range(1, 4):
            rows = pl.ds((r - 1) * feat, feat)
            total += mm(ols[r][:, :feat], first[rows, :])
            total += mm(ols[r][:, feat:], second[rows, :])
        total_ref[...] += total

    @pl.when(info_ref[3] == 0)
    def _():
        add(mine_ref, other_ref)

    @pl.when(info_ref[3] != 0)
    def _():
        add(other_ref, mine_ref)

    total = total_ref[...]
    centered = total - jnp.mean(total, axis=1, keepdims=True)
    variance = jnp.mean(centered * centered, axis=1, keepdims=True)
    inv = lax.rsqrt(variance + norm_eps)
    normed = centered * inv
    hl_ref[...] = (normed * gain_ref[...] + bias_ref[...]).astype(BF)

    @pl.when(pl.program_id(0) == 3)
    def _():
        n1_ref[...] = normed
        rstd_ref[...] = jnp.broadcast_to(inv, rstd_ref.shape)


def plane_out_norm(chain, info, order, row, ol_pieces, out_weight, mine, other, tokens, gain, bias, after=()):
    _, length, width = tokens.shape
    block = length // 4
    half = block // 2
    head_width = out_weight.shape[0]
    low = lambda i, info, order: (order[2 * i], 0)
    high = lambda i, info, order: (order[2 * i + 1], 0)

    def ol_specs(index):
        upper = lambda i, info, order: (jnp.minimum(index(i, info, order)[0], 3), 0)
        lower = lambda i, info, order: (jnp.maximum(index(i, info, order)[0] - 4, 0), 0)
        return [spec((half, head_width), f) for f in (index, index, index, upper, lower)]

    low3 = lambda i, info, order: (row, order[2 * i], 0)
    high3 = lambda i, info, order: (row, order[2 * i + 1], 0)
    return chain(
        plane_out_norm_kernel,
        "out_norm",
        (4,),
        (*ol_pieces, *ol_pieces, out_weight, mine, other, tokens, tokens, gain, bias),
        ol_specs(low)
        + ol_specs(high)
        + [const_spec(out_weight.shape), const_spec(mine.shape), const_spec(other.shape)]
        + [
            spec((None, half, width), low3),
            spec((None, half, width), high3),
            const_spec((1, width)),
            const_spec((1, width)),
        ],
        [((length, width), BF), ((block, width), F32), ((block, HEAD_DIM), F32)],
        [
            spec((block, width), lambda i, *_: (i, 0)),
            spec((block, width), lambda i, *_: (0, 0)),
            spec((block, HEAD_DIM), lambda i, *_: (0, 0)),
        ],
        scalars=(info, order),
        after=after,
        scratch=[pltpu.VMEM((block, width), F32)],
        flops=2 * length * width * width,
        nbytes=2 * width * width + 6 * length * width,
    )


def split_kernel(x_ref, y_ref, *refs):
    count = len(refs) // 2 - 1
    refs[count][...] = x_ref[...]
    refs[count + 1][...] = y_ref[...]


def forward(chain, from_x, from_y, carry=(), after=()):
    rows, width = from_x.shape
    shape = (rows // 2, width)
    any_spec = pl.BlockSpec(memory_space=ANY)
    out = chain(
        split_kernel, "split", (1,), (from_x, from_y, *carry),
        [
            pl.BlockSpec(shape, lambda i, *_: (0, 0), pipeline_mode=pl.Buffered(1)),
            pl.BlockSpec(shape, lambda i, *_: (1, 0), pipeline_mode=pl.Buffered(1)),
        ]
        + [any_spec] * len(carry),
        [(shape, BF)] * 2 + [(c.shape, c.dtype) for c in carry],
        [spec(shape, lambda i, *_: (0, 0))] * 2 + [any_spec] * len(carry),
        after=after,
        aliases={2 + k: 2 + k for k in range(len(carry))},
        nbytes=4 * rows * width,
    )
    pair = (swap(out[0], 2, 4), swap(out[1], 1, 4))
    return (pair, *out[2:]) if carry else pair


def ow_join_kernel(x_ref, y_ref, a_ref, b_ref, out_ref):
    rows = x_ref.shape[0]
    out_ref[:rows] = x_ref[...]
    out_ref[rows : 2 * rows] = y_ref[...]
    out_ref[2 * rows : 2 * rows + rows // 2] = a_ref[...]
    out_ref[2 * rows + rows // 2 :] = b_ref[...]


def ow_join(chain, pieces, after=()):
    rows, width = pieces[0].shape
    shape = (3 * rows, width)
    return chain(
        ow_join_kernel, "ow_join", (1,), pieces, [const_spec(p.shape) for p in pieces],
        [(shape, BF)], [spec(shape, lambda i, *_: (0, 0))], after=after,
    )[0]


def relay_kernel(*refs):
    refs[len(refs) // 2][...] = refs[0][...]


def relay(chain, carry, after=()):
    small = jnp.zeros((8, 128), F32)
    any_spec = pl.BlockSpec(memory_space=ANY)
    count = len(carry)
    out = chain(
        relay_kernel, "relay", (1,), (small, *carry), [const_spec(small.shape)] + [any_spec] * count,
        [(small.shape, F32)] + [(c.shape, c.dtype) for c in carry],
        [spec(small.shape, lambda i, *_: (0, 0))] + [any_spec] * count,
        after=after, aliases={1 + k: 1 + k for k in range(count)},
    )
    return out[1:]


def load_once(pairs, sem):
    copies = [pltpu.make_async_copy(src, dst, sem.at[k]) for k, (src, dst) in enumerate(pairs)]

    @pl.when(pl.program_id(0) == 0)
    def _():
        for copy in copies:
            copy.start()

    def wait(k):
        @pl.when(pl.program_id(0) == 0)
        def _():
            copies[k].wait()

    return wait


def store_half(first, part, refs):
    at = pl.program_id(0)
    half = part.shape[0] // 2
    if first is None:

        @pl.when(at == 0)
        def _():
            refs[0][...] = part

        @pl.when(at == 1)
        def _():
            refs[1][...] = part

        @pl.when(at == 2)
        def _():
            refs[2][...] = part[:half]
            refs[3][...] = part[half:]

        @pl.when(at == 3)
        def _():
            refs[4][...] = part

        return

    @pl.when(at == 0)
    def _():
        if first:
            refs[0][...] = part
        else:
            refs[0][...] = part[:half]
            refs[1][...] = part[half:]

    @pl.when(at == 1)
    def _():
        refs[-1][...] = part


def half_outs(first, block, width):
    if first is None:
        sizes = [block, block, block // 2, block // 2, block]
    else:
        sizes = [block, block] if first else [block // 2, block // 2, block]
    return [((s, width), BF) for s in sizes], [spec((s, width), lambda i, *_: (0, 0)) for s in sizes]


def plane_ffn_fwd_kernel(hl_ref, wg_hbm, wu_hbm, wd_hbm, *refs, first):
    refs, (wg, wu, wd, sem) = refs[:-4], refs[-4:]
    (al_ref, ga_ref, gb_ref), refs = refs[-3:], refs[:-3]
    wait = load_once(((wg_hbm, wg), (wu_hbm, wu), (wd_hbm, wd)), sem)
    hidden = hl_ref[...]
    wait(0)
    gate = mm(hidden, wg[...])
    wait(1)
    up = mm(hidden, wu[...])
    cdf = 0.5 + 0.5 * lax.erf(gate * (1.0 / math.sqrt(2.0)))
    pdf = jnp.exp(gate * gate * -0.5) * (1.0 / math.sqrt(2.0 * math.pi))
    act = gate * cdf
    ga_ref[...] = (up * (cdf + gate * pdf)).astype(BF)
    gb_ref[...] = act.astype(BF)
    low = (act * up).astype(BF)
    al_ref[...] = low
    wait(2)
    store_half(first, mm(low, wd[...]).astype(BF), refs)


def plane_ffn_fwd(chain, first, hidden, weights, kept, after=()):
    length, width = hidden.shape
    units = weights[0].shape[1]
    block = length // 4
    base = 2 if first is False else 0
    steps = 4 if first is None else 2
    tiled = lambda w: spec((block, w), lambda i, *_: (i + base, 0))
    outs, out_specs = half_outs(first, block, width)
    n = len(outs)
    any_spec = pl.BlockSpec(memory_space=ANY)
    kept = tuple(kept)
    carried = kept[3:]
    kernel = functools.partial(plane_ffn_fwd_kernel, first=first)
    if first is not False:
        body_kernel = kernel
    else:
        nk, nc = len(kept), len(carried)

        def body_kernel(hl, wg, wu, wd, *refs):
            refs = refs[nk:]
            kernel(hl, wg, wu, wd, *refs[:n], *refs[n + nc :])

    out = chain(
        body_kernel,
        "ffn_fwd",
        (steps,),
        (hidden, *weights, *kept),
        [tiled(width)] + [any_spec] * (3 + len(kept)),
        outs + [(c.shape, BF) for c in carried] + [((length, units), BF)] * 3,
        out_specs + [any_spec] * len(carried) + [tiled(units)] * 3,
        after=after,
        aliases={}
        if first is not False
        else {
            **{4 + k: n + len(carried) + k for k in range(3)},
            **{7 + k: n + k for k in range(len(carried))},
        },
        scratch=[
            pltpu.VMEM(weights[0].shape, BF),
            pltpu.VMEM(weights[1].shape, BF),
            pltpu.VMEM(weights[2].shape, BF),
            pltpu.SemaphoreType.DMA((3,)),
        ],
        mib=60,
        flops=3 * length * width * units * steps // 2,
        nbytes=6 * units * width + 3 * length * units,
    )
    n += len(carried)
    return out[:n], out[n:]


def plane_ffn_bwd_kernel(dffn_ref, ga_ref, gb_ref, wd_hbm, wg_hbm, wu_hbm, *refs, first):
    refs, (wd, wg, wu, sem) = refs[:-4], refs[-4:]
    (dg_ref, du_ref), refs = refs[-2:], refs[:-2]
    wait = load_once(((wd_hbm, wd), (wg_hbm, wg), (wu_hbm, wu)), sem)
    grad = dffn_ref[...]
    wait(0)
    dact = mm_nt(grad, wd[...])
    dgate = (dact * ga_ref[...].astype(F32)).astype(BF)
    dup = (dact * gb_ref[...].astype(F32)).astype(BF)
    dg_ref[...] = dgate
    du_ref[...] = dup
    wait(1)
    part = mm_nt(dgate, wg[...])
    wait(2)
    part += mm_nt(dup, wu[...])
    store_half(first, part.astype(BF), refs)


def plane_ffn_bwd(chain, first, dffn, slopes, weights, kept, after=()):
    length, width = dffn.shape
    units = weights[0].shape[1]
    block = length // 4
    base = 2 if first is False else 0
    steps = 4 if first is None else 2
    tiled = lambda w: spec((block, w), lambda i, *_: (i + base, 0))
    outs, out_specs = half_outs(first, block, width)
    n = len(outs)
    any_spec = pl.BlockSpec(memory_space=ANY)
    kept = tuple(kept)
    kernel = functools.partial(plane_ffn_bwd_kernel, first=first)
    carried = kept[2:]
    if first is not False:
        body_kernel = kernel
    else:
        nk, nc = len(kept), len(carried)

        def body_kernel(d, ga, gb, wd, wg, wu, *refs):
            refs = refs[nk:]
            kernel(d, ga, gb, wd, wg, wu, *refs[:n], *refs[n + nc :])

    out = chain(
        body_kernel,
        "ffn_bwd",
        (steps,),
        (dffn, *slopes, weights[2], weights[0], weights[1], *kept),
        [tiled(width), tiled(units), tiled(units)] + [any_spec] * (3 + len(kept)),
        outs + [(c.shape, BF) for c in carried] + [((length, units), BF)] * 2,
        out_specs + [any_spec] * len(carried) + [tiled(units)] * 2,
        after=after,
        aliases={}
        if first is not False
        else {
            **{6 + k: n + len(carried) + k for k in range(2)},
            **{8 + k: n + k for k in range(len(carried))},
        },
        scratch=[
            pltpu.VMEM(weights[2].shape, BF),
            pltpu.VMEM(weights[0].shape, BF),
            pltpu.VMEM(weights[1].shape, BF),
            pltpu.SemaphoreType.DMA((3,)),
        ],
        mib=60,
        flops=3 * length * width * units * steps // 2,
        nbytes=6 * units * width + 4 * length * units,
    )
    n += len(carried)
    return out[:n], out[n:]


def middle_kernel(x1_ref, y1_ref, r1b_ref, r2a_ref, x2_ref, y2_ref):
    half = r1b_ref.shape[0]
    x2_ref[...] = (r1b_ref[...].astype(F32) + y1_ref[half:].astype(F32)).astype(BF)
    y2_ref[...] = (r2a_ref[...].astype(F32) + x1_ref[half:].astype(F32)).astype(BF)


def middle(chain, arrived, r1b, r2a, after=()):
    x1, y1 = arrived
    shape = r1b.shape
    return chain(
        middle_kernel,
        "middle_sum",
        (1,),
        (x1, y1, r1b, r2a),
        [const_spec(a.shape) for a in (x1, y1, r1b, r2a)],
        [(shape, BF)] * 2,
        [spec(shape, lambda i, *_: (0, 0))] * 2,
        after=after,
        mib=32,
        nbytes=16 * r1b.size,
    )


def own_sum(own, x1, y1, x2, y2):
    top = pl.program_id(0) < OWN_STEPS // 2
    direct = jnp.where(top, x1[...].astype(F32), y1[...].astype(F32))
    relayed = jnp.where(top, y2[...].astype(F32), x2[...].astype(F32))
    return own[...].astype(F32) + direct + relayed


def resid_two_kernel(own, x1, y1, x2, y2, n1_ref, gain_ref, bias_ref, out_ref):
    total = own_sum(own, x1, y1, x2, y2)
    out_ref[...] = (deep_alpha * (n1_ref[...] * gain_ref[...] + bias_ref[...]) + total).astype(BF)


def norm_one_back_kernel(own, x1, y1, x2, y2, dffn_ref, n1_ref, rstd_ref, gain_ref, low_ref, dr1_ref, sums_ref):
    total = own_sum(own, x1, y1, x2, y2)
    dh = deep_alpha * dffn_ref[...].astype(F32) + total
    normed = n1_ref[...]
    scaled = dh * gain_ref[...]
    inner = jnp.mean(scaled, axis=1, keepdims=True) + normed * jnp.mean(scaled * normed, axis=1, keepdims=True)
    dr1 = rstd_ref[:, :1] * (scaled - inner)
    dr1_ref[...] = dr1
    low_ref[...] = dr1.astype(BF)
    gain_sum = jnp.sum(dh * normed, axis=0, keepdims=True)
    bias_sum = jnp.sum(dh, axis=0, keepdims=True)

    @pl.when(pl.program_id(0) == 0)
    def _():
        sums_ref[0:1, :] = gain_sum
        sums_ref[1:2, :] = bias_sum

    @pl.when(pl.program_id(0) > 0)
    def _():
        sums_ref[0:1, :] += gain_sum
        sums_ref[1:2, :] += bias_sum


def input_grad_kernel(own, x1, y1, x2, y2, dr1_ref, out_ref):
    out_ref[...] = (deep_alpha * dr1_ref[...] + own_sum(own, x1, y1, x2, y2)).astype(BF)


OWN_STEPS = 4


def rows_spec(array_shape, tile, base=0):
    return spec((tile, array_shape[1]), lambda i, *_: (i + base, 0))


def own_step(chain, kernel, name, sums, extra, extra_specs, outs, after=()):
    block, width = sums[0].shape
    tile = block // OWN_STEPS
    middle_step = OWN_STEPS // 2
    first = spec((tile, width), lambda i, *_: (jnp.minimum(i, middle_step - 1), 0))
    later = spec((tile, width), lambda i, *_: (jnp.maximum(i - middle_step, 0), 0))
    return chain(
        kernel,
        name,
        (OWN_STEPS,),
        (*sums, *extra),
        [rows_spec((block, width), tile), first, later, later, first] + extra_specs,
        outs,
        [rows_spec(s, tile) if s[0] == block else spec(s, lambda i, *_: (0, 0)) for s, _ in outs],
        after=after,
        mib=40,
        nbytes=16 * block * width,
    )


def plane_norm_two_kernel(info_ref, order_ref, share_ref, own, r1, r2, r3a, r3b, cot_ref, gain_ref, bias_ref, *refs):
    act_ref, sums_ref, dffn_ref, held = refs[-4:]
    at = pl.program_id(0)
    half = held.shape[0]
    places = (
        (r1, 0), (r3a, 0), (r2, half), (r3b, 0), (r1, half), (r2, 0), (own, 0), (own, half),
    )
    for k, (ref, start) in enumerate(places):

        @pl.when(at == k)
        def _(ref=ref, start=start):
            held[...] = ref[start : start + half]

    resid = held[...].astype(F32)
    centered = resid - jnp.mean(resid, axis=1, keepdims=True)
    variance = jnp.mean(centered * centered, axis=1, keepdims=True)
    inv = lax.rsqrt(variance + norm_eps)
    normed = centered * inv
    gain = gain_ref[...]
    act_ref[...] = (normed * gain + bias_ref[...]).astype(BF)
    dout = cot_ref[...].astype(F32) * share_ref[0]
    scaled = dout * gain
    inner = jnp.mean(scaled, axis=1, keepdims=True) + normed * jnp.mean(scaled * normed, axis=1, keepdims=True)
    dffn_ref[...] = (inv * (scaled - inner)).astype(BF)
    gain_sum = jnp.sum(dout * normed, axis=0, keepdims=True)
    bias_sum = jnp.sum(dout, axis=0, keepdims=True)

    @pl.when(at == 0)
    def _():
        sums_ref[0:1, :] = gain_sum
        sums_ref[1:2, :] = bias_sum

    @pl.when(at > 0)
    def _():
        sums_ref[0:1, :] += gain_sum
        sums_ref[1:2, :] += bias_sum


def plane_norm_two(chain, info, order, share, row, pieces, cotangent, gain, bias, before, after=()):
    rows, length, width = cotangent.shape
    half = length // 8
    natural = spec((None, half, width), lambda i, info, order, share: (row, order[i], 0))
    held = () if before is None else (before,)
    return chain(
        plane_norm_two_kernel,
        "norm_two",
        (8,),
        (*pieces, cotangent, gain, bias, *held),
        [const_spec(p.shape) for p in pieces]
        + [natural, const_spec((1, width)), const_spec((1, width))]
        + [pl.BlockSpec(memory_space=ANY)] * len(held),
        [(cotangent.shape, BF), ((2, width), F32), ((length, width), BF)],
        [natural, spec((2, width), lambda i, *_: (0, 0)), spec((half, width), lambda i, *_: (i, 0))],
        scalars=(info, order, share),
        after=after,
        aliases={len(pieces) + 3: 0} if held else {},
        scratch=[pltpu.VMEM((half, width), BF)],
        flops=20 * length * width,
        nbytes=8 * length * width,
    )


def plane_input_back_kernel(order_ref, low_ref, high_ref, w_ref, x1_ref, y1_ref, r1b_ref, r2a_ref, own_ref):
    at = pl.program_id(0)
    half = low_ref.shape[0]
    part = mm_nt(jnp.concatenate([low_ref[...], high_ref[...]], axis=0), w_ref[...]).astype(BF)

    @pl.when(at == 0)
    def _():
        x1_ref[...] = part

    @pl.when(at == 1)
    def _():
        y1_ref[...] = part

    @pl.when(at == 2)
    def _():
        r1b_ref[...] = part[:half]
        r2a_ref[...] = part[half:]

    @pl.when(at == 3)
    def _():
        own_ref[...] = part


def plane_input_back(chain, order, dqkv, qkv_weight, after=()):
    length, columns = dqkv.shape
    width = qkv_weight.shape[0]
    block = length // 4
    half = block // 2
    sizes = [block, block, half, half, block]
    return chain(
        plane_input_back_kernel,
        "input_back",
        (4,),
        (dqkv, dqkv, qkv_weight),
        [
            spec((half, columns), lambda i, order: (order[2 * i], 0)),
            spec((half, columns), lambda i, order: (order[2 * i + 1], 0)),
            const_spec(qkv_weight.shape),
        ],
        [((s, width), BF) for s in sizes],
        [spec((s, width), lambda i, *_: (0, 0)) for s in sizes],
        scalars=(order,),
        after=after,
        flops=2 * length * width * columns,
        nbytes=2 * width * columns + 4 * length * width,
    )


def plane_place_kernel(order_ref, own, r1, r2, r3a, r3b, *refs):
    out_ref = refs[-1]
    at = pl.program_id(0)
    half = r3a.shape[0]
    for k, ref in enumerate((own, r1, r2)):

        @pl.when(at == k)
        def _(ref=ref):
            out_ref[...] = ref[...]

    @pl.when(at == 3)
    def _():
        out_ref[:half] = r3a[...]
        out_ref[half:] = r3b[...]


def plane_place(chain, info, row, pieces, shape, before, after=()):
    rows, length, width = shape
    block = length // 4
    held = () if before is None else (before,)
    return chain(
        plane_place_kernel,
        "place",
        (4,),
        (*pieces, *held),
        [const_spec(p.shape) for p in pieces] + [pl.BlockSpec(memory_space=ANY)] * len(held),
        [(shape, BF)],
        [spec((None, block, width), lambda i, info: (row, i ^ info[0], 0))],
        scalars=(info,),
        after=after,
        aliases={len(pieces): 0} if held else {},
        mib=32,
        nbytes=4 * length * width,
    )[0]


def panels(ref, value):
    for c in range(value.shape[1] // 128):
        ref[c] = value[:, c * 128 : (c + 1) * 128].astype(BF)


def grad_rows_kernel(info_ref, left_a, left_b, right_a, right_b, send, keep, *, steps):
    at = pl.program_id(0)
    value = mm(left_a[...].T, right_a[...]) + mm(left_b[...].T, right_b[...])

    @pl.when(at < steps)
    def _():
        panels(send, value)

    @pl.when(at >= steps)
    def _():
        panels(keep, value)


def lhs_spec(lhs, tile, index, row):
    if lhs.ndim == 3:
        return spec((None, lhs.shape[1], tile), lambda *a: (row, 0, index(*a)))
    return spec((lhs.shape[0], tile), lambda *a: (0, index(*a)))


def grad_rows(chain, info, lefts, rights, after=()):
    rows = lefts[0].shape[-1]
    tile = 256
    steps = rows // tile // 2
    length, columns = rights[0].shape

    def at(i, info):
        other = (1 - info[3]) * steps + i
        own = info[3] * steps + i - steps
        return jnp.where(i < steps, other, own)

    shape = (columns // 128, rows // 2, 128)
    out = chain(
        functools.partial(grad_rows_kernel, steps=steps),
        "grad_rows",
        (2 * steps,),
        (*lefts, *rights),
        [lhs_spec(lefts[r], tile, at, r) for r in range(2)] + [const_spec(r.shape) for r in rights],
        [(shape, BF)] * 2,
        [
            spec((shape[0], tile, 128), lambda i, *_: (0, jnp.minimum(i, steps - 1), 0)),
            spec((shape[0], tile, 128), lambda i, *_: (0, jnp.maximum(i - steps, 0), 0)),
        ],
        scalars=(info,),
        after=after,
        flops=4 * rows * length * columns,
        nbytes=2 * rows * columns + 4 * rows * length,
    )
    return out[0].reshape(-1, 128), out[1].reshape(-1, 128)


def grad_columns_kernel(info_ref, left_a, left_b, right_a, right_b, send, keep, turned_a, turned_b, held):
    @pl.when(pl.program_id(0) == 0)
    def _():
        turned_a[...] = left_a[...].T
        turned_b[...] = left_b[...].T

    held[...] = mm(turned_a[...], right_a[...]) + mm(turned_b[...], right_b[...])
    half = held.shape[0] // 2
    core = info_ref[3]
    panels(send, held[pl.ds(pl.multiple_of((1 - core) * half, 8), half), :])
    panels(keep, held[pl.ds(pl.multiple_of(core * half, 8), half), :])


def grad_columns(chain, info, lefts, rights, after=()):
    length, rows = lefts[0].shape
    columns = rights[0].shape[1]
    tile = 256
    shape = (columns // 128, rows // 2, 128)
    out = chain(
        grad_columns_kernel,
        "grad_columns",
        (columns // tile,),
        (*lefts, *rights),
        [const_spec(left.shape) for left in lefts] + [spec((length, tile), lambda i, *_: (0, i))] * 2,
        [(shape, BF)] * 2,
        [spec((tile // 128, rows // 2, 128), lambda i, *_: (i, 0, 0))] * 2,
        scalars=(info,),
        after=after,
        scratch=[pltpu.VMEM((rows, length), BF)] * 2 + [pltpu.VMEM((rows, tile), F32)],
        flops=4 * rows * length * columns,
        nbytes=2 * rows * columns + 4 * length * (rows + columns),
    )
    return out[0].reshape(-1, 128), out[1].reshape(-1, 128)


def grad_plain_kernel(left_a, left_b, right_a, right_b, out_ref):
    out_ref[...] = (mm(left_a[...].T, right_a[...]) + mm(left_b[...].T, right_b[...])).astype(BF)


def grad_plain(chain, lefts, rights, after=()):
    rows = lefts[0].shape[-1]
    tile = 256
    length, columns = rights[0].shape
    return chain(
        grad_plain_kernel,
        "grad_plain",
        (rows // tile,),
        (*lefts, *rights),
        [lhs_spec(lefts[r], tile, lambda i, *_: i, r) for r in range(2)] + [const_spec(r.shape) for r in rights],
        [((rows, columns), BF)],
        [spec((tile, columns), lambda i, *_: (i, 0))],
        after=after,
        flops=4 * rows * length * columns,
        nbytes=2 * rows * columns + 4 * rows * length,
    )[0]


def grad_plain_columns_kernel(left_a, left_b, right_a, right_b, out_ref, turned_a, turned_b):
    @pl.when(pl.program_id(0) == 0)
    def _():
        turned_a[...] = left_a[...].T
        turned_b[...] = left_b[...].T

    out_ref[...] = (mm(turned_a[...], right_a[...]) + mm(turned_b[...], right_b[...])).astype(BF)


def grad_plain_columns(chain, lefts, rights, after=()):
    length, rows = lefts[0].shape
    columns = rights[0].shape[1]
    tile = 256
    return chain(
        grad_plain_columns_kernel,
        "grad_plain_columns",
        (columns // tile,),
        (*lefts, *rights),
        [const_spec(left.shape) for left in lefts] + [spec((length, tile), lambda i, *_: (0, i))] * 2,
        [((rows, columns), BF)],
        [spec((rows, tile), lambda i, *_: (0, i))],
        after=after,
        scratch=[pltpu.VMEM((rows, length), BF)] * 2,
        flops=4 * rows * length * columns,
        nbytes=2 * rows * columns + 4 * length * (rows + columns),
    )[0]


def grad_out(lhs, pieces, me):
    block = pieces[0].shape[0]
    half = block // 2
    total = 0.0
    for r, piece in enumerate(pieces[:3]):
        part = lhs[pl.ds(pl.multiple_of((me ^ r) * block, half), block), :]
        total = total + mm(part.T, piece[...])
    for lower, piece in ((0, pieces[3]), (half, pieces[4])):
        part = lhs[pl.ds(pl.multiple_of((me ^ 3) * block + lower, half), half), :]
        total = total + mm(part.T, piece[...])
    return total


def grad_out_kernel(info_ref, left_a, left_b, *refs):
    pieces_a, pieces_b, (send, keep, held) = refs[:5], refs[5:10], refs[10:]
    held[...] = grad_out(left_a, pieces_a, info_ref[0]) + grad_out(left_b, pieces_b, info_ref[0])
    half = held.shape[0] // 2
    core = info_ref[3]
    panels(send, held[pl.ds(pl.multiple_of((1 - core) * half, 8), half), :])
    panels(keep, held[pl.ds(pl.multiple_of(core * half, 8), half), :])


def plane_grad_out(chain, info, lefts, pieces, after=()):
    length, rows = lefts[0].shape
    columns = pieces[0][0].shape[1]
    tile = 512
    shape = (columns // 128, rows // 2, 128)
    every = (*pieces[0], *pieces[1])
    out = chain(
        grad_out_kernel,
        "grad_out",
        (columns // tile,),
        (*lefts, *every),
        [const_spec(left.shape) for left in lefts]
        + [spec((p.shape[0], tile), lambda i, *_: (0, i)) for p in every],
        [(shape, BF)] * 2,
        [spec((tile // 128, rows // 2, 128), lambda i, *_: (i, 0, 0))] * 2,
        scalars=(info,),
        after=after,
        scratch=[pltpu.VMEM((rows, tile), F32)],
        flops=4 * rows * length * columns,
        nbytes=2 * rows * columns + 4 * length * (rows + columns),
    )
    return out[0].reshape(-1, 128), out[1].reshape(-1, 128)


class Line:
    GRID = 4

    def __init__(self, chain, edge):
        self.chain, self.edge = chain, edge
        self.pending = []
        self.slots = []
        self.step = 0
        self.done = {}
        self.first = self.second = None
        self.sent = self.mid = None

    def add(self, name, keep, got, chunks):
        for k in range(chunks):
            self.pending.append((name, keep, got, k, keep.shape[0] // chunks, keep.shape[0]))

    def get(self, j):
        return self.slots[j] if j >= 0 else None

    def busy(self):
        return bool(self.pending) or any(self.slots[-3:])

    def complete(self, name):
        return not any(slot and slot[0] == name for slot in self.pending + self.slots[-3:])

    def advance(self, after=()):
        j = self.step
        self.slots.append(self.pending.pop(0) if self.pending else None)
        new, cur, prev, last = self.get(j), self.get(j - 1), self.get(j - 2), self.get(j - 3)
        ins, in_specs, outs, out_specs, aliases, roles = [], [], [], [], {}, []
        grid = self.GRID

        def give(array, rows, base, role, when):
            block = rows // grid
            if when is None:
                index = lambda i, edge: (base + i, 0)
            elif when:
                index = lambda i, edge: (base + i * edge[0], 0)
            else:
                index = lambda i, edge: (base + i * (1 - edge[0]), 0)
            ins.append(array)
            in_specs.append(spec((block, 128), index))
            roles.append(role)

        if new:
            name, keep, got, k, rows, _ = new
            give(keep, rows, k * grid, "new_keep", True)
            give(got, rows, k * grid, "new_got", True)
        if cur:
            name, keep, got, k, rows, _ = cur
            give(keep, rows, k * grid, "cur_keep", False)
            give(got, rows, k * grid, "cur_got", False)
            give(self.first, rows, 0, "cur_in", False)
        if prev:
            rows = prev[4]
            give(self.mid, rows, 0, "prev_mid", False)
            give(self.second, rows, 0, "prev_in", False)
        if last:
            rows = last[4]
            give(self.first, rows, 0, "last_in", True)
            give(self.sent, rows, 0, "last_sent", False)
            if last[3] > 0:
                ins.append(self.done[last[0]])
                in_specs.append(pl.BlockSpec(memory_space=ANY))
                roles.append("held")
        names = []
        if new or prev:
            rows = max(c[4] for c in (new, prev) if c)
            outs.append(((rows, 128), BF))
            out_specs.append(pl.BlockSpec((rows, 128), lambda i, *_: (0, 0)))
            names.append("sent")
        if cur:
            outs.append(((cur[4], 128), BF))
            out_specs.append(spec((cur[4] // grid, 128), lambda i, *_: (i, 0)))
            names.append("mid")
        if last:
            base = last[3] * grid
            outs.append(((last[5], 128), BF))
            out_specs.append(spec((last[4] // grid, 128), lambda i, *_, base=base: (base + i, 0)))
            names.append("done")
            if last[3] > 0:
                aliases = {len(ins) - 1: len(outs) - 1}

        def kernel(edge_ref, *refs):
            src = dict(zip(roles, refs[: len(roles)]))
            dst = dict(zip(names, refs[len(roles) :]))
            at = pl.program_id(0)
            is_edge = edge_ref[0] == 1
            f32 = lambda r: src[r][...].astype(F32)

            if new:
                @pl.when(is_edge)
                def _():
                    block = new[4] // grid
                    rows = pl.ds(pl.multiple_of(at * block, block), block)
                    dst["sent"][rows, :] = (f32("new_keep") + f32("new_got")).astype(BF)

            @pl.when(jnp.logical_not(is_edge))
            def _():
                if cur:
                    dst["mid"][...] = (f32("cur_keep") + f32("cur_got") + f32("cur_in")).astype(BF)
                if prev:
                    block = prev[4] // grid
                    rows = pl.ds(pl.multiple_of(at * block, block), block)
                    dst["sent"][rows, :] = (f32("prev_mid") + f32("prev_in")).astype(BF)

            if last:
                @pl.when(is_edge)
                def _():
                    dst["done"][...] = src["last_in"][...]

                @pl.when(jnp.logical_not(is_edge))
                def _():
                    dst["done"][...] = src["last_sent"][...]

        out = self.chain(
            kernel,
            "line_step",
            (grid,),
            tuple(ins),
            in_specs,
            outs,
            out_specs,
            scalars=(self.edge,),
            after=after,
            aliases=aliases,
            mib=32,
            nbytes=6 * 5632 * 256,
        )
        got = dict(zip(names, out))
        if "done" in got:
            self.done[last[0]] = got["done"]
        self.sent = got.get("sent")
        self.mid = got.get("mid")
        if self.sent is not None:
            self.first = lax.ppermute(self.sent, "obj", [(0, 1), (3, 2), (1, 0), (2, 3)])
        if self.mid is not None:
            self.second = lax.ppermute(self.mid, "obj", [(1, 2), (2, 1)])
        self.step += 1


def widen_kernel(info_ref, mine_ref, theirs_ref, out_ref, *, steps):
    at = pl.program_id(0)

    @pl.when(at < steps)
    def _():
        for c in range(mine_ref.shape[0]):
            out_ref[:, c * 128 : (c + 1) * 128] = mine_ref[c].astype(F32)

    @pl.when(at >= steps)
    def _():
        for c in range(theirs_ref.shape[0]):
            out_ref[:, c * 128 : (c + 1) * 128] = theirs_ref[c].astype(F32)


def widen(chain, info, mine, theirs, rows, columns, after=()):
    count = columns // 128
    half = rows // 2
    tile = 176 if half % 176 == 0 else min(256, half)
    steps = half // tile
    mine, theirs = (a.reshape(count, half, 128) for a in (mine, theirs))

    def at(i, info):
        return jnp.where(i < steps, info[3] * steps + i, (1 - info[3]) * steps + i - steps)

    return chain(
        functools.partial(widen_kernel, steps=steps),
        "widen",
        (2 * steps,),
        (mine, theirs),
        [
            spec((count, tile, 128), lambda i, *_: (0, jnp.minimum(i, steps - 1), 0)),
            spec((count, tile, 128), lambda i, *_: (0, jnp.maximum(i - steps, 0), 0)),
        ],
        [((rows, columns), F32)],
        [spec((tile, columns), lambda i, info: (at(i, info), 0))],
        scalars=(info,),
        after=after,
        mib=32,
        nbytes=6 * rows * columns,
    )[0]


def cast_kernel(in_ref, out_ref):
    out_ref[...] = in_ref[...].astype(F32)


def cast(chain, array, after=()):
    rows, columns = array.shape
    tile = 176 if rows % 256 else 256
    return chain(
        cast_kernel, "cast", (rows // tile,), (array,), [rows_spec(array.shape, tile)],
        [(array.shape, F32)], [rows_spec(array.shape, tile)], after=after,
    )[0]


def total_sum_kernel(in_ref, out_ref):
    out_ref[...] = jnp.sum(in_ref[...], axis=0)


def total_sum(chain, array):
    shape = array.shape[1:]
    return chain(
        total_sum_kernel, "total_sum", (1,), (array,), [const_spec(array.shape)], [(shape, F32)],
        [spec(shape, lambda i, *_: (0, 0))],
    )[0]


def plane_body(
    tokens,
    cotangent,
    segment_ids,
    mlm_mask,
    glm_prefix,
    glm_span,
    qkv_weight,
    out_weight,
    gate_weight,
    up_weight,
    down_weight,
    norm1_gain,
    norm1_bias,
    norm2_gain,
    norm2_bias,
):
    seq_here, length, width = tokens.shape
    data_ways = lax.axis_size("dp")
    objective_ways = lax.axis_size("obj")
    me = lax.axis_index("tensor").astype(jnp.int32)
    core = lax.axis_index("dp").astype(jnp.int32)
    at_obj = lax.axis_index("obj")
    edge = ((at_obj == 0) | (at_obj == objective_ways - 1)).astype(jnp.int32).reshape(1)
    block = length // 4
    units = gate_weight.shape[1]
    rows_all = mlm_mask.shape[0]
    masked_limit = seq_here * data_ways * (objective_ways // 2)
    row_ids = jnp.arange(rows_all, dtype=jnp.int32)
    counts = jnp.where(row_ids < masked_limit, jnp.sum(mlm_mask, axis=1), glm_span).astype(F32)
    weight_all = counts * rows_all / jnp.sum(counts)
    first_row = (at_obj * data_ways + core) * seq_here
    share_here = lax.dynamic_slice_in_dim(weight_all, first_row, seq_here)
    prefix_here = lax.dynamic_slice_in_dim(glm_prefix, first_row, seq_here)
    span_here = lax.dynamic_slice_in_dim(glm_span, first_row, seq_here)
    open_here = jnp.where(first_row < masked_limit, length, prefix_here)
    info = [jnp.stack([me, open_here[r], prefix_here[r] + span_here[r], core]) for r in range(2)]
    order = jnp.stack([2 * (me ^ r) + h for r, h in ORDER])
    share = [share_here[r : r + 1] for r in range(2)]
    cosine, sine = constant_tables(length)
    segc = [segment_ids[r].reshape(length, 1) for r in range(2)]
    segr = [segment_ids[r].reshape(1, length) for r in range(2)]
    gain1, bias1 = norm1_gain.reshape(1, width), norm1_bias.reshape(1, width)
    gain2, bias2 = norm2_gain.reshape(1, width), norm2_bias.reshape(1, width)
    weights = (gate_weight, up_weight, down_weight)
    chain = Chain()
    A, B = 0, 1

    ow_half = out_weight.shape[0] // 2
    ow_own = lax.dynamic_slice_in_dim(out_weight, core * ow_half, ow_half)
    owx, owy = pair_swap(ow_own, ow_own)

    def attention(r, after=()):
        return plane_attn_fwd(chain, info[r], r, tokens, qkv_weight, cosine, sine, segc[r], segr[r], after)

    def out_and_norm(r, ol_pieces, after=()):
        return plane_out_norm(
            chain, info[r], order, r, ol_pieces, out_weight, ow_mine, ow_other, tokens, gain1, bias1, after
        )

    qkv, ol, lse, hl, n1, rstd = {}, {}, {}, {}, {}, {}
    qkv[A], ol[A], lse[A] = attention(A)
    owra, owrb = forward(chain, owx, owy)
    olx, oly, olr = {}, {}, {}
    olx[A], oly[A] = pair_swap(ol[A], ol[A])
    qkv[B], ol[B], lse[B] = attention(B)
    ow_mine = ow_join(chain, (owx, owy, owra, owrb), after=(olx[A], oly[A]))
    ow_other = lax.ppermute(ow_mine, "dp", CORES)
    olr[A], ol[B] = forward(chain, olx[A], oly[A], (ol[B],))
    (ol[B],) = relay(chain, (ol[B],), after=olr[A])
    olx[B], oly[B] = pair_swap(ol[B], ol[B])
    hl[A], n1[A], rstd[A] = out_and_norm(A, (ol[A], olx[A], oly[A], *olr[A]))
    vec = const_spec((1, width))
    tile = block // OWN_STEPS
    full = rows_spec((block, width), tile)
    ff, fb, ib, rs1, rs2 = {}, {}, {}, {}, {}
    resid, rx, ry, rr = {}, {}, {}, {}

    def sums_of(own, first, second):
        return (own, first[0], first[1], second[0], second[1])

    def second_resid(r, after=()):
        return own_step(
            chain, resid_two_kernel, "resid_two", sums_of(ff[r][2], rs1[r], rs2[r]), (n1[r], gain1, bias1),
            [full, vec, vec], [((block, width), BF)], after,
        )[0]

    def second_norm(r, before, after=()):
        pieces = (resid[r], rx[r], ry[r], *rr[r])
        return plane_norm_two(
            chain, info[r], order, share[r], r, pieces, cotangent, gain2, bias2, before, after
        )

    def first_norm_back(r, after=()):
        return own_step(
            chain, norm_one_back_kernel, "norm_one_back", sums_of(fb[r][2], rs1[r], rs2[r]),
            (dffn[r], n1[r], rstd[r], gain1),
            [rows_spec((block, width), tile, 3 * OWN_STEPS), full, rows_spec((block, HEAD_DIM), tile), vec],
            [((block, width), BF), ((block, width), F32), ((2, width), F32)], after,
        )

    olr[B] = forward(chain, olx[B], oly[B])
    sent, kept_a = plane_ffn_fwd(chain, None, hl[A], weights, ())
    rs1[A], ff[A] = pair_swap(*sent[:2]), sent[2:]
    hl[B], n1[B], rstd[B] = out_and_norm(B, (ol[B], olx[B], oly[B], *olr[B]))
    rs2[A] = pair_swap(*middle(chain, rs1[A], ff[A][0], ff[A][1]))
    sent, kept = plane_ffn_fwd(chain, True, hl[B], weights, ())
    resid[A] = second_resid(A)
    rx[A], ry[A] = pair_swap(resid[A], resid[A])
    ff[B], kept_b = plane_ffn_fwd(chain, False, hl[B], weights, (*kept, *sent))
    al, slopes = {A: kept_a[0], B: kept_b[0]}, {A: kept_a[1:], B: kept_b[1:]}
    rr[A] = forward(chain, rx[A], ry[A])
    rs1[B] = pair_swap(*relay(chain, ff[B][3:], after=rr[A]))

    sums2, dffn, dgu, sums1, dr1, dattn, dax, day, dar = {}, {}, {}, {}, {}, {}, {}, {}, {}
    pieces, dqkv, dx, dxx, dxy, dxr, outs = {}, {}, {}, {}, {}, {}, {}

    def attention_back(r, after=()):
        pieces[r] = (dattn[r], dax[r], day[r], *dar[r])
        return plane_attn_bwd(
            chain, info[r], qkv[r], pieces[r], out_weight, lse[r], cosine, sine, segc[r], segr[r], after
        )

    def input_back_sums(r, after=()):
        x1, y1, r1b, r2a, own = plane_input_back(chain, order, dqkv[r], qkv_weight, after)
        ib[r] = (r1b, r2a, own)
        rs1[r] = pair_swap(x1, y1)

    def input_grad_own(r, after=()):
        return own_step(
            chain, input_grad_kernel, "input_grad", sums_of(ib[r][2], rs1[r], rs2[r]), (dr1[r],), [full],
            [((block, width), BF)], after,
        )[0]

    theirs = {}

    def begin_finish(name):
        theirs[name] = lax.ppermute(line.done[name], "dp", CORES)

    def finish_matrix(name, rows, columns, after=()):
        outs[name] = widen(chain, info[B], line.done[name], theirs[name], rows, columns, after)

    def middle_sums(r, after=()):
        part = fb[r] if r not in ib else ib[r]
        rs2[r] = pair_swap(*middle(chain, rs1[r], part[0], part[1], after))

    line = Line(chain, edge)
    activations, sums2[A], dffn[A] = second_norm(A, None)
    sent, kept = plane_ffn_bwd(chain, True, dffn[A], slopes[A], weights, ())
    rs1[A] = pair_swap(*sent)
    rs2[B] = pair_swap(*middle(chain, rs1[B], ff[B][0], ff[B][1]))
    fb[A], dgu[A] = plane_ffn_bwd(chain, False, dffn[A], slopes[A], weights, kept)
    resid[B] = second_resid(B)
    rx[B], ry[B] = pair_swap(resid[B], resid[B])
    middle_sums(A)
    rr[B] = forward(chain, rx[B], ry[B])
    dattn[A], dr1[A], sums1[A] = first_norm_back(A)
    dax[A], day[A] = pair_swap(dattn[A], dattn[A])
    activations, sums2[B], dffn[B] = second_norm(B, activations)
    down_update = grad_plain_columns(chain, (al[A], al[B]), (dffn[A], dffn[B]))
    down_sum = lax.psum(down_update, ("obj", "dp"))
    dar[A] = forward(chain, dax[A], day[A])
    sent, dgu[B] = plane_ffn_bwd(chain, None, dffn[B], slopes[B], weights, ())
    fb[B] = sent[2:]
    rs1[B] = pair_swap(*sent[:2])
    chain.close(*dar[A])
    gate_send, gate_keep = grad_rows(chain, info[B], (hl[A], hl[B]), (dgu[A][0], dgu[B][0]))
    gate_got = lax.ppermute(gate_send, "dp", CORES)
    line.add("gate", gate_keep, gate_got, 2)
    middle_sums(B)
    up_send, up_keep = grad_rows(chain, info[B], (hl[A], hl[B]), (dgu[A][1], dgu[B][1]))
    up_got = lax.ppermute(up_send, "dp", CORES)
    line.add("up", up_keep, up_got, 2)
    chain.close(gate_got)
    dattn[B], dr1[B], sums1[B] = first_norm_back(B)
    dax[B], day[B] = pair_swap(dattn[B], dattn[B])
    chain.close(up_got)
    line.advance()
    dqkv[A] = attention_back(A)
    dar[B] = forward(chain, dax[B], day[B])
    input_back_sums(A)
    line.advance()
    dqkv[B] = attention_back(B)
    line.advance()
    middle_sums(A)
    qkv_send, qkv_keep = grad_rows(chain, info[B], (tokens, tokens), (dqkv[A], dqkv[B]), after=(down_sum,))
    qkv_got = lax.ppermute(qkv_send, "dp", CORES)
    line.add("qkv", qkv_keep, qkv_got, 3)
    dx[A] = input_grad_own(A)
    dxx[A], dxy[A] = pair_swap(dx[A], dx[A])
    line.advance()
    input_back_sums(B)
    chain.close(qkv_got, dxx[A], dxy[A])
    out_send, out_keep = plane_grad_out(chain, info[B], (ol[A], ol[B]), (pieces[A], pieces[B]))
    line.advance()
    out_got = lax.ppermute(out_send, "dp", CORES)
    line.add("out", out_keep, out_got, 1)
    middle_sums(B)
    line.advance()
    chain.close(out_got)
    dxr[A] = forward(chain, dxx[A], dxy[A])
    dx[B] = input_grad_own(B)
    dxx[B], dxy[B] = pair_swap(dx[B], dx[B])
    outs["down"] = cast(chain, down_sum)
    line.advance()
    begin_finish("gate")
    input_grad = plane_place(chain, info[A], A, (dx[A], dxx[A], dxy[A], *dxr[A]), tokens.shape, None)
    dxr[B] = forward(chain, dxx[B], dxy[B])
    mine = (me == 0).astype(F32)
    sums = jnp.concatenate([sums1[A] + sums1[B], (sums2[A] + sums2[B]) * mine])
    every_sum = lax.all_gather(sums, ("obj", "dp", "tensor"))
    line.advance()
    finish_matrix("gate", width, units)
    line.advance()
    begin_finish("up")
    input_grad = plane_place(chain, info[B], B, (dx[B], dxx[B], dxy[B], *dxr[B]), tokens.shape, input_grad)
    line.advance()
    finish_matrix("up", width, units)
    begin_finish("qkv")
    line.advance()
    begin_finish("out")
    finish_matrix("qkv", width, qkv_weight.shape[1])
    sums = total_sum(chain, every_sum)
    finish_matrix("out", out_weight.shape[0], width)

    return (
        activations,
        input_grad,
        outs["qkv"],
        outs["out"],
        outs["gate"],
        outs["up"],
        outs["down"],
        sums[0],
        sums[1],
        sums[2],
        sums[3],
    )


def body(*args):
    if plane_case(args[0].shape, args[7].shape, args[10].shape):
        return plane_body(*args)
    return general_body(*args)


def solution(mesh):
    rows3 = P(("obj", "dp"), None, None)
    in_specs = (
        rows3,
        rows3,
        P(("obj", "dp"), None),
        P(),
        P(),
        P(),
        P(None, "tensor"),
        P("tensor", None),
        P(None, "tensor"),
        P(None, "tensor"),
        P("tensor", None),
        P(),
        P(),
        P(),
        P(),
    )
    out_specs = (
        rows3,
        rows3,
        P(None, "tensor"),
        P("tensor", None),
        P(None, "tensor"),
        P(None, "tensor"),
        P("tensor", None),
        P(),
        P(),
        P(),
        P(),
    )
    return jax.shard_map(body, mesh=mesh, in_specs=in_specs, out_specs=out_specs, check_vma=False)
```

```python
import functools
import math

import jax
import jax.numpy as jnp
import numpy as np
from jax import lax
from jax.experimental import pallas as pl
from jax.experimental.pallas import tpu as pltpu
from jax.sharding import PartitionSpec as P

HEAD_DIM = 128
deep_alpha = math.sqrt(48.0)
norm_eps = 1e-05
mask_fill = -1e30
score_scale = 1.0 / math.sqrt(HEAD_DIM)
MIB = 1024 * 1024
BF = jnp.bfloat16
F32 = jnp.float32
ANY = pl.ANY


def mm(a, b):
    return lax.dot_general(a, b, (((1,), (0,)), ((), ())), preferred_element_type=F32)


def mm_nt(a, b):
    return lax.dot_general(a, b, (((1,), (1,)), ((), ())), preferred_element_type=F32)


def mm_tn(a, b):
    return lax.dot_general(a, b, (((0,), (0,)), ((), ())), preferred_element_type=F32)


def params(mib, grid_rank=1):
    return pltpu.CompilerParams(
        vmem_limit_bytes=mib * MIB, dimension_semantics=("arbitrary",) * grid_rank
    )


def cost(flops, nbytes, trans=0):
    return pl.CostEstimate(flops=int(flops), bytes_accessed=int(nbytes), transcendentals=int(trans))


def const_spec(shape):
    zeros = (0,) * len(shape)
    return pl.BlockSpec(shape, lambda *_: zeros, pipeline_mode=pl.Buffered(1))


def rotary_tables(seq_length):
    half_width = HEAD_DIM // 2
    frequency = jnp.exp(
        jnp.arange(half_width, dtype=F32) * (-2.0 * math.log(10000.0) / HEAD_DIM)
    )
    angles = jnp.arange(seq_length, dtype=F32)[:, None] * frequency[None, :]
    sine = jnp.sin(angles)
    cosine = jnp.cos(angles)
    return jnp.concatenate([cosine, cosine], axis=1), jnp.concatenate([-sine, sine], axis=1)


def fill_bias(info_ref, segc_ref, segr_ref, bias_ref, tile):
    length = bias_ref.shape[0]
    prefix, limit = info_ref[1], info_ref[2]

    def one(step, carry):
        rows = pl.ds(pl.multiple_of(step * tile, tile), tile)
        key_pos = lax.broadcasted_iota(jnp.int32, (tile, length), 0) + step * tile
        query_pos = lax.broadcasted_iota(jnp.int32, (tile, length), 1)
        same = segc_ref[rows, :] == segr_ref[...]
        open_keys = (
            (key_pos < prefix)
            | ((key_pos <= query_pos) & (key_pos < limit))
            | (key_pos == query_pos)
        )
        bias_ref[rows, :] = jnp.where(same & open_keys, 0.0, mask_fill)
        return carry

    lax.fori_loop(0, length // tile, one, 0)


def attn_fwd_kernel(
    info_ref, x_ref, w_ref, cos_ref, sin_ref, segc_ref, segr_ref, qkv_ref, ol_ref, lse_ref, bias_ref, tile
):
    length = x_ref.shape[0]

    @pl.when(pl.program_id(0) == 0)
    def _():
        fill_bias(info_ref, segc_ref, segr_ref, bias_ref, tile)

    for step in range(length // tile):
        rows = pl.ds(step * tile, tile)
        proj = mm(x_ref[rows, :], w_ref[...])
        cosine, sine = cos_ref[rows, :], sin_ref[rows, :]
        for part in range(2):
            piece = proj[:, part * HEAD_DIM : (part + 1) * HEAD_DIM]
            turned = piece * cosine + pltpu.roll(piece, HEAD_DIM // 2, 1) * sine
            qkv_ref[rows, part * HEAD_DIM : (part + 1) * HEAD_DIM] = turned.astype(BF)
        qkv_ref[rows, 2 * HEAD_DIM :] = proj[:, 2 * HEAD_DIM :].astype(BF)
    keys = qkv_ref[:, HEAD_DIM : 2 * HEAD_DIM]
    values_t = qkv_ref[:, 2 * HEAD_DIM :].astype(F32).T.astype(BF)
    for step in range(length // tile):
        rows = pl.ds(step * tile, tile)
        queries = qkv_ref[rows, :HEAD_DIM]
        scores = mm_nt(keys, queries) * score_scale + bias_ref[:, rows]
        top = jnp.max(scores, axis=0, keepdims=True)
        exponent = jnp.exp(scores - top)
        total = jnp.sum(exponent, axis=0, keepdims=True)
        attended = mm(values_t, exponent.astype(BF)) * (1.0 / total)
        ol_ref[rows, :] = attended.T.astype(BF)
        lse_ref[:, rows] = top + jnp.log(total)


def attn_fwd(info, row, tokens, qkv_weight, cosine, sine, segc, segr):
    _, length, width = tokens.shape
    heads = qkv_weight.shape[1] // (3 * HEAD_DIM)
    tile = min(256, length)
    grid_spec = pltpu.PrefetchScalarGridSpec(
        num_scalar_prefetch=1,
        grid=(heads,),
        in_specs=[
            pl.BlockSpec((None, length, width), lambda h, *_: (row, 0, 0), pipeline_mode=pl.Buffered(1)),
            pl.BlockSpec((width, 3 * HEAD_DIM), lambda h, *_: (0, h)),
            const_spec((length, HEAD_DIM)),
            const_spec((length, HEAD_DIM)),
            const_spec((length, 1)),
            const_spec((1, length)),
        ],
        out_specs=[
            pl.BlockSpec((length, 3 * HEAD_DIM), lambda h, *_: (0, h)),
            pl.BlockSpec((length, HEAD_DIM), lambda h, *_: (0, h)),
            pl.BlockSpec((None, 1, length), lambda h, *_: (h, 0, 0)),
        ],
        scratch_shapes=[pltpu.VMEM((length, length), F32)],
    )
    return pl.pallas_call(
        functools.partial(attn_fwd_kernel, tile=tile),
        grid_spec=grid_spec,
        out_shape=[
            jax.ShapeDtypeStruct((length, heads * 3 * HEAD_DIM), BF),
            jax.ShapeDtypeStruct((length, heads * HEAD_DIM), BF),
            jax.ShapeDtypeStruct((heads, 1, length), F32),
        ],
        compiler_params=params(48),
        cost_estimate=cost(
            heads * (2 * length * width * 384 + 8 * length * length * HEAD_DIM),
            2 * length * width + 2 * width * heads * 384 + 8 * length * heads * 128,
        ),
        name="attn_fwd",
    )(info, tokens, qkv_weight, cosine, sine, segc, segr)


def attn_bwd_kernel(
    info_ref, qkv_ref, dol_ref, lse_ref, cos_ref, sin_ref, segc_ref, segr_ref, dqkv_ref,
    bias_ref, dol_nat, dk_ref, dv_ref, tile
):
    length = qkv_ref.shape[0]
    ways, block, _ = dol_ref.shape
    me = info_ref[0]

    @pl.when(pl.program_id(0) == 0)
    def _():
        fill_bias(info_ref, segc_ref, segr_ref, bias_ref, tile)

    for at in range(ways):
        dol_nat[pl.ds(at * block, block), :] = dol_ref[me ^ at]
    keys = qkv_ref[:, HEAD_DIM : 2 * HEAD_DIM]
    values = qkv_ref[:, 2 * HEAD_DIM :]
    keys_t = keys.astype(F32).T.astype(BF)
    for step in range(length // tile):
        rows = pl.ds(step * tile, tile)
        queries = qkv_ref[rows, :HEAD_DIM]
        dol = dol_nat[rows, :]
        scores = mm_nt(keys, queries) * score_scale + bias_ref[:, rows]
        probs = jnp.exp(scores - lse_ref[:, rows])
        dp = mm_nt(values, dol)
        inner = jnp.sum(probs * dp, axis=0, keepdims=True)
        draw = (probs * (dp - inner) * score_scale).astype(BF)
        dv = mm(probs.astype(BF), dol)
        dk = mm(draw, queries)
        if step == 0:
            dv_ref[...] = dv
            dk_ref[...] = dk
        else:
            dv_ref[...] += dv
            dk_ref[...] += dk
        dq = mm(keys_t, draw).T
        turned = dq * cos_ref[rows, :] - pltpu.roll(dq, HEAD_DIM // 2, 1) * sin_ref[rows, :]
        dqkv_ref[rows, :HEAD_DIM] = turned.astype(BF)
    dk = dk_ref[...]
    turned = dk * cos_ref[...] - pltpu.roll(dk, HEAD_DIM // 2, 1) * sin_ref[...]
    dqkv_ref[:, HEAD_DIM : 2 * HEAD_DIM] = turned.astype(BF)
    dqkv_ref[:, 2 * HEAD_DIM :] = dv_ref[...].astype(BF)


def attn_bwd(info, qkv, dol, lse, cosine, sine, segc, segr):
    length = qkv.shape[0]
    heads = qkv.shape[1] // (3 * HEAD_DIM)
    ways, block, _ = dol.shape
    tile = min(256, length)
    grid_spec = pltpu.PrefetchScalarGridSpec(
        num_scalar_prefetch=1,
        grid=(heads,),
        in_specs=[
            pl.BlockSpec((length, 3 * HEAD_DIM), lambda h, *_: (0, h)),
            pl.BlockSpec((ways, block, HEAD_DIM), lambda h, *_: (0, 0, h)),
            pl.BlockSpec((None, 1, length), lambda h, *_: (h, 0, 0)),
            const_spec((length, HEAD_DIM)),
            const_spec((length, HEAD_DIM)),
            const_spec((length, 1)),
            const_spec((1, length)),
        ],
        out_specs=pl.BlockSpec((length, 3 * HEAD_DIM), lambda h, *_: (0, h)),
        scratch_shapes=[
            pltpu.VMEM((length, length), F32),
            pltpu.VMEM((length, HEAD_DIM), BF),
            pltpu.VMEM((length, HEAD_DIM), F32),
            pltpu.VMEM((length, HEAD_DIM), F32),
        ],
    )
    return pl.pallas_call(
        functools.partial(attn_bwd_kernel, tile=tile),
        grid_spec=grid_spec,
        out_shape=jax.ShapeDtypeStruct(qkv.shape, BF),
        compiler_params=params(48),
        cost_estimate=cost(heads * 20 * length * length * HEAD_DIM, 16 * length * heads * 128),
        name="attn_bwd",
    )(info, qkv, dol, lse, cosine, sine, segc, segr)


def out_norm_kernel(info_ref, *refs, ways):
    ol_refs, ow_refs = refs[:ways], refs[ways : 2 * ways]
    x_ref, gain_ref, bias_ref, hl_ref, n1_ref, rstd_ref = refs[2 * ways :]
    total = x_ref[...].astype(F32) * deep_alpha
    for ol_ref, ow_ref in zip(ol_refs, ow_refs):
        total += mm(ol_ref[...], ow_ref[...])
    centered = total - jnp.mean(total, axis=1, keepdims=True)
    variance = jnp.mean(centered * centered, axis=1, keepdims=True)
    inv = lax.rsqrt(variance + norm_eps)
    normed = centered * inv
    hl_ref[...] = (normed * gain_ref[...] + bias_ref[...]).astype(BF)

    @pl.when(pl.program_id(0) == info_ref[0])
    def _():
        n1_ref[...] = normed
        rstd_ref[...] = jnp.broadcast_to(inv, rstd_ref.shape)


def out_norm(info, row, ol_pieces, ow_pieces, tokens, gain, bias):
    _, length, width = tokens.shape
    ways = len(ol_pieces)
    block = length // ways
    head_width = ol_pieces[0].shape[1]
    grid_spec = pltpu.PrefetchScalarGridSpec(
        num_scalar_prefetch=1,
        grid=(ways,),
        in_specs=[pl.BlockSpec((block, head_width), lambda i, *_: (i, 0))] * ways
        + [const_spec((head_width, width))] * ways
        + [
            pl.BlockSpec((None, block, width), lambda i, *_: (row, i, 0)),
            const_spec((1, width)),
            const_spec((1, width)),
        ],
        out_specs=[
            pl.BlockSpec((block, width), lambda i, info: (i ^ info[0], 0)),
            pl.BlockSpec((block, width), lambda i, *_: (0, 0)),
            pl.BlockSpec((block, HEAD_DIM), lambda i, *_: (0, 0)),
        ],
    )
    return pl.pallas_call(
        functools.partial(out_norm_kernel, ways=ways),
        grid_spec=grid_spec,
        out_shape=[
            jax.ShapeDtypeStruct((length, width), BF),
            jax.ShapeDtypeStruct((block, width), F32),
            jax.ShapeDtypeStruct((block, HEAD_DIM), F32),
        ],
        compiler_params=params(48),
        cost_estimate=cost(2 * length * width * width, 2 * width * width + 6 * length * width),
        name="out_norm",
    )(info, *ol_pieces, *ow_pieces, tokens, gain, bias)


def piece_shapes(ways, block, width):
    if ways == 4:
        sizes = [block] + [block // 2] * 6
    else:
        sizes = [block] * ways
    return [jax.ShapeDtypeStruct((size, width), BF) for size in sizes]


def store_pieces(at, part, refs, ways):
    if ways == 4:
        half = part.shape[0] // 2

        @pl.when(at == 0)
        def _():
            refs[0][...] = part

        for r in range(1, 4):

            @pl.when(at == r)
            def _(r=r):
                refs[2 * r - 1][...] = part[:half]
                refs[2 * r][...] = part[half:]
    else:
        for r in range(ways):

            @pl.when(at == r)
            def _(r=r):
                refs[r][...] = part


def piece_specs(shapes):
    return [pl.BlockSpec(s.shape, lambda *_: (0, 0)) for s in shapes]


def ffn_fwd_kernel(hl_ref, wg_ref, wu_ref, wd_ref, al_ref, ga_ref, gb_ref, *refs, ways):
    hidden = hl_ref[...]
    gate = mm(hidden, wg_ref[...])
    up = mm(hidden, wu_ref[...])
    cdf = 0.5 + 0.5 * lax.erf(gate * (1.0 / math.sqrt(2.0)))
    pdf = jnp.exp(gate * gate * -0.5) * (1.0 / math.sqrt(2.0 * math.pi))
    act = gate * cdf
    ga_ref[...] = (up * (cdf + gate * pdf)).astype(BF)
    gb_ref[...] = act.astype(BF)
    low = (act * up).astype(BF)
    al_ref[...] = low
    store_pieces(pl.program_id(0), mm(low, wd_ref[...]).astype(BF), refs, ways)


def ffn_fwd(hidden, gate_weight, up_weight, down_weight, ways):
    length, width = hidden.shape
    units = gate_weight.shape[1]
    block = length // ways
    tiled = lambda w: pl.BlockSpec((block, w), lambda i: (i, 0))
    shapes = piece_shapes(ways, block, width)
    out = pl.pallas_call(
        functools.partial(ffn_fwd_kernel, ways=ways),
        grid=(ways,),
        in_specs=[
            tiled(width),
            const_spec((width, units)),
            const_spec((width, units)),
            const_spec((units, width)),
        ],
        out_specs=[tiled(units)] * 3 + piece_specs(shapes),
        out_shape=[jax.ShapeDtypeStruct((length, units), BF)] * 3 + shapes,
        compiler_params=params(60),
        cost_estimate=cost(6 * length * width * units, 6 * units * width + 6 * length * units),
        name="ffn_fwd",
    )(hidden, gate_weight, up_weight, down_weight)
    return out[:3], out[3:]


def norm_two_kernel(info_ref, share_ref, *refs, n_in, ways):
    in_refs = refs[:n_in]
    cot_ref, gain_ref, bias_ref = refs[n_in : n_in + 3]
    act_ref, dffn_ref, sums_ref, held = refs[-4:]
    at = pl.program_id(0)
    if n_in == 5:
        half = held.shape[0] // 2
        for r in range(3):

            @pl.when(at == r)
            def _(r=r):
                held[...] = in_refs[r][...]

        @pl.when(at == 3)
        def _():
            held[:half] = in_refs[3][...]
            held[half:] = in_refs[4][...]
    else:
        for r in range(ways):

            @pl.when(at == r)
            def _(r=r):
                held[...] = in_refs[r][...]

    resid = held[...].astype(F32)
    centered = resid - jnp.mean(resid, axis=1, keepdims=True)
    variance = jnp.mean(centered * centered, axis=1, keepdims=True)
    inv = lax.rsqrt(variance + norm_eps)
    normed = centered * inv
    gain = gain_ref[...]
    act_ref[...] = (normed * gain + bias_ref[...]).astype(BF)
    dout = cot_ref[...].astype(F32) * share_ref[0]
    scaled = dout * gain
    inner = jnp.mean(scaled, axis=1, keepdims=True) + normed * jnp.mean(
        scaled * normed, axis=1, keepdims=True
    )
    dffn_ref[...] = (inv * (scaled - inner)).astype(BF)
    gain_sum = jnp.sum(dout * normed, axis=0, keepdims=True)
    bias_sum = jnp.sum(dout, axis=0, keepdims=True)

    @pl.when(at == 0)
    def _():
        sums_ref[0:1, :] = gain_sum
        sums_ref[1:2, :] = bias_sum

    @pl.when(at > 0)
    def _():
        sums_ref[0:1, :] += gain_sum
        sums_ref[1:2, :] += bias_sum


def norm_two(info, share, row, pieces, cotangent, gain, bias, before):
    rows, length, width = cotangent.shape
    block = pieces[0].shape[0]
    ways = length // block
    natural = pl.BlockSpec((None, block, width), lambda i, info, share: (row, i ^ info[0], 0))
    grid_spec = pltpu.PrefetchScalarGridSpec(
        num_scalar_prefetch=2,
        grid=(ways,),
        in_specs=[const_spec(p.shape) for p in pieces]
        + [natural, const_spec((1, width)), const_spec((1, width))]
        + ([pl.BlockSpec(memory_space=ANY)] if before is not None else []),
        out_specs=[
            natural,
            pl.BlockSpec((block, width), lambda i, *_: (i, 0)),
            pl.BlockSpec((2, width), lambda i, *_: (0, 0)),
        ],
        scratch_shapes=[pltpu.VMEM((block, width), BF)],
    )
    return pl.pallas_call(
        functools.partial(norm_two_kernel, n_in=len(pieces), ways=ways),
        grid_spec=grid_spec,
        out_shape=[
            jax.ShapeDtypeStruct(cotangent.shape, BF),
            jax.ShapeDtypeStruct((length, width), BF),
            jax.ShapeDtypeStruct((2, width), F32),
        ],
        input_output_aliases={len(pieces) + 5: 0} if before is not None else {},
        compiler_params=params(48),
        cost_estimate=cost(20 * length * width, 8 * length * width),
        name="norm_two",
    )(info, share, *pieces, cotangent, gain, bias, *([before] if before is not None else []))


def ffn_bwd_kernel(dffn_ref, ga_ref, gb_ref, wg_ref, wu_ref, wd_ref, dg_ref, du_ref, *refs, ways):
    dact = mm_nt(dffn_ref[...], wd_ref[...])
    dgate = (dact * ga_ref[...].astype(F32)).astype(BF)
    dup = (dact * gb_ref[...].astype(F32)).astype(BF)
    dg_ref[...] = dgate
    du_ref[...] = dup
    part = mm_nt(dgate, wg_ref[...]) + mm_nt(dup, wu_ref[...])
    store_pieces(pl.program_id(0), part.astype(BF), refs, ways)


def ffn_bwd(dffn, gate_slope, up_slope, gate_weight, up_weight, down_weight, ways):
    length, width = dffn.shape
    units = gate_weight.shape[1]
    block = length // ways
    tiled = lambda w: pl.BlockSpec((block, w), lambda i: (i, 0))
    shapes = piece_shapes(ways, block, width)
    out = pl.pallas_call(
        functools.partial(ffn_bwd_kernel, ways=ways),
        grid=(ways,),
        in_specs=[
            tiled(width),
            tiled(units),
            tiled(units),
            const_spec((width, units)),
            const_spec((width, units)),
            const_spec((units, width)),
        ],
        out_specs=[tiled(units)] * 2 + piece_specs(shapes),
        out_shape=[jax.ShapeDtypeStruct((length, units), BF)] * 2 + shapes,
        compiler_params=params(60),
        cost_estimate=cost(6 * length * width * units, 6 * units * width + 8 * length * units),
        name="ffn_bwd",
    )(dffn, gate_slope, up_slope, gate_weight, up_weight, down_weight)
    return out[0], out[1], out[2:]


def input_back_kernel(info_ref, dqkv_ref, w_ref, *refs, ways):
    part = mm_nt(dqkv_ref[...], w_ref[...])
    store_pieces(pl.program_id(0), part.astype(BF), refs, ways)


def input_back(info, dqkv, qkv_weight, ways):
    length, columns = dqkv.shape
    width = qkv_weight.shape[0]
    block = length // ways
    shapes = piece_shapes(ways, block, width)
    grid_spec = pltpu.PrefetchScalarGridSpec(
        num_scalar_prefetch=1,
        grid=(ways,),
        in_specs=[
            pl.BlockSpec((block, columns), lambda i, info: (i ^ info[0], 0)),
            const_spec((width, columns)),
        ],
        out_specs=piece_specs(shapes),
    )
    return pl.pallas_call(
        functools.partial(input_back_kernel, ways=ways),
        grid_spec=grid_spec,
        out_shape=shapes,
        compiler_params=params(48),
        cost_estimate=cost(2 * length * width * columns, 2 * width * columns + 2 * length * width),
        name="input_back",
    )(info, dqkv, qkv_weight)


def place_kernel(info_ref, *refs, n_in, ways):
    in_refs = refs[:n_in]
    out_ref = refs[-1]
    at = pl.program_id(0)
    if n_in == 5:
        half = out_ref.shape[0] // 2
        for r in range(3):

            @pl.when(at == r)
            def _(r=r):
                out_ref[...] = in_refs[r][...]

        @pl.when(at == 3)
        def _():
            out_ref[:half] = in_refs[3][...]
            out_ref[half:] = in_refs[4][...]
    else:
        for r in range(ways):

            @pl.when(at == r)
            def _(r=r):
                out_ref[...] = in_refs[r][...]


def place(info, row, pieces, shape, before):
    rows, length, width = shape
    block = pieces[0].shape[0]
    ways = length // block
    grid_spec = pltpu.PrefetchScalarGridSpec(
        num_scalar_prefetch=1,
        grid=(ways,),
        in_specs=[const_spec(p.shape) for p in pieces]
        + ([pl.BlockSpec(memory_space=ANY)] if before is not None else []),
        out_specs=pl.BlockSpec((None, block, width), lambda i, info: (row, i ^ info[0], 0)),
    )
    return pl.pallas_call(
        functools.partial(place_kernel, n_in=len(pieces), ways=ways),
        grid_spec=grid_spec,
        out_shape=jax.ShapeDtypeStruct(shape, BF),
        input_output_aliases={len(pieces) + 1: 0} if before is not None else {},
        compiler_params=params(32),
        cost_estimate=cost(0, 4 * length * width),
        name="place",
    )(info, *pieces, *([before] if before is not None else []))


def swap(array, bit, ways):
    return lax.ppermute(array, "tensor", [(i, i ^ bit) for i in range(ways)])


def gather_halves(own_a, own_b):
    xa = swap(own_a, 1, 4)
    yb = swap(own_b, 2, 4)
    xb = swap(own_b, 1, 4)
    ya = swap(own_a, 2, 4)
    ra = swap(xa, 2, 4)
    rb = swap(yb, 1, 4)
    return [(xa, xb), (ya, yb), (ra, rb)]


def gather_rel(own, ways):
    blocks = [own]
    bit = 1
    while bit < ways:
        blocks = blocks + [swap(b, bit, ways) for b in blocks]
        bit *= 2
    return blocks


def gather_tokens(own, ways):
    if ways == 4:
        half = own.shape[0] // 2
        (xa, xb), (ya, yb), (ra, rb) = gather_halves(own[:half], own[half:])
        return [own, jnp.concatenate([xa, xb]), jnp.concatenate([ya, yb]), ra, rb]
    return gather_rel(own, ways)


def join(pieces):
    return jnp.concatenate(pieces, axis=0)


def add_low(a, b):
    return (a.astype(F32) + b.astype(F32)).astype(BF)


def scatter_sum(pieces, ways):
    if ways == 4:
        own, r1a, r1b, r2a, r2b, r3a, r3b = pieces
        in3a = swap(r3a, 1, 4)
        in3b = swap(r3b, 2, 4)
        in1a = swap(r1a, 1, 4)
        in2b = swap(r2b, 2, 4)
        in2a = swap(add_low(r2a, in3a), 2, 4)
        in1b = swap(add_low(r1b, in3b), 1, 4)
        half = r1a.shape[0]
        top = own[:half].astype(F32) + in1a.astype(F32) + in2a.astype(F32)
        low = own[half:].astype(F32) + in1b.astype(F32) + in2b.astype(F32)
        return jnp.concatenate([top, low], axis=0)
    blocks = list(pieces)
    bit = ways // 2
    while bit >= 1:
        keep, send = blocks[:bit], blocks[bit:]
        blocks = [add_low(k, swap(s, bit, ways)) for k, s in zip(keep, send)]
        bit //= 2
    return blocks[0].astype(F32)


def sum_over_obj(array, ways):
    if ways != 4:
        return lax.psum(array, "obj")
    at = lax.axis_index("obj")
    one = add_low(array, lax.ppermute(array, "obj", [(0, 1), (3, 2)]))
    two = add_low(one, lax.ppermute(one, "obj", [(1, 2), (2, 1)]))
    back = lax.ppermute(two, "obj", [(1, 0), (2, 3)])
    return jnp.where((at == 0) | (at == 3), back, two)


def sum_gradient(update, data_ways, objective_ways):
    if data_ways != 2:
        return lax.psum(update, ("obj", "dp")).astype(F32)
    core = lax.axis_index("dp")
    half = update.shape[0] // 2
    other = [(0, 1), (1, 0)]
    mine = lax.dynamic_slice_in_dim(update, core * half, half)
    send = lax.dynamic_slice_in_dim(update, (1 - core) * half, half)
    mine = add_low(mine, lax.ppermute(send, "dp", other))
    mine = sum_over_obj(mine, objective_ways)
    theirs = lax.ppermute(mine, "dp", other)
    first = jnp.where(core == 0, mine, theirs)
    second = jnp.where(core == 0, theirs, mine)
    return jnp.concatenate([first, second], axis=0).astype(F32)


def general_body(
    tokens,
    cotangent,
    segment_ids,
    mlm_mask,
    glm_prefix,
    glm_span,
    qkv_weight,
    out_weight,
    gate_weight,
    up_weight,
    down_weight,
    norm1_gain,
    norm1_bias,
    norm2_gain,
    norm2_bias,
):
    seq_here, length, width = tokens.shape
    ways = lax.axis_size("tensor")
    data_ways = lax.axis_size("dp")
    objective_ways = lax.axis_size("obj")
    me = lax.axis_index("tensor").astype(jnp.int32)
    block = length // ways
    rows_all = mlm_mask.shape[0]
    masked_limit = seq_here * data_ways * (objective_ways // 2)
    row_ids = jnp.arange(rows_all, dtype=jnp.int32)
    counts = jnp.where(row_ids < masked_limit, jnp.sum(mlm_mask, axis=1), glm_span).astype(F32)
    weight_all = counts * rows_all / jnp.sum(counts)
    first_row = (lax.axis_index("obj") * data_ways + lax.axis_index("dp")) * seq_here
    share_here = lax.dynamic_slice_in_dim(weight_all, first_row, seq_here)
    prefix_here = lax.dynamic_slice_in_dim(glm_prefix, first_row, seq_here)
    span_here = lax.dynamic_slice_in_dim(glm_span, first_row, seq_here)
    masked_lm = first_row < masked_limit
    open_here = jnp.where(masked_lm, length, prefix_here)
    info = [jnp.stack([me, open_here[r], prefix_here[r] + span_here[r]]) for r in range(seq_here)]
    share = [share_here[r : r + 1] for r in range(seq_here)]
    cosine, sine = rotary_tables(length)
    segc = [segment_ids[r].reshape(length, 1) for r in range(seq_here)]
    segr = [segment_ids[r].reshape(1, length) for r in range(seq_here)]
    gain1, bias1 = norm1_gain.reshape(1, width), norm1_bias.reshape(1, width)
    gain2, bias2 = norm2_gain.reshape(1, width), norm2_bias.reshape(1, width)
    rows = range(seq_here)

    if ways == 4 and data_ways == 2:
        core = lax.axis_index("dp")
        half = out_weight.shape[0] // 2
        mine = lax.dynamic_slice_in_dim(out_weight, core * half, half)
        pairs = gather_halves(mine[: half // 2], mine[half // 2 :])
        ow_pieces = [out_weight]
        for a, b in pairs:
            got = jnp.concatenate([a, b])
            other = lax.ppermute(got, "dp", [(0, 1), (1, 0)])
            ow_pieces.append(
                jnp.concatenate(
                    [jnp.where(core == 0, got, other), jnp.where(core == 0, other, got)]
                )
            )
    else:
        ow_pieces = gather_rel(out_weight, ways)

    qkv, ol, lse, hl, n1, rstd1 = {}, {}, {}, {}, {}, {}
    al, slope_g, slope_u, dffn, dgate, dup = {}, {}, {}, {}, {}, {}
    r2_pieces, norm2_sums, norm1_sums, dr1, dqkv, dattn = {}, {}, {}, {}, {}, {}

    for r in rows:
        qkv[r], ol[r], lse[r] = attn_fwd(info[r], r, tokens, qkv_weight, cosine, sine, segc[r], segr[r])
    ffn_parts = {}
    for r in rows:
        if ways == 4:
            pairs = gather_halves(ol[r][: length // 2], ol[r][length // 2 :])
            ol_pieces = [ol[r]] + [jnp.concatenate(p) for p in pairs]
        else:
            ol_pieces = gather_rel(ol[r], ways)
        hl[r], n1[r], rstd1[r] = out_norm(info[r], r, ol_pieces, ow_pieces, tokens, gain1, bias1)
        (al[r], slope_g[r], slope_u[r]), ffn_parts[r] = ffn_fwd(
            hl[r], gate_weight, up_weight, down_weight, ways
        )
    for r in rows:
        total = scatter_sum(ffn_parts[r], ways)
        resid = deep_alpha * (n1[r] * gain1 + bias1) + total
        r2_pieces[r] = gather_tokens(resid.astype(BF), ways)

    activations = None
    dh_parts = {}
    for r in rows:
        activations, dffn[r], norm2_sums[r] = norm_two(
            info[r], share[r], r, r2_pieces[r], cotangent, gain2, bias2, activations
        )
        dgate[r], dup[r], dh_parts[r] = ffn_bwd(
            dffn[r], slope_g[r], slope_u[r], gate_weight, up_weight, down_weight, ways
        )

    def update(lefts, rights):
        total = None
        for r in rows:
            one = mm_tn(lefts[r], rights[r])
            total = one if total is None else total + one
        return total.astype(BF)

    def reduced(lefts, rights):
        return sum_gradient(update(lefts, rights), data_ways, objective_ways)

    down_grad = reduced(al, dffn)
    gate_grad = reduced(hl, dgate)
    up_grad = reduced(hl, dup)

    dx_parts = {}
    for r in rows:
        total = scatter_sum(dh_parts[r], ways)
        dh = deep_alpha * dffn[r][:block].astype(F32) + total
        scaled = dh * gain1
        inner = jnp.mean(scaled, axis=1, keepdims=True) + n1[r] * jnp.mean(
            scaled * n1[r], axis=1, keepdims=True
        )
        dr1[r] = rstd1[r][:, :1] * (scaled - inner)
        norm1_sums[r] = jnp.stack([jnp.sum(dh * n1[r], axis=0), jnp.sum(dh, axis=0)])
        dattn[r] = join(gather_tokens(dr1[r].astype(BF), ways))
    for r in rows:
        dol = mm_nt(dattn[r], out_weight).astype(BF).reshape(ways, block, -1)
        dqkv[r] = attn_bwd(info[r], qkv[r], dol, lse[r], cosine, sine, segc[r], segr[r])
        dx_parts[r] = input_back(info[r], dqkv[r], qkv_weight, ways)

    qkv_grad = reduced([tokens[r] for r in rows], dqkv)
    ol_rel = {}
    for r in rows:
        parts = ol[r].reshape(ways, block, -1)
        ol_rel[r] = jnp.stack(
            [lax.dynamic_index_in_dim(parts, me ^ i, 0, keepdims=False) for i in range(ways)]
        ).reshape(length, -1)
    out_grad = reduced(ol_rel, dattn)

    input_grad = None
    for r in rows:
        total = scatter_sum(dx_parts[r], ways)
        dx = (deep_alpha * dr1[r] + total).astype(BF)
        input_grad = place(info[r], r, gather_tokens(dx, ways), tokens.shape, input_grad)

    first = (me == 0).astype(F32)
    sums = jnp.concatenate(
        [sum(norm1_sums[r] for r in rows), sum(norm2_sums[r] for r in rows) * first]
    )
    sums = lax.psum(sums, ("obj", "dp", "tensor"))
    return (
        activations,
        input_grad,
        qkv_grad,
        out_grad,
        gate_grad,
        up_grad,
        down_grad,
        sums[0],
        sums[1],
        sums[2],
        sums[3],
    )


ORDER = ((1, 0), (3, 0), (2, 1), (3, 1), (1, 1), (2, 0), (0, 0), (0, 1))
CORES = ((0, 1), (1, 0))
DECLARED_FLOPS = 1e9
MICROS = {
    "attn_fwd": 1050, "split": 2, "ow_join": 4, "relay": 0.05, "out_norm": 21,
    "middle_sum": 0.6, "resid_two": 25, "norm_two": 15, "grad_columns": 1000, "grad_plain_columns": 0.57,
    "grad_plain": 3.8, "line_step": 5, "grad_rows": 1050, "attn_bwd": 1200, "norm_one_back": 30,
    "input_back": 70, "input_grad": 5, "grad_out": 0.55, "place": 5, "widen": 50,
    "cast": 9, "total_sum": 1,
}


def plane_case(token_shape, out_shape, down_shape):
    return (
        lax.axis_size("tensor") == 4
        and lax.axis_size("dp") == 2
        and lax.axis_size("obj") == 4
        and token_shape[0] == 2
        and token_shape[1] % 1024 == 0
        and token_shape[2] % 1024 == 0
        and down_shape[0] % 128 == 0
        and out_shape[0] % 256 == 0
    )


def spec(shape, index):
    return pl.BlockSpec(shape, index)


def call(
    kernel, name, grid, ins, in_specs, outs, out_specs, scalars=(), after=(), scratch=(), aliases=None,
    mib=48, flops=0, nbytes=0,
):
    ns, ni, na = len(scalars), len(ins), len(after)

    def wrapped(*refs):
        kernel(*refs[: ns + ni], *refs[ns + ni + na :])

    grid_spec = pltpu.PrefetchScalarGridSpec(
        num_scalar_prefetch=ns,
        grid=grid,
        in_specs=list(in_specs) + [pl.BlockSpec(memory_space=ANY)] * na,
        out_specs=list(out_specs),
        scratch_shapes=list(scratch),
    )
    return pl.pallas_call(
        wrapped,
        grid_spec=grid_spec,
        out_shape=[jax.ShapeDtypeStruct(s, d) for s, d in outs],
        input_output_aliases={ns + k: v for k, v in (aliases or {}).items()},
        compiler_params=params(62, len(grid)),
        cost_estimate=cost(DECLARED_FLOPS * MICROS.get(name, 9 * grid[0]), 1e6),
        name=name,
    )(*scalars, *ins, *after)


def constant_tables(length):
    half = HEAD_DIM // 2
    frequency = np.exp(np.arange(half, dtype=np.float32) * np.float32(-2.0 * math.log(10000.0) / HEAD_DIM))
    angles = np.arange(length, dtype=np.float32)[:, None] * frequency[None, :]
    cosine, sine = np.cos(angles), np.sin(angles)
    both = lambda a, b: jnp.asarray(np.concatenate([a, b], axis=1).astype(np.float32))
    return both(cosine, cosine), both(-sine, sine)


class Chain:
    def __init__(self):
        self.last = ()
        self.ended = ()

    def close(self, *arrays):
        self.ended += arrays

    def __call__(self, *args, after=(), **kwargs):
        out = call(*args, after=(*self.last, *self.ended, *after), **kwargs)
        self.last, self.ended = (out[0],), ()
        return out


def pair_swap(to_x, to_y):
    return swap(to_x, 1, 4), swap(to_y, 2, 4)


def plane_attn_fwd_kernel(
    info_ref, x_ref, w_ref, cos_ref, sin_ref, segc_ref, segr_ref, qkv_ref, ol_ref, lse_ref, bias_ref, *, tile
):
    length = x_ref.shape[0]

    @pl.when(pl.program_id(0) == 0)
    def _():
        fill_bias(info_ref, segc_ref, segr_ref, bias_ref, tile)

    for step in range(length // (2 * tile)):
        rows = pl.ds(step * 2 * tile, 2 * tile)
        proj = mm(x_ref[rows, :], w_ref[...])
        cosine, sine = cos_ref[rows, :], sin_ref[rows, :]
        for part in range(proj.shape[1] // HEAD_DIM):
            low = part * HEAD_DIM
            piece = proj[:, low : low + HEAD_DIM]
            if part % 3 < 2:
                piece = piece * cosine + pltpu.roll(piece, HEAD_DIM // 2, 1) * sine
            qkv_ref[rows, low : low + HEAD_DIM] = piece.astype(BF)

    heads = qkv_ref.shape[1] // (3 * HEAD_DIM)
    units = [(h, t) for h in range(heads) for t in range(length // tile)]
    keys, values_t = {}, {}

    def scores_of(unit):
        h, t = unit
        base = 3 * HEAD_DIM * h
        if h not in keys:
            keys[h] = qkv_ref[:, base + HEAD_DIM : base + 2 * HEAD_DIM]
            values_t[h] = qkv_ref[:, base + 2 * HEAD_DIM : base + 3 * HEAD_DIM].astype(F32).T.astype(BF)
        return mm_nt(keys[h], qkv_ref[t * tile : (t + 1) * tile, base : base + HEAD_DIM])

    later = scores_of(units[0])
    for k, (h, t) in enumerate(units):
        raw = later
        if k + 1 < len(units):
            later = scores_of(units[k + 1])
        rows = pl.ds(t * tile, tile)
        scores = raw * score_scale + bias_ref[:, rows]
        top = jnp.max(scores, axis=0, keepdims=True)
        exponent = jnp.exp(scores - top)
        total = jnp.sum(exponent, axis=0, keepdims=True)
        attended = mm(values_t[h], exponent.astype(BF)) * (1.0 / total)
        ol_ref[rows, h * HEAD_DIM : (h + 1) * HEAD_DIM] = attended.T.astype(BF)
        lse_ref[h, :, rows] = top + jnp.log(total)


def plane_attn_fwd(chain, info, row, tokens, qkv_weight, cosine, sine, segc, segr, after=()):
    _, length, width = tokens.shape
    heads = qkv_weight.shape[1] // (3 * HEAD_DIM)
    return chain(
        functools.partial(plane_attn_fwd_kernel, tile=256),
        "attn_fwd",
        (heads // 2,),
        (tokens, qkv_weight, cosine, sine, segc, segr),
        [
            pl.BlockSpec((None, length, width), lambda h, *_: (row, 0, 0), pipeline_mode=pl.Buffered(1)),
            spec((width, 768), lambda h, *_: (0, h)),
            const_spec((length, HEAD_DIM)),
            const_spec((length, HEAD_DIM)),
            const_spec((length, 1)),
            const_spec((1, length)),
        ],
        [((length, heads * 384), BF), ((length, heads * 128), BF), ((heads, 1, length), F32)],
        [
            spec((length, 768), lambda h, *_: (0, h)),
            spec((length, 256), lambda h, *_: (0, h)),
            spec((2, 1, length), lambda h, *_: (h, 0, 0)),
        ],
        scalars=(info,),
        after=after,
        scratch=[pltpu.VMEM((length, length), F32)],
        flops=heads * (2 * length * width * 384 + 8 * length * length * 128),
        nbytes=2 * length * width + 2 * width * heads * 384 + 8 * length * heads * 128,
    )


def plane_attn_bwd_kernel(
    info_ref, qkv_ref, own, r1, r2, r3a, r3b, ow_ref, lse_ref, cos_ref, sin_ref, segc_ref, segr_ref, dqkv_ref,
    bias_ref, dol_nat, *, tile
):
    length = qkv_ref.shape[0]
    block = own.shape[0]
    half = block // 2
    me = info_ref[0]

    @pl.when(pl.program_id(0) == 0)
    def _():
        fill_bias(info_ref, segc_ref, segr_ref, bias_ref, tile)

    def natural(r, lower):
        return pl.multiple_of((me ^ r) * block + lower, half)

    for r, piece in enumerate((own, r1, r2)):
        dol_nat[pl.ds(natural(r, 0), block), :] = mm_nt(piece[...], ow_ref[...]).astype(BF)
    for lower, piece in ((0, r3a), (half, r3b)):
        dol_nat[pl.ds(natural(3, lower), half), :] = mm_nt(piece[...], ow_ref[...]).astype(BF)

    heads = qkv_ref.shape[1] // (3 * HEAD_DIM)
    count = length // tile
    units = [(h, t) for h in range(heads) for t in range(count)]
    keys, values, keys_t = {}, {}, {}

    def products_of(unit):
        h, t = unit
        base = 3 * HEAD_DIM * h
        if h not in keys:
            keys[h] = qkv_ref[:, base + HEAD_DIM : base + 2 * HEAD_DIM]
            values[h] = qkv_ref[:, base + 2 * HEAD_DIM : base + 3 * HEAD_DIM]
            keys_t[h] = keys[h].astype(F32).T.astype(BF)
        rows = pl.ds(t * tile, tile)
        queries = qkv_ref[rows, base : base + HEAD_DIM]
        dol = dol_nat[rows, h * HEAD_DIM : (h + 1) * HEAD_DIM]
        return queries, dol, mm_nt(keys[h], queries), mm_nt(values[h], dol)

    dk = dv = None
    later = products_of(units[0])
    for k, (h, t) in enumerate(units):
        queries, dol, raw, dp = later
        if k + 1 < len(units):
            later = products_of(units[k + 1])
        base = 3 * HEAD_DIM * h
        rows = pl.ds(t * tile, tile)
        probs = jnp.exp(raw * score_scale + bias_ref[:, rows] - lse_ref[h, :, rows])
        weighted = probs * dp
        inner = jnp.sum(weighted, axis=0, keepdims=True)
        draw = ((weighted - probs * inner) * score_scale).astype(BF)
        dv_part, dk_part = mm(probs.astype(BF), dol), mm(draw, queries)
        dv = dv_part if t == 0 else dv + dv_part
        dk = dk_part if t == 0 else dk + dk_part
        dq = mm(keys_t[h], draw).T
        turned = dq * cos_ref[rows, :] - pltpu.roll(dq, HEAD_DIM // 2, 1) * sin_ref[rows, :]
        dqkv_ref[rows, base : base + HEAD_DIM] = turned.astype(BF)
        if t == count - 1:
            turned = dk * cos_ref[...] - pltpu.roll(dk, HEAD_DIM // 2, 1) * sin_ref[...]
            dqkv_ref[:, base + HEAD_DIM : base + 2 * HEAD_DIM] = turned.astype(BF)
            dqkv_ref[:, base + 2 * HEAD_DIM : base + 3 * HEAD_DIM] = dv.astype(BF)


def plane_attn_bwd(chain, info, qkv, pieces, out_weight, lse, cosine, sine, segc, segr, after=()):
    length = qkv.shape[0]
    heads = qkv.shape[1] // 384
    width = out_weight.shape[1]
    return chain(
        functools.partial(plane_attn_bwd_kernel, tile=256),
        "attn_bwd",
        (heads // 2,),
        (qkv, *pieces, out_weight, lse, cosine, sine, segc, segr),
        [spec((length, 768), lambda h, *_: (0, h))]
        + [const_spec(p.shape) for p in pieces]
        + [
            spec((256, width), lambda h, *_: (h, 0)),
            spec((2, 1, length), lambda h, *_: (h, 0, 0)),
            const_spec((length, HEAD_DIM)),
            const_spec((length, HEAD_DIM)),
            const_spec((length, 1)),
            const_spec((1, length)),
        ],
        [(qkv.shape, BF)],
        [spec((length, 768), lambda h, *_: (0, h))],
        scalars=(info,),
        after=after,
        scratch=[pltpu.VMEM((length, length), F32), pltpu.VMEM((length, 256), BF)],
        flops=heads * 24 * length * length * 128,
        nbytes=16 * length * heads * 128,
    )[0]


def plane_out_norm_kernel(
    info_ref, order_ref, *refs
):
    lows, highs = refs[:5], refs[5:10]
    ow_ref, mine_ref, other_ref = refs[10:13]
    xl_ref, xh_ref, gain_ref, bias_ref, hl_ref, n1_ref, rstd_ref, total_ref = refs[13:]
    half = xl_ref.shape[0]
    at = pl.program_id(0)

    def blocks(group, place):
        diagonal = jnp.where(place < 4, group[3][...].astype(F32), group[4][...].astype(F32)).astype(BF)
        return [ref[...] for ref in group[:3]] + [diagonal]

    feat = mine_ref.shape[0] // 3
    total_ref[:half] = xl_ref[...].astype(F32) * deep_alpha
    total_ref[half:] = xh_ref[...].astype(F32) * deep_alpha
    low, high = blocks(lows, order_ref[2 * at]), blocks(highs, order_ref[2 * at + 1])
    ols = [jnp.concatenate([lo, hi], axis=0) for lo, hi in zip(low, high)]

    def add(first, second):
        total = mm(ols[0], ow_ref[...])
        for r in range(1, 4):
            rows = pl.ds((r - 1) * feat, feat)
            total += mm(ols[r][:, :feat], first[rows, :])
            total += mm(ols[r][:, feat:], second[rows, :])
        total_ref[...] += total

    @pl.when(info_ref[3] == 0)
    def _():
        add(mine_ref, other_ref)

    @pl.when(info_ref[3] != 0)
    def _():
        add(other_ref, mine_ref)

    total = total_ref[...]
    centered = total - jnp.mean(total, axis=1, keepdims=True)
    variance = jnp.mean(centered * centered, axis=1, keepdims=True)
    inv = lax.rsqrt(variance + norm_eps)
    normed = centered * inv
    hl_ref[...] = (normed * gain_ref[...] + bias_ref[...]).astype(BF)

    @pl.when(pl.program_id(0) == 3)
    def _():
        n1_ref[...] = normed
        rstd_ref[...] = jnp.broadcast_to(inv, rstd_ref.shape)


def plane_out_norm(chain, info, order, row, ol_pieces, out_weight, mine, other, tokens, gain, bias, after=()):
    _, length, width = tokens.shape
    block = length // 4
    half = block // 2
    head_width = out_weight.shape[0]
    low = lambda i, info, order: (order[2 * i], 0)
    high = lambda i, info, order: (order[2 * i + 1], 0)

    def ol_specs(index):
        upper = lambda i, info, order: (jnp.minimum(index(i, info, order)[0], 3), 0)
        lower = lambda i, info, order: (jnp.maximum(index(i, info, order)[0] - 4, 0), 0)
        return [spec((half, head_width), f) for f in (index, index, index, upper, lower)]

    low3 = lambda i, info, order: (row, order[2 * i], 0)
    high3 = lambda i, info, order: (row, order[2 * i + 1], 0)
    return chain(
        plane_out_norm_kernel,
        "out_norm",
        (4,),
        (*ol_pieces, *ol_pieces, out_weight, mine, other, tokens, tokens, gain, bias),
        ol_specs(low)
        + ol_specs(high)
        + [const_spec(out_weight.shape), const_spec(mine.shape), const_spec(other.shape)]
        + [
            spec((None, half, width), low3),
            spec((None, half, width), high3),
            const_spec((1, width)),
            const_spec((1, width)),
        ],
        [((length, width), BF), ((block, width), F32), ((block, HEAD_DIM), F32)],
        [
            spec((block, width), lambda i, *_: (i, 0)),
            spec((block, width), lambda i, *_: (0, 0)),
            spec((block, HEAD_DIM), lambda i, *_: (0, 0)),
        ],
        scalars=(info, order),
        after=after,
        scratch=[pltpu.VMEM((block, width), F32)],
        flops=2 * length * width * width,
        nbytes=2 * width * width + 6 * length * width,
    )


def split_kernel(x_ref, y_ref, *refs):
    count = len(refs) // 2 - 1
    refs[count][...] = x_ref[...]
    refs[count + 1][...] = y_ref[...]


def forward(chain, from_x, from_y, carry=(), after=()):
    rows, width = from_x.shape
    shape = (rows // 2, width)
    any_spec = pl.BlockSpec(memory_space=ANY)
    out = chain(
        split_kernel, "split", (1,), (from_x, from_y, *carry),
        [
            pl.BlockSpec(shape, lambda i, *_: (0, 0), pipeline_mode=pl.Buffered(1)),
            pl.BlockSpec(shape, lambda i, *_: (1, 0), pipeline_mode=pl.Buffered(1)),
        ]
        + [any_spec] * len(carry),
        [(shape, BF)] * 2 + [(c.shape, c.dtype) for c in carry],
        [spec(shape, lambda i, *_: (0, 0))] * 2 + [any_spec] * len(carry),
        after=after,
        aliases={2 + k: 2 + k for k in range(len(carry))},
        nbytes=4 * rows * width,
    )
    pair = (swap(out[0], 2, 4), swap(out[1], 1, 4))
    return (pair, *out[2:]) if carry else pair


def ow_join_kernel(x_ref, y_ref, a_ref, b_ref, out_ref):
    rows = x_ref.shape[0]
    out_ref[:rows] = x_ref[...]
    out_ref[rows : 2 * rows] = y_ref[...]
    out_ref[2 * rows : 2 * rows + rows // 2] = a_ref[...]
    out_ref[2 * rows + rows // 2 :] = b_ref[...]


def ow_join(chain, pieces, after=()):
    rows, width = pieces[0].shape
    shape = (3 * rows, width)
    return chain(
        ow_join_kernel, "ow_join", (1,), pieces, [const_spec(p.shape) for p in pieces],
        [(shape, BF)], [spec(shape, lambda i, *_: (0, 0))], after=after,
    )[0]


def relay_kernel(*refs):
    refs[len(refs) // 2][...] = refs[0][...]


def relay(chain, carry, after=()):
    small = jnp.zeros((8, 128), F32)
    any_spec = pl.BlockSpec(memory_space=ANY)
    count = len(carry)
    out = chain(
        relay_kernel, "relay", (1,), (small, *carry), [const_spec(small.shape)] + [any_spec] * count,
        [(small.shape, F32)] + [(c.shape, c.dtype) for c in carry],
        [spec(small.shape, lambda i, *_: (0, 0))] + [any_spec] * count,
        after=after, aliases={1 + k: 1 + k for k in range(count)},
    )
    return out[1:]


def load_once(pairs, sem):
    copies = [pltpu.make_async_copy(src, dst, sem.at[k]) for k, (src, dst) in enumerate(pairs)]

    @pl.when(pl.program_id(0) == 0)
    def _():
        for copy in copies:
            copy.start()

    def wait(k):
        @pl.when(pl.program_id(0) == 0)
        def _():
            copies[k].wait()

    return wait


def store_half(first, part, refs):
    at = pl.program_id(0)
    half = part.shape[0] // 2
    if first is None:

        @pl.when(at == 0)
        def _():
            refs[0][...] = part

        @pl.when(at == 1)
        def _():
            refs[1][...] = part

        @pl.when(at == 2)
        def _():
            refs[2][...] = part[:half]
            refs[3][...] = part[half:]

        @pl.when(at == 3)
        def _():
            refs[4][...] = part

        return

    @pl.when(at == 0)
    def _():
        if first:
            refs[0][...] = part
        else:
            refs[0][...] = part[:half]
            refs[1][...] = part[half:]

    @pl.when(at == 1)
    def _():
        refs[-1][...] = part


def half_outs(first, block, width):
    if first is None:
        sizes = [block, block, block // 2, block // 2, block]
    else:
        sizes = [block, block] if first else [block // 2, block // 2, block]
    return [((s, width), BF) for s in sizes], [spec((s, width), lambda i, *_: (0, 0)) for s in sizes]


def plane_ffn_fwd_kernel(hl_ref, wg_hbm, wu_hbm, wd_hbm, *refs, first):
    refs, (wg, wu, wd, sem) = refs[:-4], refs[-4:]
    (al_ref, ga_ref, gb_ref), refs = refs[-3:], refs[:-3]
    wait = load_once(((wg_hbm, wg), (wu_hbm, wu), (wd_hbm, wd)), sem)
    hidden = hl_ref[...]
    wait(0)
    gate = mm(hidden, wg[...])
    wait(1)
    up = mm(hidden, wu[...])
    cdf = 0.5 + 0.5 * lax.erf(gate * (1.0 / math.sqrt(2.0)))
    pdf = jnp.exp(gate * gate * -0.5) * (1.0 / math.sqrt(2.0 * math.pi))
    act = gate * cdf
    ga_ref[...] = (up * (cdf + gate * pdf)).astype(BF)
    gb_ref[...] = act.astype(BF)
    low = (act * up).astype(BF)
    al_ref[...] = low
    wait(2)
    store_half(first, mm(low, wd[...]).astype(BF), refs)


def plane_ffn_fwd(chain, first, hidden, weights, kept, after=()):
    length, width = hidden.shape
    units = weights[0].shape[1]
    block = length // 4
    base = 2 if first is False else 0
    steps = 4 if first is None else 2
    tiled = lambda w: spec((block, w), lambda i, *_: (i + base, 0))
    outs, out_specs = half_outs(first, block, width)
    n = len(outs)
    any_spec = pl.BlockSpec(memory_space=ANY)
    kept = tuple(kept)
    carried = kept[3:]
    kernel = functools.partial(plane_ffn_fwd_kernel, first=first)
    if first is not False:
        body_kernel = kernel
    else:
        nk, nc = len(kept), len(carried)

        def body_kernel(hl, wg, wu, wd, *refs):
            refs = refs[nk:]
            kernel(hl, wg, wu, wd, *refs[:n], *refs[n + nc :])

    out = chain(
        body_kernel,
        "ffn_fwd",
        (steps,),
        (hidden, *weights, *kept),
        [tiled(width)] + [any_spec] * (3 + len(kept)),
        outs + [(c.shape, BF) for c in carried] + [((length, units), BF)] * 3,
        out_specs + [any_spec] * len(carried) + [tiled(units)] * 3,
        after=after,
        aliases={}
        if first is not False
        else {
            **{4 + k: n + len(carried) + k for k in range(3)},
            **{7 + k: n + k for k in range(len(carried))},
        },
        scratch=[
            pltpu.VMEM(weights[0].shape, BF),
            pltpu.VMEM(weights[1].shape, BF),
            pltpu.VMEM(weights[2].shape, BF),
            pltpu.SemaphoreType.DMA((3,)),
        ],
        mib=60,
        flops=3 * length * width * units * steps // 2,
        nbytes=6 * units * width + 3 * length * units,
    )
    n += len(carried)
    return out[:n], out[n:]


def plane_ffn_bwd_kernel(dffn_ref, ga_ref, gb_ref, wd_hbm, wg_hbm, wu_hbm, *refs, first):
    refs, (wd, wg, wu, sem) = refs[:-4], refs[-4:]
    (dg_ref, du_ref), refs = refs[-2:], refs[:-2]
    wait = load_once(((wd_hbm, wd), (wg_hbm, wg), (wu_hbm, wu)), sem)
    grad = dffn_ref[...]
    wait(0)
    dact = mm_nt(grad, wd[...])
    dgate = (dact * ga_ref[...].astype(F32)).astype(BF)
    dup = (dact * gb_ref[...].astype(F32)).astype(BF)
    dg_ref[...] = dgate
    du_ref[...] = dup
    wait(1)
    part = mm_nt(dgate, wg[...])
    wait(2)
    part += mm_nt(dup, wu[...])
    store_half(first, part.astype(BF), refs)


def plane_ffn_bwd(chain, first, dffn, slopes, weights, kept, after=()):
    length, width = dffn.shape
    units = weights[0].shape[1]
    block = length // 4
    base = 2 if first is False else 0
    steps = 4 if first is None else 2
    tiled = lambda w: spec((block, w), lambda i, *_: (i + base, 0))
    outs, out_specs = half_outs(first, block, width)
    n = len(outs)
    any_spec = pl.BlockSpec(memory_space=ANY)
    kept = tuple(kept)
    kernel = functools.partial(plane_ffn_bwd_kernel, first=first)
    carried = kept[2:]
    if first is not False:
        body_kernel = kernel
    else:
        nk, nc = len(kept), len(carried)

        def body_kernel(d, ga, gb, wd, wg, wu, *refs):
            refs = refs[nk:]
            kernel(d, ga, gb, wd, wg, wu, *refs[:n], *refs[n + nc :])

    out = chain(
        body_kernel,
        "ffn_bwd",
        (steps,),
        (dffn, *slopes, weights[2], weights[0], weights[1], *kept),
        [tiled(width), tiled(units), tiled(units)] + [any_spec] * (3 + len(kept)),
        outs + [(c.shape, BF) for c in carried] + [((length, units), BF)] * 2,
        out_specs + [any_spec] * len(carried) + [tiled(units)] * 2,
        after=after,
        aliases={}
        if first is not False
        else {
            **{6 + k: n + len(carried) + k for k in range(2)},
            **{8 + k: n + k for k in range(len(carried))},
        },
        scratch=[
            pltpu.VMEM(weights[2].shape, BF),
            pltpu.VMEM(weights[0].shape, BF),
            pltpu.VMEM(weights[1].shape, BF),
            pltpu.SemaphoreType.DMA((3,)),
        ],
        mib=60,
        flops=3 * length * width * units * steps // 2,
        nbytes=6 * units * width + 4 * length * units,
    )
    n += len(carried)
    return out[:n], out[n:]


def middle_kernel(x1_ref, y1_ref, r1b_ref, r2a_ref, x2_ref, y2_ref):
    half = r1b_ref.shape[0]
    x2_ref[...] = (r1b_ref[...].astype(F32) + y1_ref[half:].astype(F32)).astype(BF)
    y2_ref[...] = (r2a_ref[...].astype(F32) + x1_ref[half:].astype(F32)).astype(BF)


def middle(chain, arrived, r1b, r2a, after=()):
    x1, y1 = arrived
    shape = r1b.shape
    return chain(
        middle_kernel,
        "middle_sum",
        (1,),
        (x1, y1, r1b, r2a),
        [const_spec(a.shape) for a in (x1, y1, r1b, r2a)],
        [(shape, BF)] * 2,
        [spec(shape, lambda i, *_: (0, 0))] * 2,
        after=after,
        mib=32,
        nbytes=16 * r1b.size,
    )


def own_sum(own, x1, y1, x2, y2):
    top = pl.program_id(0) < OWN_STEPS // 2
    direct = jnp.where(top, x1[...].astype(F32), y1[...].astype(F32))
    relayed = jnp.where(top, y2[...].astype(F32), x2[...].astype(F32))
    return own[...].astype(F32) + direct + relayed


def resid_two_kernel(own, x1, y1, x2, y2, n1_ref, gain_ref, bias_ref, out_ref):
    total = own_sum(own, x1, y1, x2, y2)
    out_ref[...] = (deep_alpha * (n1_ref[...] * gain_ref[...] + bias_ref[...]) + total).astype(BF)


def norm_one_back_kernel(own, x1, y1, x2, y2, dffn_ref, n1_ref, rstd_ref, gain_ref, low_ref, dr1_ref, sums_ref):
    total = own_sum(own, x1, y1, x2, y2)
    dh = deep_alpha * dffn_ref[...].astype(F32) + total
    normed = n1_ref[...]
    scaled = dh * gain_ref[...]
    inner = jnp.mean(scaled, axis=1, keepdims=True) + normed * jnp.mean(scaled * normed, axis=1, keepdims=True)
    dr1 = rstd_ref[:, :1] * (scaled - inner)
    dr1_ref[...] = dr1
    low_ref[...] = dr1.astype(BF)
    gain_sum = jnp.sum(dh * normed, axis=0, keepdims=True)
    bias_sum = jnp.sum(dh, axis=0, keepdims=True)

    @pl.when(pl.program_id(0) == 0)
    def _():
        sums_ref[0:1, :] = gain_sum
        sums_ref[1:2, :] = bias_sum

    @pl.when(pl.program_id(0) > 0)
    def _():
        sums_ref[0:1, :] += gain_sum
        sums_ref[1:2, :] += bias_sum


def input_grad_kernel(own, x1, y1, x2, y2, dr1_ref, out_ref):
    out_ref[...] = (deep_alpha * dr1_ref[...] + own_sum(own, x1, y1, x2, y2)).astype(BF)


OWN_STEPS = 4


def rows_spec(array_shape, tile, base=0):
    return spec((tile, array_shape[1]), lambda i, *_: (i + base, 0))


def own_step(chain, kernel, name, sums, extra, extra_specs, outs, after=()):
    block, width = sums[0].shape
    tile = block // OWN_STEPS
    middle_step = OWN_STEPS // 2
    first = spec((tile, width), lambda i, *_: (jnp.minimum(i, middle_step - 1), 0))
    later = spec((tile, width), lambda i, *_: (jnp.maximum(i - middle_step, 0), 0))
    return chain(
        kernel,
        name,
        (OWN_STEPS,),
        (*sums, *extra),
        [rows_spec((block, width), tile), first, later, later, first] + extra_specs,
        outs,
        [rows_spec(s, tile) if s[0] == block else spec(s, lambda i, *_: (0, 0)) for s, _ in outs],
        after=after,
        mib=40,
        nbytes=16 * block * width,
    )


def plane_norm_two_kernel(info_ref, order_ref, share_ref, own, r1, r2, r3a, r3b, cot_ref, gain_ref, bias_ref, *refs):
    act_ref, sums_ref, dffn_ref, held = refs[-4:]
    at = pl.program_id(0)
    half = held.shape[0]
    places = (
        (r1, 0), (r3a, 0), (r2, half), (r3b, 0), (r1, half), (r2, 0), (own, 0), (own, half),
    )
    for k, (ref, start) in enumerate(places):

        @pl.when(at == k)
        def _(ref=ref, start=start):
            held[...] = ref[start : start + half]

    resid = held[...].astype(F32)
    centered = resid - jnp.mean(resid, axis=1, keepdims=True)
    variance = jnp.mean(centered * centered, axis=1, keepdims=True)
    inv = lax.rsqrt(variance + norm_eps)
    normed = centered * inv
    gain = gain_ref[...]
    act_ref[...] = (normed * gain + bias_ref[...]).astype(BF)
    dout = cot_ref[...].astype(F32) * share_ref[0]
    scaled = dout * gain
    inner = jnp.mean(scaled, axis=1, keepdims=True) + normed * jnp.mean(scaled * normed, axis=1, keepdims=True)
    dffn_ref[...] = (inv * (scaled - inner)).astype(BF)
    gain_sum = jnp.sum(dout * normed, axis=0, keepdims=True)
    bias_sum = jnp.sum(dout, axis=0, keepdims=True)

    @pl.when(at == 0)
    def _():
        sums_ref[0:1, :] = gain_sum
        sums_ref[1:2, :] = bias_sum

    @pl.when(at > 0)
    def _():
        sums_ref[0:1, :] += gain_sum
        sums_ref[1:2, :] += bias_sum


def plane_norm_two(chain, info, order, share, row, pieces, cotangent, gain, bias, before, after=()):
    rows, length, width = cotangent.shape
    half = length // 8
    natural = spec((None, half, width), lambda i, info, order, share: (row, order[i], 0))
    held = () if before is None else (before,)
    return chain(
        plane_norm_two_kernel,
        "norm_two",
        (8,),
        (*pieces, cotangent, gain, bias, *held),
        [const_spec(p.shape) for p in pieces]
        + [natural, const_spec((1, width)), const_spec((1, width))]
        + [pl.BlockSpec(memory_space=ANY)] * len(held),
        [(cotangent.shape, BF), ((2, width), F32), ((length, width), BF)],
        [natural, spec((2, width), lambda i, *_: (0, 0)), spec((half, width), lambda i, *_: (i, 0))],
        scalars=(info, order, share),
        after=after,
        aliases={len(pieces) + 3: 0} if held else {},
        scratch=[pltpu.VMEM((half, width), BF)],
        flops=20 * length * width,
        nbytes=8 * length * width,
    )


def plane_input_back_kernel(order_ref, low_ref, high_ref, w_ref, x1_ref, y1_ref, r1b_ref, r2a_ref, own_ref):
    at = pl.program_id(0)
    half = low_ref.shape[0]
    part = mm_nt(jnp.concatenate([low_ref[...], high_ref[...]], axis=0), w_ref[...]).astype(BF)

    @pl.when(at == 0)
    def _():
        x1_ref[...] = part

    @pl.when(at == 1)
    def _():
        y1_ref[...] = part

    @pl.when(at == 2)
    def _():
        r1b_ref[...] = part[:half]
        r2a_ref[...] = part[half:]

    @pl.when(at == 3)
    def _():
        own_ref[...] = part


def plane_input_back(chain, order, dqkv, qkv_weight, after=()):
    length, columns = dqkv.shape
    width = qkv_weight.shape[0]
    block = length // 4
    half = block // 2
    sizes = [block, block, half, half, block]
    return chain(
        plane_input_back_kernel,
        "input_back",
        (4,),
        (dqkv, dqkv, qkv_weight),
        [
            spec((half, columns), lambda i, order: (order[2 * i], 0)),
            spec((half, columns), lambda i, order: (order[2 * i + 1], 0)),
            const_spec(qkv_weight.shape),
        ],
        [((s, width), BF) for s in sizes],
        [spec((s, width), lambda i, *_: (0, 0)) for s in sizes],
        scalars=(order,),
        after=after,
        flops=2 * length * width * columns,
        nbytes=2 * width * columns + 4 * length * width,
    )


def plane_place_kernel(order_ref, own, r1, r2, r3a, r3b, *refs):
    out_ref = refs[-1]
    at = pl.program_id(0)
    half = r3a.shape[0]
    for k, ref in enumerate((own, r1, r2)):

        @pl.when(at == k)
        def _(ref=ref):
            out_ref[...] = ref[...]

    @pl.when(at == 3)
    def _():
        out_ref[:half] = r3a[...]
        out_ref[half:] = r3b[...]


def plane_place(chain, info, row, pieces, shape, before, after=()):
    rows, length, width = shape
    block = length // 4
    held = () if before is None else (before,)
    return chain(
        plane_place_kernel,
        "place",
        (4,),
        (*pieces, *held),
        [const_spec(p.shape) for p in pieces] + [pl.BlockSpec(memory_space=ANY)] * len(held),
        [(shape, BF)],
        [spec((None, block, width), lambda i, info: (row, i ^ info[0], 0))],
        scalars=(info,),
        after=after,
        aliases={len(pieces): 0} if held else {},
        mib=32,
        nbytes=4 * length * width,
    )[0]


def panels(ref, value):
    for c in range(value.shape[1] // 128):
        ref[c] = value[:, c * 128 : (c + 1) * 128].astype(BF)


def grad_rows_kernel(info_ref, left_a, left_b, right_a, right_b, send, keep, *, steps):
    at = pl.program_id(0)
    value = mm(left_a[...].T, right_a[...]) + mm(left_b[...].T, right_b[...])

    @pl.when(at < steps)
    def _():
        panels(send, value)

    @pl.when(at >= steps)
    def _():
        panels(keep, value)


def lhs_spec(lhs, tile, index, row):
    if lhs.ndim == 3:
        return spec((None, lhs.shape[1], tile), lambda *a: (row, 0, index(*a)))
    return spec((lhs.shape[0], tile), lambda *a: (0, index(*a)))


def grad_rows(chain, info, lefts, rights, after=()):
    rows = lefts[0].shape[-1]
    tile = 256
    steps = rows // tile // 2
    length, columns = rights[0].shape

    def at(i, info):
        other = (1 - info[3]) * steps + i
        own = info[3] * steps + i - steps
        return jnp.where(i < steps, other, own)

    shape = (columns // 128, rows // 2, 128)
    out = chain(
        functools.partial(grad_rows_kernel, steps=steps),
        "grad_rows",
        (2 * steps,),
        (*lefts, *rights),
        [lhs_spec(lefts[r], tile, at, r) for r in range(2)] + [const_spec(r.shape) for r in rights],
        [(shape, BF)] * 2,
        [
            spec((shape[0], tile, 128), lambda i, *_: (0, jnp.minimum(i, steps - 1), 0)),
            spec((shape[0], tile, 128), lambda i, *_: (0, jnp.maximum(i - steps, 0), 0)),
        ],
        scalars=(info,),
        after=after,
        flops=4 * rows * length * columns,
        nbytes=2 * rows * columns + 4 * rows * length,
    )
    return out[0].reshape(-1, 128), out[1].reshape(-1, 128)


def grad_columns_kernel(info_ref, left_a, left_b, right_a, right_b, send, keep, turned_a, turned_b, held):
    @pl.when(pl.program_id(0) == 0)
    def _():
        turned_a[...] = left_a[...].T
        turned_b[...] = left_b[...].T

    held[...] = mm(turned_a[...], right_a[...]) + mm(turned_b[...], right_b[...])
    half = held.shape[0] // 2
    core = info_ref[3]
    panels(send, held[pl.ds(pl.multiple_of((1 - core) * half, 8), half), :])
    panels(keep, held[pl.ds(pl.multiple_of(core * half, 8), half), :])


def grad_columns(chain, info, lefts, rights, after=()):
    length, rows = lefts[0].shape
    columns = rights[0].shape[1]
    tile = 256
    shape = (columns // 128, rows // 2, 128)
    out = chain(
        grad_columns_kernel,
        "grad_columns",
        (columns // tile,),
        (*lefts, *rights),
        [const_spec(left.shape) for left in lefts] + [spec((length, tile), lambda i, *_: (0, i))] * 2,
        [(shape, BF)] * 2,
        [spec((tile // 128, rows // 2, 128), lambda i, *_: (i, 0, 0))] * 2,
        scalars=(info,),
        after=after,
        scratch=[pltpu.VMEM((rows, length), BF)] * 2 + [pltpu.VMEM((rows, tile), F32)],
        flops=4 * rows * length * columns,
        nbytes=2 * rows * columns + 4 * length * (rows + columns),
    )
    return out[0].reshape(-1, 128), out[1].reshape(-1, 128)


def grad_plain_kernel(left_a, left_b, right_a, right_b, out_ref):
    out_ref[...] = (mm(left_a[...].T, right_a[...]) + mm(left_b[...].T, right_b[...])).astype(BF)


def grad_plain(chain, lefts, rights, after=()):
    rows = lefts[0].shape[-1]
    tile = 256
    length, columns = rights[0].shape
    return chain(
        grad_plain_kernel,
        "grad_plain",
        (rows // tile,),
        (*lefts, *rights),
        [lhs_spec(lefts[r], tile, lambda i, *_: i, r) for r in range(2)] + [const_spec(r.shape) for r in rights],
        [((rows, columns), BF)],
        [spec((tile, columns), lambda i, *_: (i, 0))],
        after=after,
        flops=4 * rows * length * columns,
        nbytes=2 * rows * columns + 4 * rows * length,
    )[0]


def grad_plain_columns_kernel(left_a, left_b, right_a, right_b, out_ref, turned_a, turned_b):
    @pl.when(pl.program_id(0) == 0)
    def _():
        turned_a[...] = left_a[...].T
        turned_b[...] = left_b[...].T

    out_ref[...] = (mm(turned_a[...], right_a[...]) + mm(turned_b[...], right_b[...])).astype(BF)


def grad_plain_columns(chain, lefts, rights, after=()):
    length, rows = lefts[0].shape
    columns = rights[0].shape[1]
    tile = 256
    return chain(
        grad_plain_columns_kernel,
        "grad_plain_columns",
        (columns // tile,),
        (*lefts, *rights),
        [const_spec(left.shape) for left in lefts] + [spec((length, tile), lambda i, *_: (0, i))] * 2,
        [((rows, columns), BF)],
        [spec((rows, tile), lambda i, *_: (0, i))],
        after=after,
        scratch=[pltpu.VMEM((rows, length), BF)] * 2,
        flops=4 * rows * length * columns,
        nbytes=2 * rows * columns + 4 * length * (rows + columns),
    )[0]


def grad_out(lhs, pieces, me):
    block = pieces[0].shape[0]
    half = block // 2
    total = 0.0
    for r, piece in enumerate(pieces[:3]):
        part = lhs[pl.ds(pl.multiple_of((me ^ r) * block, half), block), :]
        total = total + mm(part.T, piece[...])
    for lower, piece in ((0, pieces[3]), (half, pieces[4])):
        part = lhs[pl.ds(pl.multiple_of((me ^ 3) * block + lower, half), half), :]
        total = total + mm(part.T, piece[...])
    return total


def grad_out_kernel(info_ref, left_a, left_b, *refs):
    pieces_a, pieces_b, (send, keep, held) = refs[:5], refs[5:10], refs[10:]
    held[...] = grad_out(left_a, pieces_a, info_ref[0]) + grad_out(left_b, pieces_b, info_ref[0])
    half = held.shape[0] // 2
    core = info_ref[3]
    panels(send, held[pl.ds(pl.multiple_of((1 - core) * half, 8), half), :])
    panels(keep, held[pl.ds(pl.multiple_of(core * half, 8), half), :])


def plane_grad_out(chain, info, lefts, pieces, after=()):
    length, rows = lefts[0].shape
    columns = pieces[0][0].shape[1]
    tile = 512
    shape = (columns // 128, rows // 2, 128)
    every = (*pieces[0], *pieces[1])
    out = chain(
        grad_out_kernel,
        "grad_out",
        (columns // tile,),
        (*lefts, *every),
        [const_spec(left.shape) for left in lefts]
        + [spec((p.shape[0], tile), lambda i, *_: (0, i)) for p in every],
        [(shape, BF)] * 2,
        [spec((tile // 128, rows // 2, 128), lambda i, *_: (i, 0, 0))] * 2,
        scalars=(info,),
        after=after,
        scratch=[pltpu.VMEM((rows, tile), F32)],
        flops=4 * rows * length * columns,
        nbytes=2 * rows * columns + 4 * length * (rows + columns),
    )
    return out[0].reshape(-1, 128), out[1].reshape(-1, 128)


class Line:
    GRID = 4

    def __init__(self, chain, edge):
        self.chain, self.edge = chain, edge
        self.pending = []
        self.slots = []
        self.step = 0
        self.done = {}
        self.first = self.second = None
        self.sent = self.mid = None

    def add(self, name, keep, got, chunks):
        for k in range(chunks):
            self.pending.append((name, keep, got, k, keep.shape[0] // chunks, keep.shape[0]))

    def get(self, j):
        return self.slots[j] if j >= 0 else None

    def busy(self):
        return bool(self.pending) or any(self.slots[-3:])

    def complete(self, name):
        return not any(slot and slot[0] == name for slot in self.pending + self.slots[-3:])

    def advance(self, after=()):
        j = self.step
        self.slots.append(self.pending.pop(0) if self.pending else None)
        new, cur, prev, last = self.get(j), self.get(j - 1), self.get(j - 2), self.get(j - 3)
        ins, in_specs, outs, out_specs, aliases, roles = [], [], [], [], {}, []
        grid = self.GRID

        def give(array, rows, base, role, when):
            block = rows // grid
            if when is None:
                index = lambda i, edge: (base + i, 0)
            elif when:
                index = lambda i, edge: (base + i * edge[0], 0)
            else:
                index = lambda i, edge: (base + i * (1 - edge[0]), 0)
            ins.append(array)
            in_specs.append(spec((block, 128), index))
            roles.append(role)

        if new:
            name, keep, got, k, rows, _ = new
            give(keep, rows, k * grid, "new_keep", True)
            give(got, rows, k * grid, "new_got", True)
        if cur:
            name, keep, got, k, rows, _ = cur
            give(keep, rows, k * grid, "cur_keep", False)
            give(got, rows, k * grid, "cur_got", False)
            give(self.first, rows, 0, "cur_in", False)
        if prev:
            rows = prev[4]
            give(self.mid, rows, 0, "prev_mid", False)
            give(self.second, rows, 0, "prev_in", False)
        if last:
            rows = last[4]
            give(self.first, rows, 0, "last_in", True)
            give(self.sent, rows, 0, "last_sent", False)
            if last[3] > 0:
                ins.append(self.done[last[0]])
                in_specs.append(pl.BlockSpec(memory_space=ANY))
                roles.append("held")
        names = []
        if new or prev:
            rows = max(c[4] for c in (new, prev) if c)
            outs.append(((rows, 128), BF))
            out_specs.append(pl.BlockSpec((rows, 128), lambda i, *_: (0, 0)))
            names.append("sent")
        if cur:
            outs.append(((cur[4], 128), BF))
            out_specs.append(spec((cur[4] // grid, 128), lambda i, *_: (i, 0)))
            names.append("mid")
        if last:
            base = last[3] * grid
            outs.append(((last[5], 128), BF))
            out_specs.append(spec((last[4] // grid, 128), lambda i, *_, base=base: (base + i, 0)))
            names.append("done")
            if last[3] > 0:
                aliases = {len(ins) - 1: len(outs) - 1}

        def kernel(edge_ref, *refs):
            src = dict(zip(roles, refs[: len(roles)]))
            dst = dict(zip(names, refs[len(roles) :]))
            at = pl.program_id(0)
            is_edge = edge_ref[0] == 1
            f32 = lambda r: src[r][...].astype(F32)

            if new:
                @pl.when(is_edge)
                def _():
                    block = new[4] // grid
                    rows = pl.ds(pl.multiple_of(at * block, block), block)
                    dst["sent"][rows, :] = (f32("new_keep") + f32("new_got")).astype(BF)

            @pl.when(jnp.logical_not(is_edge))
            def _():
                if cur:
                    dst["mid"][...] = (f32("cur_keep") + f32("cur_got") + f32("cur_in")).astype(BF)
                if prev:
                    block = prev[4] // grid
                    rows = pl.ds(pl.multiple_of(at * block, block), block)
                    dst["sent"][rows, :] = (f32("prev_mid") + f32("prev_in")).astype(BF)

            if last:
                @pl.when(is_edge)
                def _():
                    dst["done"][...] = src["last_in"][...]

                @pl.when(jnp.logical_not(is_edge))
                def _():
                    dst["done"][...] = src["last_sent"][...]

        out = self.chain(
            kernel,
            "line_step",
            (grid,),
            tuple(ins),
            in_specs,
            outs,
            out_specs,
            scalars=(self.edge,),
            after=after,
            aliases=aliases,
            mib=32,
            nbytes=6 * 5632 * 256,
        )
        got = dict(zip(names, out))
        if "done" in got:
            self.done[last[0]] = got["done"]
        self.sent = got.get("sent")
        self.mid = got.get("mid")
        if self.sent is not None:
            self.first = lax.ppermute(self.sent, "obj", [(0, 1), (3, 2), (1, 0), (2, 3)])
        if self.mid is not None:
            self.second = lax.ppermute(self.mid, "obj", [(1, 2), (2, 1)])
        self.step += 1


def widen_kernel(info_ref, mine_ref, theirs_ref, out_ref, *, steps):
    at = pl.program_id(0)

    @pl.when(at < steps)
    def _():
        for c in range(mine_ref.shape[0]):
            out_ref[:, c * 128 : (c + 1) * 128] = mine_ref[c].astype(F32)

    @pl.when(at >= steps)
    def _():
        for c in range(theirs_ref.shape[0]):
            out_ref[:, c * 128 : (c + 1) * 128] = theirs_ref[c].astype(F32)


def widen(chain, info, mine, theirs, rows, columns, after=()):
    count = columns // 128
    half = rows // 2
    tile = 176 if half % 176 == 0 else min(256, half)
    steps = half // tile
    mine, theirs = (a.reshape(count, half, 128) for a in (mine, theirs))

    def at(i, info):
        return jnp.where(i < steps, info[3] * steps + i, (1 - info[3]) * steps + i - steps)

    return chain(
        functools.partial(widen_kernel, steps=steps),
        "widen",
        (2 * steps,),
        (mine, theirs),
        [
            spec((count, tile, 128), lambda i, *_: (0, jnp.minimum(i, steps - 1), 0)),
            spec((count, tile, 128), lambda i, *_: (0, jnp.maximum(i - steps, 0), 0)),
        ],
        [((rows, columns), F32)],
        [spec((tile, columns), lambda i, info: (at(i, info), 0))],
        scalars=(info,),
        after=after,
        mib=32,
        nbytes=6 * rows * columns,
    )[0]


def cast_kernel(in_ref, out_ref):
    out_ref[...] = in_ref[...].astype(F32)


def cast(chain, array, after=()):
    rows, columns = array.shape
    tile = 176 if rows % 256 else 256
    return chain(
        cast_kernel, "cast", (rows // tile,), (array,), [rows_spec(array.shape, tile)],
        [(array.shape, F32)], [rows_spec(array.shape, tile)], after=after,
    )[0]


def total_sum_kernel(in_ref, out_ref):
    out_ref[...] = jnp.sum(in_ref[...], axis=0)


def total_sum(chain, array):
    shape = array.shape[1:]
    return chain(
        total_sum_kernel, "total_sum", (1,), (array,), [const_spec(array.shape)], [(shape, F32)],
        [spec(shape, lambda i, *_: (0, 0))],
    )[0]


def plane_body(
    tokens,
    cotangent,
    segment_ids,
    mlm_mask,
    glm_prefix,
    glm_span,
    qkv_weight,
    out_weight,
    gate_weight,
    up_weight,
    down_weight,
    norm1_gain,
    norm1_bias,
    norm2_gain,
    norm2_bias,
):
    seq_here, length, width = tokens.shape
    data_ways = lax.axis_size("dp")
    objective_ways = lax.axis_size("obj")
    me = lax.axis_index("tensor").astype(jnp.int32)
    core = lax.axis_index("dp").astype(jnp.int32)
    at_obj = lax.axis_index("obj")
    edge = ((at_obj == 0) | (at_obj == objective_ways - 1)).astype(jnp.int32).reshape(1)
    block = length // 4
    units = gate_weight.shape[1]
    rows_all = mlm_mask.shape[0]
    masked_limit = seq_here * data_ways * (objective_ways // 2)
    row_ids = jnp.arange(rows_all, dtype=jnp.int32)
    counts = jnp.where(row_ids < masked_limit, jnp.sum(mlm_mask, axis=1), glm_span).astype(F32)
    weight_all = counts * rows_all / jnp.sum(counts)
    first_row = (at_obj * data_ways + core) * seq_here
    share_here = lax.dynamic_slice_in_dim(weight_all, first_row, seq_here)
    prefix_here = lax.dynamic_slice_in_dim(glm_prefix, first_row, seq_here)
    span_here = lax.dynamic_slice_in_dim(glm_span, first_row, seq_here)
    open_here = jnp.where(first_row < masked_limit, length, prefix_here)
    info = [jnp.stack([me, open_here[r], prefix_here[r] + span_here[r], core]) for r in range(2)]
    order = jnp.stack([2 * (me ^ r) + h for r, h in ORDER])
    share = [share_here[r : r + 1] for r in range(2)]
    cosine, sine = constant_tables(length)
    segc = [segment_ids[r].reshape(length, 1) for r in range(2)]
    segr = [segment_ids[r].reshape(1, length) for r in range(2)]
    gain1, bias1 = norm1_gain.reshape(1, width), norm1_bias.reshape(1, width)
    gain2, bias2 = norm2_gain.reshape(1, width), norm2_bias.reshape(1, width)
    weights = (gate_weight, up_weight, down_weight)
    chain = Chain()
    A, B = 0, 1

    ow_half = out_weight.shape[0] // 2
    ow_own = lax.dynamic_slice_in_dim(out_weight, core * ow_half, ow_half)
    owx, owy = pair_swap(ow_own, ow_own)

    def attention(r, after=()):
        return plane_attn_fwd(chain, info[r], r, tokens, qkv_weight, cosine, sine, segc[r], segr[r], after)

    def out_and_norm(r, ol_pieces, after=()):
        return plane_out_norm(
            chain, info[r], order, r, ol_pieces, out_weight, ow_mine, ow_other, tokens, gain1, bias1, after
        )

    qkv, ol, lse, hl, n1, rstd = {}, {}, {}, {}, {}, {}
    qkv[A], ol[A], lse[A] = attention(A)
    owra, owrb = forward(chain, owx, owy)
    olx, oly, olr = {}, {}, {}
    olx[A], oly[A] = pair_swap(ol[A], ol[A])
    qkv[B], ol[B], lse[B] = attention(B)
    ow_mine = ow_join(chain, (owx, owy, owra, owrb), after=(olx[A], oly[A]))
    ow_other = lax.ppermute(ow_mine, "dp", CORES)
    olr[A], ol[B] = forward(chain, olx[A], oly[A], (ol[B],))
    (ol[B],) = relay(chain, (ol[B],), after=olr[A])
    olx[B], oly[B] = pair_swap(ol[B], ol[B])
    hl[A], n1[A], rstd[A] = out_and_norm(A, (ol[A], olx[A], oly[A], *olr[A]))
    vec = const_spec((1, width))
    tile = block // OWN_STEPS
    full = rows_spec((block, width), tile)
    ff, fb, ib, rs1, rs2 = {}, {}, {}, {}, {}
    resid, rx, ry, rr = {}, {}, {}, {}

    def sums_of(own, first, second):
        return (own, first[0], first[1], second[0], second[1])

    def second_resid(r, after=()):
        return own_step(
            chain, resid_two_kernel, "resid_two", sums_of(ff[r][2], rs1[r], rs2[r]), (n1[r], gain1, bias1),
            [full, vec, vec], [((block, width), BF)], after,
        )[0]

    def second_norm(r, before, after=()):
        pieces = (resid[r], rx[r], ry[r], *rr[r])
        return plane_norm_two(
            chain, info[r], order, share[r], r, pieces, cotangent, gain2, bias2, before, after
        )

    def first_norm_back(r, after=()):
        return own_step(
            chain, norm_one_back_kernel, "norm_one_back", sums_of(fb[r][2], rs1[r], rs2[r]),
            (dffn[r], n1[r], rstd[r], gain1),
            [rows_spec((block, width), tile, 3 * OWN_STEPS), full, rows_spec((block, HEAD_DIM), tile), vec],
            [((block, width), BF), ((block, width), F32), ((2, width), F32)], after,
        )

    olr[B] = forward(chain, olx[B], oly[B])
    sent, kept_a = plane_ffn_fwd(chain, None, hl[A], weights, ())
    rs1[A], ff[A] = pair_swap(*sent[:2]), sent[2:]
    hl[B], n1[B], rstd[B] = out_and_norm(B, (ol[B], olx[B], oly[B], *olr[B]))
    rs2[A] = pair_swap(*middle(chain, rs1[A], ff[A][0], ff[A][1]))
    sent, kept = plane_ffn_fwd(chain, True, hl[B], weights, ())
    resid[A] = second_resid(A)
    rx[A], ry[A] = pair_swap(resid[A], resid[A])
    ff[B], kept_b = plane_ffn_fwd(chain, False, hl[B], weights, (*kept, *sent))
    al, slopes = {A: kept_a[0], B: kept_b[0]}, {A: kept_a[1:], B: kept_b[1:]}
    rr[A] = forward(chain, rx[A], ry[A])
    rs1[B] = pair_swap(*relay(chain, ff[B][3:], after=rr[A]))

    sums2, dffn, dgu, sums1, dr1, dattn, dax, day, dar = {}, {}, {}, {}, {}, {}, {}, {}, {}
    pieces, dqkv, dx, dxx, dxy, dxr, outs = {}, {}, {}, {}, {}, {}, {}

    def attention_back(r, after=()):
        pieces[r] = (dattn[r], dax[r], day[r], *dar[r])
        return plane_attn_bwd(
            chain, info[r], qkv[r], pieces[r], out_weight, lse[r], cosine, sine, segc[r], segr[r], after
        )

    def input_back_sums(r, after=()):
        x1, y1, r1b, r2a, own = plane_input_back(chain, order, dqkv[r], qkv_weight, after)
        ib[r] = (r1b, r2a, own)
        rs1[r] = pair_swap(x1, y1)

    def input_grad_own(r, after=()):
        return own_step(
            chain, input_grad_kernel, "input_grad", sums_of(ib[r][2], rs1[r], rs2[r]), (dr1[r],), [full],
            [((block, width), BF)], after,
        )[0]

    theirs = {}

    def begin_finish(name):
        theirs[name] = lax.ppermute(line.done[name], "dp", CORES)

    def finish_matrix(name, rows, columns, after=()):
        outs[name] = widen(chain, info[B], line.done[name], theirs[name], rows, columns, after)

    def middle_sums(r, after=()):
        part = fb[r] if r not in ib else ib[r]
        rs2[r] = pair_swap(*middle(chain, rs1[r], part[0], part[1], after))

    line = Line(chain, edge)
    activations, sums2[A], dffn[A] = second_norm(A, None)
    sent, kept = plane_ffn_bwd(chain, True, dffn[A], slopes[A], weights, ())
    rs1[A] = pair_swap(*sent)
    rs2[B] = pair_swap(*middle(chain, rs1[B], ff[B][0], ff[B][1]))
    fb[A], dgu[A] = plane_ffn_bwd(chain, False, dffn[A], slopes[A], weights, kept)
    resid[B] = second_resid(B)
    rx[B], ry[B] = pair_swap(resid[B], resid[B])
    middle_sums(A)
    rr[B] = forward(chain, rx[B], ry[B])
    dattn[A], dr1[A], sums1[A] = first_norm_back(A)
    dax[A], day[A] = pair_swap(dattn[A], dattn[A])
    activations, sums2[B], dffn[B] = second_norm(B, activations)
    down_update = grad_plain_columns(chain, (al[A], al[B]), (dffn[A], dffn[B]))
    down_sum = lax.psum(down_update, ("obj", "dp"))
    dar[A] = forward(chain, dax[A], day[A])
    sent, dgu[B] = plane_ffn_bwd(chain, None, dffn[B], slopes[B], weights, ())
    fb[B] = sent[2:]
    rs1[B] = pair_swap(*sent[:2])
    chain.close(*dar[A])
    gate_send, gate_keep = grad_rows(chain, info[B], (hl[A], hl[B]), (dgu[A][0], dgu[B][0]))
    gate_got = lax.ppermute(gate_send, "dp", CORES)
    line.add("gate", gate_keep, gate_got, 2)
    middle_sums(B)
    up_send, up_keep = grad_rows(chain, info[B], (hl[A], hl[B]), (dgu[A][1], dgu[B][1]))
    up_got = lax.ppermute(up_send, "dp", CORES)
    line.add("up", up_keep, up_got, 2)
    chain.close(gate_got)
    dattn[B], dr1[B], sums1[B] = first_norm_back(B)
    dax[B], day[B] = pair_swap(dattn[B], dattn[B])
    chain.close(up_got)
    line.advance()
    dqkv[A] = attention_back(A)
    dar[B] = forward(chain, dax[B], day[B])
    input_back_sums(A)
    line.advance()
    dqkv[B] = attention_back(B)
    line.advance()
    middle_sums(A)
    qkv_send, qkv_keep = grad_rows(chain, info[B], (tokens, tokens), (dqkv[A], dqkv[B]), after=(down_sum,))
    qkv_got = lax.ppermute(qkv_send, "dp", CORES)
    line.add("qkv", qkv_keep, qkv_got, 3)
    dx[A] = input_grad_own(A)
    dxx[A], dxy[A] = pair_swap(dx[A], dx[A])
    line.advance()
    input_back_sums(B)
    chain.close(qkv_got, dxx[A], dxy[A])
    out_send, out_keep = plane_grad_out(chain, info[B], (ol[A], ol[B]), (pieces[A], pieces[B]))
    line.advance()
    out_got = lax.ppermute(out_send, "dp", CORES)
    line.add("out", out_keep, out_got, 1)
    middle_sums(B)
    outs["down"] = cast(chain, down_sum)
    line.advance()
    chain.close(out_got)
    begin_finish("gate")
    dxr[A] = forward(chain, dxx[A], dxy[A])
    dx[B] = input_grad_own(B)
    dxx[B], dxy[B] = pair_swap(dx[B], dx[B])
    chain.close(theirs["gate"])
    line.advance()
    begin_finish("up")
    finish_matrix("gate", width, units)
    input_grad = plane_place(chain, info[A], A, (dx[A], dxx[A], dxy[A], *dxr[A]), tokens.shape, None)
    dxr[B] = forward(chain, dxx[B], dxy[B])
    mine = (me == 0).astype(F32)
    sums = jnp.concatenate([sums1[A] + sums1[B], (sums2[A] + sums2[B]) * mine])
    every_sum = lax.all_gather(sums, ("obj", "dp", "tensor"))
    line.advance()
    finish_matrix("up", width, units)
    input_grad = plane_place(chain, info[B], B, (dx[B], dxx[B], dxy[B], *dxr[B]), tokens.shape, input_grad)
    line.advance()
    sums = total_sum(chain, every_sum)
    line.advance()
    begin_finish("qkv")
    finish_matrix("qkv", width, qkv_weight.shape[1])
    line.advance()
    begin_finish("out")
    finish_matrix("out", out_weight.shape[0], width)

    return (
        activations,
        input_grad,
        outs["qkv"],
        outs["out"],
        outs["gate"],
        outs["up"],
        outs["down"],
        sums[0],
        sums[1],
        sums[2],
        sums[3],
    )


def body(*args):
    if plane_case(args[0].shape, args[7].shape, args[10].shape):
        return plane_body(*args)
    return general_body(*args)


def solution(mesh):
    rows3 = P(("obj", "dp"), None, None)
    in_specs = (
        rows3,
        rows3,
        P(("obj", "dp"), None),
        P(),
        P(),
        P(),
        P(None, "tensor"),
        P("tensor", None),
        P(None, "tensor"),
        P(None, "tensor"),
        P("tensor", None),
        P(),
        P(),
        P(),
        P(),
    )
    out_specs = (
        rows3,
        rows3,
        P(None, "tensor"),
        P("tensor", None),
        P(None, "tensor"),
        P(None, "tensor"),
        P("tensor", None),
        P(),
        P(),
        P(),
        P(),
    )
    return jax.shard_map(body, mesh=mesh, in_specs=in_specs, out_specs=out_specs, check_vma=False)
```

```python
import functools
import math

import jax
import jax.numpy as jnp
import numpy as np
from jax import lax
from jax.experimental import pallas as pl
from jax.experimental.pallas import tpu as pltpu
from jax.sharding import PartitionSpec as P

HEAD_DIM = 128
deep_alpha = math.sqrt(48.0)
norm_eps = 1e-05
mask_fill = -1e30
score_scale = 1.0 / math.sqrt(HEAD_DIM)
MIB = 1024 * 1024
BF = jnp.bfloat16
F32 = jnp.float32
ANY = pl.ANY


def mm(a, b):
    return lax.dot_general(a, b, (((1,), (0,)), ((), ())), preferred_element_type=F32)


def mm_nt(a, b):
    return lax.dot_general(a, b, (((1,), (1,)), ((), ())), preferred_element_type=F32)


def mm_tn(a, b):
    return lax.dot_general(a, b, (((0,), (0,)), ((), ())), preferred_element_type=F32)


def params(mib, grid_rank=1):
    return pltpu.CompilerParams(
        vmem_limit_bytes=mib * MIB, dimension_semantics=("arbitrary",) * grid_rank
    )


def cost(flops, nbytes, trans=0):
    return pl.CostEstimate(flops=int(flops), bytes_accessed=int(nbytes), transcendentals=int(trans))


def const_spec(shape):
    zeros = (0,) * len(shape)
    return pl.BlockSpec(shape, lambda *_: zeros, pipeline_mode=pl.Buffered(1))


def rotary_tables(seq_length):
    half_width = HEAD_DIM // 2
    frequency = jnp.exp(
        jnp.arange(half_width, dtype=F32) * (-2.0 * math.log(10000.0) / HEAD_DIM)
    )
    angles = jnp.arange(seq_length, dtype=F32)[:, None] * frequency[None, :]
    sine = jnp.sin(angles)
    cosine = jnp.cos(angles)
    return jnp.concatenate([cosine, cosine], axis=1), jnp.concatenate([-sine, sine], axis=1)


def fill_bias(info_ref, segc_ref, segr_ref, bias_ref, tile):
    length = bias_ref.shape[0]
    prefix, limit = info_ref[1], info_ref[2]

    def one(step, carry):
        rows = pl.ds(pl.multiple_of(step * tile, tile), tile)
        key_pos = lax.broadcasted_iota(jnp.int32, (tile, length), 0) + step * tile
        query_pos = lax.broadcasted_iota(jnp.int32, (tile, length), 1)
        same = segc_ref[rows, :] == segr_ref[...]
        open_keys = (
            (key_pos < prefix)
            | ((key_pos <= query_pos) & (key_pos < limit))
            | (key_pos == query_pos)
        )
        bias_ref[rows, :] = jnp.where(same & open_keys, 0.0, mask_fill)
        return carry

    lax.fori_loop(0, length // tile, one, 0)


def attn_fwd_kernel(
    info_ref, x_ref, w_ref, cos_ref, sin_ref, segc_ref, segr_ref, qkv_ref, ol_ref, lse_ref, bias_ref, tile
):
    length = x_ref.shape[0]

    @pl.when(pl.program_id(0) == 0)
    def _():
        fill_bias(info_ref, segc_ref, segr_ref, bias_ref, tile)

    for step in range(length // tile):
        rows = pl.ds(step * tile, tile)
        proj = mm(x_ref[rows, :], w_ref[...])
        cosine, sine = cos_ref[rows, :], sin_ref[rows, :]
        for part in range(2):
            piece = proj[:, part * HEAD_DIM : (part + 1) * HEAD_DIM]
            turned = piece * cosine + pltpu.roll(piece, HEAD_DIM // 2, 1) * sine
            qkv_ref[rows, part * HEAD_DIM : (part + 1) * HEAD_DIM] = turned.astype(BF)
        qkv_ref[rows, 2 * HEAD_DIM :] = proj[:, 2 * HEAD_DIM :].astype(BF)
    keys = qkv_ref[:, HEAD_DIM : 2 * HEAD_DIM]
    values_t = qkv_ref[:, 2 * HEAD_DIM :].astype(F32).T.astype(BF)
    for step in range(length // tile):
        rows = pl.ds(step * tile, tile)
        queries = qkv_ref[rows, :HEAD_DIM]
        scores = mm_nt(keys, queries) * score_scale + bias_ref[:, rows]
        top = jnp.max(scores, axis=0, keepdims=True)
        exponent = jnp.exp(scores - top)
        total = jnp.sum(exponent, axis=0, keepdims=True)
        attended = mm(values_t, exponent.astype(BF)) * (1.0 / total)
        ol_ref[rows, :] = attended.T.astype(BF)
        lse_ref[:, rows] = top + jnp.log(total)


def attn_fwd(info, row, tokens, qkv_weight, cosine, sine, segc, segr):
    _, length, width = tokens.shape
    heads = qkv_weight.shape[1] // (3 * HEAD_DIM)
    tile = min(256, length)
    grid_spec = pltpu.PrefetchScalarGridSpec(
        num_scalar_prefetch=1,
        grid=(heads,),
        in_specs=[
            pl.BlockSpec((None, length, width), lambda h, *_: (row, 0, 0), pipeline_mode=pl.Buffered(1)),
            pl.BlockSpec((width, 3 * HEAD_DIM), lambda h, *_: (0, h)),
            const_spec((length, HEAD_DIM)),
            const_spec((length, HEAD_DIM)),
            const_spec((length, 1)),
            const_spec((1, length)),
        ],
        out_specs=[
            pl.BlockSpec((length, 3 * HEAD_DIM), lambda h, *_: (0, h)),
            pl.BlockSpec((length, HEAD_DIM), lambda h, *_: (0, h)),
            pl.BlockSpec((None, 1, length), lambda h, *_: (h, 0, 0)),
        ],
        scratch_shapes=[pltpu.VMEM((length, length), F32)],
    )
    return pl.pallas_call(
        functools.partial(attn_fwd_kernel, tile=tile),
        grid_spec=grid_spec,
        out_shape=[
            jax.ShapeDtypeStruct((length, heads * 3 * HEAD_DIM), BF),
            jax.ShapeDtypeStruct((length, heads * HEAD_DIM), BF),
            jax.ShapeDtypeStruct((heads, 1, length), F32),
        ],
        compiler_params=params(48),
        cost_estimate=cost(
            heads * (2 * length * width * 384 + 8 * length * length * HEAD_DIM),
            2 * length * width + 2 * width * heads * 384 + 8 * length * heads * 128,
        ),
        name="attn_fwd",
    )(info, tokens, qkv_weight, cosine, sine, segc, segr)


def attn_bwd_kernel(
    info_ref, qkv_ref, dol_ref, lse_ref, cos_ref, sin_ref, segc_ref, segr_ref, dqkv_ref,
    bias_ref, dol_nat, dk_ref, dv_ref, tile
):
    length = qkv_ref.shape[0]
    ways, block, _ = dol_ref.shape
    me = info_ref[0]

    @pl.when(pl.program_id(0) == 0)
    def _():
        fill_bias(info_ref, segc_ref, segr_ref, bias_ref, tile)

    for at in range(ways):
        dol_nat[pl.ds(at * block, block), :] = dol_ref[me ^ at]
    keys = qkv_ref[:, HEAD_DIM : 2 * HEAD_DIM]
    values = qkv_ref[:, 2 * HEAD_DIM :]
    keys_t = keys.astype(F32).T.astype(BF)
    for step in range(length // tile):
        rows = pl.ds(step * tile, tile)
        queries = qkv_ref[rows, :HEAD_DIM]
        dol = dol_nat[rows, :]
        scores = mm_nt(keys, queries) * score_scale + bias_ref[:, rows]
        probs = jnp.exp(scores - lse_ref[:, rows])
        dp = mm_nt(values, dol)
        inner = jnp.sum(probs * dp, axis=0, keepdims=True)
        draw = (probs * (dp - inner) * score_scale).astype(BF)
        dv = mm(probs.astype(BF), dol)
        dk = mm(draw, queries)
        if step == 0:
            dv_ref[...] = dv
            dk_ref[...] = dk
        else:
            dv_ref[...] += dv
            dk_ref[...] += dk
        dq = mm(keys_t, draw).T
        turned = dq * cos_ref[rows, :] - pltpu.roll(dq, HEAD_DIM // 2, 1) * sin_ref[rows, :]
        dqkv_ref[rows, :HEAD_DIM] = turned.astype(BF)
    dk = dk_ref[...]
    turned = dk * cos_ref[...] - pltpu.roll(dk, HEAD_DIM // 2, 1) * sin_ref[...]
    dqkv_ref[:, HEAD_DIM : 2 * HEAD_DIM] = turned.astype(BF)
    dqkv_ref[:, 2 * HEAD_DIM :] = dv_ref[...].astype(BF)


def attn_bwd(info, qkv, dol, lse, cosine, sine, segc, segr):
    length = qkv.shape[0]
    heads = qkv.shape[1] // (3 * HEAD_DIM)
    ways, block, _ = dol.shape
    tile = min(256, length)
    grid_spec = pltpu.PrefetchScalarGridSpec(
        num_scalar_prefetch=1,
        grid=(heads,),
        in_specs=[
            pl.BlockSpec((length, 3 * HEAD_DIM), lambda h, *_: (0, h)),
            pl.BlockSpec((ways, block, HEAD_DIM), lambda h, *_: (0, 0, h)),
            pl.BlockSpec((None, 1, length), lambda h, *_: (h, 0, 0)),
            const_spec((length, HEAD_DIM)),
            const_spec((length, HEAD_DIM)),
            const_spec((length, 1)),
            const_spec((1, length)),
        ],
        out_specs=pl.BlockSpec((length, 3 * HEAD_DIM), lambda h, *_: (0, h)),
        scratch_shapes=[
            pltpu.VMEM((length, length), F32),
            pltpu.VMEM((length, HEAD_DIM), BF),
            pltpu.VMEM((length, HEAD_DIM), F32),
            pltpu.VMEM((length, HEAD_DIM), F32),
        ],
    )
    return pl.pallas_call(
        functools.partial(attn_bwd_kernel, tile=tile),
        grid_spec=grid_spec,
        out_shape=jax.ShapeDtypeStruct(qkv.shape, BF),
        compiler_params=params(48),
        cost_estimate=cost(heads * 20 * length * length * HEAD_DIM, 16 * length * heads * 128),
        name="attn_bwd",
    )(info, qkv, dol, lse, cosine, sine, segc, segr)


def out_norm_kernel(info_ref, *refs, ways):
    ol_refs, ow_refs = refs[:ways], refs[ways : 2 * ways]
    x_ref, gain_ref, bias_ref, hl_ref, n1_ref, rstd_ref = refs[2 * ways :]
    total = x_ref[...].astype(F32) * deep_alpha
    for ol_ref, ow_ref in zip(ol_refs, ow_refs):
        total += mm(ol_ref[...], ow_ref[...])
    centered = total - jnp.mean(total, axis=1, keepdims=True)
    variance = jnp.mean(centered * centered, axis=1, keepdims=True)
    inv = lax.rsqrt(variance + norm_eps)
    normed = centered * inv
    hl_ref[...] = (normed * gain_ref[...] + bias_ref[...]).astype(BF)

    @pl.when(pl.program_id(0) == info_ref[0])
    def _():
        n1_ref[...] = normed
        rstd_ref[...] = jnp.broadcast_to(inv, rstd_ref.shape)


def out_norm(info, row, ol_pieces, ow_pieces, tokens, gain, bias):
    _, length, width = tokens.shape
    ways = len(ol_pieces)
    block = length // ways
    head_width = ol_pieces[0].shape[1]
    grid_spec = pltpu.PrefetchScalarGridSpec(
        num_scalar_prefetch=1,
        grid=(ways,),
        in_specs=[pl.BlockSpec((block, head_width), lambda i, *_: (i, 0))] * ways
        + [const_spec((head_width, width))] * ways
        + [
            pl.BlockSpec((None, block, width), lambda i, *_: (row, i, 0)),
            const_spec((1, width)),
            const_spec((1, width)),
        ],
        out_specs=[
            pl.BlockSpec((block, width), lambda i, info: (i ^ info[0], 0)),
            pl.BlockSpec((block, width), lambda i, *_: (0, 0)),
            pl.BlockSpec((block, HEAD_DIM), lambda i, *_: (0, 0)),
        ],
    )
    return pl.pallas_call(
        functools.partial(out_norm_kernel, ways=ways),
        grid_spec=grid_spec,
        out_shape=[
            jax.ShapeDtypeStruct((length, width), BF),
            jax.ShapeDtypeStruct((block, width), F32),
            jax.ShapeDtypeStruct((block, HEAD_DIM), F32),
        ],
        compiler_params=params(48),
        cost_estimate=cost(2 * length * width * width, 2 * width * width + 6 * length * width),
        name="out_norm",
    )(info, *ol_pieces, *ow_pieces, tokens, gain, bias)


def piece_shapes(ways, block, width):
    if ways == 4:
        sizes = [block] + [block // 2] * 6
    else:
        sizes = [block] * ways
    return [jax.ShapeDtypeStruct((size, width), BF) for size in sizes]


def store_pieces(at, part, refs, ways):
    if ways == 4:
        half = part.shape[0] // 2

        @pl.when(at == 0)
        def _():
            refs[0][...] = part

        for r in range(1, 4):

            @pl.when(at == r)
            def _(r=r):
                refs[2 * r - 1][...] = part[:half]
                refs[2 * r][...] = part[half:]
    else:
        for r in range(ways):

            @pl.when(at == r)
            def _(r=r):
                refs[r][...] = part


def piece_specs(shapes):
    return [pl.BlockSpec(s.shape, lambda *_: (0, 0)) for s in shapes]


def ffn_fwd_kernel(hl_ref, wg_ref, wu_ref, wd_ref, al_ref, ga_ref, gb_ref, *refs, ways):
    hidden = hl_ref[...]
    gate = mm(hidden, wg_ref[...])
    up = mm(hidden, wu_ref[...])
    cdf = 0.5 + 0.5 * lax.erf(gate * (1.0 / math.sqrt(2.0)))
    pdf = jnp.exp(gate * gate * -0.5) * (1.0 / math.sqrt(2.0 * math.pi))
    act = gate * cdf
    ga_ref[...] = (up * (cdf + gate * pdf)).astype(BF)
    gb_ref[...] = act.astype(BF)
    low = (act * up).astype(BF)
    al_ref[...] = low
    store_pieces(pl.program_id(0), mm(low, wd_ref[...]).astype(BF), refs, ways)


def ffn_fwd(hidden, gate_weight, up_weight, down_weight, ways):
    length, width = hidden.shape
    units = gate_weight.shape[1]
    block = length // ways
    tiled = lambda w: pl.BlockSpec((block, w), lambda i: (i, 0))
    shapes = piece_shapes(ways, block, width)
    out = pl.pallas_call(
        functools.partial(ffn_fwd_kernel, ways=ways),
        grid=(ways,),
        in_specs=[
            tiled(width),
            const_spec((width, units)),
            const_spec((width, units)),
            const_spec((units, width)),
        ],
        out_specs=[tiled(units)] * 3 + piece_specs(shapes),
        out_shape=[jax.ShapeDtypeStruct((length, units), BF)] * 3 + shapes,
        compiler_params=params(60),
        cost_estimate=cost(6 * length * width * units, 6 * units * width + 6 * length * units),
        name="ffn_fwd",
    )(hidden, gate_weight, up_weight, down_weight)
    return out[:3], out[3:]


def norm_two_kernel(info_ref, share_ref, *refs, n_in, ways):
    in_refs = refs[:n_in]
    cot_ref, gain_ref, bias_ref = refs[n_in : n_in + 3]
    act_ref, dffn_ref, sums_ref, held = refs[-4:]
    at = pl.program_id(0)
    if n_in == 5:
        half = held.shape[0] // 2
        for r in range(3):

            @pl.when(at == r)
            def _(r=r):
                held[...] = in_refs[r][...]

        @pl.when(at == 3)
        def _():
            held[:half] = in_refs[3][...]
            held[half:] = in_refs[4][...]
    else:
        for r in range(ways):

            @pl.when(at == r)
            def _(r=r):
                held[...] = in_refs[r][...]

    resid = held[...].astype(F32)
    centered = resid - jnp.mean(resid, axis=1, keepdims=True)
    variance = jnp.mean(centered * centered, axis=1, keepdims=True)
    inv = lax.rsqrt(variance + norm_eps)
    normed = centered * inv
    gain = gain_ref[...]
    act_ref[...] = (normed * gain + bias_ref[...]).astype(BF)
    dout = cot_ref[...].astype(F32) * share_ref[0]
    scaled = dout * gain
    inner = jnp.mean(scaled, axis=1, keepdims=True) + normed * jnp.mean(
        scaled * normed, axis=1, keepdims=True
    )
    dffn_ref[...] = (inv * (scaled - inner)).astype(BF)
    gain_sum = jnp.sum(dout * normed, axis=0, keepdims=True)
    bias_sum = jnp.sum(dout, axis=0, keepdims=True)

    @pl.when(at == 0)
    def _():
        sums_ref[0:1, :] = gain_sum
        sums_ref[1:2, :] = bias_sum

    @pl.when(at > 0)
    def _():
        sums_ref[0:1, :] += gain_sum
        sums_ref[1:2, :] += bias_sum


def norm_two(info, share, row, pieces, cotangent, gain, bias, before):
    rows, length, width = cotangent.shape
    block = pieces[0].shape[0]
    ways = length // block
    natural = pl.BlockSpec((None, block, width), lambda i, info, share: (row, i ^ info[0], 0))
    grid_spec = pltpu.PrefetchScalarGridSpec(
        num_scalar_prefetch=2,
        grid=(ways,),
        in_specs=[const_spec(p.shape) for p in pieces]
        + [natural, const_spec((1, width)), const_spec((1, width))]
        + ([pl.BlockSpec(memory_space=ANY)] if before is not None else []),
        out_specs=[
            natural,
            pl.BlockSpec((block, width), lambda i, *_: (i, 0)),
            pl.BlockSpec((2, width), lambda i, *_: (0, 0)),
        ],
        scratch_shapes=[pltpu.VMEM((block, width), BF)],
    )
    return pl.pallas_call(
        functools.partial(norm_two_kernel, n_in=len(pieces), ways=ways),
        grid_spec=grid_spec,
        out_shape=[
            jax.ShapeDtypeStruct(cotangent.shape, BF),
            jax.ShapeDtypeStruct((length, width), BF),
            jax.ShapeDtypeStruct((2, width), F32),
        ],
        input_output_aliases={len(pieces) + 5: 0} if before is not None else {},
        compiler_params=params(48),
        cost_estimate=cost(20 * length * width, 8 * length * width),
        name="norm_two",
    )(info, share, *pieces, cotangent, gain, bias, *([before] if before is not None else []))


def ffn_bwd_kernel(dffn_ref, ga_ref, gb_ref, wg_ref, wu_ref, wd_ref, dg_ref, du_ref, *refs, ways):
    dact = mm_nt(dffn_ref[...], wd_ref[...])
    dgate = (dact * ga_ref[...].astype(F32)).astype(BF)
    dup = (dact * gb_ref[...].astype(F32)).astype(BF)
    dg_ref[...] = dgate
    du_ref[...] = dup
    part = mm_nt(dgate, wg_ref[...]) + mm_nt(dup, wu_ref[...])
    store_pieces(pl.program_id(0), part.astype(BF), refs, ways)


def ffn_bwd(dffn, gate_slope, up_slope, gate_weight, up_weight, down_weight, ways):
    length, width = dffn.shape
    units = gate_weight.shape[1]
    block = length // ways
    tiled = lambda w: pl.BlockSpec((block, w), lambda i: (i, 0))
    shapes = piece_shapes(ways, block, width)
    out = pl.pallas_call(
        functools.partial(ffn_bwd_kernel, ways=ways),
        grid=(ways,),
        in_specs=[
            tiled(width),
            tiled(units),
            tiled(units),
            const_spec((width, units)),
            const_spec((width, units)),
            const_spec((units, width)),
        ],
        out_specs=[tiled(units)] * 2 + piece_specs(shapes),
        out_shape=[jax.ShapeDtypeStruct((length, units), BF)] * 2 + shapes,
        compiler_params=params(60),
        cost_estimate=cost(6 * length * width * units, 6 * units * width + 8 * length * units),
        name="ffn_bwd",
    )(dffn, gate_slope, up_slope, gate_weight, up_weight, down_weight)
    return out[0], out[1], out[2:]


def input_back_kernel(info_ref, dqkv_ref, w_ref, *refs, ways):
    part = mm_nt(dqkv_ref[...], w_ref[...])
    store_pieces(pl.program_id(0), part.astype(BF), refs, ways)


def input_back(info, dqkv, qkv_weight, ways):
    length, columns = dqkv.shape
    width = qkv_weight.shape[0]
    block = length // ways
    shapes = piece_shapes(ways, block, width)
    grid_spec = pltpu.PrefetchScalarGridSpec(
        num_scalar_prefetch=1,
        grid=(ways,),
        in_specs=[
            pl.BlockSpec((block, columns), lambda i, info: (i ^ info[0], 0)),
            const_spec((width, columns)),
        ],
        out_specs=piece_specs(shapes),
    )
    return pl.pallas_call(
        functools.partial(input_back_kernel, ways=ways),
        grid_spec=grid_spec,
        out_shape=shapes,
        compiler_params=params(48),
        cost_estimate=cost(2 * length * width * columns, 2 * width * columns + 2 * length * width),
        name="input_back",
    )(info, dqkv, qkv_weight)


def place_kernel(info_ref, *refs, n_in, ways):
    in_refs = refs[:n_in]
    out_ref = refs[-1]
    at = pl.program_id(0)
    if n_in == 5:
        half = out_ref.shape[0] // 2
        for r in range(3):

            @pl.when(at == r)
            def _(r=r):
                out_ref[...] = in_refs[r][...]

        @pl.when(at == 3)
        def _():
            out_ref[:half] = in_refs[3][...]
            out_ref[half:] = in_refs[4][...]
    else:
        for r in range(ways):

            @pl.when(at == r)
            def _(r=r):
                out_ref[...] = in_refs[r][...]


def place(info, row, pieces, shape, before):
    rows, length, width = shape
    block = pieces[0].shape[0]
    ways = length // block
    grid_spec = pltpu.PrefetchScalarGridSpec(
        num_scalar_prefetch=1,
        grid=(ways,),
        in_specs=[const_spec(p.shape) for p in pieces]
        + ([pl.BlockSpec(memory_space=ANY)] if before is not None else []),
        out_specs=pl.BlockSpec((None, block, width), lambda i, info: (row, i ^ info[0], 0)),
    )
    return pl.pallas_call(
        functools.partial(place_kernel, n_in=len(pieces), ways=ways),
        grid_spec=grid_spec,
        out_shape=jax.ShapeDtypeStruct(shape, BF),
        input_output_aliases={len(pieces) + 1: 0} if before is not None else {},
        compiler_params=params(32),
        cost_estimate=cost(0, 4 * length * width),
        name="place",
    )(info, *pieces, *([before] if before is not None else []))


def swap(array, bit, ways):
    return lax.ppermute(array, "tensor", [(i, i ^ bit) for i in range(ways)])


def gather_halves(own_a, own_b):
    xa = swap(own_a, 1, 4)
    yb = swap(own_b, 2, 4)
    xb = swap(own_b, 1, 4)
    ya = swap(own_a, 2, 4)
    ra = swap(xa, 2, 4)
    rb = swap(yb, 1, 4)
    return [(xa, xb), (ya, yb), (ra, rb)]


def gather_rel(own, ways):
    blocks = [own]
    bit = 1
    while bit < ways:
        blocks = blocks + [swap(b, bit, ways) for b in blocks]
        bit *= 2
    return blocks


def gather_tokens(own, ways):
    if ways == 4:
        half = own.shape[0] // 2
        (xa, xb), (ya, yb), (ra, rb) = gather_halves(own[:half], own[half:])
        return [own, jnp.concatenate([xa, xb]), jnp.concatenate([ya, yb]), ra, rb]
    return gather_rel(own, ways)


def join(pieces):
    return jnp.concatenate(pieces, axis=0)


def add_low(a, b):
    return (a.astype(F32) + b.astype(F32)).astype(BF)


def scatter_sum(pieces, ways):
    if ways == 4:
        own, r1a, r1b, r2a, r2b, r3a, r3b = pieces
        in3a = swap(r3a, 1, 4)
        in3b = swap(r3b, 2, 4)
        in1a = swap(r1a, 1, 4)
        in2b = swap(r2b, 2, 4)
        in2a = swap(add_low(r2a, in3a), 2, 4)
        in1b = swap(add_low(r1b, in3b), 1, 4)
        half = r1a.shape[0]
        top = own[:half].astype(F32) + in1a.astype(F32) + in2a.astype(F32)
        low = own[half:].astype(F32) + in1b.astype(F32) + in2b.astype(F32)
        return jnp.concatenate([top, low], axis=0)
    blocks = list(pieces)
    bit = ways // 2
    while bit >= 1:
        keep, send = blocks[:bit], blocks[bit:]
        blocks = [add_low(k, swap(s, bit, ways)) for k, s in zip(keep, send)]
        bit //= 2
    return blocks[0].astype(F32)


def sum_over_obj(array, ways):
    if ways != 4:
        return lax.psum(array, "obj")
    at = lax.axis_index("obj")
    one = add_low(array, lax.ppermute(array, "obj", [(0, 1), (3, 2)]))
    two = add_low(one, lax.ppermute(one, "obj", [(1, 2), (2, 1)]))
    back = lax.ppermute(two, "obj", [(1, 0), (2, 3)])
    return jnp.where((at == 0) | (at == 3), back, two)


def sum_gradient(update, data_ways, objective_ways):
    if data_ways != 2:
        return lax.psum(update, ("obj", "dp")).astype(F32)
    core = lax.axis_index("dp")
    half = update.shape[0] // 2
    other = [(0, 1), (1, 0)]
    mine = lax.dynamic_slice_in_dim(update, core * half, half)
    send = lax.dynamic_slice_in_dim(update, (1 - core) * half, half)
    mine = add_low(mine, lax.ppermute(send, "dp", other))
    mine = sum_over_obj(mine, objective_ways)
    theirs = lax.ppermute(mine, "dp", other)
    first = jnp.where(core == 0, mine, theirs)
    second = jnp.where(core == 0, theirs, mine)
    return jnp.concatenate([first, second], axis=0).astype(F32)


def general_body(
    tokens,
    cotangent,
    segment_ids,
    mlm_mask,
    glm_prefix,
    glm_span,
    qkv_weight,
    out_weight,
    gate_weight,
    up_weight,
    down_weight,
    norm1_gain,
    norm1_bias,
    norm2_gain,
    norm2_bias,
):
    seq_here, length, width = tokens.shape
    ways = lax.axis_size("tensor")
    data_ways = lax.axis_size("dp")
    objective_ways = lax.axis_size("obj")
    me = lax.axis_index("tensor").astype(jnp.int32)
    block = length // ways
    rows_all = mlm_mask.shape[0]
    masked_limit = seq_here * data_ways * (objective_ways // 2)
    row_ids = jnp.arange(rows_all, dtype=jnp.int32)
    counts = jnp.where(row_ids < masked_limit, jnp.sum(mlm_mask, axis=1), glm_span).astype(F32)
    weight_all = counts * rows_all / jnp.sum(counts)
    first_row = (lax.axis_index("obj") * data_ways + lax.axis_index("dp")) * seq_here
    share_here = lax.dynamic_slice_in_dim(weight_all, first_row, seq_here)
    prefix_here = lax.dynamic_slice_in_dim(glm_prefix, first_row, seq_here)
    span_here = lax.dynamic_slice_in_dim(glm_span, first_row, seq_here)
    masked_lm = first_row < masked_limit
    open_here = jnp.where(masked_lm, length, prefix_here)
    info = [jnp.stack([me, open_here[r], prefix_here[r] + span_here[r]]) for r in range(seq_here)]
    share = [share_here[r : r + 1] for r in range(seq_here)]
    cosine, sine = rotary_tables(length)
    segc = [segment_ids[r].reshape(length, 1) for r in range(seq_here)]
    segr = [segment_ids[r].reshape(1, length) for r in range(seq_here)]
    gain1, bias1 = norm1_gain.reshape(1, width), norm1_bias.reshape(1, width)
    gain2, bias2 = norm2_gain.reshape(1, width), norm2_bias.reshape(1, width)
    rows = range(seq_here)

    if ways == 4 and data_ways == 2:
        core = lax.axis_index("dp")
        half = out_weight.shape[0] // 2
        mine = lax.dynamic_slice_in_dim(out_weight, core * half, half)
        pairs = gather_halves(mine[: half // 2], mine[half // 2 :])
        ow_pieces = [out_weight]
        for a, b in pairs:
            got = jnp.concatenate([a, b])
            other = lax.ppermute(got, "dp", [(0, 1), (1, 0)])
            ow_pieces.append(
                jnp.concatenate(
                    [jnp.where(core == 0, got, other), jnp.where(core == 0, other, got)]
                )
            )
    else:
        ow_pieces = gather_rel(out_weight, ways)

    qkv, ol, lse, hl, n1, rstd1 = {}, {}, {}, {}, {}, {}
    al, slope_g, slope_u, dffn, dgate, dup = {}, {}, {}, {}, {}, {}
    r2_pieces, norm2_sums, norm1_sums, dr1, dqkv, dattn = {}, {}, {}, {}, {}, {}

    for r in rows:
        qkv[r], ol[r], lse[r] = attn_fwd(info[r], r, tokens, qkv_weight, cosine, sine, segc[r], segr[r])
    ffn_parts = {}
    for r in rows:
        if ways == 4:
            pairs = gather_halves(ol[r][: length // 2], ol[r][length // 2 :])
            ol_pieces = [ol[r]] + [jnp.concatenate(p) for p in pairs]
        else:
            ol_pieces = gather_rel(ol[r], ways)
        hl[r], n1[r], rstd1[r] = out_norm(info[r], r, ol_pieces, ow_pieces, tokens, gain1, bias1)
        (al[r], slope_g[r], slope_u[r]), ffn_parts[r] = ffn_fwd(
            hl[r], gate_weight, up_weight, down_weight, ways
        )
    for r in rows:
        total = scatter_sum(ffn_parts[r], ways)
        resid = deep_alpha * (n1[r] * gain1 + bias1) + total
        r2_pieces[r] = gather_tokens(resid.astype(BF), ways)

    activations = None
    dh_parts = {}
    for r in rows:
        activations, dffn[r], norm2_sums[r] = norm_two(
            info[r], share[r], r, r2_pieces[r], cotangent, gain2, bias2, activations
        )
        dgate[r], dup[r], dh_parts[r] = ffn_bwd(
            dffn[r], slope_g[r], slope_u[r], gate_weight, up_weight, down_weight, ways
        )

    def update(lefts, rights):
        total = None
        for r in rows:
            one = mm_tn(lefts[r], rights[r])
            total = one if total is None else total + one
        return total.astype(BF)

    def reduced(lefts, rights):
        return sum_gradient(update(lefts, rights), data_ways, objective_ways)

    down_grad = reduced(al, dffn)
    gate_grad = reduced(hl, dgate)
    up_grad = reduced(hl, dup)

    dx_parts = {}
    for r in rows:
        total = scatter_sum(dh_parts[r], ways)
        dh = deep_alpha * dffn[r][:block].astype(F32) + total
        scaled = dh * gain1
        inner = jnp.mean(scaled, axis=1, keepdims=True) + n1[r] * jnp.mean(
            scaled * n1[r], axis=1, keepdims=True
        )
        dr1[r] = rstd1[r][:, :1] * (scaled - inner)
        norm1_sums[r] = jnp.stack([jnp.sum(dh * n1[r], axis=0), jnp.sum(dh, axis=0)])
        dattn[r] = join(gather_tokens(dr1[r].astype(BF), ways))
    for r in rows:
        dol = mm_nt(dattn[r], out_weight).astype(BF).reshape(ways, block, -1)
        dqkv[r] = attn_bwd(info[r], qkv[r], dol, lse[r], cosine, sine, segc[r], segr[r])
        dx_parts[r] = input_back(info[r], dqkv[r], qkv_weight, ways)

    qkv_grad = reduced([tokens[r] for r in rows], dqkv)
    ol_rel = {}
    for r in rows:
        parts = ol[r].reshape(ways, block, -1)
        ol_rel[r] = jnp.stack(
            [lax.dynamic_index_in_dim(parts, me ^ i, 0, keepdims=False) for i in range(ways)]
        ).reshape(length, -1)
    out_grad = reduced(ol_rel, dattn)

    input_grad = None
    for r in rows:
        total = scatter_sum(dx_parts[r], ways)
        dx = (deep_alpha * dr1[r] + total).astype(BF)
        input_grad = place(info[r], r, gather_tokens(dx, ways), tokens.shape, input_grad)

    first = (me == 0).astype(F32)
    sums = jnp.concatenate(
        [sum(norm1_sums[r] for r in rows), sum(norm2_sums[r] for r in rows) * first]
    )
    sums = lax.psum(sums, ("obj", "dp", "tensor"))
    return (
        activations,
        input_grad,
        qkv_grad,
        out_grad,
        gate_grad,
        up_grad,
        down_grad,
        sums[0],
        sums[1],
        sums[2],
        sums[3],
    )


ORDER = ((1, 0), (3, 0), (2, 1), (3, 1), (1, 1), (2, 0), (0, 0), (0, 1))
CORES = ((0, 1), (1, 0))
DECLARED_FLOPS = 1e10
MICROS = {
    "attn_fwd": 21, "split": 2, "ow_join": 4, "relay": 1, "out_norm": 21, "middle_sum": 3, "resid_two": 5,
    "norm_two": 15, "grad_columns": 20, "grad_plain_columns": 19, "grad_plain": 19, "line_step": 5, "grad_rows": 21,
    "attn_bwd": 24, "norm_one_back": 6, "input_back": 14, "input_grad": 5, "grad_out": 11, "place": 5, "widen": 10,
    "cast": 9, "total_sum": 2,
}


def plane_case(token_shape, out_shape, down_shape):
    return (
        lax.axis_size("tensor") == 4
        and lax.axis_size("dp") == 2
        and lax.axis_size("obj") == 4
        and token_shape[0] == 2
        and token_shape[1] % 1024 == 0
        and token_shape[2] % 1024 == 0
        and down_shape[0] % 128 == 0
        and out_shape[0] % 256 == 0
    )


def spec(shape, index):
    return pl.BlockSpec(shape, index)


def call(
    kernel, name, grid, ins, in_specs, outs, out_specs, scalars=(), after=(), scratch=(), aliases=None,
    mib=48, flops=0, nbytes=0,
):
    ns, ni, na = len(scalars), len(ins), len(after)

    def wrapped(*refs):
        kernel(*refs[: ns + ni], *refs[ns + ni + na :])

    grid_spec = pltpu.PrefetchScalarGridSpec(
        num_scalar_prefetch=ns,
        grid=grid,
        in_specs=list(in_specs) + [pl.BlockSpec(memory_space=ANY)] * na,
        out_specs=list(out_specs),
        scratch_shapes=list(scratch),
    )
    return pl.pallas_call(
        wrapped,
        grid_spec=grid_spec,
        out_shape=[jax.ShapeDtypeStruct(s, d) for s, d in outs],
        input_output_aliases={ns + k: v for k, v in (aliases or {}).items()},
        compiler_params=params(62, len(grid)),
        cost_estimate=cost(DECLARED_FLOPS * MICROS.get(name, 9 * grid[0]), 1e6),
        name=name,
    )(*scalars, *ins, *after)


def constant_tables(length):
    half = HEAD_DIM // 2
    frequency = np.exp(np.arange(half, dtype=np.float32) * np.float32(-2.0 * math.log(10000.0) / HEAD_DIM))
    angles = np.arange(length, dtype=np.float32)[:, None] * frequency[None, :]
    cosine, sine = np.cos(angles), np.sin(angles)
    both = lambda a, b: jnp.asarray(np.concatenate([a, b], axis=1).astype(np.float32))
    return both(cosine, cosine), both(-sine, sine)


class Chain:
    def __init__(self):
        self.last = ()
        self.ended = ()

    def close(self, *arrays):
        self.ended += arrays

    def __call__(self, *args, after=(), **kwargs):
        out = call(*args, after=(*self.last, *self.ended, *after), **kwargs)
        self.last, self.ended = (out[0],), ()
        return out


def pair_swap(to_x, to_y):
    return swap(to_x, 1, 4), swap(to_y, 2, 4)


def plane_attn_fwd_kernel(
    info_ref, x_ref, w_ref, cos_ref, sin_ref, segc_ref, segr_ref, qkv_ref, ol_ref, lse_ref, bias_ref, *, tile
):
    length = x_ref.shape[0]

    @pl.when(pl.program_id(0) == 0)
    def _():
        fill_bias(info_ref, segc_ref, segr_ref, bias_ref, tile)

    for step in range(length // (2 * tile)):
        rows = pl.ds(step * 2 * tile, 2 * tile)
        proj = mm(x_ref[rows, :], w_ref[...])
        cosine, sine = cos_ref[rows, :], sin_ref[rows, :]
        for part in range(proj.shape[1] // HEAD_DIM):
            low = part * HEAD_DIM
            piece = proj[:, low : low + HEAD_DIM]
            if part % 3 < 2:
                piece = piece * cosine + pltpu.roll(piece, HEAD_DIM // 2, 1) * sine
            qkv_ref[rows, low : low + HEAD_DIM] = piece.astype(BF)

    heads = qkv_ref.shape[1] // (3 * HEAD_DIM)
    units = [(h, t) for h in range(heads) for t in range(length // tile)]
    keys, values_t = {}, {}

    def scores_of(unit):
        h, t = unit
        base = 3 * HEAD_DIM * h
        if h not in keys:
            keys[h] = qkv_ref[:, base + HEAD_DIM : base + 2 * HEAD_DIM]
            values_t[h] = qkv_ref[:, base + 2 * HEAD_DIM : base + 3 * HEAD_DIM].astype(F32).T.astype(BF)
        return mm_nt(keys[h], qkv_ref[t * tile : (t + 1) * tile, base : base + HEAD_DIM])

    later = scores_of(units[0])
    for k, (h, t) in enumerate(units):
        raw = later
        if k + 1 < len(units):
            later = scores_of(units[k + 1])
        rows = pl.ds(t * tile, tile)
        scores = raw * score_scale + bias_ref[:, rows]
        top = jnp.max(scores, axis=0, keepdims=True)
        exponent = jnp.exp(scores - top)
        total = jnp.sum(exponent, axis=0, keepdims=True)
        attended = mm(values_t[h], exponent.astype(BF)) * (1.0 / total)
        ol_ref[rows, h * HEAD_DIM : (h + 1) * HEAD_DIM] = attended.T.astype(BF)
        lse_ref[h, :, rows] = top + jnp.log(total)


def plane_attn_fwd(chain, info, row, tokens, qkv_weight, cosine, sine, segc, segr, after=()):
    _, length, width = tokens.shape
    heads = qkv_weight.shape[1] // (3 * HEAD_DIM)
    return chain(
        functools.partial(plane_attn_fwd_kernel, tile=256),
        "attn_fwd",
        (heads // 2,),
        (tokens, qkv_weight, cosine, sine, segc, segr),
        [
            pl.BlockSpec((None, length, width), lambda h, *_: (row, 0, 0), pipeline_mode=pl.Buffered(1)),
            spec((width, 768), lambda h, *_: (0, h)),
            const_spec((length, HEAD_DIM)),
            const_spec((length, HEAD_DIM)),
            const_spec((length, 1)),
            const_spec((1, length)),
        ],
        [((length, heads * 384), BF), ((length, heads * 128), BF), ((heads, 1, length), F32)],
        [
            spec((length, 768), lambda h, *_: (0, h)),
            spec((length, 256), lambda h, *_: (0, h)),
            spec((2, 1, length), lambda h, *_: (h, 0, 0)),
        ],
        scalars=(info,),
        after=after,
        scratch=[pltpu.VMEM((length, length), F32)],
        flops=heads * (2 * length * width * 384 + 8 * length * length * 128),
        nbytes=2 * length * width + 2 * width * heads * 384 + 8 * length * heads * 128,
    )


def plane_attn_bwd_kernel(
    info_ref, qkv_ref, own, r1, r2, r3a, r3b, ow_ref, lse_ref, cos_ref, sin_ref, segc_ref, segr_ref, dqkv_ref,
    bias_ref, dol_nat, *, tile
):
    length = qkv_ref.shape[0]
    block = own.shape[0]
    half = block // 2
    me = info_ref[0]

    @pl.when(pl.program_id(0) == 0)
    def _():
        fill_bias(info_ref, segc_ref, segr_ref, bias_ref, tile)

    def natural(r, lower):
        return pl.multiple_of((me ^ r) * block + lower, half)

    for r, piece in enumerate((own, r1, r2)):
        dol_nat[pl.ds(natural(r, 0), block), :] = mm_nt(piece[...], ow_ref[...]).astype(BF)
    for lower, piece in ((0, r3a), (half, r3b)):
        dol_nat[pl.ds(natural(3, lower), half), :] = mm_nt(piece[...], ow_ref[...]).astype(BF)

    heads = qkv_ref.shape[1] // (3 * HEAD_DIM)
    count = length // tile
    units = [(h, t) for h in range(heads) for t in range(count)]
    keys, values, keys_t = {}, {}, {}

    def products_of(unit):
        h, t = unit
        base = 3 * HEAD_DIM * h
        if h not in keys:
            keys[h] = qkv_ref[:, base + HEAD_DIM : base + 2 * HEAD_DIM]
            values[h] = qkv_ref[:, base + 2 * HEAD_DIM : base + 3 * HEAD_DIM]
            keys_t[h] = keys[h].astype(F32).T.astype(BF)
        rows = pl.ds(t * tile, tile)
        queries = qkv_ref[rows, base : base + HEAD_DIM]
        dol = dol_nat[rows, h * HEAD_DIM : (h + 1) * HEAD_DIM]
        return queries, dol, mm_nt(keys[h], queries), mm_nt(values[h], dol)

    dk = dv = None
    later = products_of(units[0])
    for k, (h, t) in enumerate(units):
        queries, dol, raw, dp = later
        if k + 1 < len(units):
            later = products_of(units[k + 1])
        base = 3 * HEAD_DIM * h
        rows = pl.ds(t * tile, tile)
        probs = jnp.exp(raw * score_scale + bias_ref[:, rows] - lse_ref[h, :, rows])
        weighted = probs * dp
        inner = jnp.sum(weighted, axis=0, keepdims=True)
        draw = ((weighted - probs * inner) * score_scale).astype(BF)
        dv_part, dk_part = mm(probs.astype(BF), dol), mm(draw, queries)
        dv = dv_part if t == 0 else dv + dv_part
        dk = dk_part if t == 0 else dk + dk_part
        dq = mm(keys_t[h], draw).T
        turned = dq * cos_ref[rows, :] - pltpu.roll(dq, HEAD_DIM // 2, 1) * sin_ref[rows, :]
        dqkv_ref[rows, base : base + HEAD_DIM] = turned.astype(BF)
        if t == count - 1:
            turned = dk * cos_ref[...] - pltpu.roll(dk, HEAD_DIM // 2, 1) * sin_ref[...]
            dqkv_ref[:, base + HEAD_DIM : base + 2 * HEAD_DIM] = turned.astype(BF)
            dqkv_ref[:, base + 2 * HEAD_DIM : base + 3 * HEAD_DIM] = dv.astype(BF)


def plane_attn_bwd(chain, info, qkv, pieces, out_weight, lse, cosine, sine, segc, segr, after=()):
    length = qkv.shape[0]
    heads = qkv.shape[1] // 384
    width = out_weight.shape[1]
    return chain(
        functools.partial(plane_attn_bwd_kernel, tile=256),
        "attn_bwd",
        (heads // 2,),
        (qkv, *pieces, out_weight, lse, cosine, sine, segc, segr),
        [spec((length, 768), lambda h, *_: (0, h))]
        + [const_spec(p.shape) for p in pieces]
        + [
            spec((256, width), lambda h, *_: (h, 0)),
            spec((2, 1, length), lambda h, *_: (h, 0, 0)),
            const_spec((length, HEAD_DIM)),
            const_spec((length, HEAD_DIM)),
            const_spec((length, 1)),
            const_spec((1, length)),
        ],
        [(qkv.shape, BF)],
        [spec((length, 768), lambda h, *_: (0, h))],
        scalars=(info,),
        after=after,
        scratch=[pltpu.VMEM((length, length), F32), pltpu.VMEM((length, 256), BF)],
        flops=heads * 24 * length * length * 128,
        nbytes=16 * length * heads * 128,
    )[0]


def plane_out_norm_kernel(
    info_ref, order_ref, *refs
):
    lows, highs = refs[:5], refs[5:10]
    ow_ref, mine_ref, other_ref = refs[10:13]
    xl_ref, xh_ref, gain_ref, bias_ref, hl_ref, n1_ref, rstd_ref, total_ref = refs[13:]
    half = xl_ref.shape[0]
    at = pl.program_id(0)

    def blocks(group, place):
        diagonal = jnp.where(place < 4, group[3][...].astype(F32), group[4][...].astype(F32)).astype(BF)
        return [ref[...] for ref in group[:3]] + [diagonal]

    feat = mine_ref.shape[0] // 3
    total_ref[:half] = xl_ref[...].astype(F32) * deep_alpha
    total_ref[half:] = xh_ref[...].astype(F32) * deep_alpha
    low, high = blocks(lows, order_ref[2 * at]), blocks(highs, order_ref[2 * at + 1])
    ols = [jnp.concatenate([lo, hi], axis=0) for lo, hi in zip(low, high)]

    def add(first, second):
        total = mm(ols[0], ow_ref[...])
        for r in range(1, 4):
            rows = pl.ds((r - 1) * feat, feat)
            total += mm(ols[r][:, :feat], first[rows, :])
            total += mm(ols[r][:, feat:], second[rows, :])
        total_ref[...] += total

    @pl.when(info_ref[3] == 0)
    def _():
        add(mine_ref, other_ref)

    @pl.when(info_ref[3] != 0)
    def _():
        add(other_ref, mine_ref)

    total = total_ref[...]
    centered = total - jnp.mean(total, axis=1, keepdims=True)
    variance = jnp.mean(centered * centered, axis=1, keepdims=True)
    inv = lax.rsqrt(variance + norm_eps)
    normed = centered * inv
    hl_ref[...] = (normed * gain_ref[...] + bias_ref[...]).astype(BF)

    @pl.when(pl.program_id(0) == 3)
    def _():
        n1_ref[...] = normed
        rstd_ref[...] = jnp.broadcast_to(inv, rstd_ref.shape)


def plane_out_norm(chain, info, order, row, ol_pieces, out_weight, mine, other, tokens, gain, bias, after=()):
    _, length, width = tokens.shape
    block = length // 4
    half = block // 2
    head_width = out_weight.shape[0]
    low = lambda i, info, order: (order[2 * i], 0)
    high = lambda i, info, order: (order[2 * i + 1], 0)

    def ol_specs(index):
        upper = lambda i, info, order: (jnp.minimum(index(i, info, order)[0], 3), 0)
        lower = lambda i, info, order: (jnp.maximum(index(i, info, order)[0] - 4, 0), 0)
        return [spec((half, head_width), f) for f in (index, index, index, upper, lower)]

    low3 = lambda i, info, order: (row, order[2 * i], 0)
    high3 = lambda i, info, order: (row, order[2 * i + 1], 0)
    return chain(
        plane_out_norm_kernel,
        "out_norm",
        (4,),
        (*ol_pieces, *ol_pieces, out_weight, mine, other, tokens, tokens, gain, bias),
        ol_specs(low)
        + ol_specs(high)
        + [const_spec(out_weight.shape), const_spec(mine.shape), const_spec(other.shape)]
        + [
            spec((None, half, width), low3),
            spec((None, half, width), high3),
            const_spec((1, width)),
            const_spec((1, width)),
        ],
        [((length, width), BF), ((block, width), F32), ((block, HEAD_DIM), F32)],
        [
            spec((block, width), lambda i, *_: (i, 0)),
            spec((block, width), lambda i, *_: (0, 0)),
            spec((block, HEAD_DIM), lambda i, *_: (0, 0)),
        ],
        scalars=(info, order),
        after=after,
        scratch=[pltpu.VMEM((block, width), F32)],
        flops=2 * length * width * width,
        nbytes=2 * width * width + 6 * length * width,
    )


def split_kernel(x_ref, y_ref, *refs):
    count = len(refs) // 2 - 1
    refs[count][...] = x_ref[...]
    refs[count + 1][...] = y_ref[...]


def forward(chain, from_x, from_y, carry=(), after=()):
    rows, width = from_x.shape
    shape = (rows // 2, width)
    any_spec = pl.BlockSpec(memory_space=ANY)
    out = chain(
        split_kernel, "split", (1,), (from_x, from_y, *carry),
        [
            pl.BlockSpec(shape, lambda i, *_: (0, 0), pipeline_mode=pl.Buffered(1)),
            pl.BlockSpec(shape, lambda i, *_: (1, 0), pipeline_mode=pl.Buffered(1)),
        ]
        + [any_spec] * len(carry),
        [(shape, BF)] * 2 + [(c.shape, c.dtype) for c in carry],
        [spec(shape, lambda i, *_: (0, 0))] * 2 + [any_spec] * len(carry),
        after=after,
        aliases={2 + k: 2 + k for k in range(len(carry))},
        nbytes=4 * rows * width,
    )
    pair = (swap(out[0], 2, 4), swap(out[1], 1, 4))
    return (pair, *out[2:]) if carry else pair


def ow_join_kernel(x_ref, y_ref, a_ref, b_ref, out_ref):
    rows = x_ref.shape[0]
    out_ref[:rows] = x_ref[...]
    out_ref[rows : 2 * rows] = y_ref[...]
    out_ref[2 * rows : 2 * rows + rows // 2] = a_ref[...]
    out_ref[2 * rows + rows // 2 :] = b_ref[...]


def ow_join(chain, pieces, after=()):
    rows, width = pieces[0].shape
    shape = (3 * rows, width)
    return chain(
        ow_join_kernel, "ow_join", (1,), pieces, [const_spec(p.shape) for p in pieces],
        [(shape, BF)], [spec(shape, lambda i, *_: (0, 0))], after=after,
    )[0]


def relay_kernel(*refs):
    refs[len(refs) // 2][...] = refs[0][...]


def relay(chain, carry, after=()):
    small = jnp.zeros((8, 128), F32)
    any_spec = pl.BlockSpec(memory_space=ANY)
    count = len(carry)
    out = chain(
        relay_kernel, "relay", (1,), (small, *carry), [const_spec(small.shape)] + [any_spec] * count,
        [(small.shape, F32)] + [(c.shape, c.dtype) for c in carry],
        [spec(small.shape, lambda i, *_: (0, 0))] + [any_spec] * count,
        after=after, aliases={1 + k: 1 + k for k in range(count)},
    )
    return out[1:]


def load_once(pairs, sem):
    copies = [pltpu.make_async_copy(src, dst, sem.at[k]) for k, (src, dst) in enumerate(pairs)]

    @pl.when(pl.program_id(0) == 0)
    def _():
        for copy in copies:
            copy.start()

    def wait(k):
        @pl.when(pl.program_id(0) == 0)
        def _():
            copies[k].wait()

    return wait


def store_half(first, part, refs):
    at = pl.program_id(0)
    half = part.shape[0] // 2
    if first is None:

        @pl.when(at == 0)
        def _():
            refs[0][...] = part

        @pl.when(at == 1)
        def _():
            refs[1][...] = part

        @pl.when(at == 2)
        def _():
            refs[2][...] = part[:half]
            refs[3][...] = part[half:]

        @pl.when(at == 3)
        def _():
            refs[4][...] = part

        return

    @pl.when(at == 0)
    def _():
        if first:
            refs[0][...] = part
        else:
            refs[0][...] = part[:half]
            refs[1][...] = part[half:]

    @pl.when(at == 1)
    def _():
        refs[-1][...] = part


def half_outs(first, block, width):
    if first is None:
        sizes = [block, block, block // 2, block // 2, block]
    else:
        sizes = [block, block] if first else [block // 2, block // 2, block]
    return [((s, width), BF) for s in sizes], [spec((s, width), lambda i, *_: (0, 0)) for s in sizes]


def plane_ffn_fwd_kernel(hl_ref, wg_hbm, wu_hbm, wd_hbm, *refs, first):
    refs, (wg, wu, wd, sem) = refs[:-4], refs[-4:]
    (al_ref, ga_ref, gb_ref), refs = refs[-3:], refs[:-3]
    wait = load_once(((wg_hbm, wg), (wu_hbm, wu), (wd_hbm, wd)), sem)
    hidden = hl_ref[...]
    wait(0)
    gate = mm(hidden, wg[...])
    wait(1)
    up = mm(hidden, wu[...])
    cdf = 0.5 + 0.5 * lax.erf(gate * (1.0 / math.sqrt(2.0)))
    pdf = jnp.exp(gate * gate * -0.5) * (1.0 / math.sqrt(2.0 * math.pi))
    act = gate * cdf
    ga_ref[...] = (up * (cdf + gate * pdf)).astype(BF)
    gb_ref[...] = act.astype(BF)
    low = (act * up).astype(BF)
    al_ref[...] = low
    wait(2)
    store_half(first, mm(low, wd[...]).astype(BF), refs)


def plane_ffn_fwd(chain, first, hidden, weights, kept, after=()):
    length, width = hidden.shape
    units = weights[0].shape[1]
    block = length // 4
    base = 2 if first is False else 0
    steps = 4 if first is None else 2
    tiled = lambda w: spec((block, w), lambda i, *_: (i + base, 0))
    outs, out_specs = half_outs(first, block, width)
    n = len(outs)
    any_spec = pl.BlockSpec(memory_space=ANY)
    kept = tuple(kept)
    carried = kept[3:]
    kernel = functools.partial(plane_ffn_fwd_kernel, first=first)
    if first is not False:
        body_kernel = kernel
    else:
        nk, nc = len(kept), len(carried)

        def body_kernel(hl, wg, wu, wd, *refs):
            refs = refs[nk:]
            kernel(hl, wg, wu, wd, *refs[:n], *refs[n + nc :])

    out = chain(
        body_kernel,
        "ffn_fwd",
        (steps,),
        (hidden, *weights, *kept),
        [tiled(width)] + [any_spec] * (3 + len(kept)),
        outs + [(c.shape, BF) for c in carried] + [((length, units), BF)] * 3,
        out_specs + [any_spec] * len(carried) + [tiled(units)] * 3,
        after=after,
        aliases={}
        if first is not False
        else {
            **{4 + k: n + len(carried) + k for k in range(3)},
            **{7 + k: n + k for k in range(len(carried))},
        },
        scratch=[
            pltpu.VMEM(weights[0].shape, BF),
            pltpu.VMEM(weights[1].shape, BF),
            pltpu.VMEM(weights[2].shape, BF),
            pltpu.SemaphoreType.DMA((3,)),
        ],
        mib=60,
        flops=3 * length * width * units * steps // 2,
        nbytes=6 * units * width + 3 * length * units,
    )
    n += len(carried)
    return out[:n], out[n:]


def plane_ffn_bwd_kernel(dffn_ref, ga_ref, gb_ref, wd_hbm, wg_hbm, wu_hbm, *refs, first):
    refs, (wd, wg, wu, sem) = refs[:-4], refs[-4:]
    (dg_ref, du_ref), refs = refs[-2:], refs[:-2]
    wait = load_once(((wd_hbm, wd), (wg_hbm, wg), (wu_hbm, wu)), sem)
    grad = dffn_ref[...]
    wait(0)
    dact = mm_nt(grad, wd[...])
    dgate = (dact * ga_ref[...].astype(F32)).astype(BF)
    dup = (dact * gb_ref[...].astype(F32)).astype(BF)
    dg_ref[...] = dgate
    du_ref[...] = dup
    wait(1)
    part = mm_nt(dgate, wg[...])
    wait(2)
    part += mm_nt(dup, wu[...])
    store_half(first, part.astype(BF), refs)


def plane_ffn_bwd(chain, first, dffn, slopes, weights, kept, after=()):
    length, width = dffn.shape
    units = weights[0].shape[1]
    block = length // 4
    base = 2 if first is False else 0
    steps = 4 if first is None else 2
    tiled = lambda w: spec((block, w), lambda i, *_: (i + base, 0))
    outs, out_specs = half_outs(first, block, width)
    n = len(outs)
    any_spec = pl.BlockSpec(memory_space=ANY)
    kept = tuple(kept)
    kernel = functools.partial(plane_ffn_bwd_kernel, first=first)
    carried = kept[2:]
    if first is not False:
        body_kernel = kernel
    else:
        nk, nc = len(kept), len(carried)

        def body_kernel(d, ga, gb, wd, wg, wu, *refs):
            refs = refs[nk:]
            kernel(d, ga, gb, wd, wg, wu, *refs[:n], *refs[n + nc :])

    out = chain(
        body_kernel,
        "ffn_bwd",
        (steps,),
        (dffn, *slopes, weights[2], weights[0], weights[1], *kept),
        [tiled(width), tiled(units), tiled(units)] + [any_spec] * (3 + len(kept)),
        outs + [(c.shape, BF) for c in carried] + [((length, units), BF)] * 2,
        out_specs + [any_spec] * len(carried) + [tiled(units)] * 2,
        after=after,
        aliases={}
        if first is not False
        else {
            **{6 + k: n + len(carried) + k for k in range(2)},
            **{8 + k: n + k for k in range(len(carried))},
        },
        scratch=[
            pltpu.VMEM(weights[2].shape, BF),
            pltpu.VMEM(weights[0].shape, BF),
            pltpu.VMEM(weights[1].shape, BF),
            pltpu.SemaphoreType.DMA((3,)),
        ],
        mib=60,
        flops=3 * length * width * units * steps // 2,
        nbytes=6 * units * width + 4 * length * units,
    )
    n += len(carried)
    return out[:n], out[n:]


def middle_kernel(x1_ref, y1_ref, r1b_ref, r2a_ref, x2_ref, y2_ref):
    half = r1b_ref.shape[0]
    x2_ref[...] = (r1b_ref[...].astype(F32) + y1_ref[half:].astype(F32)).astype(BF)
    y2_ref[...] = (r2a_ref[...].astype(F32) + x1_ref[half:].astype(F32)).astype(BF)


def middle(chain, arrived, r1b, r2a, after=()):
    x1, y1 = arrived
    shape = r1b.shape
    return chain(
        middle_kernel,
        "middle_sum",
        (1,),
        (x1, y1, r1b, r2a),
        [const_spec(a.shape) for a in (x1, y1, r1b, r2a)],
        [(shape, BF)] * 2,
        [spec(shape, lambda i, *_: (0, 0))] * 2,
        after=after,
        mib=32,
        nbytes=16 * r1b.size,
    )


def own_sum(own, x1, y1, x2, y2):
    top = pl.program_id(0) < OWN_STEPS // 2
    direct = jnp.where(top, x1[...].astype(F32), y1[...].astype(F32))
    relayed = jnp.where(top, y2[...].astype(F32), x2[...].astype(F32))
    return own[...].astype(F32) + direct + relayed


def resid_two_kernel(own, x1, y1, x2, y2, n1_ref, gain_ref, bias_ref, out_ref):
    total = own_sum(own, x1, y1, x2, y2)
    out_ref[...] = (deep_alpha * (n1_ref[...] * gain_ref[...] + bias_ref[...]) + total).astype(BF)


def norm_one_back_kernel(own, x1, y1, x2, y2, dffn_ref, n1_ref, rstd_ref, gain_ref, low_ref, dr1_ref, sums_ref):
    total = own_sum(own, x1, y1, x2, y2)
    dh = deep_alpha * dffn_ref[...].astype(F32) + total
    normed = n1_ref[...]
    scaled = dh * gain_ref[...]
    inner = jnp.mean(scaled, axis=1, keepdims=True) + normed * jnp.mean(scaled * normed, axis=1, keepdims=True)
    dr1 = rstd_ref[:, :1] * (scaled - inner)
    dr1_ref[...] = dr1
    low_ref[...] = dr1.astype(BF)
    gain_sum = jnp.sum(dh * normed, axis=0, keepdims=True)
    bias_sum = jnp.sum(dh, axis=0, keepdims=True)

    @pl.when(pl.program_id(0) == 0)
    def _():
        sums_ref[0:1, :] = gain_sum
        sums_ref[1:2, :] = bias_sum

    @pl.when(pl.program_id(0) > 0)
    def _():
        sums_ref[0:1, :] += gain_sum
        sums_ref[1:2, :] += bias_sum


def input_grad_kernel(own, x1, y1, x2, y2, dr1_ref, out_ref):
    out_ref[...] = (deep_alpha * dr1_ref[...] + own_sum(own, x1, y1, x2, y2)).astype(BF)


OWN_STEPS = 4


def rows_spec(array_shape, tile, base=0):
    return spec((tile, array_shape[1]), lambda i, *_: (i + base, 0))


def own_step(chain, kernel, name, sums, extra, extra_specs, outs, after=()):
    block, width = sums[0].shape
    tile = block // OWN_STEPS
    middle_step = OWN_STEPS // 2
    first = spec((tile, width), lambda i, *_: (jnp.minimum(i, middle_step - 1), 0))
    later = spec((tile, width), lambda i, *_: (jnp.maximum(i - middle_step, 0), 0))
    return chain(
        kernel,
        name,
        (OWN_STEPS,),
        (*sums, *extra),
        [rows_spec((block, width), tile), first, later, later, first] + extra_specs,
        outs,
        [rows_spec(s, tile) if s[0] == block else spec(s, lambda i, *_: (0, 0)) for s, _ in outs],
        after=after,
        mib=40,
        nbytes=16 * block * width,
    )


def plane_norm_two_kernel(info_ref, order_ref, share_ref, own, r1, r2, r3a, r3b, cot_ref, gain_ref, bias_ref, *refs):
    act_ref, sums_ref, dffn_ref, held = refs[-4:]
    at = pl.program_id(0)
    half = held.shape[0]
    places = (
        (r1, 0), (r3a, 0), (r2, half), (r3b, 0), (r1, half), (r2, 0), (own, 0), (own, half),
    )
    for k, (ref, start) in enumerate(places):

        @pl.when(at == k)
        def _(ref=ref, start=start):
            held[...] = ref[start : start + half]

    resid = held[...].astype(F32)
    centered = resid - jnp.mean(resid, axis=1, keepdims=True)
    variance = jnp.mean(centered * centered, axis=1, keepdims=True)
    inv = lax.rsqrt(variance + norm_eps)
    normed = centered * inv
    gain = gain_ref[...]
    act_ref[...] = (normed * gain + bias_ref[...]).astype(BF)
    dout = cot_ref[...].astype(F32) * share_ref[0]
    scaled = dout * gain
    inner = jnp.mean(scaled, axis=1, keepdims=True) + normed * jnp.mean(scaled * normed, axis=1, keepdims=True)
    dffn_ref[...] = (inv * (scaled - inner)).astype(BF)
    gain_sum = jnp.sum(dout * normed, axis=0, keepdims=True)
    bias_sum = jnp.sum(dout, axis=0, keepdims=True)

    @pl.when(at == 0)
    def _():
        sums_ref[0:1, :] = gain_sum
        sums_ref[1:2, :] = bias_sum

    @pl.when(at > 0)
    def _():
        sums_ref[0:1, :] += gain_sum
        sums_ref[1:2, :] += bias_sum


def plane_norm_two(chain, info, order, share, row, pieces, cotangent, gain, bias, before, after=()):
    rows, length, width = cotangent.shape
    half = length // 8
    natural = spec((None, half, width), lambda i, info, order, share: (row, order[i], 0))
    held = () if before is None else (before,)
    return chain(
        plane_norm_two_kernel,
        "norm_two",
        (8,),
        (*pieces, cotangent, gain, bias, *held),
        [const_spec(p.shape) for p in pieces]
        + [natural, const_spec((1, width)), const_spec((1, width))]
        + [pl.BlockSpec(memory_space=ANY)] * len(held),
        [(cotangent.shape, BF), ((2, width), F32), ((length, width), BF)],
        [natural, spec((2, width), lambda i, *_: (0, 0)), spec((half, width), lambda i, *_: (i, 0))],
        scalars=(info, order, share),
        after=after,
        aliases={len(pieces) + 3: 0} if held else {},
        scratch=[pltpu.VMEM((half, width), BF)],
        flops=20 * length * width,
        nbytes=8 * length * width,
    )


def plane_input_back_kernel(order_ref, low_ref, high_ref, w_ref, x1_ref, y1_ref, r1b_ref, r2a_ref, own_ref):
    at = pl.program_id(0)
    half = low_ref.shape[0]
    part = mm_nt(jnp.concatenate([low_ref[...], high_ref[...]], axis=0), w_ref[...]).astype(BF)

    @pl.when(at == 0)
    def _():
        x1_ref[...] = part

    @pl.when(at == 1)
    def _():
        y1_ref[...] = part

    @pl.when(at == 2)
    def _():
        r1b_ref[...] = part[:half]
        r2a_ref[...] = part[half:]

    @pl.when(at == 3)
    def _():
        own_ref[...] = part


def plane_input_back(chain, order, dqkv, qkv_weight, after=()):
    length, columns = dqkv.shape
    width = qkv_weight.shape[0]
    block = length // 4
    half = block // 2
    sizes = [block, block, half, half, block]
    return chain(
        plane_input_back_kernel,
        "input_back",
        (4,),
        (dqkv, dqkv, qkv_weight),
        [
            spec((half, columns), lambda i, order: (order[2 * i], 0)),
            spec((half, columns), lambda i, order: (order[2 * i + 1], 0)),
            const_spec(qkv_weight.shape),
        ],
        [((s, width), BF) for s in sizes],
        [spec((s, width), lambda i, *_: (0, 0)) for s in sizes],
        scalars=(order,),
        after=after,
        flops=2 * length * width * columns,
        nbytes=2 * width * columns + 4 * length * width,
    )


def plane_place_kernel(order_ref, own, r1, r2, r3a, r3b, *refs):
    out_ref = refs[-1]
    at = pl.program_id(0)
    half = r3a.shape[0]
    for k, ref in enumerate((own, r1, r2)):

        @pl.when(at == k)
        def _(ref=ref):
            out_ref[...] = ref[...]

    @pl.when(at == 3)
    def _():
        out_ref[:half] = r3a[...]
        out_ref[half:] = r3b[...]


def plane_place(chain, info, row, pieces, shape, before, after=()):
    rows, length, width = shape
    block = length // 4
    held = () if before is None else (before,)
    return chain(
        plane_place_kernel,
        "place",
        (4,),
        (*pieces, *held),
        [const_spec(p.shape) for p in pieces] + [pl.BlockSpec(memory_space=ANY)] * len(held),
        [(shape, BF)],
        [spec((None, block, width), lambda i, info: (row, i ^ info[0], 0))],
        scalars=(info,),
        after=after,
        aliases={len(pieces): 0} if held else {},
        mib=32,
        nbytes=4 * length * width,
    )[0]


def panels(ref, value):
    for c in range(value.shape[1] // 128):
        ref[c] = value[:, c * 128 : (c + 1) * 128].astype(BF)


def grad_rows_kernel(info_ref, left_a, left_b, right_a, right_b, send, keep, *, steps):
    at = pl.program_id(0)
    value = mm(left_a[...].T, right_a[...]) + mm(left_b[...].T, right_b[...])

    @pl.when(at < steps)
    def _():
        panels(send, value)

    @pl.when(at >= steps)
    def _():
        panels(keep, value)


def lhs_spec(lhs, tile, index, row):
    if lhs.ndim == 3:
        return spec((None, lhs.shape[1], tile), lambda *a: (row, 0, index(*a)))
    return spec((lhs.shape[0], tile), lambda *a: (0, index(*a)))


def grad_rows(chain, info, lefts, rights, after=()):
    rows = lefts[0].shape[-1]
    tile = 256
    steps = rows // tile // 2
    length, columns = rights[0].shape

    def at(i, info):
        other = (1 - info[3]) * steps + i
        own = info[3] * steps + i - steps
        return jnp.where(i < steps, other, own)

    shape = (columns // 128, rows // 2, 128)
    out = chain(
        functools.partial(grad_rows_kernel, steps=steps),
        "grad_rows",
        (2 * steps,),
        (*lefts, *rights),
        [lhs_spec(lefts[r], tile, at, r) for r in range(2)] + [const_spec(r.shape) for r in rights],
        [(shape, BF)] * 2,
        [
            spec((shape[0], tile, 128), lambda i, *_: (0, jnp.minimum(i, steps - 1), 0)),
            spec((shape[0], tile, 128), lambda i, *_: (0, jnp.maximum(i - steps, 0), 0)),
        ],
        scalars=(info,),
        after=after,
        flops=4 * rows * length * columns,
        nbytes=2 * rows * columns + 4 * rows * length,
    )
    return out[0].reshape(-1, 128), out[1].reshape(-1, 128)


def grad_columns_kernel(info_ref, left_a, left_b, right_a, right_b, send, keep, turned_a, turned_b, held):
    @pl.when(pl.program_id(0) == 0)
    def _():
        turned_a[...] = left_a[...].T
        turned_b[...] = left_b[...].T

    held[...] = mm(turned_a[...], right_a[...]) + mm(turned_b[...], right_b[...])
    half = held.shape[0] // 2
    core = info_ref[3]
    panels(send, held[pl.ds(pl.multiple_of((1 - core) * half, 8), half), :])
    panels(keep, held[pl.ds(pl.multiple_of(core * half, 8), half), :])


def grad_columns(chain, info, lefts, rights, after=()):
    length, rows = lefts[0].shape
    columns = rights[0].shape[1]
    tile = 256
    shape = (columns // 128, rows // 2, 128)
    out = chain(
        grad_columns_kernel,
        "grad_columns",
        (columns // tile,),
        (*lefts, *rights),
        [const_spec(left.shape) for left in lefts] + [spec((length, tile), lambda i, *_: (0, i))] * 2,
        [(shape, BF)] * 2,
        [spec((tile // 128, rows // 2, 128), lambda i, *_: (i, 0, 0))] * 2,
        scalars=(info,),
        after=after,
        scratch=[pltpu.VMEM((rows, length), BF)] * 2 + [pltpu.VMEM((rows, tile), F32)],
        flops=4 * rows * length * columns,
        nbytes=2 * rows * columns + 4 * length * (rows + columns),
    )
    return out[0].reshape(-1, 128), out[1].reshape(-1, 128)


def grad_plain_kernel(left_a, left_b, right_a, right_b, out_ref):
    out_ref[...] = (mm(left_a[...].T, right_a[...]) + mm(left_b[...].T, right_b[...])).astype(BF)


def grad_plain(chain, lefts, rights, after=()):
    rows = lefts[0].shape[-1]
    tile = 256
    length, columns = rights[0].shape
    return chain(
        grad_plain_kernel,
        "grad_plain",
        (rows // tile,),
        (*lefts, *rights),
        [lhs_spec(lefts[r], tile, lambda i, *_: i, r) for r in range(2)] + [const_spec(r.shape) for r in rights],
        [((rows, columns), BF)],
        [spec((tile, columns), lambda i, *_: (i, 0))],
        after=after,
        flops=4 * rows * length * columns,
        nbytes=2 * rows * columns + 4 * rows * length,
    )[0]


def grad_plain_columns_kernel(left_a, left_b, right_a, right_b, out_ref, turned_a, turned_b):
    @pl.when(pl.program_id(0) == 0)
    def _():
        turned_a[...] = left_a[...].T
        turned_b[...] = left_b[...].T

    out_ref[...] = (mm(turned_a[...], right_a[...]) + mm(turned_b[...], right_b[...])).astype(BF)


def grad_plain_columns(chain, lefts, rights, after=()):
    length, rows = lefts[0].shape
    columns = rights[0].shape[1]
    tile = 256
    return chain(
        grad_plain_columns_kernel,
        "grad_plain_columns",
        (columns // tile,),
        (*lefts, *rights),
        [const_spec(left.shape) for left in lefts] + [spec((length, tile), lambda i, *_: (0, i))] * 2,
        [((rows, columns), BF)],
        [spec((rows, tile), lambda i, *_: (0, i))],
        after=after,
        scratch=[pltpu.VMEM((rows, length), BF)] * 2,
        flops=4 * rows * length * columns,
        nbytes=2 * rows * columns + 4 * length * (rows + columns),
    )[0]


def grad_out(lhs, pieces, me):
    block = pieces[0].shape[0]
    half = block // 2
    total = 0.0
    for r, piece in enumerate(pieces[:3]):
        part = lhs[pl.ds(pl.multiple_of((me ^ r) * block, half), block), :]
        total = total + mm(part.T, piece[...])
    for lower, piece in ((0, pieces[3]), (half, pieces[4])):
        part = lhs[pl.ds(pl.multiple_of((me ^ 3) * block + lower, half), half), :]
        total = total + mm(part.T, piece[...])
    return total


def grad_out_kernel(info_ref, left_a, left_b, *refs):
    pieces_a, pieces_b, (send, keep, held) = refs[:5], refs[5:10], refs[10:]
    held[...] = grad_out(left_a, pieces_a, info_ref[0]) + grad_out(left_b, pieces_b, info_ref[0])
    half = held.shape[0] // 2
    core = info_ref[3]
    panels(send, held[pl.ds(pl.multiple_of((1 - core) * half, 8), half), :])
    panels(keep, held[pl.ds(pl.multiple_of(core * half, 8), half), :])


def plane_grad_out(chain, info, lefts, pieces, after=()):
    length, rows = lefts[0].shape
    columns = pieces[0][0].shape[1]
    tile = 512
    shape = (columns // 128, rows // 2, 128)
    every = (*pieces[0], *pieces[1])
    out = chain(
        grad_out_kernel,
        "grad_out",
        (columns // tile,),
        (*lefts, *every),
        [const_spec(left.shape) for left in lefts]
        + [spec((p.shape[0], tile), lambda i, *_: (0, i)) for p in every],
        [(shape, BF)] * 2,
        [spec((tile // 128, rows // 2, 128), lambda i, *_: (i, 0, 0))] * 2,
        scalars=(info,),
        after=after,
        scratch=[pltpu.VMEM((rows, tile), F32)],
        flops=4 * rows * length * columns,
        nbytes=2 * rows * columns + 4 * length * (rows + columns),
    )
    return out[0].reshape(-1, 128), out[1].reshape(-1, 128)


class Line:
    GRID = 4

    def __init__(self, chain, edge):
        self.chain, self.edge = chain, edge
        self.pending = []
        self.slots = []
        self.step = 0
        self.done = {}
        self.first = self.second = None
        self.sent = self.mid = None

    def add(self, name, keep, got, chunks):
        for k in range(chunks):
            self.pending.append((name, keep, got, k, keep.shape[0] // chunks, keep.shape[0]))

    def get(self, j):
        return self.slots[j] if j >= 0 else None

    def busy(self):
        return bool(self.pending) or any(self.slots[-3:])

    def complete(self, name):
        return not any(slot and slot[0] == name for slot in self.pending + self.slots[-3:])

    def advance(self, after=()):
        j = self.step
        self.slots.append(self.pending.pop(0) if self.pending else None)
        new, cur, prev, last = self.get(j), self.get(j - 1), self.get(j - 2), self.get(j - 3)
        ins, in_specs, outs, out_specs, aliases, roles = [], [], [], [], {}, []
        grid = self.GRID

        def give(array, rows, base, role, when):
            block = rows // grid
            if when is None:
                index = lambda i, edge: (base + i, 0)
            elif when:
                index = lambda i, edge: (base + i * edge[0], 0)
            else:
                index = lambda i, edge: (base + i * (1 - edge[0]), 0)
            ins.append(array)
            in_specs.append(spec((block, 128), index))
            roles.append(role)

        if new:
            name, keep, got, k, rows, _ = new
            give(keep, rows, k * grid, "new_keep", True)
            give(got, rows, k * grid, "new_got", True)
        if cur:
            name, keep, got, k, rows, _ = cur
            give(keep, rows, k * grid, "cur_keep", False)
            give(got, rows, k * grid, "cur_got", False)
            give(self.first, rows, 0, "cur_in", False)
        if prev:
            rows = prev[4]
            give(self.mid, rows, 0, "prev_mid", False)
            give(self.second, rows, 0, "prev_in", False)
        if last:
            rows = last[4]
            give(self.first, rows, 0, "last_in", True)
            give(self.sent, rows, 0, "last_sent", False)
            if last[3] > 0:
                ins.append(self.done[last[0]])
                in_specs.append(pl.BlockSpec(memory_space=ANY))
                roles.append("held")
        names = []
        if new or prev:
            rows = max(c[4] for c in (new, prev) if c)
            outs.append(((rows, 128), BF))
            out_specs.append(pl.BlockSpec((rows, 128), lambda i, *_: (0, 0)))
            names.append("sent")
        if cur:
            outs.append(((cur[4], 128), BF))
            out_specs.append(spec((cur[4] // grid, 128), lambda i, *_: (i, 0)))
            names.append("mid")
        if last:
            base = last[3] * grid
            outs.append(((last[5], 128), BF))
            out_specs.append(spec((last[4] // grid, 128), lambda i, *_, base=base: (base + i, 0)))
            names.append("done")
            if last[3] > 0:
                aliases = {len(ins) - 1: len(outs) - 1}

        def kernel(edge_ref, *refs):
            src = dict(zip(roles, refs[: len(roles)]))
            dst = dict(zip(names, refs[len(roles) :]))
            at = pl.program_id(0)
            is_edge = edge_ref[0] == 1
            f32 = lambda r: src[r][...].astype(F32)

            if new:
                @pl.when(is_edge)
                def _():
                    block = new[4] // grid
                    rows = pl.ds(pl.multiple_of(at * block, block), block)
                    dst["sent"][rows, :] = (f32("new_keep") + f32("new_got")).astype(BF)

            @pl.when(jnp.logical_not(is_edge))
            def _():
                if cur:
                    dst["mid"][...] = (f32("cur_keep") + f32("cur_got") + f32("cur_in")).astype(BF)
                if prev:
                    block = prev[4] // grid
                    rows = pl.ds(pl.multiple_of(at * block, block), block)
                    dst["sent"][rows, :] = (f32("prev_mid") + f32("prev_in")).astype(BF)

            if last:
                @pl.when(is_edge)
                def _():
                    dst["done"][...] = src["last_in"][...]

                @pl.when(jnp.logical_not(is_edge))
                def _():
                    dst["done"][...] = src["last_sent"][...]

        out = self.chain(
            kernel,
            "line_step",
            (grid,),
            tuple(ins),
            in_specs,
            outs,
            out_specs,
            scalars=(self.edge,),
            after=after,
            aliases=aliases,
            mib=32,
            nbytes=6 * 5632 * 256,
        )
        got = dict(zip(names, out))
        if "done" in got:
            self.done[last[0]] = got["done"]
        self.sent = got.get("sent")
        self.mid = got.get("mid")
        if self.sent is not None:
            self.first = lax.ppermute(self.sent, "obj", [(0, 1), (3, 2), (1, 0), (2, 3)])
        if self.mid is not None:
            self.second = lax.ppermute(self.mid, "obj", [(1, 2), (2, 1)])
        self.step += 1


def widen_kernel(info_ref, mine_ref, theirs_ref, out_ref, *, steps):
    at = pl.program_id(0)

    @pl.when(at < steps)
    def _():
        for c in range(mine_ref.shape[0]):
            out_ref[:, c * 128 : (c + 1) * 128] = mine_ref[c].astype(F32)

    @pl.when(at >= steps)
    def _():
        for c in range(theirs_ref.shape[0]):
            out_ref[:, c * 128 : (c + 1) * 128] = theirs_ref[c].astype(F32)


def widen(chain, info, mine, theirs, rows, columns, after=()):
    count = columns // 128
    half = rows // 2
    tile = 176 if half % 176 == 0 else min(256, half)
    steps = half // tile
    mine, theirs = (a.reshape(count, half, 128) for a in (mine, theirs))

    def at(i, info):
        return jnp.where(i < steps, info[3] * steps + i, (1 - info[3]) * steps + i - steps)

    return chain(
        functools.partial(widen_kernel, steps=steps),
        "widen",
        (2 * steps,),
        (mine, theirs),
        [
            spec((count, tile, 128), lambda i, *_: (0, jnp.minimum(i, steps - 1), 0)),
            spec((count, tile, 128), lambda i, *_: (0, jnp.maximum(i - steps, 0), 0)),
        ],
        [((rows, columns), F32)],
        [spec((tile, columns), lambda i, info: (at(i, info), 0))],
        scalars=(info,),
        after=after,
        mib=32,
        nbytes=6 * rows * columns,
    )[0]


def cast_kernel(in_ref, out_ref):
    out_ref[...] = in_ref[...].astype(F32)


def cast(chain, array, after=()):
    rows, columns = array.shape
    tile = 176 if rows % 256 else 256
    return chain(
        cast_kernel, "cast", (rows // tile,), (array,), [rows_spec(array.shape, tile)],
        [(array.shape, F32)], [rows_spec(array.shape, tile)], after=after,
    )[0]


def total_sum_kernel(in_ref, out_ref):
    out_ref[...] = jnp.sum(in_ref[...], axis=0)


def total_sum(chain, array):
    shape = array.shape[1:]
    return chain(
        total_sum_kernel, "total_sum", (1,), (array,), [const_spec(array.shape)], [(shape, F32)],
        [spec(shape, lambda i, *_: (0, 0))],
    )[0]


def plane_body(
    tokens,
    cotangent,
    segment_ids,
    mlm_mask,
    glm_prefix,
    glm_span,
    qkv_weight,
    out_weight,
    gate_weight,
    up_weight,
    down_weight,
    norm1_gain,
    norm1_bias,
    norm2_gain,
    norm2_bias,
):
    seq_here, length, width = tokens.shape
    data_ways = lax.axis_size("dp")
    objective_ways = lax.axis_size("obj")
    me = lax.axis_index("tensor").astype(jnp.int32)
    core = lax.axis_index("dp").astype(jnp.int32)
    at_obj = lax.axis_index("obj")
    edge = ((at_obj == 0) | (at_obj == objective_ways - 1)).astype(jnp.int32).reshape(1)
    block = length // 4
    units = gate_weight.shape[1]
    rows_all = mlm_mask.shape[0]
    masked_limit = seq_here * data_ways * (objective_ways // 2)
    row_ids = jnp.arange(rows_all, dtype=jnp.int32)
    counts = jnp.where(row_ids < masked_limit, jnp.sum(mlm_mask, axis=1), glm_span).astype(F32)
    weight_all = counts * rows_all / jnp.sum(counts)
    first_row = (at_obj * data_ways + core) * seq_here
    share_here = lax.dynamic_slice_in_dim(weight_all, first_row, seq_here)
    prefix_here = lax.dynamic_slice_in_dim(glm_prefix, first_row, seq_here)
    span_here = lax.dynamic_slice_in_dim(glm_span, first_row, seq_here)
    open_here = jnp.where(first_row < masked_limit, length, prefix_here)
    info = [jnp.stack([me, open_here[r], prefix_here[r] + span_here[r], core]) for r in range(2)]
    order = jnp.stack([2 * (me ^ r) + h for r, h in ORDER])
    share = [share_here[r : r + 1] for r in range(2)]
    cosine, sine = constant_tables(length)
    segc = [segment_ids[r].reshape(length, 1) for r in range(2)]
    segr = [segment_ids[r].reshape(1, length) for r in range(2)]
    gain1, bias1 = norm1_gain.reshape(1, width), norm1_bias.reshape(1, width)
    gain2, bias2 = norm2_gain.reshape(1, width), norm2_bias.reshape(1, width)
    weights = (gate_weight, up_weight, down_weight)
    chain = Chain()
    A, B = 0, 1

    ow_half = out_weight.shape[0] // 2
    ow_own = lax.dynamic_slice_in_dim(out_weight, core * ow_half, ow_half)
    owx, owy = pair_swap(ow_own, ow_own)

    def attention(r, after=()):
        return plane_attn_fwd(chain, info[r], r, tokens, qkv_weight, cosine, sine, segc[r], segr[r], after)

    def out_and_norm(r, ol_pieces, after=()):
        return plane_out_norm(
            chain, info[r], order, r, ol_pieces, out_weight, ow_mine, ow_other, tokens, gain1, bias1, after
        )

    qkv, ol, lse, hl, n1, rstd = {}, {}, {}, {}, {}, {}
    qkv[A], ol[A], lse[A] = attention(A)
    owra, owrb = forward(chain, owx, owy)
    olx, oly, olr = {}, {}, {}
    olx[A], oly[A] = pair_swap(ol[A], ol[A])
    qkv[B], ol[B], lse[B] = attention(B)
    ow_mine = ow_join(chain, (owx, owy, owra, owrb), after=(olx[A], oly[A]))
    ow_other = lax.ppermute(ow_mine, "dp", CORES)
    olr[A], ol[B] = forward(chain, olx[A], oly[A], (ol[B],))
    (ol[B],) = relay(chain, (ol[B],), after=olr[A])
    olx[B], oly[B] = pair_swap(ol[B], ol[B])
    hl[A], n1[A], rstd[A] = out_and_norm(A, (ol[A], olx[A], oly[A], *olr[A]))
    vec = const_spec((1, width))
    tile = block // OWN_STEPS
    full = rows_spec((block, width), tile)
    ff, fb, ib, rs1, rs2 = {}, {}, {}, {}, {}
    resid, rx, ry, rr = {}, {}, {}, {}

    def sums_of(own, first, second):
        return (own, first[0], first[1], second[0], second[1])

    def second_resid(r, after=()):
        return own_step(
            chain, resid_two_kernel, "resid_two", sums_of(ff[r][2], rs1[r], rs2[r]), (n1[r], gain1, bias1),
            [full, vec, vec], [((block, width), BF)], after,
        )[0]

    def second_norm(r, before, after=()):
        pieces = (resid[r], rx[r], ry[r], *rr[r])
        return plane_norm_two(
            chain, info[r], order, share[r], r, pieces, cotangent, gain2, bias2, before, after
        )

    def first_norm_back(r, after=()):
        return own_step(
            chain, norm_one_back_kernel, "norm_one_back", sums_of(fb[r][2], rs1[r], rs2[r]),
            (dffn[r], n1[r], rstd[r], gain1),
            [rows_spec((block, width), tile, 3 * OWN_STEPS), full, rows_spec((block, HEAD_DIM), tile), vec],
            [((block, width), BF), ((block, width), F32), ((2, width), F32)], after,
        )

    olr[B] = forward(chain, olx[B], oly[B])
    sent, kept_a = plane_ffn_fwd(chain, None, hl[A], weights, ())
    rs1[A], ff[A] = pair_swap(*sent[:2]), sent[2:]
    hl[B], n1[B], rstd[B] = out_and_norm(B, (ol[B], olx[B], oly[B], *olr[B]))
    rs2[A] = pair_swap(*middle(chain, rs1[A], ff[A][0], ff[A][1]))
    sent, kept = plane_ffn_fwd(chain, True, hl[B], weights, ())
    resid[A] = second_resid(A)
    rx[A], ry[A] = pair_swap(resid[A], resid[A])
    ff[B], kept_b = plane_ffn_fwd(chain, False, hl[B], weights, (*kept, *sent))
    al, slopes = {A: kept_a[0], B: kept_b[0]}, {A: kept_a[1:], B: kept_b[1:]}
    rr[A] = forward(chain, rx[A], ry[A])
    rs1[B] = pair_swap(*relay(chain, ff[B][3:], after=rr[A]))

    sums2, dffn, dgu, sums1, dr1, dattn, dax, day, dar = {}, {}, {}, {}, {}, {}, {}, {}, {}
    pieces, dqkv, dx, dxx, dxy, dxr, outs = {}, {}, {}, {}, {}, {}, {}

    def attention_back(r, after=()):
        pieces[r] = (dattn[r], dax[r], day[r], *dar[r])
        return plane_attn_bwd(
            chain, info[r], qkv[r], pieces[r], out_weight, lse[r], cosine, sine, segc[r], segr[r], after
        )

    def input_back_sums(r, after=()):
        x1, y1, r1b, r2a, own = plane_input_back(chain, order, dqkv[r], qkv_weight, after)
        ib[r] = (r1b, r2a, own)
        rs1[r] = pair_swap(x1, y1)

    def input_grad_own(r, after=()):
        return own_step(
            chain, input_grad_kernel, "input_grad", sums_of(ib[r][2], rs1[r], rs2[r]), (dr1[r],), [full],
            [((block, width), BF)], after,
        )[0]

    theirs = {}

    def begin_finish(name):
        theirs[name] = lax.ppermute(line.done[name], "dp", CORES)

    def finish_matrix(name, rows, columns, after=()):
        outs[name] = widen(chain, info[B], line.done[name], theirs[name], rows, columns, after)

    def middle_sums(r, after=()):
        part = fb[r] if r not in ib else ib[r]
        rs2[r] = pair_swap(*middle(chain, rs1[r], part[0], part[1], after))

    line = Line(chain, edge)
    activations, sums2[A], dffn[A] = second_norm(A, None)
    sent, kept = plane_ffn_bwd(chain, True, dffn[A], slopes[A], weights, ())
    rs1[A] = pair_swap(*sent)
    rs2[B] = pair_swap(*middle(chain, rs1[B], ff[B][0], ff[B][1]))
    fb[A], dgu[A] = plane_ffn_bwd(chain, False, dffn[A], slopes[A], weights, kept)
    resid[B] = second_resid(B)
    rx[B], ry[B] = pair_swap(resid[B], resid[B])
    middle_sums(A)
    rr[B] = forward(chain, rx[B], ry[B])
    dattn[A], dr1[A], sums1[A] = first_norm_back(A)
    dax[A], day[A] = pair_swap(dattn[A], dattn[A])
    activations, sums2[B], dffn[B] = second_norm(B, activations)
    down_update = grad_plain_columns(chain, (al[A], al[B]), (dffn[A], dffn[B]))
    down_sum = lax.psum(down_update, ("obj", "dp"))
    dar[A] = forward(chain, dax[A], day[A])
    sent, dgu[B] = plane_ffn_bwd(chain, None, dffn[B], slopes[B], weights, ())
    fb[B] = sent[2:]
    rs1[B] = pair_swap(*sent[:2])
    chain.close(*dar[A])
    gate_send, gate_keep = grad_rows(chain, info[B], (hl[A], hl[B]), (dgu[A][0], dgu[B][0]))
    gate_got = lax.ppermute(gate_send, "dp", CORES)
    line.add("gate", gate_keep, gate_got, 2)
    middle_sums(B)
    up_send, up_keep = grad_rows(chain, info[B], (hl[A], hl[B]), (dgu[A][1], dgu[B][1]))
    up_got = lax.ppermute(up_send, "dp", CORES)
    line.add("up", up_keep, up_got, 2)
    chain.close(gate_got)
    dattn[B], dr1[B], sums1[B] = first_norm_back(B)
    dax[B], day[B] = pair_swap(dattn[B], dattn[B])
    chain.close(up_got)
    line.advance()
    dqkv[A] = attention_back(A)
    dar[B] = forward(chain, dax[B], day[B])
    input_back_sums(A)
    line.advance()
    dqkv[B] = attention_back(B)
    line.advance()
    middle_sums(A)
    qkv_send, qkv_keep = grad_rows(chain, info[B], (tokens, tokens), (dqkv[A], dqkv[B]), after=(down_sum,))
    qkv_got = lax.ppermute(qkv_send, "dp", CORES)
    line.add("qkv", qkv_keep, qkv_got, 3)
    dx[A] = input_grad_own(A)
    dxx[A], dxy[A] = pair_swap(dx[A], dx[A])
    line.advance()
    input_back_sums(B)
    chain.close(qkv_got, dxx[A], dxy[A])
    out_send, out_keep = plane_grad_out(chain, info[B], (ol[A], ol[B]), (pieces[A], pieces[B]))
    line.advance()
    out_got = lax.ppermute(out_send, "dp", CORES)
    line.add("out", out_keep, out_got, 1)
    middle_sums(B)
    outs["down"] = cast(chain, down_sum)
    line.advance()
    chain.close(out_got)
    begin_finish("gate")
    dxr[A] = forward(chain, dxx[A], dxy[A])
    dx[B] = input_grad_own(B)
    dxx[B], dxy[B] = pair_swap(dx[B], dx[B])
    chain.close(theirs["gate"])
    line.advance()
    begin_finish("up")
    finish_matrix("gate", width, units)
    input_grad = plane_place(chain, info[A], A, (dx[A], dxx[A], dxy[A], *dxr[A]), tokens.shape, None)
    dxr[B] = forward(chain, dxx[B], dxy[B])
    mine = (me == 0).astype(F32)
    sums = jnp.concatenate([sums1[A] + sums1[B], (sums2[A] + sums2[B]) * mine])
    every_sum = lax.all_gather(sums, ("obj", "dp", "tensor"))
    line.advance()
    finish_matrix("up", width, units)
    input_grad = plane_place(chain, info[B], B, (dx[B], dxx[B], dxy[B], *dxr[B]), tokens.shape, input_grad)
    line.advance()
    sums = total_sum(chain, every_sum)
    line.advance()
    begin_finish("qkv")
    finish_matrix("qkv", width, qkv_weight.shape[1])
    line.advance()
    begin_finish("out")
    finish_matrix("out", out_weight.shape[0], width)

    return (
        activations,
        input_grad,
        outs["qkv"],
        outs["out"],
        outs["gate"],
        outs["up"],
        outs["down"],
        sums[0],
        sums[1],
        sums[2],
        sums[3],
    )


def body(*args):
    if plane_case(args[0].shape, args[7].shape, args[10].shape):
        return plane_body(*args)
    return general_body(*args)


def solution(mesh):
    rows3 = P(("obj", "dp"), None, None)
    in_specs = (
        rows3,
        rows3,
        P(("obj", "dp"), None),
        P(),
        P(),
        P(),
        P(None, "tensor"),
        P("tensor", None),
        P(None, "tensor"),
        P(None, "tensor"),
        P("tensor", None),
        P(),
        P(),
        P(),
        P(),
    )
    out_specs = (
        rows3,
        rows3,
        P(None, "tensor"),
        P("tensor", None),
        P(None, "tensor"),
        P(None, "tensor"),
        P("tensor", None),
        P(),
        P(),
        P(),
        P(),
    )
    return jax.shard_map(body, mesh=mesh, in_specs=in_specs, out_specs=out_specs, check_vma=False)
```

```python
import functools
import math

import jax
import jax.numpy as jnp
import numpy as np
from jax import lax
from jax.experimental import pallas as pl
from jax.experimental.pallas import tpu as pltpu
from jax.sharding import PartitionSpec as P

HEAD_DIM = 128
deep_alpha = math.sqrt(48.0)
norm_eps = 1e-05
mask_fill = -1e30
score_scale = 1.0 / math.sqrt(HEAD_DIM)
MIB = 1024 * 1024
BF = jnp.bfloat16
F32 = jnp.float32
ANY = pl.ANY


def mm(a, b):
    return lax.dot_general(a, b, (((1,), (0,)), ((), ())), preferred_element_type=F32)


def mm_nt(a, b):
    return lax.dot_general(a, b, (((1,), (1,)), ((), ())), preferred_element_type=F32)


def mm_tn(a, b):
    return lax.dot_general(a, b, (((0,), (0,)), ((), ())), preferred_element_type=F32)


def params(mib, grid_rank=1):
    return pltpu.CompilerParams(
        vmem_limit_bytes=mib * MIB, dimension_semantics=("arbitrary",) * grid_rank
    )


def cost(flops, nbytes, trans=0):
    return pl.CostEstimate(flops=int(flops), bytes_accessed=int(nbytes), transcendentals=int(trans))


def const_spec(shape):
    zeros = (0,) * len(shape)
    return pl.BlockSpec(shape, lambda *_: zeros, pipeline_mode=pl.Buffered(1))


def rotary_tables(seq_length):
    half_width = HEAD_DIM // 2
    frequency = jnp.exp(
        jnp.arange(half_width, dtype=F32) * (-2.0 * math.log(10000.0) / HEAD_DIM)
    )
    angles = jnp.arange(seq_length, dtype=F32)[:, None] * frequency[None, :]
    sine = jnp.sin(angles)
    cosine = jnp.cos(angles)
    return jnp.concatenate([cosine, cosine], axis=1), jnp.concatenate([-sine, sine], axis=1)


def fill_bias(info_ref, segc_ref, segr_ref, bias_ref, tile):
    length = bias_ref.shape[0]
    prefix, limit = info_ref[1], info_ref[2]

    def one(step, carry):
        rows = pl.ds(pl.multiple_of(step * tile, tile), tile)
        key_pos = lax.broadcasted_iota(jnp.int32, (tile, length), 0) + step * tile
        query_pos = lax.broadcasted_iota(jnp.int32, (tile, length), 1)
        same = segc_ref[rows, :] == segr_ref[...]
        open_keys = (
            (key_pos < prefix)
            | ((key_pos <= query_pos) & (key_pos < limit))
            | (key_pos == query_pos)
        )
        bias_ref[rows, :] = jnp.where(same & open_keys, 0.0, mask_fill)
        return carry

    lax.fori_loop(0, length // tile, one, 0)


def attn_fwd_kernel(
    info_ref, x_ref, w_ref, cos_ref, sin_ref, segc_ref, segr_ref, qkv_ref, ol_ref, lse_ref, bias_ref, tile
):
    length = x_ref.shape[0]

    @pl.when(pl.program_id(0) == 0)
    def _():
        fill_bias(info_ref, segc_ref, segr_ref, bias_ref, tile)

    for step in range(length // tile):
        rows = pl.ds(step * tile, tile)
        proj = mm(x_ref[rows, :], w_ref[...])
        cosine, sine = cos_ref[rows, :], sin_ref[rows, :]
        for part in range(2):
            piece = proj[:, part * HEAD_DIM : (part + 1) * HEAD_DIM]
            turned = piece * cosine + pltpu.roll(piece, HEAD_DIM // 2, 1) * sine
            qkv_ref[rows, part * HEAD_DIM : (part + 1) * HEAD_DIM] = turned.astype(BF)
        qkv_ref[rows, 2 * HEAD_DIM :] = proj[:, 2 * HEAD_DIM :].astype(BF)
    keys = qkv_ref[:, HEAD_DIM : 2 * HEAD_DIM]
    values_t = qkv_ref[:, 2 * HEAD_DIM :].astype(F32).T.astype(BF)
    for step in range(length // tile):
        rows = pl.ds(step * tile, tile)
        queries = qkv_ref[rows, :HEAD_DIM]
        scores = mm_nt(keys, queries) * score_scale + bias_ref[:, rows]
        top = jnp.max(scores, axis=0, keepdims=True)
        exponent = jnp.exp(scores - top)
        total = jnp.sum(exponent, axis=0, keepdims=True)
        attended = mm(values_t, exponent.astype(BF)) * (1.0 / total)
        ol_ref[rows, :] = attended.T.astype(BF)
        lse_ref[:, rows] = top + jnp.log(total)


def attn_fwd(info, row, tokens, qkv_weight, cosine, sine, segc, segr):
    _, length, width = tokens.shape
    heads = qkv_weight.shape[1] // (3 * HEAD_DIM)
    tile = min(256, length)
    grid_spec = pltpu.PrefetchScalarGridSpec(
        num_scalar_prefetch=1,
        grid=(heads,),
        in_specs=[
            pl.BlockSpec((None, length, width), lambda h, *_: (row, 0, 0), pipeline_mode=pl.Buffered(1)),
            pl.BlockSpec((width, 3 * HEAD_DIM), lambda h, *_: (0, h)),
            const_spec((length, HEAD_DIM)),
            const_spec((length, HEAD_DIM)),
            const_spec((length, 1)),
            const_spec((1, length)),
        ],
        out_specs=[
            pl.BlockSpec((length, 3 * HEAD_DIM), lambda h, *_: (0, h)),
            pl.BlockSpec((length, HEAD_DIM), lambda h, *_: (0, h)),
            pl.BlockSpec((None, 1, length), lambda h, *_: (h, 0, 0)),
        ],
        scratch_shapes=[pltpu.VMEM((length, length), F32)],
    )
    return pl.pallas_call(
        functools.partial(attn_fwd_kernel, tile=tile),
        grid_spec=grid_spec,
        out_shape=[
            jax.ShapeDtypeStruct((length, heads * 3 * HEAD_DIM), BF),
            jax.ShapeDtypeStruct((length, heads * HEAD_DIM), BF),
            jax.ShapeDtypeStruct((heads, 1, length), F32),
        ],
        compiler_params=params(48),
        cost_estimate=cost(
            heads * (2 * length * width * 384 + 8 * length * length * HEAD_DIM),
            2 * length * width + 2 * width * heads * 384 + 8 * length * heads * 128,
        ),
        name="attn_fwd",
    )(info, tokens, qkv_weight, cosine, sine, segc, segr)


def attn_bwd_kernel(
    info_ref, qkv_ref, dol_ref, lse_ref, cos_ref, sin_ref, segc_ref, segr_ref, dqkv_ref,
    bias_ref, dol_nat, dk_ref, dv_ref, tile
):
    length = qkv_ref.shape[0]
    ways, block, _ = dol_ref.shape
    me = info_ref[0]

    @pl.when(pl.program_id(0) == 0)
    def _():
        fill_bias(info_ref, segc_ref, segr_ref, bias_ref, tile)

    for at in range(ways):
        dol_nat[pl.ds(at * block, block), :] = dol_ref[me ^ at]
    keys = qkv_ref[:, HEAD_DIM : 2 * HEAD_DIM]
    values = qkv_ref[:, 2 * HEAD_DIM :]
    keys_t = keys.astype(F32).T.astype(BF)
    for step in range(length // tile):
        rows = pl.ds(step * tile, tile)
        queries = qkv_ref[rows, :HEAD_DIM]
        dol = dol_nat[rows, :]
        scores = mm_nt(keys, queries) * score_scale + bias_ref[:, rows]
        probs = jnp.exp(scores - lse_ref[:, rows])
        dp = mm_nt(values, dol)
        inner = jnp.sum(probs * dp, axis=0, keepdims=True)
        draw = (probs * (dp - inner) * score_scale).astype(BF)
        dv = mm(probs.astype(BF), dol)
        dk = mm(draw, queries)
        if step == 0:
            dv_ref[...] = dv
            dk_ref[...] = dk
        else:
            dv_ref[...] += dv
            dk_ref[...] += dk
        dq = mm(keys_t, draw).T
        turned = dq * cos_ref[rows, :] - pltpu.roll(dq, HEAD_DIM // 2, 1) * sin_ref[rows, :]
        dqkv_ref[rows, :HEAD_DIM] = turned.astype(BF)
    dk = dk_ref[...]
    turned = dk * cos_ref[...] - pltpu.roll(dk, HEAD_DIM // 2, 1) * sin_ref[...]
    dqkv_ref[:, HEAD_DIM : 2 * HEAD_DIM] = turned.astype(BF)
    dqkv_ref[:, 2 * HEAD_DIM :] = dv_ref[...].astype(BF)


def attn_bwd(info, qkv, dol, lse, cosine, sine, segc, segr):
    length = qkv.shape[0]
    heads = qkv.shape[1] // (3 * HEAD_DIM)
    ways, block, _ = dol.shape
    tile = min(256, length)
    grid_spec = pltpu.PrefetchScalarGridSpec(
        num_scalar_prefetch=1,
        grid=(heads,),
        in_specs=[
            pl.BlockSpec((length, 3 * HEAD_DIM), lambda h, *_: (0, h)),
            pl.BlockSpec((ways, block, HEAD_DIM), lambda h, *_: (0, 0, h)),
            pl.BlockSpec((None, 1, length), lambda h, *_: (h, 0, 0)),
            const_spec((length, HEAD_DIM)),
            const_spec((length, HEAD_DIM)),
            const_spec((length, 1)),
            const_spec((1, length)),
        ],
        out_specs=pl.BlockSpec((length, 3 * HEAD_DIM), lambda h, *_: (0, h)),
        scratch_shapes=[
            pltpu.VMEM((length, length), F32),
            pltpu.VMEM((length, HEAD_DIM), BF),
            pltpu.VMEM((length, HEAD_DIM), F32),
            pltpu.VMEM((length, HEAD_DIM), F32),
        ],
    )
    return pl.pallas_call(
        functools.partial(attn_bwd_kernel, tile=tile),
        grid_spec=grid_spec,
        out_shape=jax.ShapeDtypeStruct(qkv.shape, BF),
        compiler_params=params(48),
        cost_estimate=cost(heads * 20 * length * length * HEAD_DIM, 16 * length * heads * 128),
        name="attn_bwd",
    )(info, qkv, dol, lse, cosine, sine, segc, segr)


def out_norm_kernel(info_ref, *refs, ways):
    ol_refs, ow_refs = refs[:ways], refs[ways : 2 * ways]
    x_ref, gain_ref, bias_ref, hl_ref, n1_ref, rstd_ref = refs[2 * ways :]
    total = x_ref[...].astype(F32) * deep_alpha
    for ol_ref, ow_ref in zip(ol_refs, ow_refs):
        total += mm(ol_ref[...], ow_ref[...])
    centered = total - jnp.mean(total, axis=1, keepdims=True)
    variance = jnp.mean(centered * centered, axis=1, keepdims=True)
    inv = lax.rsqrt(variance + norm_eps)
    normed = centered * inv
    hl_ref[...] = (normed * gain_ref[...] + bias_ref[...]).astype(BF)

    @pl.when(pl.program_id(0) == info_ref[0])
    def _():
        n1_ref[...] = normed
        rstd_ref[...] = jnp.broadcast_to(inv, rstd_ref.shape)


def out_norm(info, row, ol_pieces, ow_pieces, tokens, gain, bias):
    _, length, width = tokens.shape
    ways = len(ol_pieces)
    block = length // ways
    head_width = ol_pieces[0].shape[1]
    grid_spec = pltpu.PrefetchScalarGridSpec(
        num_scalar_prefetch=1,
        grid=(ways,),
        in_specs=[pl.BlockSpec((block, head_width), lambda i, *_: (i, 0))] * ways
        + [const_spec((head_width, width))] * ways
        + [
            pl.BlockSpec((None, block, width), lambda i, *_: (row, i, 0)),
            const_spec((1, width)),
            const_spec((1, width)),
        ],
        out_specs=[
            pl.BlockSpec((block, width), lambda i, info: (i ^ info[0], 0)),
            pl.BlockSpec((block, width), lambda i, *_: (0, 0)),
            pl.BlockSpec((block, HEAD_DIM), lambda i, *_: (0, 0)),
        ],
    )
    return pl.pallas_call(
        functools.partial(out_norm_kernel, ways=ways),
        grid_spec=grid_spec,
        out_shape=[
            jax.ShapeDtypeStruct((length, width), BF),
            jax.ShapeDtypeStruct((block, width), F32),
            jax.ShapeDtypeStruct((block, HEAD_DIM), F32),
        ],
        compiler_params=params(48),
        cost_estimate=cost(2 * length * width * width, 2 * width * width + 6 * length * width),
        name="out_norm",
    )(info, *ol_pieces, *ow_pieces, tokens, gain, bias)


def piece_shapes(ways, block, width):
    if ways == 4:
        sizes = [block] + [block // 2] * 6
    else:
        sizes = [block] * ways
    return [jax.ShapeDtypeStruct((size, width), BF) for size in sizes]


def store_pieces(at, part, refs, ways):
    if ways == 4:
        half = part.shape[0] // 2

        @pl.when(at == 0)
        def _():
            refs[0][...] = part

        for r in range(1, 4):

            @pl.when(at == r)
            def _(r=r):
                refs[2 * r - 1][...] = part[:half]
                refs[2 * r][...] = part[half:]
    else:
        for r in range(ways):

            @pl.when(at == r)
            def _(r=r):
                refs[r][...] = part


def piece_specs(shapes):
    return [pl.BlockSpec(s.shape, lambda *_: (0, 0)) for s in shapes]


def ffn_fwd_kernel(hl_ref, wg_ref, wu_ref, wd_ref, al_ref, ga_ref, gb_ref, *refs, ways):
    hidden = hl_ref[...]
    gate = mm(hidden, wg_ref[...])
    up = mm(hidden, wu_ref[...])
    cdf = 0.5 + 0.5 * lax.erf(gate * (1.0 / math.sqrt(2.0)))
    pdf = jnp.exp(gate * gate * -0.5) * (1.0 / math.sqrt(2.0 * math.pi))
    act = gate * cdf
    ga_ref[...] = (up * (cdf + gate * pdf)).astype(BF)
    gb_ref[...] = act.astype(BF)
    low = (act * up).astype(BF)
    al_ref[...] = low
    store_pieces(pl.program_id(0), mm(low, wd_ref[...]).astype(BF), refs, ways)


def ffn_fwd(hidden, gate_weight, up_weight, down_weight, ways):
    length, width = hidden.shape
    units = gate_weight.shape[1]
    block = length // ways
    tiled = lambda w: pl.BlockSpec((block, w), lambda i: (i, 0))
    shapes = piece_shapes(ways, block, width)
    out = pl.pallas_call(
        functools.partial(ffn_fwd_kernel, ways=ways),
        grid=(ways,),
        in_specs=[
            tiled(width),
            const_spec((width, units)),
            const_spec((width, units)),
            const_spec((units, width)),
        ],
        out_specs=[tiled(units)] * 3 + piece_specs(shapes),
        out_shape=[jax.ShapeDtypeStruct((length, units), BF)] * 3 + shapes,
        compiler_params=params(60),
        cost_estimate=cost(6 * length * width * units, 6 * units * width + 6 * length * units),
        name="ffn_fwd",
    )(hidden, gate_weight, up_weight, down_weight)
    return out[:3], out[3:]


def norm_two_kernel(info_ref, share_ref, *refs, n_in, ways):
    in_refs = refs[:n_in]
    cot_ref, gain_ref, bias_ref = refs[n_in : n_in + 3]
    act_ref, dffn_ref, sums_ref, held = refs[-4:]
    at = pl.program_id(0)
    if n_in == 5:
        half = held.shape[0] // 2
        for r in range(3):

            @pl.when(at == r)
            def _(r=r):
                held[...] = in_refs[r][...]

        @pl.when(at == 3)
        def _():
            held[:half] = in_refs[3][...]
            held[half:] = in_refs[4][...]
    else:
        for r in range(ways):

            @pl.when(at == r)
            def _(r=r):
                held[...] = in_refs[r][...]

    resid = held[...].astype(F32)
    centered = resid - jnp.mean(resid, axis=1, keepdims=True)
    variance = jnp.mean(centered * centered, axis=1, keepdims=True)
    inv = lax.rsqrt(variance + norm_eps)
    normed = centered * inv
    gain = gain_ref[...]
    act_ref[...] = (normed * gain + bias_ref[...]).astype(BF)
    dout = cot_ref[...].astype(F32) * share_ref[0]
    scaled = dout * gain
    inner = jnp.mean(scaled, axis=1, keepdims=True) + normed * jnp.mean(
        scaled * normed, axis=1, keepdims=True
    )
    dffn_ref[...] = (inv * (scaled - inner)).astype(BF)
    gain_sum = jnp.sum(dout * normed, axis=0, keepdims=True)
    bias_sum = jnp.sum(dout, axis=0, keepdims=True)

    @pl.when(at == 0)
    def _():
        sums_ref[0:1, :] = gain_sum
        sums_ref[1:2, :] = bias_sum

    @pl.when(at > 0)
    def _():
        sums_ref[0:1, :] += gain_sum
        sums_ref[1:2, :] += bias_sum


def norm_two(info, share, row, pieces, cotangent, gain, bias, before):
    rows, length, width = cotangent.shape
    block = pieces[0].shape[0]
    ways = length // block
    natural = pl.BlockSpec((None, block, width), lambda i, info, share: (row, i ^ info[0], 0))
    grid_spec = pltpu.PrefetchScalarGridSpec(
        num_scalar_prefetch=2,
        grid=(ways,),
        in_specs=[const_spec(p.shape) for p in pieces]
        + [natural, const_spec((1, width)), const_spec((1, width))]
        + ([pl.BlockSpec(memory_space=ANY)] if before is not None else []),
        out_specs=[
            natural,
            pl.BlockSpec((block, width), lambda i, *_: (i, 0)),
            pl.BlockSpec((2, width), lambda i, *_: (0, 0)),
        ],
        scratch_shapes=[pltpu.VMEM((block, width), BF)],
    )
    return pl.pallas_call(
        functools.partial(norm_two_kernel, n_in=len(pieces), ways=ways),
        grid_spec=grid_spec,
        out_shape=[
            jax.ShapeDtypeStruct(cotangent.shape, BF),
            jax.ShapeDtypeStruct((length, width), BF),
            jax.ShapeDtypeStruct((2, width), F32),
        ],
        input_output_aliases={len(pieces) + 5: 0} if before is not None else {},
        compiler_params=params(48),
        cost_estimate=cost(20 * length * width, 8 * length * width),
        name="norm_two",
    )(info, share, *pieces, cotangent, gain, bias, *([before] if before is not None else []))


def ffn_bwd_kernel(dffn_ref, ga_ref, gb_ref, wg_ref, wu_ref, wd_ref, dg_ref, du_ref, *refs, ways):
    dact = mm_nt(dffn_ref[...], wd_ref[...])
    dgate = (dact * ga_ref[...].astype(F32)).astype(BF)
    dup = (dact * gb_ref[...].astype(F32)).astype(BF)
    dg_ref[...] = dgate
    du_ref[...] = dup
    part = mm_nt(dgate, wg_ref[...]) + mm_nt(dup, wu_ref[...])
    store_pieces(pl.program_id(0), part.astype(BF), refs, ways)


def ffn_bwd(dffn, gate_slope, up_slope, gate_weight, up_weight, down_weight, ways):
    length, width = dffn.shape
    units = gate_weight.shape[1]
    block = length // ways
    tiled = lambda w: pl.BlockSpec((block, w), lambda i: (i, 0))
    shapes = piece_shapes(ways, block, width)
    out = pl.pallas_call(
        functools.partial(ffn_bwd_kernel, ways=ways),
        grid=(ways,),
        in_specs=[
            tiled(width),
            tiled(units),
            tiled(units),
            const_spec((width, units)),
            const_spec((width, units)),
            const_spec((units, width)),
        ],
        out_specs=[tiled(units)] * 2 + piece_specs(shapes),
        out_shape=[jax.ShapeDtypeStruct((length, units), BF)] * 2 + shapes,
        compiler_params=params(60),
        cost_estimate=cost(6 * length * width * units, 6 * units * width + 8 * length * units),
        name="ffn_bwd",
    )(dffn, gate_slope, up_slope, gate_weight, up_weight, down_weight)
    return out[0], out[1], out[2:]


def input_back_kernel(info_ref, dqkv_ref, w_ref, *refs, ways):
    part = mm_nt(dqkv_ref[...], w_ref[...])
    store_pieces(pl.program_id(0), part.astype(BF), refs, ways)


def input_back(info, dqkv, qkv_weight, ways):
    length, columns = dqkv.shape
    width = qkv_weight.shape[0]
    block = length // ways
    shapes = piece_shapes(ways, block, width)
    grid_spec = pltpu.PrefetchScalarGridSpec(
        num_scalar_prefetch=1,
        grid=(ways,),
        in_specs=[
            pl.BlockSpec((block, columns), lambda i, info: (i ^ info[0], 0)),
            const_spec((width, columns)),
        ],
        out_specs=piece_specs(shapes),
    )
    return pl.pallas_call(
        functools.partial(input_back_kernel, ways=ways),
        grid_spec=grid_spec,
        out_shape=shapes,
        compiler_params=params(48),
        cost_estimate=cost(2 * length * width * columns, 2 * width * columns + 2 * length * width),
        name="input_back",
    )(info, dqkv, qkv_weight)


def place_kernel(info_ref, *refs, n_in, ways):
    in_refs = refs[:n_in]
    out_ref = refs[-1]
    at = pl.program_id(0)
    if n_in == 5:
        half = out_ref.shape[0] // 2
        for r in range(3):

            @pl.when(at == r)
            def _(r=r):
                out_ref[...] = in_refs[r][...]

        @pl.when(at == 3)
        def _():
            out_ref[:half] = in_refs[3][...]
            out_ref[half:] = in_refs[4][...]
    else:
        for r in range(ways):

            @pl.when(at == r)
            def _(r=r):
                out_ref[...] = in_refs[r][...]


def place(info, row, pieces, shape, before):
    rows, length, width = shape
    block = pieces[0].shape[0]
    ways = length // block
    grid_spec = pltpu.PrefetchScalarGridSpec(
        num_scalar_prefetch=1,
        grid=(ways,),
        in_specs=[const_spec(p.shape) for p in pieces]
        + ([pl.BlockSpec(memory_space=ANY)] if before is not None else []),
        out_specs=pl.BlockSpec((None, block, width), lambda i, info: (row, i ^ info[0], 0)),
    )
    return pl.pallas_call(
        functools.partial(place_kernel, n_in=len(pieces), ways=ways),
        grid_spec=grid_spec,
        out_shape=jax.ShapeDtypeStruct(shape, BF),
        input_output_aliases={len(pieces) + 1: 0} if before is not None else {},
        compiler_params=params(32),
        cost_estimate=cost(0, 4 * length * width),
        name="place",
    )(info, *pieces, *([before] if before is not None else []))


def swap(array, bit, ways):
    return lax.ppermute(array, "tensor", [(i, i ^ bit) for i in range(ways)])


def gather_halves(own_a, own_b):
    xa = swap(own_a, 1, 4)
    yb = swap(own_b, 2, 4)
    xb = swap(own_b, 1, 4)
    ya = swap(own_a, 2, 4)
    ra = swap(xa, 2, 4)
    rb = swap(yb, 1, 4)
    return [(xa, xb), (ya, yb), (ra, rb)]


def gather_rel(own, ways):
    blocks = [own]
    bit = 1
    while bit < ways:
        blocks = blocks + [swap(b, bit, ways) for b in blocks]
        bit *= 2
    return blocks


def gather_tokens(own, ways):
    if ways == 4:
        half = own.shape[0] // 2
        (xa, xb), (ya, yb), (ra, rb) = gather_halves(own[:half], own[half:])
        return [own, jnp.concatenate([xa, xb]), jnp.concatenate([ya, yb]), ra, rb]
    return gather_rel(own, ways)


def join(pieces):
    return jnp.concatenate(pieces, axis=0)


def add_low(a, b):
    return (a.astype(F32) + b.astype(F32)).astype(BF)


def scatter_sum(pieces, ways):
    if ways == 4:
        own, r1a, r1b, r2a, r2b, r3a, r3b = pieces
        in3a = swap(r3a, 1, 4)
        in3b = swap(r3b, 2, 4)
        in1a = swap(r1a, 1, 4)
        in2b = swap(r2b, 2, 4)
        in2a = swap(add_low(r2a, in3a), 2, 4)
        in1b = swap(add_low(r1b, in3b), 1, 4)
        half = r1a.shape[0]
        top = own[:half].astype(F32) + in1a.astype(F32) + in2a.astype(F32)
        low = own[half:].astype(F32) + in1b.astype(F32) + in2b.astype(F32)
        return jnp.concatenate([top, low], axis=0)
    blocks = list(pieces)
    bit = ways // 2
    while bit >= 1:
        keep, send = blocks[:bit], blocks[bit:]
        blocks = [add_low(k, swap(s, bit, ways)) for k, s in zip(keep, send)]
        bit //= 2
    return blocks[0].astype(F32)


def sum_over_obj(array, ways):
    if ways != 4:
        return lax.psum(array, "obj")
    at = lax.axis_index("obj")
    one = add_low(array, lax.ppermute(array, "obj", [(0, 1), (3, 2)]))
    two = add_low(one, lax.ppermute(one, "obj", [(1, 2), (2, 1)]))
    back = lax.ppermute(two, "obj", [(1, 0), (2, 3)])
    return jnp.where((at == 0) | (at == 3), back, two)


def sum_gradient(update, data_ways, objective_ways):
    if data_ways != 2:
        return lax.psum(update, ("obj", "dp")).astype(F32)
    core = lax.axis_index("dp")
    half = update.shape[0] // 2
    other = [(0, 1), (1, 0)]
    mine = lax.dynamic_slice_in_dim(update, core * half, half)
    send = lax.dynamic_slice_in_dim(update, (1 - core) * half, half)
    mine = add_low(mine, lax.ppermute(send, "dp", other))
    mine = sum_over_obj(mine, objective_ways)
    theirs = lax.ppermute(mine, "dp", other)
    first = jnp.where(core == 0, mine, theirs)
    second = jnp.where(core == 0, theirs, mine)
    return jnp.concatenate([first, second], axis=0).astype(F32)


def general_body(
    tokens,
    cotangent,
    segment_ids,
    mlm_mask,
    glm_prefix,
    glm_span,
    qkv_weight,
    out_weight,
    gate_weight,
    up_weight,
    down_weight,
    norm1_gain,
    norm1_bias,
    norm2_gain,
    norm2_bias,
):
    seq_here, length, width = tokens.shape
    ways = lax.axis_size("tensor")
    data_ways = lax.axis_size("dp")
    objective_ways = lax.axis_size("obj")
    me = lax.axis_index("tensor").astype(jnp.int32)
    block = length // ways
    rows_all = mlm_mask.shape[0]
    masked_limit = seq_here * data_ways * (objective_ways // 2)
    row_ids = jnp.arange(rows_all, dtype=jnp.int32)
    counts = jnp.where(row_ids < masked_limit, jnp.sum(mlm_mask, axis=1), glm_span).astype(F32)
    weight_all = counts * rows_all / jnp.sum(counts)
    first_row = (lax.axis_index("obj") * data_ways + lax.axis_index("dp")) * seq_here
    share_here = lax.dynamic_slice_in_dim(weight_all, first_row, seq_here)
    prefix_here = lax.dynamic_slice_in_dim(glm_prefix, first_row, seq_here)
    span_here = lax.dynamic_slice_in_dim(glm_span, first_row, seq_here)
    masked_lm = first_row < masked_limit
    open_here = jnp.where(masked_lm, length, prefix_here)
    info = [jnp.stack([me, open_here[r], prefix_here[r] + span_here[r]]) for r in range(seq_here)]
    share = [share_here[r : r + 1] for r in range(seq_here)]
    cosine, sine = rotary_tables(length)
    segc = [segment_ids[r].reshape(length, 1) for r in range(seq_here)]
    segr = [segment_ids[r].reshape(1, length) for r in range(seq_here)]
    gain1, bias1 = norm1_gain.reshape(1, width), norm1_bias.reshape(1, width)
    gain2, bias2 = norm2_gain.reshape(1, width), norm2_bias.reshape(1, width)
    rows = range(seq_here)

    if ways == 4 and data_ways == 2:
        core = lax.axis_index("dp")
        half = out_weight.shape[0] // 2
        mine = lax.dynamic_slice_in_dim(out_weight, core * half, half)
        pairs = gather_halves(mine[: half // 2], mine[half // 2 :])
        ow_pieces = [out_weight]
        for a, b in pairs:
            got = jnp.concatenate([a, b])
            other = lax.ppermute(got, "dp", [(0, 1), (1, 0)])
            ow_pieces.append(
                jnp.concatenate(
                    [jnp.where(core == 0, got, other), jnp.where(core == 0, other, got)]
                )
            )
    else:
        ow_pieces = gather_rel(out_weight, ways)

    qkv, ol, lse, hl, n1, rstd1 = {}, {}, {}, {}, {}, {}
    al, slope_g, slope_u, dffn, dgate, dup = {}, {}, {}, {}, {}, {}
    r2_pieces, norm2_sums, norm1_sums, dr1, dqkv, dattn = {}, {}, {}, {}, {}, {}

    for r in rows:
        qkv[r], ol[r], lse[r] = attn_fwd(info[r], r, tokens, qkv_weight, cosine, sine, segc[r], segr[r])
    ffn_parts = {}
    for r in rows:
        if ways == 4:
            pairs = gather_halves(ol[r][: length // 2], ol[r][length // 2 :])
            ol_pieces = [ol[r]] + [jnp.concatenate(p) for p in pairs]
        else:
            ol_pieces = gather_rel(ol[r], ways)
        hl[r], n1[r], rstd1[r] = out_norm(info[r], r, ol_pieces, ow_pieces, tokens, gain1, bias1)
        (al[r], slope_g[r], slope_u[r]), ffn_parts[r] = ffn_fwd(
            hl[r], gate_weight, up_weight, down_weight, ways
        )
    for r in rows:
        total = scatter_sum(ffn_parts[r], ways)
        resid = deep_alpha * (n1[r] * gain1 + bias1) + total
        r2_pieces[r] = gather_tokens(resid.astype(BF), ways)

    activations = None
    dh_parts = {}
    for r in rows:
        activations, dffn[r], norm2_sums[r] = norm_two(
            info[r], share[r], r, r2_pieces[r], cotangent, gain2, bias2, activations
        )
        dgate[r], dup[r], dh_parts[r] = ffn_bwd(
            dffn[r], slope_g[r], slope_u[r], gate_weight, up_weight, down_weight, ways
        )

    def update(lefts, rights):
        total = None
        for r in rows:
            one = mm_tn(lefts[r], rights[r])
            total = one if total is None else total + one
        return total.astype(BF)

    def reduced(lefts, rights):
        return sum_gradient(update(lefts, rights), data_ways, objective_ways)

    down_grad = reduced(al, dffn)
    gate_grad = reduced(hl, dgate)
    up_grad = reduced(hl, dup)

    dx_parts = {}
    for r in rows:
        total = scatter_sum(dh_parts[r], ways)
        dh = deep_alpha * dffn[r][:block].astype(F32) + total
        scaled = dh * gain1
        inner = jnp.mean(scaled, axis=1, keepdims=True) + n1[r] * jnp.mean(
            scaled * n1[r], axis=1, keepdims=True
        )
        dr1[r] = rstd1[r][:, :1] * (scaled - inner)
        norm1_sums[r] = jnp.stack([jnp.sum(dh * n1[r], axis=0), jnp.sum(dh, axis=0)])
        dattn[r] = join(gather_tokens(dr1[r].astype(BF), ways))
    for r in rows:
        dol = mm_nt(dattn[r], out_weight).astype(BF).reshape(ways, block, -1)
        dqkv[r] = attn_bwd(info[r], qkv[r], dol, lse[r], cosine, sine, segc[r], segr[r])
        dx_parts[r] = input_back(info[r], dqkv[r], qkv_weight, ways)

    qkv_grad = reduced([tokens[r] for r in rows], dqkv)
    ol_rel = {}
    for r in rows:
        parts = ol[r].reshape(ways, block, -1)
        ol_rel[r] = jnp.stack(
            [lax.dynamic_index_in_dim(parts, me ^ i, 0, keepdims=False) for i in range(ways)]
        ).reshape(length, -1)
    out_grad = reduced(ol_rel, dattn)

    input_grad = None
    for r in rows:
        total = scatter_sum(dx_parts[r], ways)
        dx = (deep_alpha * dr1[r] + total).astype(BF)
        input_grad = place(info[r], r, gather_tokens(dx, ways), tokens.shape, input_grad)

    first = (me == 0).astype(F32)
    sums = jnp.concatenate(
        [sum(norm1_sums[r] for r in rows), sum(norm2_sums[r] for r in rows) * first]
    )
    sums = lax.psum(sums, ("obj", "dp", "tensor"))
    return (
        activations,
        input_grad,
        qkv_grad,
        out_grad,
        gate_grad,
        up_grad,
        down_grad,
        sums[0],
        sums[1],
        sums[2],
        sums[3],
    )


ORDER = ((1, 0), (3, 0), (2, 1), (3, 1), (1, 1), (2, 0), (0, 0), (0, 1))
CORES = ((0, 1), (1, 0))
DECLARED_FLOPS = 1e10
MICROS = {
    "attn_fwd": 21, "split": 2, "ow_join": 4, "relay": 1, "out_norm": 21, "middle_sum": 3, "resid_two": 5,
    "norm_two": 15, "grad_columns": 20, "grad_plain_columns": 19, "grad_plain": 19, "line_step": 5, "grad_rows": 21,
    "attn_bwd": 24, "norm_one_back": 6, "input_back": 14, "input_grad": 5, "grad_out": 11, "place": 5, "widen": 10,
    "cast": 9, "total_sum": 2,
}


def plane_case(token_shape, out_shape, down_shape):
    return (
        lax.axis_size("tensor") == 4
        and lax.axis_size("dp") == 2
        and lax.axis_size("obj") == 4
        and token_shape[0] == 2
        and token_shape[1] % 1024 == 0
        and token_shape[2] % 1024 == 0
        and down_shape[0] % 128 == 0
        and out_shape[0] % 256 == 0
    )


def spec(shape, index):
    return pl.BlockSpec(shape, index)


def call(
    kernel, name, grid, ins, in_specs, outs, out_specs, scalars=(), after=(), scratch=(), aliases=None,
    mib=48, flops=0, nbytes=0,
):
    ns, ni, na = len(scalars), len(ins), len(after)

    def wrapped(*refs):
        kernel(*refs[: ns + ni], *refs[ns + ni + na :])

    grid_spec = pltpu.PrefetchScalarGridSpec(
        num_scalar_prefetch=ns,
        grid=grid,
        in_specs=list(in_specs) + [pl.BlockSpec(memory_space=ANY)] * na,
        out_specs=list(out_specs),
        scratch_shapes=list(scratch),
    )
    return pl.pallas_call(
        wrapped,
        grid_spec=grid_spec,
        out_shape=[jax.ShapeDtypeStruct(s, d) for s, d in outs],
        input_output_aliases={ns + k: v for k, v in (aliases or {}).items()},
        compiler_params=params(62, len(grid)),
        cost_estimate=cost(DECLARED_FLOPS * MICROS.get(name, 9 * grid[0]), 1e6),
        name=name,
    )(*scalars, *ins, *after)


def constant_tables(length):
    half = HEAD_DIM // 2
    frequency = np.exp(np.arange(half, dtype=np.float32) * np.float32(-2.0 * math.log(10000.0) / HEAD_DIM))
    angles = np.arange(length, dtype=np.float32)[:, None] * frequency[None, :]
    cosine, sine = np.cos(angles), np.sin(angles)
    both = lambda a, b: jnp.asarray(np.concatenate([a, b], axis=1).astype(np.float32))
    return both(cosine, cosine), both(-sine, sine)


class Chain:
    def __init__(self):
        self.last = ()
        self.ended = ()

    def close(self, *arrays):
        self.ended += arrays

    def __call__(self, *args, after=(), **kwargs):
        out = call(*args, after=(*self.last, *self.ended, *after), **kwargs)
        self.last, self.ended = (out[0],), ()
        return out


def pair_swap(to_x, to_y):
    return swap(to_x, 1, 4), swap(to_y, 2, 4)


def plane_attn_fwd_kernel(
    info_ref, x_ref, w_ref, cos_ref, sin_ref, segc_ref, segr_ref, qkv_ref, ol_ref, lse_ref, bias_ref, *, tile
):
    length = x_ref.shape[0]

    @pl.when(pl.program_id(0) == 0)
    def _():
        fill_bias(info_ref, segc_ref, segr_ref, bias_ref, tile)

    for step in range(length // (2 * tile)):
        rows = pl.ds(step * 2 * tile, 2 * tile)
        proj = mm(x_ref[rows, :], w_ref[...])
        cosine, sine = cos_ref[rows, :], sin_ref[rows, :]
        for part in range(proj.shape[1] // HEAD_DIM):
            low = part * HEAD_DIM
            piece = proj[:, low : low + HEAD_DIM]
            if part % 3 < 2:
                piece = piece * cosine + pltpu.roll(piece, HEAD_DIM // 2, 1) * sine
            qkv_ref[rows, low : low + HEAD_DIM] = piece.astype(BF)

    heads = qkv_ref.shape[1] // (3 * HEAD_DIM)
    units = [(h, t) for h in range(heads) for t in range(length // tile)]
    keys, values_t = {}, {}

    def scores_of(unit):
        h, t = unit
        base = 3 * HEAD_DIM * h
        if h not in keys:
            keys[h] = qkv_ref[:, base + HEAD_DIM : base + 2 * HEAD_DIM]
            values_t[h] = qkv_ref[:, base + 2 * HEAD_DIM : base + 3 * HEAD_DIM].astype(F32).T.astype(BF)
        return mm_nt(keys[h], qkv_ref[t * tile : (t + 1) * tile, base : base + HEAD_DIM])

    later = scores_of(units[0])
    for k, (h, t) in enumerate(units):
        raw = later
        if k + 1 < len(units):
            later = scores_of(units[k + 1])
        rows = pl.ds(t * tile, tile)
        scores = raw * score_scale + bias_ref[:, rows]
        top = jnp.max(scores, axis=0, keepdims=True)
        exponent = jnp.exp(scores - top)
        total = jnp.sum(exponent, axis=0, keepdims=True)
        attended = mm(values_t[h], exponent.astype(BF)) * (1.0 / total)
        ol_ref[rows, h * HEAD_DIM : (h + 1) * HEAD_DIM] = attended.T.astype(BF)
        lse_ref[h, :, rows] = top + jnp.log(total)


def plane_attn_fwd(chain, info, row, tokens, qkv_weight, cosine, sine, segc, segr, after=()):
    _, length, width = tokens.shape
    heads = qkv_weight.shape[1] // (3 * HEAD_DIM)
    return chain(
        functools.partial(plane_attn_fwd_kernel, tile=256),
        "attn_fwd",
        (heads // 2,),
        (tokens, qkv_weight, cosine, sine, segc, segr),
        [
            pl.BlockSpec((None, length, width), lambda h, *_: (row, 0, 0), pipeline_mode=pl.Buffered(1)),
            spec((width, 768), lambda h, *_: (0, h)),
            const_spec((length, HEAD_DIM)),
            const_spec((length, HEAD_DIM)),
            const_spec((length, 1)),
            const_spec((1, length)),
        ],
        [((length, heads * 384), BF), ((length, heads * 128), BF), ((heads, 1, length), F32)],
        [
            spec((length, 768), lambda h, *_: (0, h)),
            spec((length, 256), lambda h, *_: (0, h)),
            spec((2, 1, length), lambda h, *_: (h, 0, 0)),
        ],
        scalars=(info,),
        after=after,
        scratch=[pltpu.VMEM((length, length), F32)],
        flops=heads * (2 * length * width * 384 + 8 * length * length * 128),
        nbytes=2 * length * width + 2 * width * heads * 384 + 8 * length * heads * 128,
    )


def plane_attn_bwd_kernel(
    info_ref, qkv_ref, own, r1, r2, r3a, r3b, ow_ref, lse_ref, cos_ref, sin_ref, segc_ref, segr_ref, dqkv_ref,
    bias_ref, dol_nat, *, tile
):
    length = qkv_ref.shape[0]
    block = own.shape[0]
    half = block // 2
    me = info_ref[0]

    @pl.when(pl.program_id(0) == 0)
    def _():
        fill_bias(info_ref, segc_ref, segr_ref, bias_ref, tile)

    def natural(r, lower):
        return pl.multiple_of((me ^ r) * block + lower, half)

    for r, piece in enumerate((own, r1, r2)):
        dol_nat[pl.ds(natural(r, 0), block), :] = mm_nt(piece[...], ow_ref[...]).astype(BF)
    for lower, piece in ((0, r3a), (half, r3b)):
        dol_nat[pl.ds(natural(3, lower), half), :] = mm_nt(piece[...], ow_ref[...]).astype(BF)

    heads = qkv_ref.shape[1] // (3 * HEAD_DIM)
    count = length // tile
    units = [(h, t) for h in range(heads) for t in range(count)]
    keys, values, keys_t = {}, {}, {}

    def products_of(unit):
        h, t = unit
        base = 3 * HEAD_DIM * h
        if h not in keys:
            keys[h] = qkv_ref[:, base + HEAD_DIM : base + 2 * HEAD_DIM]
            values[h] = qkv_ref[:, base + 2 * HEAD_DIM : base + 3 * HEAD_DIM]
            keys_t[h] = keys[h].astype(F32).T.astype(BF)
        rows = pl.ds(t * tile, tile)
        queries = qkv_ref[rows, base : base + HEAD_DIM]
        dol = dol_nat[rows, h * HEAD_DIM : (h + 1) * HEAD_DIM]
        return queries, dol, mm_nt(keys[h], queries), mm_nt(values[h], dol)

    dk = dv = None
    later = products_of(units[0])
    for k, (h, t) in enumerate(units):
        queries, dol, raw, dp = later
        if k + 1 < len(units):
            later = products_of(units[k + 1])
        base = 3 * HEAD_DIM * h
        rows = pl.ds(t * tile, tile)
        probs = jnp.exp(raw * score_scale + bias_ref[:, rows] - lse_ref[h, :, rows])
        weighted = probs * dp
        inner = jnp.sum(weighted, axis=0, keepdims=True)
        draw = ((weighted - probs * inner) * score_scale).astype(BF)
        dv_part, dk_part = mm(probs.astype(BF), dol), mm(draw, queries)
        dv = dv_part if t == 0 else dv + dv_part
        dk = dk_part if t == 0 else dk + dk_part
        dq = mm(keys_t[h], draw).T
        turned = dq * cos_ref[rows, :] - pltpu.roll(dq, HEAD_DIM // 2, 1) * sin_ref[rows, :]
        dqkv_ref[rows, base : base + HEAD_DIM] = turned.astype(BF)
        if t == count - 1:
            turned = dk * cos_ref[...] - pltpu.roll(dk, HEAD_DIM // 2, 1) * sin_ref[...]
            dqkv_ref[:, base + HEAD_DIM : base + 2 * HEAD_DIM] = turned.astype(BF)
            dqkv_ref[:, base + 2 * HEAD_DIM : base + 3 * HEAD_DIM] = dv.astype(BF)


def plane_attn_bwd(chain, info, qkv, pieces, out_weight, lse, cosine, sine, segc, segr, after=()):
    length = qkv.shape[0]
    heads = qkv.shape[1] // 384
    width = out_weight.shape[1]
    return chain(
        functools.partial(plane_attn_bwd_kernel, tile=256),
        "attn_bwd",
        (heads // 2,),
        (qkv, *pieces, out_weight, lse, cosine, sine, segc, segr),
        [spec((length, 768), lambda h, *_: (0, h))]
        + [const_spec(p.shape) for p in pieces]
        + [
            spec((256, width), lambda h, *_: (h, 0)),
            spec((2, 1, length), lambda h, *_: (h, 0, 0)),
            const_spec((length, HEAD_DIM)),
            const_spec((length, HEAD_DIM)),
            const_spec((length, 1)),
            const_spec((1, length)),
        ],
        [(qkv.shape, BF)],
        [spec((length, 768), lambda h, *_: (0, h))],
        scalars=(info,),
        after=after,
        scratch=[pltpu.VMEM((length, length), F32), pltpu.VMEM((length, 256), BF)],
        flops=heads * 24 * length * length * 128,
        nbytes=16 * length * heads * 128,
    )[0]


def plane_out_norm_kernel(
    info_ref, order_ref, *refs
):
    lows, highs = refs[:5], refs[5:10]
    ow_ref, mine_ref, other_ref = refs[10:13]
    xl_ref, xh_ref, gain_ref, bias_ref, hl_ref, n1_ref, rstd_ref, total_ref = refs[13:]
    half = xl_ref.shape[0]
    at = pl.program_id(0)

    def blocks(group, place):
        diagonal = jnp.where(place < 4, group[3][...].astype(F32), group[4][...].astype(F32)).astype(BF)
        return [ref[...] for ref in group[:3]] + [diagonal]

    feat = mine_ref.shape[0] // 3
    total_ref[:half] = xl_ref[...].astype(F32) * deep_alpha
    total_ref[half:] = xh_ref[...].astype(F32) * deep_alpha
    low, high = blocks(lows, order_ref[2 * at]), blocks(highs, order_ref[2 * at + 1])
    ols = [jnp.concatenate([lo, hi], axis=0) for lo, hi in zip(low, high)]

    def add(first, second):
        total = mm(ols[0], ow_ref[...])
        for r in range(1, 4):
            rows = pl.ds((r - 1) * feat, feat)
            total += mm(ols[r][:, :feat], first[rows, :])
            total += mm(ols[r][:, feat:], second[rows, :])
        total_ref[...] += total

    @pl.when(info_ref[3] == 0)
    def _():
        add(mine_ref, other_ref)

    @pl.when(info_ref[3] != 0)
    def _():
        add(other_ref, mine_ref)

    total = total_ref[...]
    centered = total - jnp.mean(total, axis=1, keepdims=True)
    variance = jnp.mean(centered * centered, axis=1, keepdims=True)
    inv = lax.rsqrt(variance + norm_eps)
    normed = centered * inv
    hl_ref[...] = (normed * gain_ref[...] + bias_ref[...]).astype(BF)

    @pl.when(pl.program_id(0) == 3)
    def _():
        n1_ref[...] = normed
        rstd_ref[...] = jnp.broadcast_to(inv, rstd_ref.shape)


def plane_out_norm(chain, info, order, row, ol_pieces, out_weight, mine, other, tokens, gain, bias, after=()):
    _, length, width = tokens.shape
    block = length // 4
    half = block // 2
    head_width = out_weight.shape[0]
    low = lambda i, info, order: (order[2 * i], 0)
    high = lambda i, info, order: (order[2 * i + 1], 0)

    def ol_specs(index):
        upper = lambda i, info, order: (jnp.minimum(index(i, info, order)[0], 3), 0)
        lower = lambda i, info, order: (jnp.maximum(index(i, info, order)[0] - 4, 0), 0)
        return [spec((half, head_width), f) for f in (index, index, index, upper, lower)]

    low3 = lambda i, info, order: (row, order[2 * i], 0)
    high3 = lambda i, info, order: (row, order[2 * i + 1], 0)
    return chain(
        plane_out_norm_kernel,
        "out_norm",
        (4,),
        (*ol_pieces, *ol_pieces, out_weight, mine, other, tokens, tokens, gain, bias),
        ol_specs(low)
        + ol_specs(high)
        + [const_spec(out_weight.shape), const_spec(mine.shape), const_spec(other.shape)]
        + [
            spec((None, half, width), low3),
            spec((None, half, width), high3),
            const_spec((1, width)),
            const_spec((1, width)),
        ],
        [((length, width), BF), ((block, width), F32), ((block, HEAD_DIM), F32)],
        [
            spec((block, width), lambda i, *_: (i, 0)),
            spec((block, width), lambda i, *_: (0, 0)),
            spec((block, HEAD_DIM), lambda i, *_: (0, 0)),
        ],
        scalars=(info, order),
        after=after,
        scratch=[pltpu.VMEM((block, width), F32)],
        flops=2 * length * width * width,
        nbytes=2 * width * width + 6 * length * width,
    )


def split_kernel(x_ref, y_ref, *refs):
    count = len(refs) // 2 - 1
    refs[count][...] = x_ref[...]
    refs[count + 1][...] = y_ref[...]


def forward(chain, from_x, from_y, carry=(), after=()):
    rows, width = from_x.shape
    shape = (rows // 2, width)
    any_spec = pl.BlockSpec(memory_space=ANY)
    out = chain(
        split_kernel, "split", (1,), (from_x, from_y, *carry),
        [
            pl.BlockSpec(shape, lambda i, *_: (0, 0), pipeline_mode=pl.Buffered(1)),
            pl.BlockSpec(shape, lambda i, *_: (1, 0), pipeline_mode=pl.Buffered(1)),
        ]
        + [any_spec] * len(carry),
        [(shape, BF)] * 2 + [(c.shape, c.dtype) for c in carry],
        [spec(shape, lambda i, *_: (0, 0))] * 2 + [any_spec] * len(carry),
        after=after,
        aliases={2 + k: 2 + k for k in range(len(carry))},
        nbytes=4 * rows * width,
    )
    pair = (swap(out[0], 2, 4), swap(out[1], 1, 4))
    return (pair, *out[2:]) if carry else pair


def ow_join_kernel(x_ref, y_ref, a_ref, b_ref, out_ref):
    rows = x_ref.shape[0]
    out_ref[:rows] = x_ref[...]
    out_ref[rows : 2 * rows] = y_ref[...]
    out_ref[2 * rows : 2 * rows + rows // 2] = a_ref[...]
    out_ref[2 * rows + rows // 2 :] = b_ref[...]


def ow_join(chain, pieces, after=()):
    rows, width = pieces[0].shape
    shape = (3 * rows, width)
    return chain(
        ow_join_kernel, "ow_join", (1,), pieces, [const_spec(p.shape) for p in pieces],
        [(shape, BF)], [spec(shape, lambda i, *_: (0, 0))], after=after,
    )[0]


def relay_kernel(*refs):
    refs[len(refs) // 2][...] = refs[0][...]


def relay(chain, carry, after=()):
    small = jnp.zeros((8, 128), F32)
    any_spec = pl.BlockSpec(memory_space=ANY)
    count = len(carry)
    out = chain(
        relay_kernel, "relay", (1,), (small, *carry), [const_spec(small.shape)] + [any_spec] * count,
        [(small.shape, F32)] + [(c.shape, c.dtype) for c in carry],
        [spec(small.shape, lambda i, *_: (0, 0))] + [any_spec] * count,
        after=after, aliases={1 + k: 1 + k for k in range(count)},
    )
    return out[1:]


def load_once(pairs, sem):
    copies = [pltpu.make_async_copy(src, dst, sem.at[k]) for k, (src, dst) in enumerate(pairs)]

    @pl.when(pl.program_id(0) == 0)
    def _():
        for copy in copies:
            copy.start()

    def wait(k):
        @pl.when(pl.program_id(0) == 0)
        def _():
            copies[k].wait()

    return wait


def store_half(first, part, refs):
    at = pl.program_id(0)
    half = part.shape[0] // 2
    if first is None:

        @pl.when(at == 0)
        def _():
            refs[0][...] = part

        @pl.when(at == 1)
        def _():
            refs[1][...] = part

        @pl.when(at == 2)
        def _():
            refs[2][...] = part[:half]
            refs[3][...] = part[half:]

        @pl.when(at == 3)
        def _():
            refs[4][...] = part

        return

    @pl.when(at == 0)
    def _():
        if first:
            refs[0][...] = part
        else:
            refs[0][...] = part[:half]
            refs[1][...] = part[half:]

    @pl.when(at == 1)
    def _():
        refs[-1][...] = part


def half_outs(first, block, width):
    if first is None:
        sizes = [block, block, block // 2, block // 2, block]
    else:
        sizes = [block, block] if first else [block // 2, block // 2, block]
    return [((s, width), BF) for s in sizes], [spec((s, width), lambda i, *_: (0, 0)) for s in sizes]


def plane_ffn_fwd_kernel(hl_ref, wg_hbm, wu_hbm, wd_hbm, *refs, first):
    refs, (wg, wu, wd, sem) = refs[:-4], refs[-4:]
    (al_ref, ga_ref, gb_ref), refs = refs[-3:], refs[:-3]
    wait = load_once(((wg_hbm, wg), (wu_hbm, wu), (wd_hbm, wd)), sem)
    hidden = hl_ref[...]
    wait(0)
    gate = mm(hidden, wg[...])
    wait(1)
    up = mm(hidden, wu[...])
    cdf = 0.5 + 0.5 * lax.erf(gate * (1.0 / math.sqrt(2.0)))
    pdf = jnp.exp(gate * gate * -0.5) * (1.0 / math.sqrt(2.0 * math.pi))
    act = gate * cdf
    ga_ref[...] = (up * (cdf + gate * pdf)).astype(BF)
    gb_ref[...] = act.astype(BF)
    low = (act * up).astype(BF)
    al_ref[...] = low
    wait(2)
    store_half(first, mm(low, wd[...]).astype(BF), refs)


def plane_ffn_fwd(chain, first, hidden, weights, kept, after=()):
    length, width = hidden.shape
    units = weights[0].shape[1]
    block = length // 4
    base = 2 if first is False else 0
    steps = 4 if first is None else 2
    tiled = lambda w: spec((block, w), lambda i, *_: (i + base, 0))
    outs, out_specs = half_outs(first, block, width)
    n = len(outs)
    any_spec = pl.BlockSpec(memory_space=ANY)
    kept = tuple(kept)
    carried = kept[3:]
    kernel = functools.partial(plane_ffn_fwd_kernel, first=first)
    if first is not False:
        body_kernel = kernel
    else:
        nk, nc = len(kept), len(carried)

        def body_kernel(hl, wg, wu, wd, *refs):
            refs = refs[nk:]
            kernel(hl, wg, wu, wd, *refs[:n], *refs[n + nc :])

    out = chain(
        body_kernel,
        "ffn_fwd",
        (steps,),
        (hidden, *weights, *kept),
        [tiled(width)] + [any_spec] * (3 + len(kept)),
        outs + [(c.shape, BF) for c in carried] + [((length, units), BF)] * 3,
        out_specs + [any_spec] * len(carried) + [tiled(units)] * 3,
        after=after,
        aliases={}
        if first is not False
        else {
            **{4 + k: n + len(carried) + k for k in range(3)},
            **{7 + k: n + k for k in range(len(carried))},
        },
        scratch=[
            pltpu.VMEM(weights[0].shape, BF),
            pltpu.VMEM(weights[1].shape, BF),
            pltpu.VMEM(weights[2].shape, BF),
            pltpu.SemaphoreType.DMA((3,)),
        ],
        mib=60,
        flops=3 * length * width * units * steps // 2,
        nbytes=6 * units * width + 3 * length * units,
    )
    n += len(carried)
    return out[:n], out[n:]


def plane_ffn_bwd_kernel(dffn_ref, ga_ref, gb_ref, wd_hbm, wg_hbm, wu_hbm, *refs, first):
    refs, (wd, wg, wu, sem) = refs[:-4], refs[-4:]
    (dg_ref, du_ref), refs = refs[-2:], refs[:-2]
    wait = load_once(((wd_hbm, wd), (wg_hbm, wg), (wu_hbm, wu)), sem)
    grad = dffn_ref[...]
    wait(0)
    dact = mm_nt(grad, wd[...])
    dgate = (dact * ga_ref[...].astype(F32)).astype(BF)
    dup = (dact * gb_ref[...].astype(F32)).astype(BF)
    dg_ref[...] = dgate
    du_ref[...] = dup
    wait(1)
    part = mm_nt(dgate, wg[...])
    wait(2)
    part += mm_nt(dup, wu[...])
    store_half(first, part.astype(BF), refs)


def plane_ffn_bwd(chain, first, dffn, slopes, weights, kept, after=()):
    length, width = dffn.shape
    units = weights[0].shape[1]
    block = length // 4
    base = 2 if first is False else 0
    steps = 4 if first is None else 2
    tiled = lambda w: spec((block, w), lambda i, *_: (i + base, 0))
    outs, out_specs = half_outs(first, block, width)
    n = len(outs)
    any_spec = pl.BlockSpec(memory_space=ANY)
    kept = tuple(kept)
    kernel = functools.partial(plane_ffn_bwd_kernel, first=first)
    carried = kept[2:]
    if first is not False:
        body_kernel = kernel
    else:
        nk, nc = len(kept), len(carried)

        def body_kernel(d, ga, gb, wd, wg, wu, *refs):
            refs = refs[nk:]
            kernel(d, ga, gb, wd, wg, wu, *refs[:n], *refs[n + nc :])

    out = chain(
        body_kernel,
        "ffn_bwd",
        (steps,),
        (dffn, *slopes, weights[2], weights[0], weights[1], *kept),
        [tiled(width), tiled(units), tiled(units)] + [any_spec] * (3 + len(kept)),
        outs + [(c.shape, BF) for c in carried] + [((length, units), BF)] * 2,
        out_specs + [any_spec] * len(carried) + [tiled(units)] * 2,
        after=after,
        aliases={}
        if first is not False
        else {
            **{6 + k: n + len(carried) + k for k in range(2)},
            **{8 + k: n + k for k in range(len(carried))},
        },
        scratch=[
            pltpu.VMEM(weights[2].shape, BF),
            pltpu.VMEM(weights[0].shape, BF),
            pltpu.VMEM(weights[1].shape, BF),
            pltpu.SemaphoreType.DMA((3,)),
        ],
        mib=60,
        flops=3 * length * width * units * steps // 2,
        nbytes=6 * units * width + 4 * length * units,
    )
    n += len(carried)
    return out[:n], out[n:]


def middle_kernel(x1_ref, y1_ref, r1b_ref, r2a_ref, x2_ref, y2_ref):
    half = r1b_ref.shape[0]
    x2_ref[...] = (r1b_ref[...].astype(F32) + y1_ref[half:].astype(F32)).astype(BF)
    y2_ref[...] = (r2a_ref[...].astype(F32) + x1_ref[half:].astype(F32)).astype(BF)


def middle(chain, arrived, r1b, r2a, after=()):
    x1, y1 = arrived
    shape = r1b.shape
    return chain(
        middle_kernel,
        "middle_sum",
        (1,),
        (x1, y1, r1b, r2a),
        [const_spec(a.shape) for a in (x1, y1, r1b, r2a)],
        [(shape, BF)] * 2,
        [spec(shape, lambda i, *_: (0, 0))] * 2,
        after=after,
        mib=32,
        nbytes=16 * r1b.size,
    )


def own_sum(own, x1, y1, x2, y2):
    top = pl.program_id(0) < OWN_STEPS // 2
    direct = jnp.where(top, x1[...].astype(F32), y1[...].astype(F32))
    relayed = jnp.where(top, y2[...].astype(F32), x2[...].astype(F32))
    return own[...].astype(F32) + direct + relayed


def resid_two_kernel(own, x1, y1, x2, y2, n1_ref, gain_ref, bias_ref, out_ref):
    total = own_sum(own, x1, y1, x2, y2)
    out_ref[...] = (deep_alpha * (n1_ref[...] * gain_ref[...] + bias_ref[...]) + total).astype(BF)


def norm_one_back_kernel(own, x1, y1, x2, y2, dffn_ref, n1_ref, rstd_ref, gain_ref, low_ref, dr1_ref, sums_ref):
    total = own_sum(own, x1, y1, x2, y2)
    dh = deep_alpha * dffn_ref[...].astype(F32) + total
    normed = n1_ref[...]
    scaled = dh * gain_ref[...]
    inner = jnp.mean(scaled, axis=1, keepdims=True) + normed * jnp.mean(scaled * normed, axis=1, keepdims=True)
    dr1 = rstd_ref[:, :1] * (scaled - inner)
    dr1_ref[...] = dr1
    low_ref[...] = dr1.astype(BF)
    gain_sum = jnp.sum(dh * normed, axis=0, keepdims=True)
    bias_sum = jnp.sum(dh, axis=0, keepdims=True)

    @pl.when(pl.program_id(0) == 0)
    def _():
        sums_ref[0:1, :] = gain_sum
        sums_ref[1:2, :] = bias_sum

    @pl.when(pl.program_id(0) > 0)
    def _():
        sums_ref[0:1, :] += gain_sum
        sums_ref[1:2, :] += bias_sum


def input_grad_kernel(own, x1, y1, x2, y2, dr1_ref, out_ref):
    out_ref[...] = (deep_alpha * dr1_ref[...] + own_sum(own, x1, y1, x2, y2)).astype(BF)


OWN_STEPS = 4


def rows_spec(array_shape, tile, base=0):
    return spec((tile, array_shape[1]), lambda i, *_: (i + base, 0))


def own_step(chain, kernel, name, sums, extra, extra_specs, outs, after=()):
    block, width = sums[0].shape
    tile = block // OWN_STEPS
    middle_step = OWN_STEPS // 2
    first = spec((tile, width), lambda i, *_: (jnp.minimum(i, middle_step - 1), 0))
    later = spec((tile, width), lambda i, *_: (jnp.maximum(i - middle_step, 0), 0))
    return chain(
        kernel,
        name,
        (OWN_STEPS,),
        (*sums, *extra),
        [rows_spec((block, width), tile), first, later, later, first] + extra_specs,
        outs,
        [rows_spec(s, tile) if s[0] == block else spec(s, lambda i, *_: (0, 0)) for s, _ in outs],
        after=after,
        mib=40,
        nbytes=16 * block * width,
    )


def plane_norm_two_kernel(info_ref, order_ref, share_ref, own, r1, r2, r3a, r3b, cot_ref, gain_ref, bias_ref, *refs):
    act_ref, sums_ref, dffn_ref, held = refs[-4:]
    at = pl.program_id(0)
    half = held.shape[0]
    places = (
        (r1, 0), (r3a, 0), (r2, half), (r3b, 0), (r1, half), (r2, 0), (own, 0), (own, half),
    )
    for k, (ref, start) in enumerate(places):

        @pl.when(at == k)
        def _(ref=ref, start=start):
            held[...] = ref[start : start + half]

    resid = held[...].astype(F32)
    centered = resid - jnp.mean(resid, axis=1, keepdims=True)
    variance = jnp.mean(centered * centered, axis=1, keepdims=True)
    inv = lax.rsqrt(variance + norm_eps)
    normed = centered * inv
    gain = gain_ref[...]
    act_ref[...] = (normed * gain + bias_ref[...]).astype(BF)
    dout = cot_ref[...].astype(F32) * share_ref[0]
    scaled = dout * gain
    inner = jnp.mean(scaled, axis=1, keepdims=True) + normed * jnp.mean(scaled * normed, axis=1, keepdims=True)
    dffn_ref[...] = (inv * (scaled - inner)).astype(BF)
    gain_sum = jnp.sum(dout * normed, axis=0, keepdims=True)
    bias_sum = jnp.sum(dout, axis=0, keepdims=True)

    @pl.when(at == 0)
    def _():
        sums_ref[0:1, :] = gain_sum
        sums_ref[1:2, :] = bias_sum

    @pl.when(at > 0)
    def _():
        sums_ref[0:1, :] += gain_sum
        sums_ref[1:2, :] += bias_sum


def plane_norm_two(chain, info, order, share, row, pieces, cotangent, gain, bias, before, after=()):
    rows, length, width = cotangent.shape
    half = length // 8
    natural = spec((None, half, width), lambda i, info, order, share: (row, order[i], 0))
    held = () if before is None else (before,)
    return chain(
        plane_norm_two_kernel,
        "norm_two",
        (8,),
        (*pieces, cotangent, gain, bias, *held),
        [const_spec(p.shape) for p in pieces]
        + [natural, const_spec((1, width)), const_spec((1, width))]
        + [pl.BlockSpec(memory_space=ANY)] * len(held),
        [(cotangent.shape, BF), ((2, width), F32), ((length, width), BF)],
        [natural, spec((2, width), lambda i, *_: (0, 0)), spec((half, width), lambda i, *_: (i, 0))],
        scalars=(info, order, share),
        after=after,
        aliases={len(pieces) + 3: 0} if held else {},
        scratch=[pltpu.VMEM((half, width), BF)],
        flops=20 * length * width,
        nbytes=8 * length * width,
    )


def plane_input_back_kernel(order_ref, low_ref, high_ref, w_ref, x1_ref, y1_ref, r1b_ref, r2a_ref, own_ref):
    at = pl.program_id(0)
    half = low_ref.shape[0]
    part = mm_nt(jnp.concatenate([low_ref[...], high_ref[...]], axis=0), w_ref[...]).astype(BF)

    @pl.when(at == 0)
    def _():
        x1_ref[...] = part

    @pl.when(at == 1)
    def _():
        y1_ref[...] = part

    @pl.when(at == 2)
    def _():
        r1b_ref[...] = part[:half]
        r2a_ref[...] = part[half:]

    @pl.when(at == 3)
    def _():
        own_ref[...] = part


def plane_input_back(chain, order, dqkv, qkv_weight, after=()):
    length, columns = dqkv.shape
    width = qkv_weight.shape[0]
    block = length // 4
    half = block // 2
    sizes = [block, block, half, half, block]
    return chain(
        plane_input_back_kernel,
        "input_back",
        (4,),
        (dqkv, dqkv, qkv_weight),
        [
            spec((half, columns), lambda i, order: (order[2 * i], 0)),
            spec((half, columns), lambda i, order: (order[2 * i + 1], 0)),
            const_spec(qkv_weight.shape),
        ],
        [((s, width), BF) for s in sizes],
        [spec((s, width), lambda i, *_: (0, 0)) for s in sizes],
        scalars=(order,),
        after=after,
        flops=2 * length * width * columns,
        nbytes=2 * width * columns + 4 * length * width,
    )


def plane_place_kernel(order_ref, own, r1, r2, r3a, r3b, *refs):
    out_ref = refs[-1]
    at = pl.program_id(0)
    half = r3a.shape[0]
    for k, ref in enumerate((own, r1, r2)):

        @pl.when(at == k)
        def _(ref=ref):
            out_ref[...] = ref[...]

    @pl.when(at == 3)
    def _():
        out_ref[:half] = r3a[...]
        out_ref[half:] = r3b[...]


def plane_place(chain, info, row, pieces, shape, before, after=()):
    rows, length, width = shape
    block = length // 4
    held = () if before is None else (before,)
    return chain(
        plane_place_kernel,
        "place",
        (4,),
        (*pieces, *held),
        [const_spec(p.shape) for p in pieces] + [pl.BlockSpec(memory_space=ANY)] * len(held),
        [(shape, BF)],
        [spec((None, block, width), lambda i, info: (row, i ^ info[0], 0))],
        scalars=(info,),
        after=after,
        aliases={len(pieces): 0} if held else {},
        mib=32,
        nbytes=4 * length * width,
    )[0]


def panels(ref, value):
    for c in range(value.shape[1] // 128):
        ref[c] = value[:, c * 128 : (c + 1) * 128].astype(BF)


def grad_rows_kernel(info_ref, left_a, left_b, right_a, right_b, send, keep, *, steps):
    at = pl.program_id(0)
    value = mm(left_a[...].T, right_a[...]) + mm(left_b[...].T, right_b[...])

    @pl.when(at < steps)
    def _():
        panels(send, value)

    @pl.when(at >= steps)
    def _():
        panels(keep, value)


def lhs_spec(lhs, tile, index, row):
    if lhs.ndim == 3:
        return spec((None, lhs.shape[1], tile), lambda *a: (row, 0, index(*a)))
    return spec((lhs.shape[0], tile), lambda *a: (0, index(*a)))


def grad_rows(chain, info, lefts, rights, after=()):
    rows = lefts[0].shape[-1]
    tile = 256
    steps = rows // tile // 2
    length, columns = rights[0].shape

    def at(i, info):
        other = (1 - info[3]) * steps + i
        own = info[3] * steps + i - steps
        return jnp.where(i < steps, other, own)

    shape = (columns // 128, rows // 2, 128)
    out = chain(
        functools.partial(grad_rows_kernel, steps=steps),
        "grad_rows",
        (2 * steps,),
        (*lefts, *rights),
        [lhs_spec(lefts[r], tile, at, r) for r in range(2)] + [const_spec(r.shape) for r in rights],
        [(shape, BF)] * 2,
        [
            spec((shape[0], tile, 128), lambda i, *_: (0, jnp.minimum(i, steps - 1), 0)),
            spec((shape[0], tile, 128), lambda i, *_: (0, jnp.maximum(i - steps, 0), 0)),
        ],
        scalars=(info,),
        after=after,
        flops=4 * rows * length * columns,
        nbytes=2 * rows * columns + 4 * rows * length,
    )
    return out[0].reshape(-1, 128), out[1].reshape(-1, 128)


def grad_columns_kernel(info_ref, left_a, left_b, right_a, right_b, send, keep, turned_a, turned_b, held):
    @pl.when(pl.program_id(0) == 0)
    def _():
        turned_a[...] = left_a[...].T
        turned_b[...] = left_b[...].T

    held[...] = mm(turned_a[...], right_a[...]) + mm(turned_b[...], right_b[...])
    half = held.shape[0] // 2
    core = info_ref[3]
    panels(send, held[pl.ds(pl.multiple_of((1 - core) * half, 8), half), :])
    panels(keep, held[pl.ds(pl.multiple_of(core * half, 8), half), :])


def grad_columns(chain, info, lefts, rights, after=()):
    length, rows = lefts[0].shape
    columns = rights[0].shape[1]
    tile = 256
    shape = (columns // 128, rows // 2, 128)
    out = chain(
        grad_columns_kernel,
        "grad_columns",
        (columns // tile,),
        (*lefts, *rights),
        [const_spec(left.shape) for left in lefts] + [spec((length, tile), lambda i, *_: (0, i))] * 2,
        [(shape, BF)] * 2,
        [spec((tile // 128, rows // 2, 128), lambda i, *_: (i, 0, 0))] * 2,
        scalars=(info,),
        after=after,
        scratch=[pltpu.VMEM((rows, length), BF)] * 2 + [pltpu.VMEM((rows, tile), F32)],
        flops=4 * rows * length * columns,
        nbytes=2 * rows * columns + 4 * length * (rows + columns),
    )
    return out[0].reshape(-1, 128), out[1].reshape(-1, 128)


def grad_plain_kernel(left_a, left_b, right_a, right_b, out_ref):
    out_ref[...] = (mm(left_a[...].T, right_a[...]) + mm(left_b[...].T, right_b[...])).astype(BF)


def grad_plain(chain, lefts, rights, after=()):
    rows = lefts[0].shape[-1]
    tile = 256
    length, columns = rights[0].shape
    return chain(
        grad_plain_kernel,
        "grad_plain",
        (rows // tile,),
        (*lefts, *rights),
        [lhs_spec(lefts[r], tile, lambda i, *_: i, r) for r in range(2)] + [const_spec(r.shape) for r in rights],
        [((rows, columns), BF)],
        [spec((tile, columns), lambda i, *_: (i, 0))],
        after=after,
        flops=4 * rows * length * columns,
        nbytes=2 * rows * columns + 4 * rows * length,
    )[0]


def grad_plain_columns_kernel(left_a, left_b, right_a, right_b, out_ref, turned_a, turned_b):
    @pl.when(pl.program_id(0) == 0)
    def _():
        turned_a[...] = left_a[...].T
        turned_b[...] = left_b[...].T

    out_ref[...] = (mm(turned_a[...], right_a[...]) + mm(turned_b[...], right_b[...])).astype(BF)


def grad_plain_columns(chain, lefts, rights, after=()):
    length, rows = lefts[0].shape
    columns = rights[0].shape[1]
    tile = 256
    return chain(
        grad_plain_columns_kernel,
        "grad_plain_columns",
        (columns // tile,),
        (*lefts, *rights),
        [const_spec(left.shape) for left in lefts] + [spec((length, tile), lambda i, *_: (0, i))] * 2,
        [((rows, columns), BF)],
        [spec((rows, tile), lambda i, *_: (0, i))],
        after=after,
        scratch=[pltpu.VMEM((rows, length), BF)] * 2,
        flops=4 * rows * length * columns,
        nbytes=2 * rows * columns + 4 * length * (rows + columns),
    )[0]


def grad_out(lhs, pieces, me):
    block = pieces[0].shape[0]
    half = block // 2
    total = 0.0
    for r, piece in enumerate(pieces[:3]):
        part = lhs[pl.ds(pl.multiple_of((me ^ r) * block, half), block), :]
        total = total + mm(part.T, piece[...])
    for lower, piece in ((0, pieces[3]), (half, pieces[4])):
        part = lhs[pl.ds(pl.multiple_of((me ^ 3) * block + lower, half), half), :]
        total = total + mm(part.T, piece[...])
    return total


def grad_out_kernel(info_ref, left_a, left_b, *refs):
    pieces_a, pieces_b, (send, keep, held) = refs[:5], refs[5:10], refs[10:]
    held[...] = grad_out(left_a, pieces_a, info_ref[0]) + grad_out(left_b, pieces_b, info_ref[0])
    half = held.shape[0] // 2
    core = info_ref[3]
    panels(send, held[pl.ds(pl.multiple_of((1 - core) * half, 8), half), :])
    panels(keep, held[pl.ds(pl.multiple_of(core * half, 8), half), :])


def plane_grad_out(chain, info, lefts, pieces, after=()):
    length, rows = lefts[0].shape
    columns = pieces[0][0].shape[1]
    tile = 512
    shape = (columns // 128, rows // 2, 128)
    every = (*pieces[0], *pieces[1])
    out = chain(
        grad_out_kernel,
        "grad_out",
        (columns // tile,),
        (*lefts, *every),
        [const_spec(left.shape) for left in lefts]
        + [spec((p.shape[0], tile), lambda i, *_: (0, i)) for p in every],
        [(shape, BF)] * 2,
        [spec((tile // 128, rows // 2, 128), lambda i, *_: (i, 0, 0))] * 2,
        scalars=(info,),
        after=after,
        scratch=[pltpu.VMEM((rows, tile), F32)],
        flops=4 * rows * length * columns,
        nbytes=2 * rows * columns + 4 * length * (rows + columns),
    )
    return out[0].reshape(-1, 128), out[1].reshape(-1, 128)


class Line:
    GRID = 4

    def __init__(self, chain, edge):
        self.chain, self.edge = chain, edge
        self.pending = []
        self.slots = []
        self.step = 0
        self.done = {}
        self.first = self.second = None
        self.sent = self.mid = None

    def add(self, name, keep, got, chunks):
        for k in range(chunks):
            self.pending.append((name, keep, got, k, keep.shape[0] // chunks, keep.shape[0]))

    def get(self, j):
        return self.slots[j] if j >= 0 else None

    def busy(self):
        return bool(self.pending) or any(self.slots[-3:])

    def complete(self, name):
        return not any(slot and slot[0] == name for slot in self.pending + self.slots[-3:])

    def advance(self, after=()):
        j = self.step
        self.slots.append(self.pending.pop(0) if self.pending else None)
        new, cur, prev, last = self.get(j), self.get(j - 1), self.get(j - 2), self.get(j - 3)
        ins, in_specs, outs, out_specs, aliases, roles = [], [], [], [], {}, []
        grid = self.GRID

        def give(array, rows, base, role, when):
            block = rows // grid
            if when is None:
                index = lambda i, edge: (base + i, 0)
            elif when:
                index = lambda i, edge: (base + i * edge[0], 0)
            else:
                index = lambda i, edge: (base + i * (1 - edge[0]), 0)
            ins.append(array)
            in_specs.append(spec((block, 128), index))
            roles.append(role)

        if new:
            name, keep, got, k, rows, _ = new
            give(keep, rows, k * grid, "new_keep", True)
            give(got, rows, k * grid, "new_got", True)
        if cur:
            name, keep, got, k, rows, _ = cur
            give(keep, rows, k * grid, "cur_keep", False)
            give(got, rows, k * grid, "cur_got", False)
            give(self.first, rows, 0, "cur_in", False)
        if prev:
            rows = prev[4]
            give(self.mid, rows, 0, "prev_mid", False)
            give(self.second, rows, 0, "prev_in", False)
        if last:
            rows = last[4]
            give(self.first, rows, 0, "last_in", True)
            give(self.sent, rows, 0, "last_sent", False)
            if last[3] > 0:
                ins.append(self.done[last[0]])
                in_specs.append(pl.BlockSpec(memory_space=ANY))
                roles.append("held")
        names = []
        if new or prev:
            rows = max(c[4] for c in (new, prev) if c)
            outs.append(((rows, 128), BF))
            out_specs.append(pl.BlockSpec((rows, 128), lambda i, *_: (0, 0)))
            names.append("sent")
        if cur:
            outs.append(((cur[4], 128), BF))
            out_specs.append(spec((cur[4] // grid, 128), lambda i, *_: (i, 0)))
            names.append("mid")
        if last:
            base = last[3] * grid
            outs.append(((last[5], 128), BF))
            out_specs.append(spec((last[4] // grid, 128), lambda i, *_, base=base: (base + i, 0)))
            names.append("done")
            if last[3] > 0:
                aliases = {len(ins) - 1: len(outs) - 1}

        def kernel(edge_ref, *refs):
            src = dict(zip(roles, refs[: len(roles)]))
            dst = dict(zip(names, refs[len(roles) :]))
            at = pl.program_id(0)
            is_edge = edge_ref[0] == 1
            f32 = lambda r: src[r][...].astype(F32)

            if new:
                @pl.when(is_edge)
                def _():
                    block = new[4] // grid
                    rows = pl.ds(pl.multiple_of(at * block, block), block)
                    dst["sent"][rows, :] = (f32("new_keep") + f32("new_got")).astype(BF)

            @pl.when(jnp.logical_not(is_edge))
            def _():
                if cur:
                    dst["mid"][...] = (f32("cur_keep") + f32("cur_got") + f32("cur_in")).astype(BF)
                if prev:
                    block = prev[4] // grid
                    rows = pl.ds(pl.multiple_of(at * block, block), block)
                    dst["sent"][rows, :] = (f32("prev_mid") + f32("prev_in")).astype(BF)

            if last:
                @pl.when(is_edge)
                def _():
                    dst["done"][...] = src["last_in"][...]

                @pl.when(jnp.logical_not(is_edge))
                def _():
                    dst["done"][...] = src["last_sent"][...]

        out = self.chain(
            kernel,
            "line_step",
            (grid,),
            tuple(ins),
            in_specs,
            outs,
            out_specs,
            scalars=(self.edge,),
            after=after,
            aliases=aliases,
            mib=32,
            nbytes=6 * 5632 * 256,
        )
        got = dict(zip(names, out))
        if "done" in got:
            self.done[last[0]] = got["done"]
        self.sent = got.get("sent")
        self.mid = got.get("mid")
        if self.sent is not None:
            self.first = lax.ppermute(self.sent, "obj", [(0, 1), (3, 2), (1, 0), (2, 3)])
        if self.mid is not None:
            self.second = lax.ppermute(self.mid, "obj", [(1, 2), (2, 1)])
        self.step += 1


def widen_kernel(info_ref, mine_ref, theirs_ref, out_ref, *, steps):
    at = pl.program_id(0)

    @pl.when(at < steps)
    def _():
        for c in range(mine_ref.shape[0]):
            out_ref[:, c * 128 : (c + 1) * 128] = mine_ref[c].astype(F32)

    @pl.when(at >= steps)
    def _():
        for c in range(theirs_ref.shape[0]):
            out_ref[:, c * 128 : (c + 1) * 128] = theirs_ref[c].astype(F32)


def widen(chain, info, mine, theirs, rows, columns, after=()):
    count = columns // 128
    half = rows // 2
    tile = 176 if half % 176 == 0 else min(256, half)
    steps = half // tile
    mine, theirs = (a.reshape(count, half, 128) for a in (mine, theirs))

    def at(i, info):
        return jnp.where(i < steps, info[3] * steps + i, (1 - info[3]) * steps + i - steps)

    return chain(
        functools.partial(widen_kernel, steps=steps),
        "widen",
        (2 * steps,),
        (mine, theirs),
        [
            spec((count, tile, 128), lambda i, *_: (0, jnp.minimum(i, steps - 1), 0)),
            spec((count, tile, 128), lambda i, *_: (0, jnp.maximum(i - steps, 0), 0)),
        ],
        [((rows, columns), F32)],
        [spec((tile, columns), lambda i, info: (at(i, info), 0))],
        scalars=(info,),
        after=after,
        mib=32,
        nbytes=6 * rows * columns,
    )[0]


def cast_kernel(in_ref, out_ref):
    out_ref[...] = in_ref[...].astype(F32)


def cast(chain, array, after=()):
    rows, columns = array.shape
    tile = 176 if rows % 256 else 256
    return chain(
        cast_kernel, "cast", (rows // tile,), (array,), [rows_spec(array.shape, tile)],
        [(array.shape, F32)], [rows_spec(array.shape, tile)], after=after,
    )[0]


def total_sum_kernel(in_ref, out_ref):
    out_ref[...] = jnp.sum(in_ref[...], axis=0)


def total_sum(chain, array):
    shape = array.shape[1:]
    return chain(
        total_sum_kernel, "total_sum", (1,), (array,), [const_spec(array.shape)], [(shape, F32)],
        [spec(shape, lambda i, *_: (0, 0))],
    )[0]


def plane_body(
    tokens,
    cotangent,
    segment_ids,
    mlm_mask,
    glm_prefix,
    glm_span,
    qkv_weight,
    out_weight,
    gate_weight,
    up_weight,
    down_weight,
    norm1_gain,
    norm1_bias,
    norm2_gain,
    norm2_bias,
):
    seq_here, length, width = tokens.shape
    data_ways = lax.axis_size("dp")
    objective_ways = lax.axis_size("obj")
    me = lax.axis_index("tensor").astype(jnp.int32)
    core = lax.axis_index("dp").astype(jnp.int32)
    at_obj = lax.axis_index("obj")
    edge = ((at_obj == 0) | (at_obj == objective_ways - 1)).astype(jnp.int32).reshape(1)
    block = length // 4
    units = gate_weight.shape[1]
    rows_all = mlm_mask.shape[0]
    masked_limit = seq_here * data_ways * (objective_ways // 2)
    row_ids = jnp.arange(rows_all, dtype=jnp.int32)
    counts = jnp.where(row_ids < masked_limit, jnp.sum(mlm_mask, axis=1), glm_span).astype(F32)
    weight_all = counts * rows_all / jnp.sum(counts)
    first_row = (at_obj * data_ways + core) * seq_here
    share_here = lax.dynamic_slice_in_dim(weight_all, first_row, seq_here)
    prefix_here = lax.dynamic_slice_in_dim(glm_prefix, first_row, seq_here)
    span_here = lax.dynamic_slice_in_dim(glm_span, first_row, seq_here)
    open_here = jnp.where(first_row < masked_limit, length, prefix_here)
    info = [jnp.stack([me, open_here[r], prefix_here[r] + span_here[r], core]) for r in range(2)]
    order = jnp.stack([2 * (me ^ r) + h for r, h in ORDER])
    share = [share_here[r : r + 1] for r in range(2)]
    cosine, sine = constant_tables(length)
    segc = [segment_ids[r].reshape(length, 1) for r in range(2)]
    segr = [segment_ids[r].reshape(1, length) for r in range(2)]
    gain1, bias1 = norm1_gain.reshape(1, width), norm1_bias.reshape(1, width)
    gain2, bias2 = norm2_gain.reshape(1, width), norm2_bias.reshape(1, width)
    weights = (gate_weight, up_weight, down_weight)
    chain = Chain()
    A, B = 0, 1

    ow_half = out_weight.shape[0] // 2
    ow_own = lax.dynamic_slice_in_dim(out_weight, core * ow_half, ow_half)
    owx, owy = pair_swap(ow_own, ow_own)

    def attention(r, after=()):
        return plane_attn_fwd(chain, info[r], r, tokens, qkv_weight, cosine, sine, segc[r], segr[r], after)

    def out_and_norm(r, ol_pieces, after=()):
        return plane_out_norm(
            chain, info[r], order, r, ol_pieces, out_weight, ow_mine, ow_other, tokens, gain1, bias1, after
        )

    qkv, ol, lse, hl, n1, rstd = {}, {}, {}, {}, {}, {}
    qkv[A], ol[A], lse[A] = attention(A)
    owra, owrb = forward(chain, owx, owy)
    olx, oly, olr = {}, {}, {}
    olx[A], oly[A] = pair_swap(ol[A], ol[A])
    qkv[B], ol[B], lse[B] = attention(B)
    ow_mine = ow_join(chain, (owx, owy, owra, owrb), after=(olx[A], oly[A]))
    ow_other = lax.ppermute(ow_mine, "dp", CORES)
    olr[A], ol[B] = forward(chain, olx[A], oly[A], (ol[B],))
    (ol[B],) = relay(chain, (ol[B],), after=olr[A])
    olx[B], oly[B] = pair_swap(ol[B], ol[B])
    hl[A], n1[A], rstd[A] = out_and_norm(A, (ol[A], olx[A], oly[A], *olr[A]))
    vec = const_spec((1, width))
    tile = block // OWN_STEPS
    full = rows_spec((block, width), tile)
    ff, fb, ib, rs1, rs2 = {}, {}, {}, {}, {}
    resid, rx, ry, rr = {}, {}, {}, {}

    def sums_of(own, first, second):
        return (own, first[0], first[1], second[0], second[1])

    def second_resid(r, after=()):
        return own_step(
            chain, resid_two_kernel, "resid_two", sums_of(ff[r][2], rs1[r], rs2[r]), (n1[r], gain1, bias1),
            [full, vec, vec], [((block, width), BF)], after,
        )[0]

    def second_norm(r, before, after=()):
        pieces = (resid[r], rx[r], ry[r], *rr[r])
        return plane_norm_two(
            chain, info[r], order, share[r], r, pieces, cotangent, gain2, bias2, before, after
        )

    def first_norm_back(r, after=()):
        return own_step(
            chain, norm_one_back_kernel, "norm_one_back", sums_of(fb[r][2], rs1[r], rs2[r]),
            (dffn[r], n1[r], rstd[r], gain1),
            [rows_spec((block, width), tile, 3 * OWN_STEPS), full, rows_spec((block, HEAD_DIM), tile), vec],
            [((block, width), BF), ((block, width), F32), ((2, width), F32)], after,
        )

    olr[B] = forward(chain, olx[B], oly[B])
    sent, kept_a = plane_ffn_fwd(chain, None, hl[A], weights, ())
    rs1[A], ff[A] = pair_swap(*sent[:2]), sent[2:]
    hl[B], n1[B], rstd[B] = out_and_norm(B, (ol[B], olx[B], oly[B], *olr[B]))
    rs2[A] = pair_swap(*middle(chain, rs1[A], ff[A][0], ff[A][1]))
    sent, kept = plane_ffn_fwd(chain, True, hl[B], weights, ())
    resid[A] = second_resid(A)
    rx[A], ry[A] = pair_swap(resid[A], resid[A])
    ff[B], kept_b = plane_ffn_fwd(chain, False, hl[B], weights, (*kept, *sent))
    al, slopes = {A: kept_a[0], B: kept_b[0]}, {A: kept_a[1:], B: kept_b[1:]}
    rr[A] = forward(chain, rx[A], ry[A])
    rs1[B] = pair_swap(*relay(chain, ff[B][3:], after=rr[A]))

    sums2, dffn, dgu, sums1, dr1, dattn, dax, day, dar = {}, {}, {}, {}, {}, {}, {}, {}, {}
    pieces, dqkv, dx, dxx, dxy, dxr, outs = {}, {}, {}, {}, {}, {}, {}

    def attention_back(r, after=()):
        pieces[r] = (dattn[r], dax[r], day[r], *dar[r])
        return plane_attn_bwd(
            chain, info[r], qkv[r], pieces[r], out_weight, lse[r], cosine, sine, segc[r], segr[r], after
        )

    def input_back_sums(r, after=()):
        x1, y1, r1b, r2a, own = plane_input_back(chain, order, dqkv[r], qkv_weight, after)
        ib[r] = (r1b, r2a, own)
        rs1[r] = pair_swap(x1, y1)

    def input_grad_own(r, after=()):
        return own_step(
            chain, input_grad_kernel, "input_grad", sums_of(ib[r][2], rs1[r], rs2[r]), (dr1[r],), [full],
            [((block, width), BF)], after,
        )[0]

    theirs = {}

    def begin_finish(name):
        theirs[name] = lax.ppermute(line.done[name], "dp", CORES)

    def finish_matrix(name, rows, columns, after=()):
        outs[name] = widen(chain, info[B], line.done[name], theirs[name], rows, columns, after)

    def middle_sums(r, after=()):
        part = fb[r] if r not in ib else ib[r]
        rs2[r] = pair_swap(*middle(chain, rs1[r], part[0], part[1], after))

    line = Line(chain, edge)
    activations, sums2[A], dffn[A] = second_norm(A, None)
    sent, kept = plane_ffn_bwd(chain, True, dffn[A], slopes[A], weights, ())
    rs1[A] = pair_swap(*sent)
    rs2[B] = pair_swap(*middle(chain, rs1[B], ff[B][0], ff[B][1]))
    fb[A], dgu[A] = plane_ffn_bwd(chain, False, dffn[A], slopes[A], weights, kept)
    resid[B] = second_resid(B)
    rx[B], ry[B] = pair_swap(resid[B], resid[B])
    middle_sums(A)
    rr[B] = forward(chain, rx[B], ry[B])
    dattn[A], dr1[A], sums1[A] = first_norm_back(A)
    dax[A], day[A] = pair_swap(dattn[A], dattn[A])
    activations, sums2[B], dffn[B] = second_norm(B, activations)
    down_update = grad_plain_columns(chain, (al[A], al[B]), (dffn[A], dffn[B]))
    down_sum = lax.psum(down_update, ("obj", "dp"))
    dar[A] = forward(chain, dax[A], day[A])
    sent, dgu[B] = plane_ffn_bwd(chain, None, dffn[B], slopes[B], weights, ())
    fb[B] = sent[2:]
    rs1[B] = pair_swap(*sent[:2])
    chain.close(*dar[A])
    gate_send, gate_keep = grad_rows(chain, info[B], (hl[A], hl[B]), (dgu[A][0], dgu[B][0]))
    gate_got = lax.ppermute(gate_send, "dp", CORES)
    line.add("gate", gate_keep, gate_got, 2)
    middle_sums(B)
    up_send, up_keep = grad_rows(chain, info[B], (hl[A], hl[B]), (dgu[A][1], dgu[B][1]))
    up_got = lax.ppermute(up_send, "dp", CORES)
    line.add("up", up_keep, up_got, 2)
    chain.close(gate_got)
    dattn[B], dr1[B], sums1[B] = first_norm_back(B)
    dax[B], day[B] = pair_swap(dattn[B], dattn[B])
    chain.close(up_got)
    line.advance()
    dqkv[A] = attention_back(A)
    dar[B] = forward(chain, dax[B], day[B])
    input_back_sums(A)
    line.advance()
    dqkv[B] = attention_back(B)
    line.advance()
    middle_sums(A)
    qkv_send, qkv_keep = grad_rows(chain, info[B], (tokens, tokens), (dqkv[A], dqkv[B]), after=(down_sum,))
    qkv_got = lax.ppermute(qkv_send, "dp", CORES)
    line.add("qkv", qkv_keep, qkv_got, 2)
    dx[A] = input_grad_own(A)
    dxx[A], dxy[A] = pair_swap(dx[A], dx[A])
    line.advance()
    input_back_sums(B)
    chain.close(qkv_got, dxx[A], dxy[A])
    out_send, out_keep = plane_grad_out(chain, info[B], (ol[A], ol[B]), (pieces[A], pieces[B]))
    line.advance()
    out_got = lax.ppermute(out_send, "dp", CORES)
    line.add("out", out_keep, out_got, 1)
    middle_sums(B)
    outs["down"] = cast(chain, down_sum)
    line.advance()
    chain.close(out_got)
    begin_finish("gate")
    dxr[A] = forward(chain, dxx[A], dxy[A])
    dx[B] = input_grad_own(B)
    dxx[B], dxy[B] = pair_swap(dx[B], dx[B])
    chain.close(theirs["gate"])
    line.advance()
    begin_finish("up")
    finish_matrix("gate", width, units)
    input_grad = plane_place(chain, info[A], A, (dx[A], dxx[A], dxy[A], *dxr[A]), tokens.shape, None)
    dxr[B] = forward(chain, dxx[B], dxy[B])
    mine = (me == 0).astype(F32)
    sums = jnp.concatenate([sums1[A] + sums1[B], (sums2[A] + sums2[B]) * mine])
    every_sum = lax.all_gather(sums, ("obj", "dp", "tensor"))
    line.advance()
    finish_matrix("up", width, units)
    input_grad = plane_place(chain, info[B], B, (dx[B], dxx[B], dxy[B], *dxr[B]), tokens.shape, input_grad)
    line.advance()
    begin_finish("qkv")
    sums = total_sum(chain, every_sum)
    finish_matrix("qkv", width, qkv_weight.shape[1])
    line.advance()
    begin_finish("out")
    finish_matrix("out", out_weight.shape[0], width)

    return (
        activations,
        input_grad,
        outs["qkv"],
        outs["out"],
        outs["gate"],
        outs["up"],
        outs["down"],
        sums[0],
        sums[1],
        sums[2],
        sums[3],
    )


def body(*args):
    if plane_case(args[0].shape, args[7].shape, args[10].shape):
        return plane_body(*args)
    return general_body(*args)


def solution(mesh):
    rows3 = P(("obj", "dp"), None, None)
    in_specs = (
        rows3,
        rows3,
        P(("obj", "dp"), None),
        P(),
        P(),
        P(),
        P(None, "tensor"),
        P("tensor", None),
        P(None, "tensor"),
        P(None, "tensor"),
        P("tensor", None),
        P(),
        P(),
        P(),
        P(),
    )
    out_specs = (
        rows3,
        rows3,
        P(None, "tensor"),
        P("tensor", None),
        P(None, "tensor"),
        P(None, "tensor"),
        P("tensor", None),
        P(),
        P(),
        P(),
        P(),
    )
    return jax.shard_map(body, mesh=mesh, in_specs=in_specs, out_specs=out_specs, check_vma=False)
```
